32 devices in a mesh: section: 2 (over core), tile: 16 (over z, y, x).
Axes of the slice: x: 2, y: 2, z: 4, core: 2. Of those that a mesh axis runs over, the one named last changes fastest.
Arguments:
- aerial_patch_grid: bfloat16 [384, 384, 768], P('tile'), may hold values from -6 to 6
- patch_conv_weight: bfloat16 [3, 4, 4, 96], replicated, may hold values from -0.875 to 0.875
- patch_bias: float32 [96], replicated, may hold values from -3 to 3
- merging_conv_weight: bfloat16 [2, 2, 96, 192], replicated, may hold values from -0.3125 to 0.3125
- merge_bias: float32 [192], replicated, may hold values from -3 to 3
- down_weight: bfloat16 [3, 3, 192, 384], replicated, may hold values from -0.15625 to 0.15625
- down_bias: float32 [384], replicated, may hold values from -3 to 3
- norm_gain: float32 [384], replicated, may hold values from 0.1 to 1.9
- spectral_filter: bfloat16 [384, 2, 384, 384], P('tile'), may hold values from -6 to 6
Outputs:
- block_output: bfloat16 [384, 384, 384], P('section', 'tile')
The draws below stay inside these ranges and needn't reach their ends.
All inputs are finite; a program needn't handle non-finite values.
Results may differ from the reference program's by a relative error of at most 0.015.
Values may be sent and summed in bfloat16 or wider, within the bound.
No kernel may reach another device: no remote copies, remote signals or barrier semaphores. Data moves between devices by JAX's collectives and lax.ppermute only.
A program may use at most 192 MiB of HBM per device.

```python
import math
import jax
import jax.numpy as jnp
from jax import lax

BANDS = 3
C1 = 96
C2 = 192
C = 384
FH = 384
FW = 384
IH = 6144
IW = 6144


def steps_of(stream_key, extent, split, least, high):
    loudness = 1.0
    for position, parts in split:
        steps = jax.random.uniform(jax.random.fold_in(jax.random.fold_in(stream_key, 6), position), (parts,), jnp.float32, least / len(split), high / len(split))
        loudness = loudness * jnp.repeat(jnp.exp(steps), extent[position] // parts).reshape((-1,) + (1,) * (len(extent) - 1 - position))
    return loudness


def noise(stream_key, dims, spread, reach, shards=(), kind=jnp.bfloat16):
    values = jax.random.normal(stream_key, dims, jnp.float32) * spread
    if len(shards) > 0:
        values = steps_of(stream_key, dims, shards, -0.22, 0.18) * values
    return jnp.clip(values, min=-reach, max=reach).astype(kind)


def setup_inputs(seed: int = 0) -> dict:
    arg_keys = jax.random.split(jax.random.key(seed), 10)
    aerial_patch_grid = noise(arg_keys[0], (FH, FW, 256 * BANDS), 1.0, 6.0, ((0, 16),))
    patch_conv_weight = noise(arg_keys[1], (BANDS, 4, 4, C1), (BANDS * 16) ** -0.5, 0.875)
    patch_bias = noise(arg_keys[2], (C1,), 0.5, 3.0, (), jnp.float32)
    merging_conv_weight = noise(arg_keys[3], (2, 2, C1, C2), (4 * C1) ** -0.5, 0.3125)
    merge_bias = noise(arg_keys[4], (C2,), 0.5, 3.0, (), jnp.float32)
    down_weight = noise(arg_keys[5], (3, 3, C2, C), (9 * C2) ** -0.5, 0.15625)
    down_bias = noise(arg_keys[6], (C,), 0.5, 3.0, (), jnp.float32)
    norm_gain = jnp.clip(1.0 + 0.18 * jax.random.normal(arg_keys[7], (C,), jnp.float32), 0.1, 1.9)
    spectral_filter = noise(arg_keys[8], (C, 2, FH, FW), 1.0, 6.0, ((0, 16),))
    return dict(aerial_patch_grid=aerial_patch_grid, patch_conv_weight=patch_conv_weight, patch_bias=patch_bias, merging_conv_weight=merging_conv_weight, merge_bias=merge_bias, down_weight=down_weight, down_bias=down_bias, norm_gain=norm_gain, spectral_filter=spectral_filter)


EPSILON = 1e-05

def fourier_tables(length):
    indices = jnp.arange(length, dtype=jnp.int32)
    product = indices[:, None] * indices[None, :] % length
    angles = product.astype(jnp.float32) * (2.0 * math.pi / length)
    return (jnp.cos(angles).astype(jnp.bfloat16), jnp.sin(angles).astype(jnp.bfloat16))

def stem_block(padded_image, block_index, block_rows, patch_conv_weight, patch_bias, merging_conv_weight, merge_bias, down_weight, down_bias):
    band_count = padded_image.shape[0]
    image_rows = 16 * block_rows + 16
    row_begin = (block_index * (16 * block_rows)).astype(jnp.int32)
    piece = lax.dynamic_slice_in_dim(padded_image, row_begin, image_rows, 1).astype(jnp.float32)
    image_cols = piece.shape[2]
    blocks = piece.reshape(band_count, image_rows // 4, 4, image_cols // 4, 4)
    initial_layer = jnp.einsum('brawq,baqc->rwc', blocks, patch_conv_weight.astype(jnp.float32))
    initial_layer = jax.nn.gelu(initial_layer + patch_bias, approximate=True).astype(jnp.bfloat16)
    one_rows, one_cols, one_width = initial_layer.shape
    pairs = initial_layer.astype(jnp.float32).reshape(one_rows // 2, 2, one_cols // 2, 2, one_width)
    layer_two = jnp.einsum('rawqk,aqkc->rwc', pairs, merging_conv_weight.astype(jnp.float32))
    layer_two = jax.nn.gelu(layer_two + merge_bias, approximate=True).astype(jnp.bfloat16)
    global_rows = block_index * (2 * block_rows) - 2 + jnp.arange(2 * block_rows + 2, dtype=jnp.int32)
    layer_two = jnp.where((global_rows >= 0)[:, None, None], layer_two, jnp.zeros_like(layer_two))
    padded = jnp.pad(layer_two, ((0, 0), (1, 0), (0, 0)))
    out_cols = layer_two.shape[1] // 2
    summed = jnp.zeros((down_weight.shape[3], block_rows, out_cols), jnp.float32)
    for row_tap in range(3):
        for col_tap in range(3):
            window = padded[1 + row_tap:1 + row_tap + 2 * block_rows:2, col_tap:col_tap + 2 * out_cols:2, :]
            summed = summed + jnp.einsum('rwk,kc->crw', window.astype(jnp.float32), down_weight[row_tap, col_tap].astype(jnp.float32))
    return (summed + down_bias[:, None, None]).astype(jnp.bfloat16)

def layer_norm(features, norm_gain):
    values = features.astype(jnp.float32)
    mean_value = lax.optimization_barrier(jnp.mean(values, axis=0, keepdims=True))
    centered = values - mean_value
    variance = lax.optimization_barrier(jnp.mean(centered * centered, axis=0, keepdims=True))
    return (norm_gain[:, None, None] * centered * lax.rsqrt(variance + EPSILON)).astype(jnp.bfloat16)

def filter_channel(field, kernel, forward_table, forward_h, inverse_h, inverse_table, norm_scale):
    row_spectrum = jnp.einsum('hx,xqw->hqw', field.astype(jnp.float32), forward_table.astype(jnp.float32)).astype(jnp.bfloat16)
    spectrum = jnp.einsum('puqh,hqw->puw', forward_h.astype(jnp.float32), row_spectrum.astype(jnp.float32)).astype(jnp.bfloat16)
    spec_real = spectrum[0].astype(jnp.float32)
    spec_imag = spectrum[1].astype(jnp.float32)
    filter_real = kernel[0].astype(jnp.float32)
    filter_imag = kernel[1].astype(jnp.float32)
    weighted = jnp.stack([filter_real * spec_real - filter_imag * spec_imag, filter_real * spec_imag + filter_imag * spec_real], axis=0).astype(jnp.bfloat16)
    back_rows = jnp.einsum('qhpu,puw->hqw', inverse_h.astype(jnp.float32), weighted.astype(jnp.float32)).astype(jnp.bfloat16)
    result = jnp.einsum('hqw,qwv->hv', back_rows.astype(jnp.float32), inverse_table.astype(jnp.float32))
    return (result * norm_scale).astype(jnp.bfloat16)

def reference(aerial_patch_grid, patch_conv_weight, patch_bias, merging_conv_weight, merge_bias, down_weight, down_bias, norm_gain, spectral_filter):
    block_rows = math.gcd(FH, 8)
    block_count = FH // block_rows
    image = aerial_patch_grid.reshape(FH, FW, BANDS, 16, 16)
    image = jnp.transpose(image, (2, 0, 3, 1, 4)).reshape(BANDS, IH, IW)
    padded_image = jnp.pad(image, ((0, 0), (16, 0), (0, 0)))

    def one_block(block_index):
        return stem_block(padded_image, block_index, block_rows, patch_conv_weight, patch_bias, merging_conv_weight, merge_bias, down_weight, down_bias)
    pieces = lax.map(one_block, jnp.arange(block_count, dtype=jnp.int32))
    features = jnp.transpose(pieces, (1, 0, 2, 3)).reshape(C, FH, FW)
    normed = layer_norm(features, norm_gain)
    cos_h, sin_h = fourier_tables(FH)
    cos_w, sin_w = fourier_tables(FW)
    forward_table = jnp.stack([cos_w, -sin_w], axis=1)
    forward_h = jnp.stack([jnp.stack([cos_h, sin_h], axis=1), jnp.stack([-sin_h, cos_h], axis=1)], axis=0)
    inverse_h = jnp.stack([jnp.stack([cos_h, -sin_h], axis=1), jnp.stack([sin_h, cos_h], axis=1)], axis=0)
    inverse_table = jnp.stack([cos_w, -sin_w], axis=0)
    norm_scale = 1.0 / (FH * FW)

    def one_channel(operands):
        return filter_channel(operands[0], operands[1], forward_table, forward_h, inverse_h, inverse_table, norm_scale)
    filtered = lax.map(one_channel, (normed, spectral_filter))
    return (features.astype(jnp.float32) + filtered.astype(jnp.float32)).astype(jnp.bfloat16)
```

```python
import functools
import math

import jax
import jax.numpy as jnp
from jax import lax
from jax.experimental import pallas as pl
from jax.experimental.pallas import tpu as pltpu
from jax.sharding import PartitionSpec as P

EPSILON = 1e-05


def from_behind(block, axis, distance):
    devices = range(lax.axis_size(axis))
    route = [(i - distance, i) for i in devices if i - distance in devices]
    return lax.ppermute(block, axis, route)


def fourier_tables(length):
    indices = jnp.arange(length, dtype=jnp.int32)
    product = indices[:, None] * indices[None, :] % length
    angles = product.astype(jnp.float32) * (2.0 * math.pi / length)
    return (jnp.cos(angles).astype(jnp.bfloat16), jnp.sin(angles).astype(jnp.bfloat16))


def patch_kernel_matrix(patch_conv_weight):
    identity = jnp.eye(4, dtype=jnp.float32)
    larger = jnp.einsum(
        "baqk,xy,uv->bxauqyvk", patch_conv_weight.astype(jnp.float32), identity, identity
    )
    band_count = patch_conv_weight.shape[0]
    width = patch_conv_weight.shape[3]
    return larger.reshape(band_count * 256, 16 * width).astype(jnp.bfloat16)


def merging_kernel_matrix(merging_conv_weight):
    identity = jnp.eye(2, dtype=jnp.float32)
    larger = jnp.einsum(
        "aqjk,xy,uv->xauqjyvk", merging_conv_weight.astype(jnp.float32), identity, identity
    )
    in_width = merging_conv_weight.shape[2]
    out_width = merging_conv_weight.shape[3]
    return larger.reshape(16 * in_width, 4 * out_width).astype(jnp.bfloat16)


def down_matrices(down_weight):
    nothing = jnp.zeros_like(down_weight[0, 0])
    in_width = down_weight.shape[2]
    out_width = down_weight.shape[3]

    def arrange(entries):
        return jnp.stack(
            [jnp.stack(entries[0], axis=0), jnp.stack(entries[1], axis=0)], axis=0
        ).reshape(4 * in_width, out_width)

    own_taps = arrange(
        [[down_weight[1, 1], down_weight[1, 2]], [down_weight[2, 1], down_weight[2, 2]]]
    )
    upper_taps = arrange([[nothing, nothing], [down_weight[0, 1], down_weight[0, 2]]])
    left_taps = arrange([[nothing, down_weight[1, 0]], [nothing, down_weight[2, 0]]])
    corner_taps = arrange([[nothing, nothing], [nothing, down_weight[0, 0]]])
    return (own_taps, upper_taps, left_taps, corner_taps)


def stem_layers(aerial_patch_grid, patch_conv_weight, patch_bias, merging_conv_weight, merge_bias):
    initial_layer = jnp.einsum(
        "zji,if->zjf",
        aerial_patch_grid,
        patch_kernel_matrix(patch_conv_weight),
        preferred_element_type=jnp.float32,
    )
    initial_layer = jax.nn.gelu(initial_layer + jnp.tile(patch_bias, 16), approximate=True).astype(
        jnp.bfloat16
    )
    layer_two = jnp.einsum(
        "zji,if->zjf",
        initial_layer,
        merging_kernel_matrix(merging_conv_weight),
        preferred_element_type=jnp.float32,
    )
    return jax.nn.gelu(layer_two + jnp.tile(merge_bias, 4), approximate=True).astype(jnp.bfloat16)


def rim_above(extended):
    return from_behind(extended[-1:], "tile", 1)


def down_conv(upper_rim, extended, down_weight, down_bias):
    stacked = jnp.concatenate([upper_rim, extended], axis=0)
    own_taps, upper_taps, left_taps, corner_taps = down_matrices(down_weight)
    summed = jnp.einsum(
        "rwk,kc->crw", stacked[1:, 1:], own_taps, preferred_element_type=jnp.float32
    )
    summed = summed + jnp.einsum(
        "rwk,kc->crw", stacked[:-1, 1:], upper_taps, preferred_element_type=jnp.float32
    )
    summed = summed + jnp.einsum(
        "rwk,kc->crw", stacked[1:, :-1], left_taps, preferred_element_type=jnp.float32
    )
    summed = summed + jnp.einsum(
        "rwk,kc->crw", stacked[:-1, :-1], corner_taps, preferred_element_type=jnp.float32
    )
    return (summed + down_bias[:, None, None]).astype(jnp.bfloat16)


def layer_norm(features, norm_gain):
    values = features.astype(jnp.float32)
    mean_value = jnp.mean(values, axis=0, keepdims=True)
    centered = values - mean_value
    variance = jnp.mean(centered * centered, axis=0, keepdims=True)
    return (norm_gain[:, None, None] * centered * lax.rsqrt(variance + EPSILON)).astype(
        jnp.bfloat16
    )


def filter_columns(row_spectrum, kernel, forward_h, inverse_h):
    spectrum = jnp.einsum(
        "puqh,chqw->cpuw", forward_h, row_spectrum, preferred_element_type=jnp.float32
    ).astype(jnp.bfloat16)
    spec_real = spectrum[:, 0].astype(jnp.float32)
    spec_imag = spectrum[:, 1].astype(jnp.float32)
    filter_real = kernel[:, 0].astype(jnp.float32)
    filter_imag = kernel[:, 1].astype(jnp.float32)
    weighted = jnp.stack(
        [
            filter_real * spec_real - filter_imag * spec_imag,
            filter_real * spec_imag + filter_imag * spec_real,
        ],
        axis=1,
    ).astype(jnp.bfloat16)
    return jnp.einsum(
        "qhpu,cpuw->chqw", inverse_h, weighted, preferred_element_type=jnp.float32
    ).astype(jnp.bfloat16)


def general_local(
    aerial_patch_grid,
    patch_conv_weight,
    patch_bias,
    merging_conv_weight,
    merge_bias,
    down_weight,
    down_bias,
    norm_gain,
    spectral_filter,
):
    section_index = lax.axis_index("section")
    first_section = section_index == 0
    field_cols = aerial_patch_grid.shape[1]
    channels = down_weight.shape[3]
    group_width = spectral_filter.shape[0]
    full_rows = spectral_filter.shape[2]
    half_channels = channels // 2
    cell_half = field_cols // 2
    image_part = lax.dynamic_slice_in_dim(
        aerial_patch_grid, section_index * cell_half, cell_half, 1
    )
    layer_two = stem_layers(
        image_part, patch_conv_weight, patch_bias, merging_conv_weight, merge_bias
    )
    left_column = from_behind(layer_two[:, -1:], "section", 1)
    extended = jnp.concatenate([left_column, layer_two], axis=1)
    upper_rim = rim_above(extended)
    feature_half = down_conv(upper_rim, extended, down_weight, down_bias)
    features = lax.all_gather(feature_half, "section", axis=2, tiled=True)
    normed = layer_norm(features, norm_gain)
    cos_h, sin_h = fourier_tables(full_rows)
    cos_w, sin_w = fourier_tables(field_cols)
    forward_table = jnp.stack([cos_w, -sin_w], axis=1)
    forward_h = jnp.stack(
        [jnp.stack([cos_h, sin_h], axis=1), jnp.stack([-sin_h, cos_h], axis=1)], axis=0
    )
    inverse_h = jnp.stack(
        [jnp.stack([cos_h, -sin_h], axis=1), jnp.stack([sin_h, cos_h], axis=1)], axis=0
    )
    inverse_table = jnp.stack([cos_w, -sin_w], axis=0)
    norm_scale = 1.0 / (full_rows * field_cols)
    fields = lax.all_to_all(normed, "tile", split_axis=0, concat_axis=1, tiled=True)

    def whole_filter():
        frequency_rows = jnp.einsum(
            "chx,xqw->chqw", fields, forward_table, preferred_element_type=jnp.float32
        ).astype(jnp.bfloat16)
        back_rows = filter_columns(frequency_rows, spectral_filter, forward_h, inverse_h)
        result = jnp.einsum(
            "chqw,qwv->chv", back_rows, inverse_table, preferred_element_type=jnp.float32
        )
        return (result * norm_scale).astype(jnp.bfloat16)

    def empty_fields():
        return jnp.zeros((group_width, full_rows, field_cols), jnp.bfloat16)

    filtered_fields = lax.cond(first_section, empty_fields, whole_filter)
    rows_back = lax.all_to_all(filtered_fields, "tile", split_axis=1, concat_axis=0, tiled=True)
    returned = from_behind(rows_back[:half_channels], "section", -1)
    filtered = jnp.where(first_section, returned, rows_back[half_channels:])
    own_part = lax.dynamic_slice_in_dim(features, section_index * half_channels, half_channels, 0)
    return (own_part.astype(jnp.float32) + filtered.astype(jnp.float32)).astype(jnp.bfloat16)


DEVICES = ("tile", "section")
GELU_LINEAR = 2.0 * math.sqrt(2.0 / math.pi)
GELU_CUBIC = 4.0 * 0.044715 * GELU_LINEAR
ONES = 16


def split_bias(bias):
    parts = []
    left = bias
    for _ in range(3):
        part = left.astype(jnp.bfloat16)
        parts.append(part)
        left = left - part.astype(jnp.float32)
    parts += [jnp.zeros_like(parts[0])] * (ONES - 3)
    return jnp.stack(parts, axis=1)


def stem_weights(
    patch_conv_weight, patch_bias, merging_conv_weight, merge_bias, down_weight, down_bias
):
    half = jnp.asarray(0.5, jnp.bfloat16)
    width = patch_conv_weight.shape[3]
    bands = patch_conv_weight.shape[0]
    identity = jnp.eye(4, dtype=jnp.bfloat16)
    first = jnp.einsum("baqk,vw->vkbawq", patch_conv_weight, identity)
    first = first.reshape(4 * width, bands * 64) * half
    first = jnp.concatenate([first, split_bias(jnp.tile(0.5 * patch_bias, 4))], axis=1)
    merged = merging_conv_weight.shape[3]
    second = merging_conv_weight.reshape(4 * width, merged).T * half
    second = jnp.concatenate([second, split_bias(0.5 * merge_bias)], axis=1)
    taps = [(1, 1), (1, 2), (2, 1), (2, 2), (1, 0), (2, 0), (0, 1), (0, 2), (0, 0)]
    third = jnp.concatenate([down_weight[a, q] for a, q in taps], axis=0).T
    third = jnp.concatenate([third, split_bias(down_bias)], axis=1)
    return first, second, third


def half_gelu(h):
    return h + h * jnp.tanh(h * (GELU_LINEAR + GELU_CUBIC * (h * h)))


def stem_kernel(
    place_ref, x_ref, halo_ref, w1_ref, w2_ref, w3_ref, gain_ref, normed_ref, feat_ref, field
):
    step = pl.program_id(0)
    rows, cols, depth = x_ref.shape
    bands = depth // 256
    channels = w3_ref.shape[0]
    merged = w2_ref.shape[0]
    group = normed_ref.shape[2] // rows
    cells = rows * cols
    w1 = w1_ref[...]
    w2 = w2_ref[...]

    def ones(n):
        return jnp.where(lax.broadcasted_iota(jnp.int32, (ONES, n), 0) < 3, 1.0, 0.0).astype(
            jnp.bfloat16
        )

    def layer_one(turned, offsets):
        n = turned.shape[1]
        parts = [turned[o : o + 64] for o in offsets] + [ones(n)]
        h = jnp.dot(w1, jnp.concatenate(parts, axis=0), preferred_element_type=jnp.float32)
        return half_gelu(h).astype(jnp.bfloat16)

    def layer_two(upper, lower, y):
        n = upper.shape[1]
        span = slice(2 * y * (w1.shape[0] // 4), 2 * (y + 1) * (w1.shape[0] // 4))
        stacked = jnp.concatenate([upper[span], lower[span], ones(n)], axis=0)
        return half_gelu(jnp.dot(w2, stacked, preferred_element_type=jnp.float32))

    def shifted(values):
        lanes = lax.broadcasted_iota(jnp.int32, values.shape, 1)
        moved = pltpu.roll(values, 1, 1)
        return jnp.where(lax.rem(lanes, cols) == 0, 0.0, moved)

    def put(block, lanes, values):
        field[block * merged : (block + 1) * merged, lanes] = values.astype(jnp.bfloat16)

    first_row = slice(0, cols)
    last_row = slice(cells - cols, cells)
    later_rows = slice(cols, cells)
    earlier_rows = slice(0, cells - cols)

    @pl.when(step == 0)
    def _():
        field[9 * merged : 9 * merged + ONES, :] = ones(cells)
        turned = halo_ref[...].T
        keep = place_ref[1].astype(jnp.float32)
        upper, lower = (
            layer_one(turned, [128 * b + 64 * a for b in range(bands)]) for a in range(2)
        )
        put(6, first_row, layer_two(upper, lower, 0) * keep)
        right = layer_two(upper, lower, 1) * keep
        put(7, first_row, right)
        put(8, first_row, shifted(right))

    @pl.when(step > 0)
    def _():
        for source, target in ((2, 6), (3, 7), (5, 8)):
            field[target * merged : (target + 1) * merged, first_row] = field[
                source * merged : (source + 1) * merged, last_row
            ]

    turned = x_ref[...].reshape(cells, depth).T
    for x in range(2):
        upper, lower = (
            layer_one(turned, [256 * b + 64 * (2 * x + a) for b in range(bands)])
            for a in range(2)
        )
        left = layer_two(upper, lower, 0)
        right = layer_two(upper, lower, 1)
        put(2 * x, slice(None), left)
        put(2 * x + 1, slice(None), right)
        moved = shifted(right)
        put(4 + x, slice(None), moved)
        if x == 1:
            put(6, later_rows, left[:, earlier_rows])
            put(7, later_rows, right[:, earlier_rows])
            put(8, later_rows, moved[:, earlier_rows])

    features = jnp.dot(w3_ref[...], field[...], preferred_element_type=jnp.float32).astype(
        jnp.bfloat16
    )
    for r in range(rows):
        feat_ref[r] = features[:, r * cols : (r + 1) * cols]
    values = features.astype(jnp.float32)
    centered = values - jnp.mean(values, axis=0, keepdims=True)
    variance = jnp.mean(centered * centered, axis=0, keepdims=True)
    normed = gain_ref[...] * (centered * lax.rsqrt(variance + EPSILON))
    pair = 2 * group
    index = lax.broadcasted_iota(jnp.int32, (pair, cols), 0)
    for t in range(channels // pair):
        one = normed[pair * t : pair * (t + 1), :cols]
        two = normed[pair * t : pair * (t + 1), cols:]
        normed_ref[2 * t, 0] = jnp.where(index < group, one, pltpu.roll(two, group, 0)).astype(
            jnp.bfloat16
        )
        normed_ref[2 * t + 1, 0] = jnp.where(
            index < group, pltpu.roll(one, group, 0), two
        ).astype(jnp.bfloat16)


def stem(image, halo, place, weights, norm_gain, devices):
    tile_rows, cols, depth = image.shape
    rows = tile_rows // 2
    first, second, third = weights
    channels = third.shape[0]
    merged = second.shape[0]
    steps = rows // 2
    group = channels // devices
    gain = jnp.broadcast_to(norm_gain[:, None], (channels, 2 * cols)).astype(jnp.float32)

    def whole(array):
        return pl.BlockSpec(array.shape, lambda i, place: (0,) * array.ndim)

    operands = (halo, first, second, third, gain)
    macs = rows * cols * (16 * 208 * 96 + 4 * 400 * merged + third.shape[1] * channels)
    return pl.pallas_call(
        stem_kernel,
        grid_spec=pltpu.PrefetchScalarGridSpec(
            num_scalar_prefetch=1,
            grid=(steps,),
            in_specs=[pl.BlockSpec((2, cols, depth), lambda i, place: (place[0] + i, 0, 0))]
            + [whole(a) for a in operands],
            out_specs=[
                pl.BlockSpec((devices, 1, 2 * group, cols), lambda i, place: (0, i, 0, 0)),
                pl.BlockSpec((2, channels, cols), lambda i, place: (i, 0, 0)),
            ],
            scratch_shapes=[pltpu.VMEM((9 * merged + ONES, 2 * cols), jnp.bfloat16)],
        ),
        out_shape=[
            jax.ShapeDtypeStruct((devices, steps, 2 * group, cols), jnp.bfloat16),
            jax.ShapeDtypeStruct((rows, channels, cols), jnp.bfloat16),
        ],
        compiler_params=pltpu.CompilerParams(vmem_limit_bytes=56 * 1024 * 1024),
        cost_estimate=pl.CostEstimate(
            flops=2 * macs, bytes_accessed=rows * cols * 3000, transcendentals=0
        ),
        name="stem",
    )(place, image, *operands)


def symmetric_kernel(place_ref, f_ref, turn_w_ref, turn_u_ref, g_ref):
    width = g_ref.shape[3]
    for part in range(2):
        block = f_ref[0, part]
        across = jnp.dot(block, turn_w_ref[...], preferred_element_type=jnp.float32)
        turned = jnp.dot(
            turn_u_ref[...], across.astype(jnp.bfloat16), preferred_element_type=jnp.float32
        )
        own = block[:, :width].astype(jnp.float32)
        g_ref[0, part] = 0.5 * (own + turned if part == 0 else own - turned)


def symmetric_filter(spectral_filter, place, group, width):
    full_rows, full_cols = spectral_filter.shape[2:]
    u = jnp.arange(full_rows, dtype=jnp.int32)
    w = jnp.arange(full_cols, dtype=jnp.int32)
    turn_u = ((u[:, None] + u[None, :]) % full_rows == 0).astype(jnp.bfloat16)
    turn_w = ((w[:, None] + w[None, :width]) % full_cols == 0).astype(jnp.bfloat16)
    return pl.pallas_call(
        symmetric_kernel,
        grid_spec=pltpu.PrefetchScalarGridSpec(
            num_scalar_prefetch=1,
            grid=(group,),
            in_specs=[
                pl.BlockSpec(
                    (1, 2, full_rows, full_cols), lambda i, place: (place[0] + i, 0, 0, 0)
                ),
                pl.BlockSpec(turn_w.shape, lambda i, place: (0, 0)),
                pl.BlockSpec(turn_u.shape, lambda i, place: (0, 0)),
            ],
            out_specs=pl.BlockSpec((1, 2, full_rows, width), lambda i, place: (i, 0, 0, 0)),
        ),
        out_shape=jax.ShapeDtypeStruct((group, 2, full_rows, width), jnp.float32),
        compiler_params=pltpu.CompilerParams(vmem_limit_bytes=32 * 1024 * 1024),
        cost_estimate=pl.CostEstimate(
            flops=8 * group * full_rows * full_cols * width,
            bytes_accessed=group * full_rows * width * 14,
            transcendentals=0,
        ),
        name="symmetric_filter",
    )(place, spectral_filter, turn_w, turn_u)


def to_lane_tiles(target, rows, values):
    for j in range(target.shape[0]):
        target[j, rows, :] = values[:, 128 * j : 128 * (j + 1)]


def from_lane_tiles(source, rows):
    return jnp.concatenate([source[j, rows, :] for j in range(source.shape[0])], axis=1)


def filter_kernel(
    first, norm_scale, fields_ref, g_ref, row_table_ref, fwd_ref, inv_ref, back_ref, out_ref, held, made
):
    step = pl.program_id(0)
    full_rows = fwd_ref.shape[0] // 2
    width = g_ref.shape[3]
    group = held.shape[1] // full_rows
    count = made.shape[1] // full_rows
    per_step = g_ref.shape[0]

    @pl.when(step == 0)
    def _():
        to_lane_tiles(held, slice(None), fields_ref[...].astype(jnp.float32))

    blocks = []
    for k in range(per_step):
        rows = pl.ds(first + step * per_step + k, full_rows, stride=group)
        field = from_lane_tiles(held, rows)
        spread = jnp.dot(
            field.astype(jnp.bfloat16), row_table_ref[...], preferred_element_type=jnp.float32
        ).astype(jnp.bfloat16)
        blocks.append(jnp.concatenate([spread[:, :width], spread[:, width:]], axis=0))
    spectrum = jnp.dot(
        fwd_ref[...], jnp.concatenate(blocks, axis=1), preferred_element_type=jnp.float32
    )
    blocks = []
    for k in range(per_step):
        real = spectrum[:full_rows, k * width : (k + 1) * width]
        imag = spectrum[full_rows:, k * width : (k + 1) * width]
        g_real = g_ref[k, 0]
        g_imag = g_ref[k, 1]
        blocks.append(
            jnp.concatenate(
                [g_real * real - g_imag * imag, g_real * imag + g_imag * real], axis=0
            ).astype(jnp.bfloat16)
        )
    back = jnp.dot(
        inv_ref[...], jnp.concatenate(blocks, axis=1), preferred_element_type=jnp.float32
    ).astype(jnp.bfloat16)
    for k in range(per_step):
        lanes = slice(k * width, (k + 1) * width)
        both = jnp.concatenate([back[:full_rows, lanes], back[full_rows:, lanes]], axis=1)
        result = jnp.dot(both, back_ref[...], preferred_element_type=jnp.float32)
        rows = pl.ds(step * per_step + k, full_rows, stride=count)
        to_lane_tiles(made, rows, result * norm_scale)

    @pl.when(step == pl.num_programs(0) - 1)
    def _():
        out_ref[...] = from_lane_tiles(made, slice(None)).astype(jnp.bfloat16)


def filter_tables(full_rows, field_cols, width):
    cos_h, sin_h = fourier_tables(full_rows)
    cos_w, sin_w = fourier_tables(field_cols)
    fwd = jnp.concatenate(
        [jnp.concatenate([cos_h, sin_h], 1), jnp.concatenate([-sin_h, cos_h], 1)], 0
    )
    inv = jnp.concatenate(
        [jnp.concatenate([cos_h, -sin_h], 1), jnp.concatenate([sin_h, cos_h], 1)], 0
    )
    w = jnp.arange(width, dtype=jnp.int32)
    half = field_cols // 2
    valid = (w <= half).astype(jnp.bfloat16)
    times = jnp.where((w == 0) | (w == half), 1.0, 2.0).astype(jnp.bfloat16) * valid
    row_table = jnp.concatenate([cos_w[:, :width] * valid, -sin_w[:, :width] * valid], 1)
    back_table = jnp.concatenate(
        [cos_w[:width] * times[:, None], -sin_w[:width] * times[:, None]], 0
    )
    return row_table, fwd, inv, back_table


def filter_channels(fields, symmetric, tables, first, count, per_step, devices):
    row_table, fwd, inv, back_table = tables
    full_rows = fwd.shape[0] // 2
    cols = fields.shape[1]
    group = fields.shape[0] // full_rows
    width = symmetric.shape[3]

    def whole(array):
        return pl.BlockSpec(array.shape, lambda i: (0,) * array.ndim)

    macs = count * (2 * 4 * full_rows * full_rows * width + 4 * full_rows * cols * width)
    made = pl.pallas_call(
        functools.partial(filter_kernel, first, 1.0 / (full_rows * cols)),
        grid=(count // per_step,),
        in_specs=[
            whole(fields),
            pl.BlockSpec(
                (per_step, 2, full_rows, width), lambda i: (first // per_step + i, 0, 0, 0)
            ),
            whole(row_table),
            whole(fwd),
            whole(inv),
            whole(back_table),
        ],
        out_specs=pl.BlockSpec((full_rows * count, cols), lambda i: (0, 0)),
        out_shape=jax.ShapeDtypeStruct((full_rows * count, cols), jnp.bfloat16),
        scratch_shapes=[
            pltpu.VMEM((cols // 128, full_rows * group, 128), jnp.float32),
            pltpu.VMEM((cols // 128, full_rows * count, 128), jnp.float32),
        ],
        compiler_params=pltpu.CompilerParams(vmem_limit_bytes=56 * 1024 * 1024),
        cost_estimate=pl.CostEstimate(
            flops=2 * macs, bytes_accessed=count * full_rows * cols * 8, transcendentals=0
        ),
        name="spectral_filter",
    )(fields, symmetric, row_table, fwd, inv, back_table)
    return made.reshape(devices, full_rows // devices * count, cols)


def residual_kernel(count, place_ref, kept_ref, other_ref, feat_ref, *refs):
    out_ref, held = refs[-2:]
    span = kept_ref.shape[1]
    rows = held.shape[1] // count
    own = pl.multiple_of(place_ref[0] * span, 8)
    far = pl.multiple_of((1 - place_ref[0]) * span, 8)
    to_lane_tiles(held, pl.ds(own, span), kept_ref[0].astype(jnp.float32))
    to_lane_tiles(held, pl.ds(far, span), other_ref[0].astype(jnp.float32))
    for k in range(count):
        filtered = from_lane_tiles(held, pl.ds(k, rows, stride=count))
        out_ref[0, k] = (feat_ref[0, k].astype(jnp.float32) + filtered).astype(jnp.bfloat16)


def add_residual(place, returned, other, features, previous, part, parts):
    halves, span, cols = other.shape
    group, rows = features.shape[1:3]
    count = group // parts
    block = pl.BlockSpec((1, count, rows, cols), lambda i, place: (i, part, 0, 0))
    operands = [returned, other, features]
    in_specs = [
        pl.BlockSpec((1, span, cols), lambda i, place: (place[0] * halves + i, 0, 0)),
        pl.BlockSpec((1, span, cols), lambda i, place: (i, 0, 0)),
        block,
    ]
    aliases = {}
    if previous is not None:
        operands.append(previous)
        in_specs.append(pl.BlockSpec(memory_space=pl.ANY))
        aliases = {4: 0}
    return pl.pallas_call(
        functools.partial(residual_kernel, count),
        grid_spec=pltpu.PrefetchScalarGridSpec(
            num_scalar_prefetch=1,
            grid=(halves,),
            in_specs=in_specs,
            out_specs=block,
            scratch_shapes=[pltpu.VMEM((cols // 128, rows * count, 128), jnp.float32)],
        ),
        out_shape=jax.ShapeDtypeStruct(features.shape, jnp.bfloat16),
        input_output_aliases=aliases,
        compiler_params=pltpu.CompilerParams(vmem_limit_bytes=32 * 1024 * 1024),
        cost_estimate=pl.CostEstimate(
            flops=halves * count * rows * cols,
            bytes_accessed=halves * count * rows * cols * 8,
            transcendentals=0,
        ),
        name="residual",
    )(place, *operands)


def swap(block):
    return lax.ppermute(block, "section", [(0, 1), (1, 0)])


def local(
    aerial_patch_grid,
    patch_conv_weight,
    patch_bias,
    merging_conv_weight,
    merge_bias,
    down_weight,
    down_bias,
    norm_gain,
    spectral_filter,
):
    tile_rows, field_cols, depth = aerial_patch_grid.shape
    channels = down_weight.shape[3]
    tile_channels = spectral_filter.shape[0]
    full_rows = spectral_filter.shape[2]
    sections = lax.axis_size("section")
    devices = sections * lax.axis_size("tile")
    suits = (
        sections == 2
        and tile_rows % 4 == 0
        and tile_channels % 4 == 0
        and (tile_rows // 2) * (tile_channels // 4) % 8 == 0
        and field_cols % 128 == 0
        and full_rows % 128 == 0
        and tile_channels % 8 == 0
    )
    arguments = (
        aerial_patch_grid,
        patch_conv_weight,
        patch_bias,
        merging_conv_weight,
        merge_bias,
        down_weight,
        down_bias,
        norm_gain,
        spectral_filter,
    )
    if not suits:
        return general_local(*arguments)
    section = lax.axis_index("section")
    tile = lax.axis_index("tile")
    rows = tile_rows // 2
    group = tile_channels // 2
    half_channels = channels // 2
    width = -(-(field_cols // 2 + 1) // 128) * 128

    def lower_half(row):
        return jnp.concatenate(
            [row[:, 256 * b + 128 : 256 * b + 256] for b in range(depth // 256)], axis=1
        )

    arriving = from_behind(lower_half(aerial_patch_grid[-1]), "tile", 1)
    halo = jnp.where(section == 0, arriving, lower_half(aerial_patch_grid[rows - 1]))
    inside = ((section > 0) | (tile > 0)).astype(jnp.int32)
    weights = stem_weights(*arguments[1:7])
    place = jnp.stack([section * (rows // 2), inside]).astype(jnp.int32)
    normed, features = stem(aerial_patch_grid, halo, place, weights, norm_gain, devices)
    fields = lax.all_to_all(normed, DEVICES, split_axis=0, concat_axis=0, tiled=True)
    fields = fields.reshape(full_rows * group, field_cols)

    channel_place = jnp.reshape(section * group, (1,)).astype(jnp.int32)
    symmetric = symmetric_filter(spectral_filter, channel_place, group, width)
    tables = filter_tables(full_rows, field_cols, width)

    own = lax.dynamic_slice_in_dim(features, section * half_channels, half_channels, 1)
    sent = lax.dynamic_slice_in_dim(features, (1 - section) * half_channels, half_channels, 1)
    arrived = swap(sent)
    low = jnp.where(section == 0, own, arrived)
    high = jnp.where(section == 0, arrived, own)
    residual = jnp.transpose(jnp.concatenate([low, high], axis=0), (1, 0, 2))
    residual = residual.reshape(half_channels // group, group, tile_rows, field_cols)

    parts = 2
    count = group // parts
    section_place = jnp.reshape(section, (1,)).astype(jnp.int32)
    output = None
    for part in range(parts):
        made = filter_channels(fields, symmetric, tables, part * count, count, 2, devices)
        returned = lax.all_to_all(made, DEVICES, split_axis=0, concat_axis=0, tiled=True)
        halves = devices // 2
        other = swap(lax.dynamic_slice_in_dim(returned, (1 - section) * halves, halves, 0))
        output = add_residual(section_place, returned, other, residual, output, part, parts)
    return output.reshape(half_channels, tile_rows, field_cols)


def solution(mesh):
    return jax.shard_map(
        local,
        mesh=mesh,
        in_specs=(
            P("tile", None, None),
            P(),
            P(),
            P(),
            P(),
            P(),
            P(),
            P(),
            P("tile", None, None, None),
        ),
        out_specs=P("section", "tile", None),
        check_vma=False,
    )
```

```python
import functools
import math

import jax
import jax.numpy as jnp
import numpy as np
from jax import lax
from jax.experimental import pallas as pl
from jax.experimental.pallas import tpu as pltpu
from jax.sharding import PartitionSpec as P

EPSILON = 1e-05


def from_behind(block, axis, distance):
    devices = range(lax.axis_size(axis))
    route = [(i - distance, i) for i in devices if i - distance in devices]
    return lax.ppermute(block, axis, route)


def fourier_tables(length, columns=None):
    indices = jnp.arange(length, dtype=jnp.int32)
    columns = indices if columns is None else jnp.asarray(columns, jnp.int32)
    product = indices[:, None] * columns[None, :] % length
    angles = product.astype(jnp.float32) * (2.0 * math.pi / length)
    return (jnp.cos(angles).astype(jnp.bfloat16), jnp.sin(angles).astype(jnp.bfloat16))


def patch_kernel_matrix(patch_conv_weight):
    identity = jnp.eye(4, dtype=jnp.float32)
    larger = jnp.einsum(
        "baqk,xy,uv->bxauqyvk", patch_conv_weight.astype(jnp.float32), identity, identity
    )
    band_count = patch_conv_weight.shape[0]
    width = patch_conv_weight.shape[3]
    return larger.reshape(band_count * 256, 16 * width).astype(jnp.bfloat16)


def merging_kernel_matrix(merging_conv_weight):
    identity = jnp.eye(2, dtype=jnp.float32)
    larger = jnp.einsum(
        "aqjk,xy,uv->xauqjyvk", merging_conv_weight.astype(jnp.float32), identity, identity
    )
    in_width = merging_conv_weight.shape[2]
    out_width = merging_conv_weight.shape[3]
    return larger.reshape(16 * in_width, 4 * out_width).astype(jnp.bfloat16)


def down_matrices(down_weight):
    nothing = jnp.zeros_like(down_weight[0, 0])
    in_width = down_weight.shape[2]
    out_width = down_weight.shape[3]

    def arrange(entries):
        return jnp.stack(
            [jnp.stack(entries[0], axis=0), jnp.stack(entries[1], axis=0)], axis=0
        ).reshape(4 * in_width, out_width)

    own_taps = arrange(
        [[down_weight[1, 1], down_weight[1, 2]], [down_weight[2, 1], down_weight[2, 2]]]
    )
    upper_taps = arrange([[nothing, nothing], [down_weight[0, 1], down_weight[0, 2]]])
    left_taps = arrange([[nothing, down_weight[1, 0]], [nothing, down_weight[2, 0]]])
    corner_taps = arrange([[nothing, nothing], [nothing, down_weight[0, 0]]])
    return (own_taps, upper_taps, left_taps, corner_taps)


def stem_layers(aerial_patch_grid, patch_conv_weight, patch_bias, merging_conv_weight, merge_bias):
    initial_layer = jnp.einsum(
        "zji,if->zjf",
        aerial_patch_grid,
        patch_kernel_matrix(patch_conv_weight),
        preferred_element_type=jnp.float32,
    )
    initial_layer = jax.nn.gelu(initial_layer + jnp.tile(patch_bias, 16), approximate=True).astype(
        jnp.bfloat16
    )
    layer_two = jnp.einsum(
        "zji,if->zjf",
        initial_layer,
        merging_kernel_matrix(merging_conv_weight),
        preferred_element_type=jnp.float32,
    )
    return jax.nn.gelu(layer_two + jnp.tile(merge_bias, 4), approximate=True).astype(jnp.bfloat16)


def rim_above(extended):
    return from_behind(extended[-1:], "tile", 1)


def down_conv(upper_rim, extended, down_weight, down_bias):
    stacked = jnp.concatenate([upper_rim, extended], axis=0)
    own_taps, upper_taps, left_taps, corner_taps = down_matrices(down_weight)
    summed = jnp.einsum(
        "rwk,kc->crw", stacked[1:, 1:], own_taps, preferred_element_type=jnp.float32
    )
    summed = summed + jnp.einsum(
        "rwk,kc->crw", stacked[:-1, 1:], upper_taps, preferred_element_type=jnp.float32
    )
    summed = summed + jnp.einsum(
        "rwk,kc->crw", stacked[1:, :-1], left_taps, preferred_element_type=jnp.float32
    )
    summed = summed + jnp.einsum(
        "rwk,kc->crw", stacked[:-1, :-1], corner_taps, preferred_element_type=jnp.float32
    )
    return (summed + down_bias[:, None, None]).astype(jnp.bfloat16)


def layer_norm(features, norm_gain):
    values = features.astype(jnp.float32)
    mean_value = jnp.mean(values, axis=0, keepdims=True)
    centered = values - mean_value
    variance = jnp.mean(centered * centered, axis=0, keepdims=True)
    return (norm_gain[:, None, None] * centered * lax.rsqrt(variance + EPSILON)).astype(
        jnp.bfloat16
    )


def filter_columns(row_spectrum, kernel, forward_h, inverse_h):
    spectrum = jnp.einsum(
        "puqh,chqw->cpuw", forward_h, row_spectrum, preferred_element_type=jnp.float32
    ).astype(jnp.bfloat16)
    spec_real = spectrum[:, 0].astype(jnp.float32)
    spec_imag = spectrum[:, 1].astype(jnp.float32)
    filter_real = kernel[:, 0].astype(jnp.float32)
    filter_imag = kernel[:, 1].astype(jnp.float32)
    weighted = jnp.stack(
        [
            filter_real * spec_real - filter_imag * spec_imag,
            filter_real * spec_imag + filter_imag * spec_real,
        ],
        axis=1,
    ).astype(jnp.bfloat16)
    return jnp.einsum(
        "qhpu,cpuw->chqw", inverse_h, weighted, preferred_element_type=jnp.float32
    ).astype(jnp.bfloat16)


def general_local(
    aerial_patch_grid,
    patch_conv_weight,
    patch_bias,
    merging_conv_weight,
    merge_bias,
    down_weight,
    down_bias,
    norm_gain,
    spectral_filter,
):
    section_index = lax.axis_index("section")
    first_section = section_index == 0
    field_cols = aerial_patch_grid.shape[1]
    channels = down_weight.shape[3]
    group_width = spectral_filter.shape[0]
    full_rows = spectral_filter.shape[2]
    half_channels = channels // 2
    cell_half = field_cols // 2
    image_part = lax.dynamic_slice_in_dim(
        aerial_patch_grid, section_index * cell_half, cell_half, 1
    )
    layer_two = stem_layers(
        image_part, patch_conv_weight, patch_bias, merging_conv_weight, merge_bias
    )
    left_column = from_behind(layer_two[:, -1:], "section", 1)
    extended = jnp.concatenate([left_column, layer_two], axis=1)
    upper_rim = rim_above(extended)
    feature_half = down_conv(upper_rim, extended, down_weight, down_bias)
    features = lax.all_gather(feature_half, "section", axis=2, tiled=True)
    normed = layer_norm(features, norm_gain)
    cos_h, sin_h = fourier_tables(full_rows)
    cos_w, sin_w = fourier_tables(field_cols)
    forward_table = jnp.stack([cos_w, -sin_w], axis=1)
    forward_h = jnp.stack(
        [jnp.stack([cos_h, sin_h], axis=1), jnp.stack([-sin_h, cos_h], axis=1)], axis=0
    )
    inverse_h = jnp.stack(
        [jnp.stack([cos_h, -sin_h], axis=1), jnp.stack([sin_h, cos_h], axis=1)], axis=0
    )
    inverse_table = jnp.stack([cos_w, -sin_w], axis=0)
    norm_scale = 1.0 / (full_rows * field_cols)
    fields = lax.all_to_all(normed, "tile", split_axis=0, concat_axis=1, tiled=True)

    def whole_filter():
        frequency_rows = jnp.einsum(
            "chx,xqw->chqw", fields, forward_table, preferred_element_type=jnp.float32
        ).astype(jnp.bfloat16)
        back_rows = filter_columns(frequency_rows, spectral_filter, forward_h, inverse_h)
        result = jnp.einsum(
            "chqw,qwv->chv", back_rows, inverse_table, preferred_element_type=jnp.float32
        )
        return (result * norm_scale).astype(jnp.bfloat16)

    def empty_fields():
        return jnp.zeros((group_width, full_rows, field_cols), jnp.bfloat16)

    filtered_fields = lax.cond(first_section, empty_fields, whole_filter)
    rows_back = lax.all_to_all(filtered_fields, "tile", split_axis=1, concat_axis=0, tiled=True)
    returned = from_behind(rows_back[:half_channels], "section", -1)
    filtered = jnp.where(first_section, returned, rows_back[half_channels:])
    own_part = lax.dynamic_slice_in_dim(features, section_index * half_channels, half_channels, 0)
    return (own_part.astype(jnp.float32) + filtered.astype(jnp.float32)).astype(jnp.bfloat16)


DEVICES = ("tile", "section")
VMEM_BYTES = 60 * 1024 * 1024
GELU_LINEAR = 2.0 * math.sqrt(2.0 / math.pi)
GELU_CUBIC = 4.0 * 0.044715 * GELU_LINEAR
ONES = (64, 128, 64)
TAPS = ((1, 1), (1, 2), (2, 1), (2, 2), (1, 0), (2, 0), (0, 1), (0, 2), (0, 0))


def bias_rows(bias, count):
    high = bias.astype(jnp.bfloat16)
    rest = bias - high.astype(jnp.float32)
    middle = rest.astype(jnp.bfloat16)
    low = (rest - middle.astype(jnp.float32)).astype(jnp.bfloat16)
    shape = (count, bias.shape[1])
    row = lax.broadcasted_iota(jnp.int32, shape, 0)
    rows = jnp.zeros(shape, jnp.float32)
    for k, part in enumerate((high, middle, low)):
        rows = jnp.where(row == k, jnp.broadcast_to(part.astype(jnp.float32), shape), rows)
    return rows.astype(jnp.bfloat16)


def weights_kernel(
    patch_ref, patch_bias_ref, merge_ref, merge_bias_ref, down_ref, down_bias_ref, gain_ref,
    w1_ref, w2_ref, w3_ref, column_ref,
):
    def exact(a, b):
        return jnp.dot(
            a.astype(jnp.bfloat16), b.astype(jnp.bfloat16), preferred_element_type=jnp.float32
        )

    taps, width = patch_ref.shape
    row = lax.broadcasted_iota(jnp.int32, (4 * taps, taps), 0)
    col = lax.broadcasted_iota(jnp.int32, (4 * taps, taps), 1)
    pick = jnp.where(row // 16 * 4 + row % 4 == col, 1.0, 0.0)
    row = lax.broadcasted_iota(jnp.int32, (width, 4 * width), 0)
    col = lax.broadcasted_iota(jnp.int32, (width, 4 * width), 1)
    repeat = jnp.where(col % width == row, 1.0, 0.0)
    spread = exact(pick, exact(patch_ref[...], repeat))
    row = lax.broadcasted_iota(jnp.int32, spread.shape, 0)
    col = lax.broadcasted_iota(jnp.int32, spread.shape, 1)
    spread = jnp.where(row // 4 % 4 == col // width, 0.5 * spread, 0.0).astype(jnp.bfloat16)
    bias = jnp.broadcast_to(0.5 * patch_bias_ref[...], (8, width))
    tiled = jnp.zeros((8, 4 * width), jnp.float32)
    for _ in range(3):
        part = bias.astype(jnp.bfloat16).astype(jnp.float32)
        tiled = tiled + exact(part, repeat)
        bias = bias - part
    first = jnp.concatenate([spread, bias_rows(tiled[:1], ONES[0])], axis=0)
    w1_ref[...] = first.T
    half = (merge_ref[...].astype(jnp.float32) * 0.5).astype(jnp.bfloat16)
    second = jnp.concatenate([half, bias_rows(0.5 * merge_bias_ref[...], ONES[1])], axis=0)
    w2_ref[...] = second.T
    third = [down_ref[3 * a + q] for a, q in TAPS]
    third = jnp.concatenate(third + [bias_rows(down_bias_ref[...], ONES[2])], axis=0)
    w3_ref[...] = third.T
    column_ref[...] = jnp.broadcast_to(gain_ref[...], (128, gain_ref.shape[1])).T


def stem_weights(
    patch_conv_weight, patch_bias, merging_conv_weight, merge_bias, down_weight, down_bias,
    norm_gain,
):
    width = patch_conv_weight.shape[3]
    merged = merging_conv_weight.shape[3]
    channels = down_weight.shape[3]
    patch = patch_conv_weight.reshape(-1, width)
    depths = (4 * patch.shape[0] + ONES[0], 4 * width + ONES[1], 9 * merged + ONES[2])
    return pl.pallas_call(
        weights_kernel,
        out_shape=[
            jax.ShapeDtypeStruct((4 * width, depths[0]), jnp.bfloat16),
            jax.ShapeDtypeStruct((merged, depths[1]), jnp.bfloat16),
            jax.ShapeDtypeStruct((channels, depths[2]), jnp.bfloat16),
            jax.ShapeDtypeStruct((channels, 128), jnp.float32),
        ],
        compiler_params=pltpu.CompilerParams(vmem_limit_bytes=VMEM_BYTES),
        cost_estimate=pl.CostEstimate(flops=1000000, bytes_accessed=4000000, transcendentals=0),
        name="stem_weights",
    )(
        patch,
        patch_bias[None],
        merging_conv_weight.reshape(-1, merged),
        merge_bias[None],
        down_weight.reshape(9, merged, channels),
        down_bias[None],
        norm_gain[None],
    )


def half_gelu(h):
    return h + h * jnp.tanh(h * (GELU_LINEAR + GELU_CUBIC * (h * h)))


def lower_half(row):
    depth = row.shape[1]
    return jnp.concatenate(
        [row[:, 256 * b + 128 : 256 * b + 256] for b in range(depth // 256)], axis=1
    )


def stem_kernel(place_ref, x_ref, above_ref, *refs):
    w1_ref, w2_ref, w3_ref, gain_ref, normed_ref, feat_ref, field = refs[-7:]
    step = pl.program_id(0)
    rows, cols, depth = x_ref.shape
    bands = depth // 256
    channels = w3_ref.shape[0]
    merged = w2_ref.shape[0]
    group = normed_ref.shape[2] // rows
    cells = rows * cols
    w1 = w1_ref[...]
    w2 = w2_ref[...]

    def ones(count, n):
        return jnp.where(lax.broadcasted_iota(jnp.int32, (count, n), 0) < 3, 1.0, 0.0).astype(
            jnp.bfloat16
        )

    def layer_one(turned, offsets):
        n = turned.shape[1]
        parts = [turned[o : o + 64] for o in offsets] + [ones(ONES[0], n)]
        h = jnp.dot(w1, jnp.concatenate(parts, axis=0), preferred_element_type=jnp.float32)
        return half_gelu(h).astype(jnp.bfloat16)

    def layer_two(upper, lower, y):
        n = upper.shape[1]
        span = slice(2 * y * (w1.shape[0] // 4), 2 * (y + 1) * (w1.shape[0] // 4))
        stacked = jnp.concatenate([upper[span], lower[span], ones(ONES[1], n)], axis=0)
        return half_gelu(jnp.dot(w2, stacked, preferred_element_type=jnp.float32))

    def shifted(values):
        lanes = lax.broadcasted_iota(jnp.int32, values.shape, 1)
        moved = pltpu.roll(values, 1, 1)
        return jnp.where(lax.rem(lanes, cols) == 0, 0.0, moved)

    def put(block, lanes, values):
        field[block * merged : (block + 1) * merged, lanes] = values.astype(jnp.bfloat16)

    first_row = slice(0, cols)
    last_row = slice(cells - cols, cells)
    later_rows = slice(cols, cells)
    earlier_rows = slice(0, cells - cols)

    @pl.when(step == 0)
    def _():
        field[9 * merged :, :] = ones(ONES[2], cells)
        above = lower_half(above_ref[0])
        keep = 1.0
        if len(refs) > 7:
            keep = place_ref[1].astype(jnp.float32)
            above = jnp.where(place_ref[2] > 0, refs[0][...], above)
        turned = above.T
        upper, lower = (
            layer_one(turned, [128 * b + 64 * a for b in range(bands)]) for a in range(2)
        )
        put(6, first_row, layer_two(upper, lower, 0) * keep)
        right = layer_two(upper, lower, 1) * keep
        put(7, first_row, right)
        put(8, first_row, shifted(right))

    @pl.when(step > 0)
    def _():
        for source, target in ((2, 6), (3, 7), (5, 8)):
            field[target * merged : (target + 1) * merged, first_row] = field[
                source * merged : (source + 1) * merged, last_row
            ]

    turned = x_ref[...].reshape(cells, depth).T
    for x in range(2):
        upper, lower = (
            layer_one(turned, [256 * b + 64 * (2 * x + a) for b in range(bands)])
            for a in range(2)
        )
        left = layer_two(upper, lower, 0)
        right = layer_two(upper, lower, 1)
        put(2 * x, slice(None), left)
        put(2 * x + 1, slice(None), right)
        moved = shifted(right)
        put(4 + x, slice(None), moved)
        if x == 1:
            put(6, later_rows, left[:, earlier_rows])
            put(7, later_rows, right[:, earlier_rows])
            put(8, later_rows, moved[:, earlier_rows])

    features = jnp.dot(w3_ref[...], field[...], preferred_element_type=jnp.float32).astype(
        jnp.bfloat16
    )
    for r in range(rows):
        feat_ref[r] = features[:, r * cols : (r + 1) * cols]
    values = features.astype(jnp.float32)
    centered = values - jnp.mean(values, axis=0, keepdims=True)
    variance = jnp.mean(centered * centered, axis=0, keepdims=True)
    gain = jnp.concatenate([gain_ref[...]] * (cells // 128), axis=1)
    normed = gain * (centered * lax.rsqrt(variance + EPSILON))
    pair = 2 * group
    index = lax.broadcasted_iota(jnp.int32, (pair, cols), 0)
    for t in range(channels // pair):
        one = normed[pair * t : pair * (t + 1), :cols]
        two = normed[pair * t : pair * (t + 1), cols:]
        normed_ref[2 * t, 0] = jnp.where(index < group, one, pltpu.roll(two, group, 0)).astype(
            jnp.bfloat16
        )
        normed_ref[2 * t + 1, 0] = jnp.where(
            index < group, pltpu.roll(one, group, 0), two
        ).astype(jnp.bfloat16)


def stem(image, arriving, place, weights, first, steps, devices):
    cols, depth = image.shape[1:]
    rows = 2 * steps
    channels, third_depth = weights[2].shape
    merged = weights[1].shape[0]
    group = channels // devices

    def whole(array):
        return pl.BlockSpec(array.shape, lambda i, place: (0,) * array.ndim)

    operands = list(weights)
    if arriving is not None:
        operands = [arriving] + operands
    macs = rows * cols * (16 * 208 * 96 + 4 * 400 * merged + third_depth * channels)
    return pl.pallas_call(
        stem_kernel,
        grid_spec=pltpu.PrefetchScalarGridSpec(
            num_scalar_prefetch=1,
            grid=(steps,),
            in_specs=[
                pl.BlockSpec((2, cols, depth), lambda i, place: (place[0] + first + i, 0, 0)),
                pl.BlockSpec(
                    (1, cols, depth),
                    lambda i, place: (jnp.maximum(2 * (place[0] + first) - 1, 0), 0, 0),
                ),
            ]
            + [whole(a) for a in operands],
            out_specs=[
                pl.BlockSpec((devices, 1, 2 * group, cols), lambda i, place: (0, i, 0, 0)),
                pl.BlockSpec((2, channels, cols), lambda i, place: (i, 0, 0)),
            ],
            scratch_shapes=[pltpu.VMEM((third_depth, 2 * cols), jnp.bfloat16)],
        ),
        out_shape=[
            jax.ShapeDtypeStruct((devices, steps, 2 * group, cols), jnp.bfloat16),
            jax.ShapeDtypeStruct((rows, channels, cols), jnp.bfloat16),
        ],
        compiler_params=pltpu.CompilerParams(vmem_limit_bytes=VMEM_BYTES),
        cost_estimate=pl.CostEstimate(
            flops=4 * macs, bytes_accessed=rows * cols * 3000, transcendentals=0
        ),
        name="stem",
    )(place, image, image, *operands)


def symmetric_kernel(place_ref, f_ref, turn_w_ref, turn_u_ref, g_ref):
    width = g_ref.shape[3]
    for part in range(2):
        block = f_ref[0, part]
        across = jnp.dot(block, turn_w_ref[...], preferred_element_type=jnp.float32)
        turned = jnp.dot(
            turn_u_ref[...], across.astype(jnp.bfloat16), preferred_element_type=jnp.float32
        )
        own = block[:, :width].astype(jnp.float32)
        g_ref[0, part] = 0.5 * (own + turned if part == 0 else own - turned)


def symmetric_filter(spectral_filter, place, group, width):
    full_rows, full_cols = spectral_filter.shape[2:]
    u = jnp.arange(full_rows, dtype=jnp.int32)
    w = jnp.arange(full_cols, dtype=jnp.int32)
    turn_u = ((u[:, None] + u[None, :]) % full_rows == 0).astype(jnp.bfloat16)
    turn_w = ((w[:, None] + w[None, :width]) % full_cols == 0).astype(jnp.bfloat16)
    return pl.pallas_call(
        symmetric_kernel,
        grid_spec=pltpu.PrefetchScalarGridSpec(
            num_scalar_prefetch=1,
            grid=(group,),
            in_specs=[
                pl.BlockSpec(
                    (1, 2, full_rows, full_cols), lambda i, place: (place[0] + i, 0, 0, 0)
                ),
                pl.BlockSpec(turn_w.shape, lambda i, place: (0, 0)),
                pl.BlockSpec(turn_u.shape, lambda i, place: (0, 0)),
            ],
            out_specs=pl.BlockSpec((1, 2, full_rows, width), lambda i, place: (i, 0, 0, 0)),
        ),
        out_shape=jax.ShapeDtypeStruct((group, 2, full_rows, width), jnp.float32),
        compiler_params=pltpu.CompilerParams(vmem_limit_bytes=VMEM_BYTES),
        cost_estimate=pl.CostEstimate(
            flops=8 * group * full_rows * full_cols * width,
            bytes_accessed=group * full_rows * width * 14,
            transcendentals=0,
        ),
        name="symmetric_filter",
    )(place, spectral_filter, turn_w, turn_u)


def to_lane_tiles(target, rows, values):
    for j in range(target.shape[0]):
        target[j, rows, :] = values[:, 128 * j : 128 * (j + 1)]


def from_lane_tiles(source, rows):
    return jnp.concatenate([source[j, rows, :] for j in range(source.shape[0])], axis=1)


def filter_kernel(
    first, norm_scale, *refs
):
    *pieces, g_ref, row_table_ref, fwd_ref, inv_ref, back_ref, out_ref, held, made = refs
    step = pl.program_id(0)
    full_rows = fwd_ref.shape[0] // 2
    width = g_ref.shape[3]
    group = held.shape[1] // full_rows
    count = made.shape[1] // full_rows
    per_step = g_ref.shape[0]

    @pl.when(step == 0)
    def _():
        begin = 0
        for piece in pieces:
            end = begin + piece.shape[0]
            to_lane_tiles(held, slice(begin, end), piece[...].astype(jnp.float32))
            begin = end

    blocks = []
    for k in range(per_step):
        rows = pl.ds(first + step * per_step + k, full_rows, stride=group)
        field = from_lane_tiles(held, rows)
        spread = jnp.dot(
            field.astype(jnp.bfloat16), row_table_ref[...], preferred_element_type=jnp.float32
        ).astype(jnp.bfloat16)
        blocks.append(jnp.concatenate([spread[:, :width], spread[:, width:]], axis=0))
    spectrum = jnp.dot(
        fwd_ref[...], jnp.concatenate(blocks, axis=1), preferred_element_type=jnp.float32
    )
    blocks = []
    for k in range(per_step):
        real = spectrum[:full_rows, k * width : (k + 1) * width]
        imag = spectrum[full_rows:, k * width : (k + 1) * width]
        g_real = g_ref[k, 0]
        g_imag = g_ref[k, 1]
        blocks.append(
            jnp.concatenate(
                [g_real * real - g_imag * imag, g_real * imag + g_imag * real], axis=0
            ).astype(jnp.bfloat16)
        )
    back = jnp.dot(
        inv_ref[...], jnp.concatenate(blocks, axis=1), preferred_element_type=jnp.float32
    ).astype(jnp.bfloat16)
    for k in range(per_step):
        lanes = slice(k * width, (k + 1) * width)
        both = jnp.concatenate([back[:full_rows, lanes], back[full_rows:, lanes]], axis=1)
        result = jnp.dot(both, back_ref[...], preferred_element_type=jnp.float32)
        rows = pl.ds(step * per_step + k, full_rows, stride=count)
        to_lane_tiles(made, rows, result * norm_scale)

    @pl.when(step == pl.num_programs(0) - 1)
    def _():
        out_ref[...] = from_lane_tiles(made, slice(None)).astype(jnp.bfloat16)


def filter_tables(full_rows, field_cols, width, row_order):
    cos_h, sin_h = fourier_tables(full_rows)
    cos_f, sin_f = fourier_tables(full_rows, row_order)
    cos_w, sin_w = fourier_tables(field_cols)
    fwd = jnp.concatenate(
        [jnp.concatenate([cos_f, sin_f], 1), jnp.concatenate([-sin_f, cos_f], 1)], 0
    )
    inv = jnp.concatenate(
        [jnp.concatenate([cos_h, -sin_h], 1), jnp.concatenate([sin_h, cos_h], 1)], 0
    )
    w = jnp.arange(width, dtype=jnp.int32)
    half = field_cols // 2
    valid = (w <= half).astype(jnp.bfloat16)
    times = jnp.where((w == 0) | (w == half), 1.0, 2.0).astype(jnp.bfloat16) * valid
    row_table = jnp.concatenate([cos_w[:, :width] * valid, -sin_w[:, :width] * valid], 1)
    back_table = jnp.concatenate(
        [cos_w[:width] * times[:, None], -sin_w[:width] * times[:, None]], 0
    )
    return row_table, fwd, inv, back_table


def filter_channels(pieces, symmetric, tables, first, count, per_step, devices):
    row_table, fwd, inv, back_table = tables
    full_rows = fwd.shape[0] // 2
    cols = pieces[0].shape[1]
    group = sum(piece.shape[0] for piece in pieces) // full_rows
    width = symmetric.shape[3]

    def whole(array):
        return pl.BlockSpec(array.shape, lambda i: (0,) * array.ndim)

    macs = count * (2 * 4 * full_rows * full_rows * width + 4 * full_rows * cols * width)
    made = pl.pallas_call(
        functools.partial(filter_kernel, first, 1.0 / (full_rows * cols)),
        grid=(count // per_step,),
        in_specs=[
            *[whole(piece) for piece in pieces],
            pl.BlockSpec(
                (per_step, 2, full_rows, width), lambda i: (first // per_step + i, 0, 0, 0)
            ),
            whole(row_table),
            whole(fwd),
            whole(inv),
            whole(back_table),
        ],
        out_specs=pl.BlockSpec((full_rows * count, cols), lambda i: (0, 0)),
        out_shape=jax.ShapeDtypeStruct((full_rows * count, cols), jnp.bfloat16),
        scratch_shapes=[
            pltpu.VMEM((cols // 128, full_rows * group, 128), jnp.float32),
            pltpu.VMEM((cols // 128, full_rows * count, 128), jnp.float32),
        ],
        compiler_params=pltpu.CompilerParams(vmem_limit_bytes=VMEM_BYTES),
        cost_estimate=pl.CostEstimate(
            flops=2 * macs, bytes_accessed=count * full_rows * cols * 8, transcendentals=0
        ),
        name="spectral_filter",
    )(*pieces, symmetric, row_table, fwd, inv, back_table)
    return made.reshape(devices, full_rows // devices * count, cols)


def residual_kernel(count, place_ref, kept_ref, other_ref, feat_ref, *refs):
    out_ref, held = refs[-2:]
    groups, span, cols = kept_ref.shape
    rows = held.shape[1] // count
    own = pl.multiple_of(place_ref[0] * span, 8)
    far = pl.multiple_of((1 - place_ref[0]) * span, 8)
    for g in range(groups):
        to_lane_tiles(held, pl.ds(own, span), kept_ref[g].astype(jnp.float32))
        to_lane_tiles(held, pl.ds(far, span), other_ref[g].astype(jnp.float32))
        for k in range(count):
            filtered = from_lane_tiles(held, pl.ds(k, rows, stride=count))
            out_ref[g, k] = (feat_ref[g, k].astype(jnp.float32) + filtered).astype(jnp.bfloat16)


def add_residual(place, returned, other, features, previous, first, count):
    halves, span, cols = other.shape
    group, rows = features.shape[1:3]
    groups = 4 if halves % 4 == 0 else 1
    steps = halves // groups
    operands = [returned, other, features]
    in_specs = [
        pl.BlockSpec((groups, span, cols), lambda i, place: (place[0] * steps + i, 0, 0)),
        pl.BlockSpec((groups, span, cols), lambda i, place: (i, 0, 0)),
        pl.BlockSpec(
            (groups, count, rows, cols),
            lambda i, place: (i, first // count, 0, 0),
        ),
    ]
    aliases = {}
    if previous is not None:
        operands.append(previous)
        in_specs.append(pl.BlockSpec(memory_space=pl.ANY))
        aliases = {4: 0}
    return pl.pallas_call(
        functools.partial(residual_kernel, count),
        grid_spec=pltpu.PrefetchScalarGridSpec(
            num_scalar_prefetch=1,
            grid=(steps,),
            in_specs=in_specs,
            out_specs=in_specs[2],
            scratch_shapes=[pltpu.VMEM((cols // 128, rows * count, 128), jnp.float32)],
        ),
        out_shape=jax.ShapeDtypeStruct(features.shape, jnp.bfloat16),
        input_output_aliases=aliases,
        compiler_params=pltpu.CompilerParams(vmem_limit_bytes=VMEM_BYTES),
        cost_estimate=pl.CostEstimate(
            flops=halves * count * rows * cols,
            bytes_accessed=halves * count * rows * cols * 8,
            transcendentals=0,
        ),
        name="residual",
    )(place, *operands)


def swap(block):
    return lax.ppermute(block, "section", [(0, 1), (1, 0)])


def local(
    aerial_patch_grid,
    patch_conv_weight,
    patch_bias,
    merging_conv_weight,
    merge_bias,
    down_weight,
    down_bias,
    norm_gain,
    spectral_filter,
):
    tile_rows, field_cols, depth = aerial_patch_grid.shape
    channels = down_weight.shape[3]
    tile_channels = spectral_filter.shape[0]
    full_rows = spectral_filter.shape[2]
    sections = lax.axis_size("section")
    devices = sections * lax.axis_size("tile")
    suits = (
        sections == 2
        and tile_rows % 4 == 0
        and tile_channels % 4 == 0
        and (tile_rows // 2) * (tile_channels // 4) % 8 == 0
        and field_cols % 128 == 0
        and full_rows % 128 == 0
        and tile_channels % 8 == 0
    )
    arguments = (
        aerial_patch_grid,
        patch_conv_weight,
        patch_bias,
        merging_conv_weight,
        merge_bias,
        down_weight,
        down_bias,
        norm_gain,
        spectral_filter,
    )
    if not suits:
        return general_local(*arguments)
    section = lax.axis_index("section")
    tile = lax.axis_index("tile")
    rows = tile_rows // 2
    group = tile_channels // 2
    half_channels = channels // 2
    width = -(-(field_cols // 2 + 1) // 128) * 128

    arriving = from_behind(lower_half(aerial_patch_grid[-1]), "tile", 1)
    inside = (section > 0) | (tile > 0)
    place = jnp.stack([section * (rows // 2), inside, section == 0]).astype(jnp.int32)
    weights = stem_weights(*arguments[1:8])
    pairs = rows // 2
    early = max(pairs // 3, 1)
    spans = [(pairs - early, early), (0, pairs - early)]
    pieces = []
    features = []
    row_order = []
    for first, steps in spans:
        normed, part = stem(
            aerial_patch_grid,
            arriving if first == 0 else None,
            place,
            weights,
            first,
            steps,
            devices,
        )
        normed, arriving = lax.optimization_barrier((normed, arriving))
        normed = lax.all_to_all(normed, DEVICES, split_axis=0, concat_axis=0, tiled=True)
        pieces.append(normed.reshape(2 * steps * devices * group, field_cols))
        features.insert(0, part)
        own_rows = np.arange(2 * first, 2 * (first + steps))
        row_order.append((rows * np.arange(devices)[:, None] + own_rows).reshape(-1))
    features = jnp.concatenate(features, axis=0)
    row_order = np.concatenate(row_order).astype(np.int32)

    channel_place = jnp.reshape(section * group, (1,)).astype(jnp.int32)
    symmetric = symmetric_filter(spectral_filter, channel_place, group, width)
    tables = filter_tables(full_rows, field_cols, width, row_order)

    own = lax.dynamic_slice_in_dim(features, section * half_channels, half_channels, 1)
    sent = lax.dynamic_slice_in_dim(features, (1 - section) * half_channels, half_channels, 1)
    arrived = swap(sent)
    low = jnp.where(section == 0, own, arrived)
    high = jnp.where(section == 0, arrived, own)
    residual = jnp.transpose(jnp.concatenate([low, high], axis=0), (1, 0, 2))
    residual = residual.reshape(half_channels // group, group, tile_rows, field_cols)
    pieces, residual, symmetric, tables = lax.optimization_barrier(
        (pieces, residual, symmetric, tables)
    )

    section_place = jnp.reshape(section, (1,)).astype(jnp.int32)
    halves = devices // 2
    output = None
    for first, count in ((group - 2, 2), (0, group - 2)):
        made = filter_channels(pieces, symmetric, tables, first, count, 2, devices)
        returned = lax.all_to_all(made, DEVICES, split_axis=0, concat_axis=0, tiled=True)
        if output is not None:
            returned, output = lax.optimization_barrier((returned, output))
        other = swap(lax.dynamic_slice_in_dim(returned, (1 - section) * halves, halves, 0))
        output = add_residual(section_place, returned, other, residual, output, first, count)
    return output.reshape(half_channels, tile_rows, field_cols)


def solution(mesh):
    return jax.shard_map(
        local,
        mesh=mesh,
        in_specs=(
            P("tile", None, None),
            P(),
            P(),
            P(),
            P(),
            P(),
            P(),
            P(),
            P("tile", None, None, None),
        ),
        out_specs=P("section", "tile", None),
        check_vma=False,
    )
```

```python
import functools
import math

import jax
import jax.numpy as jnp
import numpy as np
from jax import lax
from jax.experimental import pallas as pl
from jax.experimental.pallas import tpu as pltpu
from jax.sharding import PartitionSpec as P

EPSILON = 1e-05


def from_behind(block, axis, distance):
    devices = range(lax.axis_size(axis))
    route = [(i - distance, i) for i in devices if i - distance in devices]
    return lax.ppermute(block, axis, route)


def fourier_tables(length, columns=None):
    indices = jnp.arange(length, dtype=jnp.int32)
    columns = indices if columns is None else jnp.asarray(columns, jnp.int32)
    product = indices[:, None] * columns[None, :] % length
    angles = product.astype(jnp.float32) * (2.0 * math.pi / length)
    return (jnp.cos(angles).astype(jnp.bfloat16), jnp.sin(angles).astype(jnp.bfloat16))


def patch_kernel_matrix(patch_conv_weight):
    identity = jnp.eye(4, dtype=jnp.float32)
    larger = jnp.einsum(
        "baqk,xy,uv->bxauqyvk", patch_conv_weight.astype(jnp.float32), identity, identity
    )
    band_count = patch_conv_weight.shape[0]
    width = patch_conv_weight.shape[3]
    return larger.reshape(band_count * 256, 16 * width).astype(jnp.bfloat16)


def merging_kernel_matrix(merging_conv_weight):
    identity = jnp.eye(2, dtype=jnp.float32)
    larger = jnp.einsum(
        "aqjk,xy,uv->xauqjyvk", merging_conv_weight.astype(jnp.float32), identity, identity
    )
    in_width = merging_conv_weight.shape[2]
    out_width = merging_conv_weight.shape[3]
    return larger.reshape(16 * in_width, 4 * out_width).astype(jnp.bfloat16)


def down_matrices(down_weight):
    nothing = jnp.zeros_like(down_weight[0, 0])
    in_width = down_weight.shape[2]
    out_width = down_weight.shape[3]

    def arrange(entries):
        return jnp.stack(
            [jnp.stack(entries[0], axis=0), jnp.stack(entries[1], axis=0)], axis=0
        ).reshape(4 * in_width, out_width)

    own_taps = arrange(
        [[down_weight[1, 1], down_weight[1, 2]], [down_weight[2, 1], down_weight[2, 2]]]
    )
    upper_taps = arrange([[nothing, nothing], [down_weight[0, 1], down_weight[0, 2]]])
    left_taps = arrange([[nothing, down_weight[1, 0]], [nothing, down_weight[2, 0]]])
    corner_taps = arrange([[nothing, nothing], [nothing, down_weight[0, 0]]])
    return (own_taps, upper_taps, left_taps, corner_taps)


def stem_layers(aerial_patch_grid, patch_conv_weight, patch_bias, merging_conv_weight, merge_bias):
    initial_layer = jnp.einsum(
        "zji,if->zjf",
        aerial_patch_grid,
        patch_kernel_matrix(patch_conv_weight),
        preferred_element_type=jnp.float32,
    )
    initial_layer = jax.nn.gelu(initial_layer + jnp.tile(patch_bias, 16), approximate=True).astype(
        jnp.bfloat16
    )
    layer_two = jnp.einsum(
        "zji,if->zjf",
        initial_layer,
        merging_kernel_matrix(merging_conv_weight),
        preferred_element_type=jnp.float32,
    )
    return jax.nn.gelu(layer_two + jnp.tile(merge_bias, 4), approximate=True).astype(jnp.bfloat16)


def rim_above(extended):
    return from_behind(extended[-1:], "tile", 1)


def down_conv(upper_rim, extended, down_weight, down_bias):
    stacked = jnp.concatenate([upper_rim, extended], axis=0)
    own_taps, upper_taps, left_taps, corner_taps = down_matrices(down_weight)
    summed = jnp.einsum(
        "rwk,kc->crw", stacked[1:, 1:], own_taps, preferred_element_type=jnp.float32
    )
    summed = summed + jnp.einsum(
        "rwk,kc->crw", stacked[:-1, 1:], upper_taps, preferred_element_type=jnp.float32
    )
    summed = summed + jnp.einsum(
        "rwk,kc->crw", stacked[1:, :-1], left_taps, preferred_element_type=jnp.float32
    )
    summed = summed + jnp.einsum(
        "rwk,kc->crw", stacked[:-1, :-1], corner_taps, preferred_element_type=jnp.float32
    )
    return (summed + down_bias[:, None, None]).astype(jnp.bfloat16)


def layer_norm(features, norm_gain):
    values = features.astype(jnp.float32)
    mean_value = jnp.mean(values, axis=0, keepdims=True)
    centered = values - mean_value
    variance = jnp.mean(centered * centered, axis=0, keepdims=True)
    return (norm_gain[:, None, None] * centered * lax.rsqrt(variance + EPSILON)).astype(
        jnp.bfloat16
    )


def filter_columns(row_spectrum, kernel, forward_h, inverse_h):
    spectrum = jnp.einsum(
        "puqh,chqw->cpuw", forward_h, row_spectrum, preferred_element_type=jnp.float32
    ).astype(jnp.bfloat16)
    spec_real = spectrum[:, 0].astype(jnp.float32)
    spec_imag = spectrum[:, 1].astype(jnp.float32)
    filter_real = kernel[:, 0].astype(jnp.float32)
    filter_imag = kernel[:, 1].astype(jnp.float32)
    weighted = jnp.stack(
        [
            filter_real * spec_real - filter_imag * spec_imag,
            filter_real * spec_imag + filter_imag * spec_real,
        ],
        axis=1,
    ).astype(jnp.bfloat16)
    return jnp.einsum(
        "qhpu,cpuw->chqw", inverse_h, weighted, preferred_element_type=jnp.float32
    ).astype(jnp.bfloat16)


def general_local(
    aerial_patch_grid,
    patch_conv_weight,
    patch_bias,
    merging_conv_weight,
    merge_bias,
    down_weight,
    down_bias,
    norm_gain,
    spectral_filter,
):
    section_index = lax.axis_index("section")
    first_section = section_index == 0
    field_cols = aerial_patch_grid.shape[1]
    channels = down_weight.shape[3]
    group_width = spectral_filter.shape[0]
    full_rows = spectral_filter.shape[2]
    half_channels = channels // 2
    cell_half = field_cols // 2
    image_part = lax.dynamic_slice_in_dim(
        aerial_patch_grid, section_index * cell_half, cell_half, 1
    )
    layer_two = stem_layers(
        image_part, patch_conv_weight, patch_bias, merging_conv_weight, merge_bias
    )
    left_column = from_behind(layer_two[:, -1:], "section", 1)
    extended = jnp.concatenate([left_column, layer_two], axis=1)
    upper_rim = rim_above(extended)
    feature_half = down_conv(upper_rim, extended, down_weight, down_bias)
    features = lax.all_gather(feature_half, "section", axis=2, tiled=True)
    normed = layer_norm(features, norm_gain)
    cos_h, sin_h = fourier_tables(full_rows)
    cos_w, sin_w = fourier_tables(field_cols)
    forward_table = jnp.stack([cos_w, -sin_w], axis=1)
    forward_h = jnp.stack(
        [jnp.stack([cos_h, sin_h], axis=1), jnp.stack([-sin_h, cos_h], axis=1)], axis=0
    )
    inverse_h = jnp.stack(
        [jnp.stack([cos_h, -sin_h], axis=1), jnp.stack([sin_h, cos_h], axis=1)], axis=0
    )
    inverse_table = jnp.stack([cos_w, -sin_w], axis=0)
    norm_scale = 1.0 / (full_rows * field_cols)
    fields = lax.all_to_all(normed, "tile", split_axis=0, concat_axis=1, tiled=True)

    def whole_filter():
        frequency_rows = jnp.einsum(
            "chx,xqw->chqw", fields, forward_table, preferred_element_type=jnp.float32
        ).astype(jnp.bfloat16)
        back_rows = filter_columns(frequency_rows, spectral_filter, forward_h, inverse_h)
        result = jnp.einsum(
            "chqw,qwv->chv", back_rows, inverse_table, preferred_element_type=jnp.float32
        )
        return (result * norm_scale).astype(jnp.bfloat16)

    def empty_fields():
        return jnp.zeros((group_width, full_rows, field_cols), jnp.bfloat16)

    filtered_fields = lax.cond(first_section, empty_fields, whole_filter)
    rows_back = lax.all_to_all(filtered_fields, "tile", split_axis=1, concat_axis=0, tiled=True)
    returned = from_behind(rows_back[:half_channels], "section", -1)
    filtered = jnp.where(first_section, returned, rows_back[half_channels:])
    own_part = lax.dynamic_slice_in_dim(features, section_index * half_channels, half_channels, 0)
    return (own_part.astype(jnp.float32) + filtered.astype(jnp.float32)).astype(jnp.bfloat16)


DEVICES = ("tile", "section")
VMEM_BYTES = 60 * 1024 * 1024
GELU_LINEAR = 2.0 * math.sqrt(2.0 / math.pi)
GELU_CUBIC = 4.0 * 0.044715 * GELU_LINEAR
ONES = (64, 128, 64)
TAPS = ((1, 1), (1, 2), (2, 1), (2, 2), (1, 0), (2, 0), (0, 1), (0, 2), (0, 0))


def bias_rows(bias, count):
    high = bias.astype(jnp.bfloat16)
    rest = bias - high.astype(jnp.float32)
    middle = rest.astype(jnp.bfloat16)
    low = (rest - middle.astype(jnp.float32)).astype(jnp.bfloat16)
    shape = (count, bias.shape[1])
    row = lax.broadcasted_iota(jnp.int32, shape, 0)
    rows = jnp.zeros(shape, jnp.float32)
    for k, part in enumerate((high, middle, low)):
        rows = jnp.where(row == k, jnp.broadcast_to(part.astype(jnp.float32), shape), rows)
    return rows.astype(jnp.bfloat16)


def build_weights(sources, targets):
    patch_ref, patch_bias_ref, merge_ref, merge_bias_ref, down_ref, down_bias_ref, gain_ref = sources
    w1_ref, w2_ref, w3_ref, column_ref = targets

    def exact(a, b):
        return jnp.dot(
            a.astype(jnp.bfloat16), b.astype(jnp.bfloat16), preferred_element_type=jnp.float32
        )

    taps, width = patch_ref.shape
    row = lax.broadcasted_iota(jnp.int32, (4 * taps, taps), 0)
    col = lax.broadcasted_iota(jnp.int32, (4 * taps, taps), 1)
    pick = jnp.where(row // 16 * 4 + row % 4 == col, 1.0, 0.0)
    row = lax.broadcasted_iota(jnp.int32, (width, 4 * width), 0)
    col = lax.broadcasted_iota(jnp.int32, (width, 4 * width), 1)
    repeat = jnp.where(col % width == row, 1.0, 0.0)
    spread = exact(pick, exact(patch_ref[...], repeat))
    row = lax.broadcasted_iota(jnp.int32, spread.shape, 0)
    col = lax.broadcasted_iota(jnp.int32, spread.shape, 1)
    spread = jnp.where(row // 4 % 4 == col // width, 0.5 * spread, 0.0).astype(jnp.bfloat16)
    bias = jnp.broadcast_to(0.5 * patch_bias_ref[...], (8, width))
    tiled = jnp.zeros((8, 4 * width), jnp.float32)
    for _ in range(3):
        part = bias.astype(jnp.bfloat16).astype(jnp.float32)
        tiled = tiled + exact(part, repeat)
        bias = bias - part
    first = jnp.concatenate([spread, bias_rows(tiled[:1], ONES[0])], axis=0)
    w1_ref[...] = first.T
    half = (merge_ref[...].astype(jnp.float32) * 0.5).astype(jnp.bfloat16)
    second = jnp.concatenate([half, bias_rows(0.5 * merge_bias_ref[...], ONES[1])], axis=0)
    w2_ref[...] = second.T
    third = [down_ref[3 * a + q] for a, q in TAPS]
    third = jnp.concatenate(third + [bias_rows(down_bias_ref[...], ONES[2])], axis=0)
    w3_ref[...] = third.T
    column_ref[...] = jnp.broadcast_to(gain_ref[...], (128, gain_ref.shape[1])).T


def weight_sources(
    patch_conv_weight, patch_bias, merging_conv_weight, merge_bias, down_weight, down_bias,
    norm_gain,
):
    width = patch_conv_weight.shape[3]
    merged = merging_conv_weight.shape[3]
    return [
        patch_conv_weight.reshape(-1, width),
        patch_bias[None],
        merging_conv_weight.reshape(-1, merged),
        merge_bias[None],
        down_weight.reshape(-1, merged, down_weight.shape[3]),
        down_bias[None],
        norm_gain[None],
    ]


def weight_shapes(sources):
    taps, width = sources[0].shape
    merged, channels = sources[4].shape[1:]
    return [
        jax.ShapeDtypeStruct((4 * width, 4 * taps + ONES[0]), jnp.bfloat16),
        jax.ShapeDtypeStruct((merged, 4 * width + ONES[1]), jnp.bfloat16),
        jax.ShapeDtypeStruct((channels, 9 * merged + ONES[2]), jnp.bfloat16),
        jax.ShapeDtypeStruct((channels, 128), jnp.float32),
    ]


def half_gelu(h):
    return h + h * jnp.tanh(h * (GELU_LINEAR + GELU_CUBIC * (h * h)))


def lower_half(row):
    depth = row.shape[1]
    return jnp.concatenate(
        [row[:, 256 * b + 128 : 256 * b + 256] for b in range(depth // 256)], axis=1
    )


def stem_kernel(kind, place_ref, x_ref, above_ref, *refs):
    if kind == "first":
        sources = refs[:7]
        normed_ref, feat_ref, w1_ref, w2_ref, w3_ref, gain_ref, field = refs[7:]
    else:
        w1_ref, w2_ref, w3_ref, gain_ref = refs[:4]
        normed_ref, feat_ref, field = refs[-3:]
    step = pl.program_id(0)
    rows, cols, depth = x_ref.shape
    bands = depth // 256
    channels = w3_ref.shape[0]
    merged = w2_ref.shape[0]
    group = normed_ref.shape[2] // rows
    cells = rows * cols

    if kind == "first":

        @pl.when(step == 0)
        def _():
            build_weights(sources, (w1_ref, w2_ref, w3_ref, gain_ref))

    w1 = w1_ref[...]
    w2 = w2_ref[...]

    def ones(count, n):
        return jnp.where(lax.broadcasted_iota(jnp.int32, (count, n), 0) < 3, 1.0, 0.0).astype(
            jnp.bfloat16
        )

    def layer_one(turned, offsets):
        n = turned.shape[1]
        parts = [turned[o : o + 64] for o in offsets] + [ones(ONES[0], n)]
        h = jnp.dot(w1, jnp.concatenate(parts, axis=0), preferred_element_type=jnp.float32)
        return half_gelu(h).astype(jnp.bfloat16)

    def layer_two(upper, lower, y):
        n = upper.shape[1]
        span = slice(2 * y * (w1.shape[0] // 4), 2 * (y + 1) * (w1.shape[0] // 4))
        stacked = jnp.concatenate([upper[span], lower[span], ones(ONES[1], n)], axis=0)
        return half_gelu(jnp.dot(w2, stacked, preferred_element_type=jnp.float32))

    def shifted(values):
        lanes = lax.broadcasted_iota(jnp.int32, values.shape, 1)
        moved = pltpu.roll(values, 1, 1)
        return jnp.where(lax.rem(lanes, cols) == 0, 0.0, moved)

    def put(block, lanes, values):
        field[block * merged : (block + 1) * merged, lanes] = values.astype(jnp.bfloat16)

    first_row = slice(0, cols)
    last_row = slice(cells - cols, cells)
    later_rows = slice(cols, cells)
    earlier_rows = slice(0, cells - cols)

    @pl.when(step == 0)
    def _():
        field[9 * merged :, :] = ones(ONES[2], cells)
        above = lower_half(above_ref[0])
        keep = 1.0
        if kind == "last":
            keep = place_ref[1].astype(jnp.float32)
            above = jnp.where(place_ref[2] > 0, refs[4][...], above)
        turned = above.T
        upper, lower = (
            layer_one(turned, [128 * b + 64 * a for b in range(bands)]) for a in range(2)
        )
        put(6, first_row, layer_two(upper, lower, 0) * keep)
        right = layer_two(upper, lower, 1) * keep
        put(7, first_row, right)
        put(8, first_row, shifted(right))

    @pl.when(step > 0)
    def _():
        for source, target in ((2, 6), (3, 7), (5, 8)):
            field[target * merged : (target + 1) * merged, first_row] = field[
                source * merged : (source + 1) * merged, last_row
            ]

    turned = x_ref[...].reshape(cells, depth).T
    for x in range(2):
        upper, lower = (
            layer_one(turned, [256 * b + 64 * (2 * x + a) for b in range(bands)])
            for a in range(2)
        )
        left = layer_two(upper, lower, 0)
        right = layer_two(upper, lower, 1)
        put(2 * x, slice(None), left)
        put(2 * x + 1, slice(None), right)
        moved = shifted(right)
        put(4 + x, slice(None), moved)
        if x == 1:
            put(6, later_rows, left[:, earlier_rows])
            put(7, later_rows, right[:, earlier_rows])
            put(8, later_rows, moved[:, earlier_rows])

    features = jnp.dot(w3_ref[...], field[...], preferred_element_type=jnp.float32).astype(
        jnp.bfloat16
    )
    for r in range(rows):
        feat_ref[r] = features[:, r * cols : (r + 1) * cols]
    values = features.astype(jnp.float32)
    centered = values - jnp.mean(values, axis=0, keepdims=True)
    variance = jnp.mean(centered * centered, axis=0, keepdims=True)
    gain = jnp.concatenate([gain_ref[...]] * (cells // 128), axis=1)
    normed = gain * (centered * lax.rsqrt(variance + EPSILON))
    pair = 2 * group
    index = lax.broadcasted_iota(jnp.int32, (pair, cols), 0)
    for t in range(channels // pair):
        one = normed[pair * t : pair * (t + 1), :cols]
        two = normed[pair * t : pair * (t + 1), cols:]
        normed_ref[2 * t, 0] = jnp.where(index < group, one, pltpu.roll(two, group, 0)).astype(
            jnp.bfloat16
        )
        normed_ref[2 * t + 1, 0] = jnp.where(
            index < group, pltpu.roll(one, group, 0), two
        ).astype(jnp.bfloat16)


def stem(kind, image, place, weights, first, steps, base, pairs, devices, extra=()):
    cols, depth = image.shape[1:]
    rows = 2 * steps
    shapes = weight_shapes(weights) if kind == "first" else weights
    channels, third_depth = shapes[2].shape
    merged = shapes[1].shape[0]
    group = channels // devices

    def whole(array):
        return pl.BlockSpec(array.shape, lambda i, place: (0,) * len(array.shape))

    operands = list(weights) + list(extra)
    in_specs = [whole(a) for a in weights]
    out_specs = [
        pl.BlockSpec(
            (devices, 1, 2 * group, cols), lambda i, place: (0, first - base + i, 0, 0)
        ),
        pl.BlockSpec((2, channels, cols), lambda i, place: (first - base + i, 0, 0)),
    ]
    out_shape = [
        jax.ShapeDtypeStruct((devices, pairs, 2 * group, cols), jnp.bfloat16),
        jax.ShapeDtypeStruct((2 * pairs, channels, cols), jnp.bfloat16),
    ]
    aliases = {}
    if kind == "first":
        out_specs += [whole(a) for a in shapes]
        out_shape += shapes
    if kind == "last":
        in_specs += [whole(extra[0])] + [pl.BlockSpec(memory_space=pl.ANY)] * 2
        aliases = {8: 0, 9: 1}
    macs = rows * cols * (16 * 208 * 96 + 4 * 400 * merged + third_depth * channels)
    return pl.pallas_call(
        functools.partial(stem_kernel, kind),
        grid_spec=pltpu.PrefetchScalarGridSpec(
            num_scalar_prefetch=1,
            grid=(steps,),
            in_specs=[
                pl.BlockSpec((2, cols, depth), lambda i, place: (place[0] + first + i, 0, 0)),
                pl.BlockSpec(
                    (1, cols, depth),
                    lambda i, place: (jnp.maximum(2 * (place[0] + first) - 1, 0), 0, 0),
                ),
            ]
            + in_specs,
            out_specs=out_specs,
            scratch_shapes=[pltpu.VMEM((third_depth, 2 * cols), jnp.bfloat16)],
        ),
        out_shape=out_shape,
        input_output_aliases=aliases,
        compiler_params=pltpu.CompilerParams(vmem_limit_bytes=VMEM_BYTES),
        cost_estimate=pl.CostEstimate(
            flops=4 * macs, bytes_accessed=rows * cols * 3000, transcendentals=0
        ),
        name="stem",
    )(place, image, image, *operands)


def symmetric_kernel(place_ref, f_ref, turn_w_ref, turn_u_ref, g_ref):
    width = g_ref.shape[3]
    for part in range(2):
        block = f_ref[0, part]
        across = jnp.dot(block, turn_w_ref[...], preferred_element_type=jnp.float32)
        turned = jnp.dot(
            turn_u_ref[...], across.astype(jnp.bfloat16), preferred_element_type=jnp.float32
        )
        own = block[:, :width].astype(jnp.float32)
        g_ref[0, part] = 0.5 * (own + turned if part == 0 else own - turned)


def symmetric_filter(spectral_filter, place, group, width):
    full_rows, full_cols = spectral_filter.shape[2:]
    u = jnp.arange(full_rows, dtype=jnp.int32)
    w = jnp.arange(full_cols, dtype=jnp.int32)
    turn_u = ((u[:, None] + u[None, :]) % full_rows == 0).astype(jnp.bfloat16)
    turn_w = ((w[:, None] + w[None, :width]) % full_cols == 0).astype(jnp.bfloat16)
    return pl.pallas_call(
        symmetric_kernel,
        grid_spec=pltpu.PrefetchScalarGridSpec(
            num_scalar_prefetch=1,
            grid=(group,),
            in_specs=[
                pl.BlockSpec(
                    (1, 2, full_rows, full_cols), lambda i, place: (place[0] + i, 0, 0, 0)
                ),
                pl.BlockSpec(turn_w.shape, lambda i, place: (0, 0)),
                pl.BlockSpec(turn_u.shape, lambda i, place: (0, 0)),
            ],
            out_specs=pl.BlockSpec((1, 2, full_rows, width), lambda i, place: (i, 0, 0, 0)),
        ),
        out_shape=jax.ShapeDtypeStruct((group, 2, full_rows, width), jnp.float32),
        compiler_params=pltpu.CompilerParams(vmem_limit_bytes=VMEM_BYTES),
        cost_estimate=pl.CostEstimate(
            flops=8 * group * full_rows * full_cols * width,
            bytes_accessed=group * full_rows * width * 14,
            transcendentals=0,
        ),
        name="symmetric_filter",
    )(place, spectral_filter, turn_w, turn_u)


def to_lane_tiles(target, rows, values):
    for j in range(target.shape[0]):
        target[j, rows, :] = values[:, 128 * j : 128 * (j + 1)]


def from_lane_tiles(source, rows):
    return jnp.concatenate([source[j, rows, :] for j in range(source.shape[0])], axis=1)


def filter_kernel(
    first, norm_scale, *refs
):
    *pieces, g_ref, row_table_ref, fwd_ref, inv_ref, back_ref, out_ref, held, made = refs
    step = pl.program_id(0)
    full_rows = fwd_ref.shape[0] // 2
    width = g_ref.shape[3]
    group = held.shape[1] // full_rows
    count = made.shape[1] // full_rows
    per_step = g_ref.shape[0]

    @pl.when(step == 0)
    def _():
        begin = 0
        for piece in pieces:
            end = begin + piece.shape[0]
            to_lane_tiles(held, slice(begin, end), piece[...].astype(jnp.float32))
            begin = end

    blocks = []
    for k in range(per_step):
        rows = pl.ds(first + step * per_step + k, full_rows, stride=group)
        field = from_lane_tiles(held, rows)
        spread = jnp.dot(
            field.astype(jnp.bfloat16), row_table_ref[...], preferred_element_type=jnp.float32
        ).astype(jnp.bfloat16)
        blocks.append(jnp.concatenate([spread[:, :width], spread[:, width:]], axis=0))
    spectrum = jnp.dot(
        fwd_ref[...], jnp.concatenate(blocks, axis=1), preferred_element_type=jnp.float32
    )
    blocks = []
    for k in range(per_step):
        real = spectrum[:full_rows, k * width : (k + 1) * width]
        imag = spectrum[full_rows:, k * width : (k + 1) * width]
        g_real = g_ref[k, 0]
        g_imag = g_ref[k, 1]
        blocks.append(
            jnp.concatenate(
                [g_real * real - g_imag * imag, g_real * imag + g_imag * real], axis=0
            ).astype(jnp.bfloat16)
        )
    back = jnp.dot(
        inv_ref[...], jnp.concatenate(blocks, axis=1), preferred_element_type=jnp.float32
    ).astype(jnp.bfloat16)
    for k in range(per_step):
        lanes = slice(k * width, (k + 1) * width)
        both = jnp.concatenate([back[:full_rows, lanes], back[full_rows:, lanes]], axis=1)
        result = jnp.dot(both, back_ref[...], preferred_element_type=jnp.float32)
        rows = pl.ds(step * per_step + k, full_rows, stride=count)
        to_lane_tiles(made, rows, result * norm_scale)

    @pl.when(step == pl.num_programs(0) - 1)
    def _():
        out_ref[...] = from_lane_tiles(made, slice(None)).astype(jnp.bfloat16)


def filter_tables(full_rows, field_cols, width, row_order):
    cos_h, sin_h = fourier_tables(full_rows)
    cos_f, sin_f = fourier_tables(full_rows, row_order)
    cos_w, sin_w = fourier_tables(field_cols)
    fwd = jnp.concatenate(
        [jnp.concatenate([cos_f, sin_f], 1), jnp.concatenate([-sin_f, cos_f], 1)], 0
    )
    inv = jnp.concatenate(
        [jnp.concatenate([cos_h, -sin_h], 1), jnp.concatenate([sin_h, cos_h], 1)], 0
    )
    w = jnp.arange(width, dtype=jnp.int32)
    half = field_cols // 2
    valid = (w <= half).astype(jnp.bfloat16)
    times = jnp.where((w == 0) | (w == half), 1.0, 2.0).astype(jnp.bfloat16) * valid
    row_table = jnp.concatenate([cos_w[:, :width] * valid, -sin_w[:, :width] * valid], 1)
    back_table = jnp.concatenate(
        [cos_w[:width] * times[:, None], -sin_w[:width] * times[:, None]], 0
    )
    return row_table, fwd, inv, back_table


def filter_channels(pieces, symmetric, tables, first, count, per_step, devices):
    row_table, fwd, inv, back_table = tables
    full_rows = fwd.shape[0] // 2
    cols = pieces[0].shape[1]
    group = sum(piece.shape[0] for piece in pieces) // full_rows
    width = symmetric.shape[3]

    def whole(array):
        return pl.BlockSpec(array.shape, lambda i: (0,) * array.ndim)

    macs = count * (2 * 4 * full_rows * full_rows * width + 4 * full_rows * cols * width)
    made = pl.pallas_call(
        functools.partial(filter_kernel, first, 1.0 / (full_rows * cols)),
        grid=(count // per_step,),
        in_specs=[
            *[whole(piece) for piece in pieces],
            pl.BlockSpec(
                (per_step, 2, full_rows, width), lambda i: (first // per_step + i, 0, 0, 0)
            ),
            whole(row_table),
            whole(fwd),
            whole(inv),
            whole(back_table),
        ],
        out_specs=pl.BlockSpec((full_rows * count, cols), lambda i: (0, 0)),
        out_shape=jax.ShapeDtypeStruct((full_rows * count, cols), jnp.bfloat16),
        scratch_shapes=[
            pltpu.VMEM((cols // 128, full_rows * group, 128), jnp.float32),
            pltpu.VMEM((cols // 128, full_rows * count, 128), jnp.float32),
        ],
        compiler_params=pltpu.CompilerParams(vmem_limit_bytes=VMEM_BYTES * 2 // 3),
        cost_estimate=pl.CostEstimate(
            flops=2 * macs, bytes_accessed=count * full_rows * cols * 8, transcendentals=0
        ),
        name="spectral_filter",
    )(*pieces, symmetric, row_table, fwd, inv, back_table)
    return made.reshape(devices, full_rows // devices * count, cols)


def residual_kernel(count, place_ref, kept_ref, other_ref, feat_ref, *refs):
    out_ref, held = refs[-2:]
    groups, span, cols = kept_ref.shape
    rows = held.shape[1] // count
    own = pl.multiple_of(place_ref[0] * span, 8)
    far = pl.multiple_of((1 - place_ref[0]) * span, 8)
    for g in range(groups):
        to_lane_tiles(held, pl.ds(own, span), kept_ref[g].astype(jnp.float32))
        to_lane_tiles(held, pl.ds(far, span), other_ref[g].astype(jnp.float32))
        for k in range(count):
            filtered = from_lane_tiles(held, pl.ds(k, rows, stride=count))
            out_ref[g, k] = (feat_ref[g, k].astype(jnp.float32) + filtered).astype(jnp.bfloat16)


def add_residual(place, returned, other, features, previous, first, count):
    halves, span, cols = other.shape
    group, rows = features.shape[1:3]
    groups = 4 if halves % 4 == 0 else 1
    steps = halves // groups
    operands = [returned, other, features]
    in_specs = [
        pl.BlockSpec((groups, span, cols), lambda i, place: (place[0] * steps + i, 0, 0)),
        pl.BlockSpec((groups, span, cols), lambda i, place: (i, 0, 0)),
        pl.BlockSpec(
            (groups, count, rows, cols),
            lambda i, place: (i, first // count, 0, 0),
        ),
    ]
    aliases = {}
    if previous is not None:
        operands.append(previous)
        in_specs.append(pl.BlockSpec(memory_space=pl.ANY))
        aliases = {4: 0}
    return pl.pallas_call(
        functools.partial(residual_kernel, count),
        grid_spec=pltpu.PrefetchScalarGridSpec(
            num_scalar_prefetch=1,
            grid=(steps,),
            in_specs=in_specs,
            out_specs=in_specs[2],
            scratch_shapes=[pltpu.VMEM((cols // 128, rows * count, 128), jnp.float32)],
        ),
        out_shape=jax.ShapeDtypeStruct(features.shape, jnp.bfloat16),
        input_output_aliases=aliases,
        compiler_params=pltpu.CompilerParams(vmem_limit_bytes=VMEM_BYTES // 3),
        cost_estimate=pl.CostEstimate(
            flops=halves * count * rows * cols,
            bytes_accessed=halves * count * rows * cols * 8,
            transcendentals=0,
        ),
        name="residual",
    )(place, *operands)


def swap(block):
    return lax.ppermute(block, "section", [(0, 1), (1, 0)])


def local(
    aerial_patch_grid,
    patch_conv_weight,
    patch_bias,
    merging_conv_weight,
    merge_bias,
    down_weight,
    down_bias,
    norm_gain,
    spectral_filter,
):
    tile_rows, field_cols, depth = aerial_patch_grid.shape
    channels = down_weight.shape[3]
    tile_channels = spectral_filter.shape[0]
    full_rows = spectral_filter.shape[2]
    sections = lax.axis_size("section")
    devices = sections * lax.axis_size("tile")
    suits = (
        sections == 2
        and tile_rows % 8 == 0
        and tile_rows >= 16
        and field_cols % 128 == 0
        and full_rows % 128 == 0
        and tile_channels % 8 == 0
    )
    arguments = (
        aerial_patch_grid,
        patch_conv_weight,
        patch_bias,
        merging_conv_weight,
        merge_bias,
        down_weight,
        down_bias,
        norm_gain,
        spectral_filter,
    )
    if not suits:
        return general_local(*arguments)
    section = lax.axis_index("section")
    tile = lax.axis_index("tile")
    rows = tile_rows // 2
    group = tile_channels // 2
    half_channels = channels // 2
    width = -(-(field_cols // 2 + 1) // 128) * 128

    arriving = from_behind(lower_half(aerial_patch_grid[-1]), "tile", 1)
    inside = (section > 0) | (tile > 0)
    place = jnp.stack([section * (rows // 2), inside, section == 0]).astype(jnp.int32)
    sources = weight_sources(*arguments[1:8])
    pairs = rows // 2
    early = max(pairs // 3, 1)
    late = pairs - early
    normed_early, feat_early, *weights = stem(
        "first", aerial_patch_grid, place, sources, late, early, late, early, devices
    )
    normed_late = stem(
        "middle", aerial_patch_grid, place, weights, 1, late - 1, 0, late, devices
    )
    normed_late, feat_late = stem(
        "last", aerial_patch_grid, place, weights, 0, 1, 0, late, devices, (arriving, *normed_late)
    )
    pieces = []
    row_order = []
    for normed, first, count in ((normed_early, late, early), (normed_late, 0, late)):
        normed = lax.all_to_all(normed, DEVICES, split_axis=0, concat_axis=0, tiled=True)
        pieces.append(normed.reshape(2 * count * devices * group, field_cols))
        own_rows = np.arange(2 * first, 2 * (first + count))
        row_order.append((rows * np.arange(devices)[:, None] + own_rows).reshape(-1))
    features = [feat_late, feat_early]
    features = jnp.concatenate(features, axis=0)
    row_order = np.concatenate(row_order).astype(np.int32)

    channel_place = jnp.reshape(section * group, (1,)).astype(jnp.int32)
    symmetric = symmetric_filter(spectral_filter, channel_place, group, width)
    tables = filter_tables(full_rows, field_cols, width, row_order)

    own = lax.dynamic_slice_in_dim(features, section * half_channels, half_channels, 1)
    sent = lax.dynamic_slice_in_dim(features, (1 - section) * half_channels, half_channels, 1)
    arrived = swap(sent)
    low = jnp.where(section == 0, own, arrived)
    high = jnp.where(section == 0, arrived, own)
    residual = jnp.transpose(jnp.concatenate([low, high], axis=0), (1, 0, 2))
    residual = residual.reshape(half_channels // group, group, tile_rows, field_cols)
    pieces, residual, symmetric, tables = lax.optimization_barrier(
        (pieces, residual, symmetric, tables)
    )

    section_place = jnp.reshape(section, (1,)).astype(jnp.int32)
    halves = devices // 2
    output = None
    for first, count in ((group - 2, 2), (0, group - 2)):
        made = filter_channels(pieces, symmetric, tables, first, count, 2, devices)
        returned = lax.all_to_all(made, DEVICES, split_axis=0, concat_axis=0, tiled=True)
        if output is not None:
            returned, output = lax.optimization_barrier((returned, output))
        other = swap(lax.dynamic_slice_in_dim(returned, (1 - section) * halves, halves, 0))
        output = add_residual(section_place, returned, other, residual, output, first, count)
    return output.reshape(half_channels, tile_rows, field_cols)


def solution(mesh):
    return jax.shard_map(
        local,
        mesh=mesh,
        in_specs=(
            P("tile", None, None),
            P(),
            P(),
            P(),
            P(),
            P(),
            P(),
            P(),
            P("tile", None, None, None),
        ),
        out_specs=P("section", "tile", None),
        check_vma=False,
    )
```

```python
import functools
import math

import jax
import jax.numpy as jnp
import numpy as np
from jax import lax
from jax.experimental import pallas as pl
from jax.experimental.pallas import tpu as pltpu
from jax.sharding import PartitionSpec as P

EPSILON = 1e-05


def from_behind(block, axis, distance):
    devices = range(lax.axis_size(axis))
    route = [(i - distance, i) for i in devices if i - distance in devices]
    return lax.ppermute(block, axis, route)


def fourier_tables(length, columns=None):
    indices = jnp.arange(length, dtype=jnp.int32)
    columns = indices if columns is None else jnp.asarray(columns, jnp.int32)
    product = indices[:, None] * columns[None, :] % length
    angles = product.astype(jnp.float32) * (2.0 * math.pi / length)
    return (jnp.cos(angles).astype(jnp.bfloat16), jnp.sin(angles).astype(jnp.bfloat16))


def patch_kernel_matrix(patch_conv_weight):
    identity = jnp.eye(4, dtype=jnp.float32)
    larger = jnp.einsum(
        "baqk,xy,uv->bxauqyvk", patch_conv_weight.astype(jnp.float32), identity, identity
    )
    band_count = patch_conv_weight.shape[0]
    width = patch_conv_weight.shape[3]
    return larger.reshape(band_count * 256, 16 * width).astype(jnp.bfloat16)


def merging_kernel_matrix(merging_conv_weight):
    identity = jnp.eye(2, dtype=jnp.float32)
    larger = jnp.einsum(
        "aqjk,xy,uv->xauqjyvk", merging_conv_weight.astype(jnp.float32), identity, identity
    )
    in_width = merging_conv_weight.shape[2]
    out_width = merging_conv_weight.shape[3]
    return larger.reshape(16 * in_width, 4 * out_width).astype(jnp.bfloat16)


def down_matrices(down_weight):
    nothing = jnp.zeros_like(down_weight[0, 0])
    in_width = down_weight.shape[2]
    out_width = down_weight.shape[3]

    def arrange(entries):
        return jnp.stack(
            [jnp.stack(entries[0], axis=0), jnp.stack(entries[1], axis=0)], axis=0
        ).reshape(4 * in_width, out_width)

    own_taps = arrange(
        [[down_weight[1, 1], down_weight[1, 2]], [down_weight[2, 1], down_weight[2, 2]]]
    )
    upper_taps = arrange([[nothing, nothing], [down_weight[0, 1], down_weight[0, 2]]])
    left_taps = arrange([[nothing, down_weight[1, 0]], [nothing, down_weight[2, 0]]])
    corner_taps = arrange([[nothing, nothing], [nothing, down_weight[0, 0]]])
    return (own_taps, upper_taps, left_taps, corner_taps)


def stem_layers(aerial_patch_grid, patch_conv_weight, patch_bias, merging_conv_weight, merge_bias):
    initial_layer = jnp.einsum(
        "zji,if->zjf",
        aerial_patch_grid,
        patch_kernel_matrix(patch_conv_weight),
        preferred_element_type=jnp.float32,
    )
    initial_layer = jax.nn.gelu(initial_layer + jnp.tile(patch_bias, 16), approximate=True).astype(
        jnp.bfloat16
    )
    layer_two = jnp.einsum(
        "zji,if->zjf",
        initial_layer,
        merging_kernel_matrix(merging_conv_weight),
        preferred_element_type=jnp.float32,
    )
    return jax.nn.gelu(layer_two + jnp.tile(merge_bias, 4), approximate=True).astype(jnp.bfloat16)


def rim_above(extended):
    return from_behind(extended[-1:], "tile", 1)


def down_conv(upper_rim, extended, down_weight, down_bias):
    stacked = jnp.concatenate([upper_rim, extended], axis=0)
    own_taps, upper_taps, left_taps, corner_taps = down_matrices(down_weight)
    summed = jnp.einsum(
        "rwk,kc->crw", stacked[1:, 1:], own_taps, preferred_element_type=jnp.float32
    )
    summed = summed + jnp.einsum(
        "rwk,kc->crw", stacked[:-1, 1:], upper_taps, preferred_element_type=jnp.float32
    )
    summed = summed + jnp.einsum(
        "rwk,kc->crw", stacked[1:, :-1], left_taps, preferred_element_type=jnp.float32
    )
    summed = summed + jnp.einsum(
        "rwk,kc->crw", stacked[:-1, :-1], corner_taps, preferred_element_type=jnp.float32
    )
    return (summed + down_bias[:, None, None]).astype(jnp.bfloat16)


def layer_norm(features, norm_gain):
    values = features.astype(jnp.float32)
    mean_value = jnp.mean(values, axis=0, keepdims=True)
    centered = values - mean_value
    variance = jnp.mean(centered * centered, axis=0, keepdims=True)
    return (norm_gain[:, None, None] * centered * lax.rsqrt(variance + EPSILON)).astype(
        jnp.bfloat16
    )


def filter_columns(row_spectrum, kernel, forward_h, inverse_h):
    spectrum = jnp.einsum(
        "puqh,chqw->cpuw", forward_h, row_spectrum, preferred_element_type=jnp.float32
    ).astype(jnp.bfloat16)
    spec_real = spectrum[:, 0].astype(jnp.float32)
    spec_imag = spectrum[:, 1].astype(jnp.float32)
    filter_real = kernel[:, 0].astype(jnp.float32)
    filter_imag = kernel[:, 1].astype(jnp.float32)
    weighted = jnp.stack(
        [
            filter_real * spec_real - filter_imag * spec_imag,
            filter_real * spec_imag + filter_imag * spec_real,
        ],
        axis=1,
    ).astype(jnp.bfloat16)
    return jnp.einsum(
        "qhpu,cpuw->chqw", inverse_h, weighted, preferred_element_type=jnp.float32
    ).astype(jnp.bfloat16)


def general_local(
    aerial_patch_grid,
    patch_conv_weight,
    patch_bias,
    merging_conv_weight,
    merge_bias,
    down_weight,
    down_bias,
    norm_gain,
    spectral_filter,
):
    section_index = lax.axis_index("section")
    first_section = section_index == 0
    field_cols = aerial_patch_grid.shape[1]
    channels = down_weight.shape[3]
    group_width = spectral_filter.shape[0]
    full_rows = spectral_filter.shape[2]
    half_channels = channels // 2
    cell_half = field_cols // 2
    image_part = lax.dynamic_slice_in_dim(
        aerial_patch_grid, section_index * cell_half, cell_half, 1
    )
    layer_two = stem_layers(
        image_part, patch_conv_weight, patch_bias, merging_conv_weight, merge_bias
    )
    left_column = from_behind(layer_two[:, -1:], "section", 1)
    extended = jnp.concatenate([left_column, layer_two], axis=1)
    upper_rim = rim_above(extended)
    feature_half = down_conv(upper_rim, extended, down_weight, down_bias)
    features = lax.all_gather(feature_half, "section", axis=2, tiled=True)
    normed = layer_norm(features, norm_gain)
    cos_h, sin_h = fourier_tables(full_rows)
    cos_w, sin_w = fourier_tables(field_cols)
    forward_table = jnp.stack([cos_w, -sin_w], axis=1)
    forward_h = jnp.stack(
        [jnp.stack([cos_h, sin_h], axis=1), jnp.stack([-sin_h, cos_h], axis=1)], axis=0
    )
    inverse_h = jnp.stack(
        [jnp.stack([cos_h, -sin_h], axis=1), jnp.stack([sin_h, cos_h], axis=1)], axis=0
    )
    inverse_table = jnp.stack([cos_w, -sin_w], axis=0)
    norm_scale = 1.0 / (full_rows * field_cols)
    fields = lax.all_to_all(normed, "tile", split_axis=0, concat_axis=1, tiled=True)

    def whole_filter():
        frequency_rows = jnp.einsum(
            "chx,xqw->chqw", fields, forward_table, preferred_element_type=jnp.float32
        ).astype(jnp.bfloat16)
        back_rows = filter_columns(frequency_rows, spectral_filter, forward_h, inverse_h)
        result = jnp.einsum(
            "chqw,qwv->chv", back_rows, inverse_table, preferred_element_type=jnp.float32
        )
        return (result * norm_scale).astype(jnp.bfloat16)

    def empty_fields():
        return jnp.zeros((group_width, full_rows, field_cols), jnp.bfloat16)

    filtered_fields = lax.cond(first_section, empty_fields, whole_filter)
    rows_back = lax.all_to_all(filtered_fields, "tile", split_axis=1, concat_axis=0, tiled=True)
    returned = from_behind(rows_back[:half_channels], "section", -1)
    filtered = jnp.where(first_section, returned, rows_back[half_channels:])
    own_part = lax.dynamic_slice_in_dim(features, section_index * half_channels, half_channels, 0)
    return (own_part.astype(jnp.float32) + filtered.astype(jnp.float32)).astype(jnp.bfloat16)


DEVICES = ("tile", "section")
VMEM_BYTES = 60 * 1024 * 1024
GELU_LINEAR = 2.0 * math.sqrt(2.0 / math.pi)
GELU_CUBIC = 4.0 * 0.044715 * GELU_LINEAR
ONES = (64, 128, 64)
TAPS = ((1, 1), (1, 2), (2, 1), (2, 2), (1, 0), (2, 0), (0, 1), (0, 2), (0, 0))


def bias_rows(bias, count):
    high = bias.astype(jnp.bfloat16)
    rest = bias - high.astype(jnp.float32)
    middle = rest.astype(jnp.bfloat16)
    low = (rest - middle.astype(jnp.float32)).astype(jnp.bfloat16)
    shape = (count, bias.shape[1])
    row = lax.broadcasted_iota(jnp.int32, shape, 0)
    rows = jnp.zeros(shape, jnp.float32)
    for k, part in enumerate((high, middle, low)):
        rows = jnp.where(row == k, jnp.broadcast_to(part.astype(jnp.float32), shape), rows)
    return rows.astype(jnp.bfloat16)


def build_weights(sources, targets):
    patch_ref, patch_bias_ref, merge_ref, merge_bias_ref, down_ref, down_bias_ref, gain_ref = sources
    w1_ref, w2_ref, w3_ref, column_ref = targets

    def exact(a, b):
        return jnp.dot(
            a.astype(jnp.bfloat16), b.astype(jnp.bfloat16), preferred_element_type=jnp.float32
        )

    taps, width = patch_ref.shape
    row = lax.broadcasted_iota(jnp.int32, (4 * taps, taps), 0)
    col = lax.broadcasted_iota(jnp.int32, (4 * taps, taps), 1)
    pick = jnp.where(row // 16 * 4 + row % 4 == col, 1.0, 0.0)
    row = lax.broadcasted_iota(jnp.int32, (width, 4 * width), 0)
    col = lax.broadcasted_iota(jnp.int32, (width, 4 * width), 1)
    repeat = jnp.where(col % width == row, 1.0, 0.0)
    spread = exact(pick, exact(patch_ref[...], repeat))
    row = lax.broadcasted_iota(jnp.int32, spread.shape, 0)
    col = lax.broadcasted_iota(jnp.int32, spread.shape, 1)
    spread = jnp.where(row // 4 % 4 == col // width, 0.5 * spread, 0.0).astype(jnp.bfloat16)
    bias = jnp.broadcast_to(0.5 * patch_bias_ref[...][None], (8, width))
    tiled = jnp.zeros((8, 4 * width), jnp.float32)
    for _ in range(3):
        part = bias.astype(jnp.bfloat16).astype(jnp.float32)
        tiled = tiled + exact(part, repeat)
        bias = bias - part
    first = jnp.concatenate([spread, bias_rows(tiled[:1], ONES[0])], axis=0)
    w1_ref[...] = first.T
    half = (merge_ref[...].astype(jnp.float32) * 0.5).astype(jnp.bfloat16)
    second = jnp.concatenate([half, bias_rows(0.5 * merge_bias_ref[...][None], ONES[1])], axis=0)
    w2_ref[...] = second.T
    third = [down_ref[3 * a + q] for a, q in TAPS]
    third = jnp.concatenate(third + [bias_rows(down_bias_ref[...][None], ONES[2])], axis=0)
    w3_ref[...] = third.T
    column_ref[...] = jnp.broadcast_to(gain_ref[...][None], (128, gain_ref.shape[0])).T


def weight_sources(
    patch_conv_weight, patch_bias, merging_conv_weight, merge_bias, down_weight, down_bias,
    norm_gain,
):
    width = patch_conv_weight.shape[3]
    merged = merging_conv_weight.shape[3]
    return [
        patch_conv_weight.reshape(-1, width),
        patch_bias,
        merging_conv_weight.reshape(-1, merged),
        merge_bias,
        down_weight.reshape(-1, merged, down_weight.shape[3]),
        down_bias,
        norm_gain,
    ]


def weight_shapes(sources):
    taps, width = sources[0].shape
    merged, channels = sources[4].shape[1:]
    return [
        jax.ShapeDtypeStruct((4 * width, 4 * taps + ONES[0]), jnp.bfloat16),
        jax.ShapeDtypeStruct((merged, 4 * width + ONES[1]), jnp.bfloat16),
        jax.ShapeDtypeStruct((channels, 9 * merged + ONES[2]), jnp.bfloat16),
        jax.ShapeDtypeStruct((channels, 128), jnp.float32),
    ]


def half_gelu(h):
    return h + h * jnp.tanh(h * (GELU_LINEAR + GELU_CUBIC * (h * h)))


def lower_half(row):
    depth = row.shape[1]
    return jnp.concatenate(
        [row[:, 256 * b + 128 : 256 * b + 256] for b in range(depth // 256)], axis=1
    )


def stem_kernel(kind, place_ref, x_ref, above_ref, *refs):
    if kind == "first":
        sources = refs[:7]
        normed_ref, feat_ref, w1_ref, w2_ref, w3_ref, gain_ref, field = refs[7:]
    else:
        w1_ref, w2_ref, w3_ref, gain_ref = refs[:4]
        normed_ref, feat_ref, field = refs[-3:]
    step = pl.program_id(0)
    rows, cols, depth = x_ref.shape
    bands = depth // 256
    channels = w3_ref.shape[0]
    merged = w2_ref.shape[0]
    group = normed_ref.shape[2] // rows
    cells = rows * cols

    if kind == "first":

        @pl.when(step == 0)
        def _():
            build_weights(sources, (w1_ref, w2_ref, w3_ref, gain_ref))

    w1 = w1_ref[...]
    w2 = w2_ref[...]

    def ones(count, n):
        return jnp.where(lax.broadcasted_iota(jnp.int32, (count, n), 0) < 3, 1.0, 0.0).astype(
            jnp.bfloat16
        )

    def layer_one(turned, offsets):
        n = turned.shape[1]
        parts = [turned[o : o + 64] for o in offsets] + [ones(ONES[0], n)]
        h = jnp.dot(w1, jnp.concatenate(parts, axis=0), preferred_element_type=jnp.float32)
        return half_gelu(h).astype(jnp.bfloat16)

    def layer_two(upper, lower, y):
        n = upper.shape[1]
        span = slice(2 * y * (w1.shape[0] // 4), 2 * (y + 1) * (w1.shape[0] // 4))
        stacked = jnp.concatenate([upper[span], lower[span], ones(ONES[1], n)], axis=0)
        return half_gelu(jnp.dot(w2, stacked, preferred_element_type=jnp.float32))

    def shifted(values):
        lanes = lax.broadcasted_iota(jnp.int32, values.shape, 1)
        moved = pltpu.roll(values, 1, 1)
        return jnp.where(lax.rem(lanes, cols) == 0, 0.0, moved)

    def put(block, lanes, values):
        field[block * merged : (block + 1) * merged, lanes] = values.astype(jnp.bfloat16)

    first_row = slice(0, cols)
    last_row = slice(cells - cols, cells)
    later_rows = slice(cols, cells)
    earlier_rows = slice(0, cells - cols)

    @pl.when(step == 0)
    def _():
        field[9 * merged :, :] = ones(ONES[2], cells)
        above = lower_half(above_ref[0])
        keep = 1.0
        if kind == "last":
            keep = place_ref[1].astype(jnp.float32)
            above = jnp.where(place_ref[2] > 0, refs[4][...], above)
        turned = above.T
        upper, lower = (
            layer_one(turned, [128 * b + 64 * a for b in range(bands)]) for a in range(2)
        )
        put(6, first_row, layer_two(upper, lower, 0) * keep)
        right = layer_two(upper, lower, 1) * keep
        put(7, first_row, right)
        put(8, first_row, shifted(right))

    @pl.when(step > 0)
    def _():
        for source, target in ((2, 6), (3, 7), (5, 8)):
            field[target * merged : (target + 1) * merged, first_row] = field[
                source * merged : (source + 1) * merged, last_row
            ]

    turned = x_ref[...].reshape(cells, depth).T
    for x in range(2):
        upper, lower = (
            layer_one(turned, [256 * b + 64 * (2 * x + a) for b in range(bands)])
            for a in range(2)
        )
        left = layer_two(upper, lower, 0)
        right = layer_two(upper, lower, 1)
        put(2 * x, slice(None), left)
        put(2 * x + 1, slice(None), right)
        moved = shifted(right)
        put(4 + x, slice(None), moved)
        if x == 1:
            put(6, later_rows, left[:, earlier_rows])
            put(7, later_rows, right[:, earlier_rows])
            put(8, later_rows, moved[:, earlier_rows])

    features = jnp.dot(w3_ref[...], field[...], preferred_element_type=jnp.float32).astype(
        jnp.bfloat16
    )
    for r in range(rows):
        feat_ref[r] = features[:, r * cols : (r + 1) * cols]
    values = features.astype(jnp.float32)
    centered = values - jnp.mean(values, axis=0, keepdims=True)
    variance = jnp.mean(centered * centered, axis=0, keepdims=True)
    gain = jnp.concatenate([gain_ref[...]] * (cells // 128), axis=1)
    normed = gain * (centered * lax.rsqrt(variance + EPSILON))
    pair = 2 * group
    index = lax.broadcasted_iota(jnp.int32, (pair, cols), 0)
    for t in range(channels // pair):
        one = normed[pair * t : pair * (t + 1), :cols]
        two = normed[pair * t : pair * (t + 1), cols:]
        normed_ref[2 * t, 0] = jnp.where(index < group, one, pltpu.roll(two, group, 0)).astype(
            jnp.bfloat16
        )
        normed_ref[2 * t + 1, 0] = jnp.where(
            index < group, pltpu.roll(one, group, 0), two
        ).astype(jnp.bfloat16)


def stem(kind, image, place, weights, first, steps, devices, extra=()):
    cols, depth = image.shape[1:]
    rows = 2 * steps
    shapes = weight_shapes(weights) if kind == "first" else weights
    channels, third_depth = shapes[2].shape
    merged = shapes[1].shape[0]
    group = channels // devices

    def whole(array):
        return pl.BlockSpec(array.shape, lambda i, place: (0,) * len(array.shape))

    operands = list(weights) + list(extra)
    in_specs = [whole(a) for a in weights]
    out_specs = [
        pl.BlockSpec((devices, 1, 2 * group, cols), lambda i, place: (0, i, 0, 0)),
        pl.BlockSpec((2, channels, cols), lambda i, place: (i, 0, 0)),
    ]
    out_shape = [
        jax.ShapeDtypeStruct((devices, steps, 2 * group, cols), jnp.bfloat16),
        jax.ShapeDtypeStruct((rows, channels, cols), jnp.bfloat16),
    ]
    if kind == "first":
        out_specs += [whole(a) for a in shapes]
        out_shape += shapes
    if kind == "last":
        in_specs += [whole(extra[0])]
    macs = rows * cols * (16 * 208 * 96 + 4 * 400 * merged + third_depth * channels)
    return pl.pallas_call(
        functools.partial(stem_kernel, kind),
        grid_spec=pltpu.PrefetchScalarGridSpec(
            num_scalar_prefetch=1,
            grid=(steps,),
            in_specs=[
                pl.BlockSpec((2, cols, depth), lambda i, place: (place[0] + first + i, 0, 0)),
                pl.BlockSpec(
                    (1, cols, depth),
                    lambda i, place: (jnp.maximum(2 * (place[0] + first) - 1, 0), 0, 0),
                ),
            ]
            + in_specs,
            out_specs=out_specs,
            scratch_shapes=[pltpu.VMEM((third_depth, 2 * cols), jnp.bfloat16)],
        ),
        out_shape=out_shape,
        compiler_params=pltpu.CompilerParams(vmem_limit_bytes=VMEM_BYTES),
        cost_estimate=pl.CostEstimate(
            flops=4 * macs, bytes_accessed=rows * cols * 3000, transcendentals=0
        ),
        name="stem",
    )(place, image, image, *operands)


def symmetric_kernel(place_ref, f_ref, turn_w_ref, turn_u_ref, g_ref):
    width = g_ref.shape[3]
    for part in range(2):
        block = f_ref[0, part]
        across = jnp.dot(block, turn_w_ref[...], preferred_element_type=jnp.float32)
        turned = jnp.dot(
            turn_u_ref[...], across.astype(jnp.bfloat16), preferred_element_type=jnp.float32
        )
        own = block[:, :width].astype(jnp.float32)
        g_ref[0, part] = 0.5 * (own + turned if part == 0 else own - turned)


def symmetric_filter(spectral_filter, place, group, width):
    full_rows, full_cols = spectral_filter.shape[2:]
    u = jnp.arange(full_rows, dtype=jnp.int32)
    w = jnp.arange(full_cols, dtype=jnp.int32)
    turn_u = ((u[:, None] + u[None, :]) % full_rows == 0).astype(jnp.bfloat16)
    turn_w = ((w[:, None] + w[None, :width]) % full_cols == 0).astype(jnp.bfloat16)
    return pl.pallas_call(
        symmetric_kernel,
        grid_spec=pltpu.PrefetchScalarGridSpec(
            num_scalar_prefetch=1,
            grid=(group,),
            in_specs=[
                pl.BlockSpec(
                    (1, 2, full_rows, full_cols), lambda i, place: (place[0] + i, 0, 0, 0)
                ),
                pl.BlockSpec(turn_w.shape, lambda i, place: (0, 0)),
                pl.BlockSpec(turn_u.shape, lambda i, place: (0, 0)),
            ],
            out_specs=pl.BlockSpec((1, 2, full_rows, width), lambda i, place: (i, 0, 0, 0)),
        ),
        out_shape=jax.ShapeDtypeStruct((group, 2, full_rows, width), jnp.float32),
        compiler_params=pltpu.CompilerParams(vmem_limit_bytes=VMEM_BYTES),
        cost_estimate=pl.CostEstimate(
            flops=8 * group * full_rows * full_cols * width,
            bytes_accessed=group * full_rows * width * 14,
            transcendentals=0,
        ),
        name="symmetric_filter",
    )(place, spectral_filter, turn_w, turn_u)


def to_lane_tiles(target, rows, values):
    for j in range(target.shape[0]):
        target[j, rows, :] = values[:, 128 * j : 128 * (j + 1)]


def from_lane_tiles(source, rows):
    return jnp.concatenate([source[j, rows, :] for j in range(source.shape[0])], axis=1)


def filter_kernel(
    first, norm_scale, *refs
):
    *pieces, g_ref, row_table_ref, fwd_ref, inv_ref, back_ref, out_ref, held, made = refs
    step = pl.program_id(0)
    full_rows = fwd_ref.shape[0] // 2
    width = g_ref.shape[3]
    group = held.shape[1] // full_rows
    count = made.shape[1] // full_rows
    per_step = g_ref.shape[0]

    @pl.when(step == 0)
    def _():
        begin = 0
        for piece in pieces:
            end = begin + piece.shape[0]
            to_lane_tiles(held, slice(begin, end), piece[...].astype(jnp.float32))
            begin = end

    blocks = []
    for k in range(per_step):
        rows = pl.ds(first + step * per_step + k, full_rows, stride=group)
        field = from_lane_tiles(held, rows)
        spread = jnp.dot(
            field.astype(jnp.bfloat16), row_table_ref[...], preferred_element_type=jnp.float32
        ).astype(jnp.bfloat16)
        blocks.append(jnp.concatenate([spread[:, :width], spread[:, width:]], axis=0))
    spectrum = jnp.dot(
        fwd_ref[...], jnp.concatenate(blocks, axis=1), preferred_element_type=jnp.float32
    )
    blocks = []
    for k in range(per_step):
        real = spectrum[:full_rows, k * width : (k + 1) * width]
        imag = spectrum[full_rows:, k * width : (k + 1) * width]
        g_real = g_ref[k, 0]
        g_imag = g_ref[k, 1]
        blocks.append(
            jnp.concatenate(
                [g_real * real - g_imag * imag, g_real * imag + g_imag * real], axis=0
            ).astype(jnp.bfloat16)
        )
    back = jnp.dot(
        inv_ref[...], jnp.concatenate(blocks, axis=1), preferred_element_type=jnp.float32
    ).astype(jnp.bfloat16)
    for k in range(per_step):
        lanes = slice(k * width, (k + 1) * width)
        both = jnp.concatenate([back[:full_rows, lanes], back[full_rows:, lanes]], axis=1)
        result = jnp.dot(both, back_ref[...], preferred_element_type=jnp.float32)
        rows = pl.ds(step * per_step + k, full_rows, stride=count)
        to_lane_tiles(made, rows, result * norm_scale)

    @pl.when(step == pl.num_programs(0) - 1)
    def _():
        out_ref[...] = from_lane_tiles(made, slice(None)).astype(jnp.bfloat16)


def filter_tables(full_rows, field_cols, width, row_order):
    cos_h, sin_h = fourier_tables(full_rows)
    cos_f, sin_f = fourier_tables(full_rows, row_order)
    cos_w, sin_w = fourier_tables(field_cols)
    fwd = jnp.concatenate(
        [jnp.concatenate([cos_f, sin_f], 1), jnp.concatenate([-sin_f, cos_f], 1)], 0
    )
    inv = jnp.concatenate(
        [jnp.concatenate([cos_h, -sin_h], 1), jnp.concatenate([sin_h, cos_h], 1)], 0
    )
    w = jnp.arange(width, dtype=jnp.int32)
    half = field_cols // 2
    valid = (w <= half).astype(jnp.bfloat16)
    times = jnp.where((w == 0) | (w == half), 1.0, 2.0).astype(jnp.bfloat16) * valid
    row_table = jnp.concatenate([cos_w[:, :width] * valid, -sin_w[:, :width] * valid], 1)
    back_table = jnp.concatenate(
        [cos_w[:width] * times[:, None], -sin_w[:width] * times[:, None]], 0
    )
    return row_table, fwd, inv, back_table


def filter_channels(pieces, symmetric, tables, first, count, per_step, devices):
    row_table, fwd, inv, back_table = tables
    full_rows = fwd.shape[0] // 2
    cols = pieces[0].shape[1]
    group = sum(piece.shape[0] for piece in pieces) // full_rows
    width = symmetric.shape[3]

    def whole(array):
        return pl.BlockSpec(array.shape, lambda i: (0,) * array.ndim)

    macs = count * (2 * 4 * full_rows * full_rows * width + 4 * full_rows * cols * width)
    made = pl.pallas_call(
        functools.partial(filter_kernel, first, 1.0 / (full_rows * cols)),
        grid=(count // per_step,),
        in_specs=[
            *[whole(piece) for piece in pieces],
            pl.BlockSpec(
                (per_step, 2, full_rows, width), lambda i: (first // per_step + i, 0, 0, 0)
            ),
            whole(row_table),
            whole(fwd),
            whole(inv),
            whole(back_table),
        ],
        out_specs=pl.BlockSpec((full_rows * count, cols), lambda i: (0, 0)),
        out_shape=jax.ShapeDtypeStruct((full_rows * count, cols), jnp.bfloat16),
        scratch_shapes=[
            pltpu.VMEM((cols // 128, full_rows * group, 128), jnp.float32),
            pltpu.VMEM((cols // 128, full_rows * count, 128), jnp.float32),
        ],
        compiler_params=pltpu.CompilerParams(vmem_limit_bytes=VMEM_BYTES),
        cost_estimate=pl.CostEstimate(
            flops=2 * macs, bytes_accessed=count * full_rows * cols * 8, transcendentals=0
        ),
        name="spectral_filter",
    )(*pieces, symmetric, row_table, fwd, inv, back_table)
    return made.reshape(devices, full_rows // devices * count, cols)


def residual_kernel(count, place_ref, kept_ref, other_ref, feat_ref, *refs):
    out_ref, held = refs[-2:]
    groups, span, cols = kept_ref.shape
    rows = held.shape[1] // count
    own = pl.multiple_of(place_ref[0] * span, 8)
    far = pl.multiple_of((1 - place_ref[0]) * span, 8)
    for g in range(groups):
        to_lane_tiles(held, pl.ds(own, span), kept_ref[g].astype(jnp.float32))
        to_lane_tiles(held, pl.ds(far, span), other_ref[g].astype(jnp.float32))
        for k in range(count):
            filtered = from_lane_tiles(held, pl.ds(k, rows, stride=count))
            out_ref[g, k] = (feat_ref[g, k].astype(jnp.float32) + filtered).astype(jnp.bfloat16)


def add_residual(place, returned, other, features, previous, first, count):
    halves, span, cols = other.shape
    group, rows = features.shape[1:3]
    groups = 4 if halves % 4 == 0 else 1
    steps = halves // groups
    operands = [returned, other, features]
    in_specs = [
        pl.BlockSpec((groups, span, cols), lambda i, place: (place[0] * steps + i, 0, 0)),
        pl.BlockSpec((groups, span, cols), lambda i, place: (i, 0, 0)),
        pl.BlockSpec(
            (groups, count, rows, cols),
            lambda i, place: (i, first // count, 0, 0),
        ),
    ]
    aliases = {}
    if previous is not None:
        operands.append(previous)
        in_specs.append(pl.BlockSpec(memory_space=pl.ANY))
        aliases = {4: 0}
    return pl.pallas_call(
        functools.partial(residual_kernel, count),
        grid_spec=pltpu.PrefetchScalarGridSpec(
            num_scalar_prefetch=1,
            grid=(steps,),
            in_specs=in_specs,
            out_specs=in_specs[2],
            scratch_shapes=[pltpu.VMEM((cols // 128, rows * count, 128), jnp.float32)],
        ),
        out_shape=jax.ShapeDtypeStruct(features.shape, jnp.bfloat16),
        input_output_aliases=aliases,
        compiler_params=pltpu.CompilerParams(vmem_limit_bytes=VMEM_BYTES),
        cost_estimate=pl.CostEstimate(
            flops=halves * count * rows * cols,
            bytes_accessed=halves * count * rows * cols * 8,
            transcendentals=0,
        ),
        name="residual",
    )(place, *operands)


def swap(block):
    return lax.ppermute(block, "section", [(0, 1), (1, 0)])


def local(
    aerial_patch_grid,
    patch_conv_weight,
    patch_bias,
    merging_conv_weight,
    merge_bias,
    down_weight,
    down_bias,
    norm_gain,
    spectral_filter,
):
    tile_rows, field_cols, depth = aerial_patch_grid.shape
    channels = down_weight.shape[3]
    tile_channels = spectral_filter.shape[0]
    full_rows = spectral_filter.shape[2]
    sections = lax.axis_size("section")
    devices = sections * lax.axis_size("tile")
    suits = (
        sections == 2
        and tile_rows % 8 == 0
        and tile_rows >= 16
        and field_cols % 128 == 0
        and full_rows % 128 == 0
        and tile_channels % 8 == 0
    )
    arguments = (
        aerial_patch_grid,
        patch_conv_weight,
        patch_bias,
        merging_conv_weight,
        merge_bias,
        down_weight,
        down_bias,
        norm_gain,
        spectral_filter,
    )
    if not suits:
        return general_local(*arguments)
    section = lax.axis_index("section")
    tile = lax.axis_index("tile")
    rows = tile_rows // 2
    group = tile_channels // 2
    half_channels = channels // 2
    width = -(-(field_cols // 2 + 1) // 128) * 128

    arriving = from_behind(lower_half(aerial_patch_grid[-1]), "tile", 1)
    inside = (section > 0) | (tile > 0)
    place = jnp.stack([section * (rows // 2), inside, section == 0]).astype(jnp.int32)
    sources = weight_sources(*arguments[1:8])
    pairs = rows // 2
    early = max(pairs // 3, 1)
    late = pairs - early
    normed_early, feat_early, *weights = stem(
        "first", aerial_patch_grid, place, sources, late, early, devices
    )
    normed_early, arriving = lax.optimization_barrier((normed_early, arriving))
    normed_late, feat_late = stem(
        "last", aerial_patch_grid, place, weights, 0, late, devices, (arriving,)
    )
    pieces = []
    row_order = []
    for normed, first, count in ((normed_early, late, early), (normed_late, 0, late)):
        normed = lax.all_to_all(normed, DEVICES, split_axis=0, concat_axis=0, tiled=True)
        pieces.append(normed.reshape(2 * count * devices * group, field_cols))
        own_rows = np.arange(2 * first, 2 * (first + count))
        row_order.append((rows * np.arange(devices)[:, None] + own_rows).reshape(-1))
    features = [feat_late, feat_early]
    features = jnp.concatenate(features, axis=0)
    row_order = np.concatenate(row_order).astype(np.int32)

    channel_place = jnp.reshape(section * group, (1,)).astype(jnp.int32)
    symmetric = symmetric_filter(spectral_filter, channel_place, group, width)
    tables = filter_tables(full_rows, field_cols, width, row_order)

    own = lax.dynamic_slice_in_dim(features, section * half_channels, half_channels, 1)
    sent = lax.dynamic_slice_in_dim(features, (1 - section) * half_channels, half_channels, 1)
    arrived = swap(sent)
    low = jnp.where(section == 0, own, arrived)
    high = jnp.where(section == 0, arrived, own)
    residual = jnp.transpose(jnp.concatenate([low, high], axis=0), (1, 0, 2))
    residual = residual.reshape(half_channels // group, group, tile_rows, field_cols)
    pieces, residual, symmetric, tables = lax.optimization_barrier(
        (pieces, residual, symmetric, tables)
    )

    section_place = jnp.reshape(section, (1,)).astype(jnp.int32)
    halves = devices // 2
    output = None
    for first, count in ((group - 2, 2), (0, group - 2)):
        made = filter_channels(pieces, symmetric, tables, first, count, 2, devices)
        returned = lax.all_to_all(made, DEVICES, split_axis=0, concat_axis=0, tiled=True)
        if output is not None:
            returned, output = lax.optimization_barrier((returned, output))
        other = swap(lax.dynamic_slice_in_dim(returned, (1 - section) * halves, halves, 0))
        output = add_residual(section_place, returned, other, residual, output, first, count)
    return output.reshape(half_channels, tile_rows, field_cols)


def solution(mesh):
    return jax.shard_map(
        local,
        mesh=mesh,
        in_specs=(
            P("tile", None, None),
            P(),
            P(),
            P(),
            P(),
            P(),
            P(),
            P(),
            P("tile", None, None, None),
        ),
        out_specs=P("section", "tile", None),
        check_vma=False,
    )
```

```python
import functools
import math

import jax
import jax.numpy as jnp
import numpy as np
from jax import lax
from jax.experimental import pallas as pl
from jax.experimental.pallas import tpu as pltpu
from jax.sharding import PartitionSpec as P

EPSILON = 1e-05


def from_behind(block, axis, distance):
    devices = range(lax.axis_size(axis))
    route = [(i - distance, i) for i in devices if i - distance in devices]
    return lax.ppermute(block, axis, route)


def fourier_tables(length, columns=None):
    indices = jnp.arange(length, dtype=jnp.int32)
    columns = indices if columns is None else jnp.asarray(columns, jnp.int32)
    product = indices[:, None] * columns[None, :] % length
    angles = product.astype(jnp.float32) * (2.0 * math.pi / length)
    return (jnp.cos(angles).astype(jnp.bfloat16), jnp.sin(angles).astype(jnp.bfloat16))


def patch_kernel_matrix(patch_conv_weight):
    identity = jnp.eye(4, dtype=jnp.float32)
    larger = jnp.einsum(
        "baqk,xy,uv->bxauqyvk", patch_conv_weight.astype(jnp.float32), identity, identity
    )
    band_count = patch_conv_weight.shape[0]
    width = patch_conv_weight.shape[3]
    return larger.reshape(band_count * 256, 16 * width).astype(jnp.bfloat16)


def merging_kernel_matrix(merging_conv_weight):
    identity = jnp.eye(2, dtype=jnp.float32)
    larger = jnp.einsum(
        "aqjk,xy,uv->xauqjyvk", merging_conv_weight.astype(jnp.float32), identity, identity
    )
    in_width = merging_conv_weight.shape[2]
    out_width = merging_conv_weight.shape[3]
    return larger.reshape(16 * in_width, 4 * out_width).astype(jnp.bfloat16)


def down_matrices(down_weight):
    nothing = jnp.zeros_like(down_weight[0, 0])
    in_width = down_weight.shape[2]
    out_width = down_weight.shape[3]

    def arrange(entries):
        return jnp.stack(
            [jnp.stack(entries[0], axis=0), jnp.stack(entries[1], axis=0)], axis=0
        ).reshape(4 * in_width, out_width)

    own_taps = arrange(
        [[down_weight[1, 1], down_weight[1, 2]], [down_weight[2, 1], down_weight[2, 2]]]
    )
    upper_taps = arrange([[nothing, nothing], [down_weight[0, 1], down_weight[0, 2]]])
    left_taps = arrange([[nothing, down_weight[1, 0]], [nothing, down_weight[2, 0]]])
    corner_taps = arrange([[nothing, nothing], [nothing, down_weight[0, 0]]])
    return (own_taps, upper_taps, left_taps, corner_taps)


def stem_layers(aerial_patch_grid, patch_conv_weight, patch_bias, merging_conv_weight, merge_bias):
    initial_layer = jnp.einsum(
        "zji,if->zjf",
        aerial_patch_grid,
        patch_kernel_matrix(patch_conv_weight),
        preferred_element_type=jnp.float32,
    )
    initial_layer = jax.nn.gelu(initial_layer + jnp.tile(patch_bias, 16), approximate=True).astype(
        jnp.bfloat16
    )
    layer_two = jnp.einsum(
        "zji,if->zjf",
        initial_layer,
        merging_kernel_matrix(merging_conv_weight),
        preferred_element_type=jnp.float32,
    )
    return jax.nn.gelu(layer_two + jnp.tile(merge_bias, 4), approximate=True).astype(jnp.bfloat16)


def rim_above(extended):
    return from_behind(extended[-1:], "tile", 1)


def down_conv(upper_rim, extended, down_weight, down_bias):
    stacked = jnp.concatenate([upper_rim, extended], axis=0)
    own_taps, upper_taps, left_taps, corner_taps = down_matrices(down_weight)
    summed = jnp.einsum(
        "rwk,kc->crw", stacked[1:, 1:], own_taps, preferred_element_type=jnp.float32
    )
    summed = summed + jnp.einsum(
        "rwk,kc->crw", stacked[:-1, 1:], upper_taps, preferred_element_type=jnp.float32
    )
    summed = summed + jnp.einsum(
        "rwk,kc->crw", stacked[1:, :-1], left_taps, preferred_element_type=jnp.float32
    )
    summed = summed + jnp.einsum(
        "rwk,kc->crw", stacked[:-1, :-1], corner_taps, preferred_element_type=jnp.float32
    )
    return (summed + down_bias[:, None, None]).astype(jnp.bfloat16)


def layer_norm(features, norm_gain):
    values = features.astype(jnp.float32)
    mean_value = jnp.mean(values, axis=0, keepdims=True)
    centered = values - mean_value
    variance = jnp.mean(centered * centered, axis=0, keepdims=True)
    return (norm_gain[:, None, None] * centered * lax.rsqrt(variance + EPSILON)).astype(
        jnp.bfloat16
    )


def filter_columns(row_spectrum, kernel, forward_h, inverse_h):
    spectrum = jnp.einsum(
        "puqh,chqw->cpuw", forward_h, row_spectrum, preferred_element_type=jnp.float32
    ).astype(jnp.bfloat16)
    spec_real = spectrum[:, 0].astype(jnp.float32)
    spec_imag = spectrum[:, 1].astype(jnp.float32)
    filter_real = kernel[:, 0].astype(jnp.float32)
    filter_imag = kernel[:, 1].astype(jnp.float32)
    weighted = jnp.stack(
        [
            filter_real * spec_real - filter_imag * spec_imag,
            filter_real * spec_imag + filter_imag * spec_real,
        ],
        axis=1,
    ).astype(jnp.bfloat16)
    return jnp.einsum(
        "qhpu,cpuw->chqw", inverse_h, weighted, preferred_element_type=jnp.float32
    ).astype(jnp.bfloat16)


def general_local(
    aerial_patch_grid,
    patch_conv_weight,
    patch_bias,
    merging_conv_weight,
    merge_bias,
    down_weight,
    down_bias,
    norm_gain,
    spectral_filter,
):
    section_index = lax.axis_index("section")
    first_section = section_index == 0
    field_cols = aerial_patch_grid.shape[1]
    channels = down_weight.shape[3]
    group_width = spectral_filter.shape[0]
    full_rows = spectral_filter.shape[2]
    half_channels = channels // 2
    cell_half = field_cols // 2
    image_part = lax.dynamic_slice_in_dim(
        aerial_patch_grid, section_index * cell_half, cell_half, 1
    )
    layer_two = stem_layers(
        image_part, patch_conv_weight, patch_bias, merging_conv_weight, merge_bias
    )
    left_column = from_behind(layer_two[:, -1:], "section", 1)
    extended = jnp.concatenate([left_column, layer_two], axis=1)
    upper_rim = rim_above(extended)
    feature_half = down_conv(upper_rim, extended, down_weight, down_bias)
    features = lax.all_gather(feature_half, "section", axis=2, tiled=True)
    normed = layer_norm(features, norm_gain)
    cos_h, sin_h = fourier_tables(full_rows)
    cos_w, sin_w = fourier_tables(field_cols)
    forward_table = jnp.stack([cos_w, -sin_w], axis=1)
    forward_h = jnp.stack(
        [jnp.stack([cos_h, sin_h], axis=1), jnp.stack([-sin_h, cos_h], axis=1)], axis=0
    )
    inverse_h = jnp.stack(
        [jnp.stack([cos_h, -sin_h], axis=1), jnp.stack([sin_h, cos_h], axis=1)], axis=0
    )
    inverse_table = jnp.stack([cos_w, -sin_w], axis=0)
    norm_scale = 1.0 / (full_rows * field_cols)
    fields = lax.all_to_all(normed, "tile", split_axis=0, concat_axis=1, tiled=True)

    def whole_filter():
        frequency_rows = jnp.einsum(
            "chx,xqw->chqw", fields, forward_table, preferred_element_type=jnp.float32
        ).astype(jnp.bfloat16)
        back_rows = filter_columns(frequency_rows, spectral_filter, forward_h, inverse_h)
        result = jnp.einsum(
            "chqw,qwv->chv", back_rows, inverse_table, preferred_element_type=jnp.float32
        )
        return (result * norm_scale).astype(jnp.bfloat16)

    def empty_fields():
        return jnp.zeros((group_width, full_rows, field_cols), jnp.bfloat16)

    filtered_fields = lax.cond(first_section, empty_fields, whole_filter)
    rows_back = lax.all_to_all(filtered_fields, "tile", split_axis=1, concat_axis=0, tiled=True)
    returned = from_behind(rows_back[:half_channels], "section", -1)
    filtered = jnp.where(first_section, returned, rows_back[half_channels:])
    own_part = lax.dynamic_slice_in_dim(features, section_index * half_channels, half_channels, 0)
    return (own_part.astype(jnp.float32) + filtered.astype(jnp.float32)).astype(jnp.bfloat16)


DEVICES = ("tile", "section")
VMEM_BYTES = 60 * 1024 * 1024
GELU_LINEAR = 2.0 * math.sqrt(2.0 / math.pi)
GELU_CUBIC = 4.0 * 0.044715 * GELU_LINEAR
ONES = (64, 128, 64)
TAPS = ((1, 1), (1, 2), (2, 1), (2, 2), (1, 0), (2, 0), (0, 1), (0, 2), (0, 0))


def bias_rows(bias, count):
    high = bias.astype(jnp.bfloat16)
    rest = bias - high.astype(jnp.float32)
    middle = rest.astype(jnp.bfloat16)
    low = (rest - middle.astype(jnp.float32)).astype(jnp.bfloat16)
    shape = (count, bias.shape[1])
    row = lax.broadcasted_iota(jnp.int32, shape, 0)
    rows = jnp.zeros(shape, jnp.float32)
    for k, part in enumerate((high, middle, low)):
        rows = jnp.where(row == k, jnp.broadcast_to(part.astype(jnp.float32), shape), rows)
    return rows.astype(jnp.bfloat16)


def build_weights(sources, targets):
    patch_ref, patch_bias_ref, merge_ref, merge_bias_ref, down_ref, down_bias_ref, gain_ref = sources
    w1_ref, w2_ref, w3_ref, column_ref = targets

    def exact(a, b):
        return jnp.dot(
            a.astype(jnp.bfloat16), b.astype(jnp.bfloat16), preferred_element_type=jnp.float32
        )

    taps, width = patch_ref.shape
    row = lax.broadcasted_iota(jnp.int32, (4 * taps, taps), 0)
    col = lax.broadcasted_iota(jnp.int32, (4 * taps, taps), 1)
    pick = jnp.where(row // 16 * 4 + row % 4 == col, 1.0, 0.0)
    row = lax.broadcasted_iota(jnp.int32, (width, 4 * width), 0)
    col = lax.broadcasted_iota(jnp.int32, (width, 4 * width), 1)
    repeat = jnp.where(col % width == row, 1.0, 0.0)
    spread = exact(pick, exact(patch_ref[...], repeat))
    row = lax.broadcasted_iota(jnp.int32, spread.shape, 0)
    col = lax.broadcasted_iota(jnp.int32, spread.shape, 1)
    spread = jnp.where(row // 4 % 4 == col // width, 0.5 * spread, 0.0).astype(jnp.bfloat16)
    bias = jnp.broadcast_to(0.5 * patch_bias_ref[...][None], (8, width))
    tiled = jnp.zeros((8, 4 * width), jnp.float32)
    for _ in range(3):
        part = bias.astype(jnp.bfloat16).astype(jnp.float32)
        tiled = tiled + exact(part, repeat)
        bias = bias - part
    first = jnp.concatenate([spread, bias_rows(tiled[:1], ONES[0])], axis=0)
    w1_ref[...] = first.T
    half = (merge_ref[...].astype(jnp.float32) * 0.5).astype(jnp.bfloat16)
    second = jnp.concatenate([half, bias_rows(0.5 * merge_bias_ref[...][None], ONES[1])], axis=0)
    w2_ref[...] = second.T
    third = [down_ref[3 * a + q] for a, q in TAPS]
    third = jnp.concatenate(third + [bias_rows(down_bias_ref[...][None], ONES[2])], axis=0)
    w3_ref[...] = third.T
    column_ref[...] = jnp.broadcast_to(gain_ref[...][None], (128, gain_ref.shape[0])).T


def weight_sources(
    patch_conv_weight, patch_bias, merging_conv_weight, merge_bias, down_weight, down_bias,
    norm_gain,
):
    width = patch_conv_weight.shape[3]
    merged = merging_conv_weight.shape[3]
    return [
        patch_conv_weight.reshape(-1, width),
        patch_bias,
        merging_conv_weight.reshape(-1, merged),
        merge_bias,
        down_weight.reshape(-1, merged, down_weight.shape[3]),
        down_bias,
        norm_gain,
    ]


def weight_shapes(sources):
    taps, width = sources[0].shape
    merged, channels = sources[4].shape[1:]
    return [
        jax.ShapeDtypeStruct((4 * width, 4 * taps + ONES[0]), jnp.bfloat16),
        jax.ShapeDtypeStruct((merged, 4 * width + ONES[1]), jnp.bfloat16),
        jax.ShapeDtypeStruct((channels, 9 * merged + ONES[2]), jnp.bfloat16),
        jax.ShapeDtypeStruct((channels, 128), jnp.float32),
    ]


def half_gelu(h):
    return h + h * jnp.tanh(h * (GELU_LINEAR + GELU_CUBIC * (h * h)))


def lower_half(row):
    depth = row.shape[1]
    return jnp.concatenate(
        [row[:, 256 * b + 128 : 256 * b + 256] for b in range(depth // 256)], axis=1
    )


def stem_kernel(kind, place_ref, x_ref, above_ref, *refs):
    sources = refs[:7]
    normed_ref, feat_ref, w1_ref, w2_ref, w3_ref, gain_ref, field = refs[-7:]
    step = pl.program_id(0)
    rows, cols, depth = x_ref.shape
    bands = depth // 256
    channels = w3_ref.shape[0]
    merged = w2_ref.shape[0]
    group = normed_ref.shape[2] // rows
    cells = rows * cols

    @pl.when(step == 0)
    def _():
        build_weights(sources, (w1_ref, w2_ref, w3_ref, gain_ref))

    w1 = w1_ref[...]
    w2 = w2_ref[...]

    def ones(count, n):
        return jnp.where(lax.broadcasted_iota(jnp.int32, (count, n), 0) < 3, 1.0, 0.0).astype(
            jnp.bfloat16
        )

    def layer_one(turned, offsets):
        n = turned.shape[1]
        parts = [turned[o : o + 64] for o in offsets] + [ones(ONES[0], n)]
        h = jnp.dot(w1, jnp.concatenate(parts, axis=0), preferred_element_type=jnp.float32)
        return half_gelu(h).astype(jnp.bfloat16)

    def layer_two(upper, lower, y):
        n = upper.shape[1]
        span = slice(2 * y * (w1.shape[0] // 4), 2 * (y + 1) * (w1.shape[0] // 4))
        stacked = jnp.concatenate([upper[span], lower[span], ones(ONES[1], n)], axis=0)
        return half_gelu(jnp.dot(w2, stacked, preferred_element_type=jnp.float32))

    def shifted(values):
        lanes = lax.broadcasted_iota(jnp.int32, values.shape, 1)
        moved = pltpu.roll(values, 1, 1)
        return jnp.where(lax.rem(lanes, cols) == 0, 0.0, moved)

    def put(block, lanes, values):
        field[block * merged : (block + 1) * merged, lanes] = values.astype(jnp.bfloat16)

    first_row = slice(0, cols)
    last_row = slice(cells - cols, cells)
    later_rows = slice(cols, cells)
    earlier_rows = slice(0, cells - cols)

    @pl.when(step == 0)
    def _():
        field[9 * merged :, :] = ones(ONES[2], cells)
        above = lower_half(above_ref[0])
        keep = 1.0
        if kind == "last":
            keep = place_ref[1].astype(jnp.float32)
            above = jnp.where(place_ref[2] > 0, refs[7][...], above)
        turned = above.T
        upper, lower = (
            layer_one(turned, [128 * b + 64 * a for b in range(bands)]) for a in range(2)
        )
        put(6, first_row, layer_two(upper, lower, 0) * keep)
        right = layer_two(upper, lower, 1) * keep
        put(7, first_row, right)
        put(8, first_row, shifted(right))

    @pl.when(step > 0)
    def _():
        for source, target in ((2, 6), (3, 7), (5, 8)):
            field[target * merged : (target + 1) * merged, first_row] = field[
                source * merged : (source + 1) * merged, last_row
            ]

    turned = x_ref[...].reshape(cells, depth).T
    for x in range(2):
        upper, lower = (
            layer_one(turned, [256 * b + 64 * (2 * x + a) for b in range(bands)])
            for a in range(2)
        )
        left = layer_two(upper, lower, 0)
        right = layer_two(upper, lower, 1)
        put(2 * x, slice(None), left)
        put(2 * x + 1, slice(None), right)
        moved = shifted(right)
        put(4 + x, slice(None), moved)
        if x == 1:
            put(6, later_rows, left[:, earlier_rows])
            put(7, later_rows, right[:, earlier_rows])
            put(8, later_rows, moved[:, earlier_rows])

    features = jnp.dot(w3_ref[...], field[...], preferred_element_type=jnp.float32).astype(
        jnp.bfloat16
    )
    for r in range(rows):
        feat_ref[r] = features[:, r * cols : (r + 1) * cols]
    values = features.astype(jnp.float32)
    centered = values - jnp.mean(values, axis=0, keepdims=True)
    variance = jnp.mean(centered * centered, axis=0, keepdims=True)
    gain = jnp.concatenate([gain_ref[...]] * (cells // 128), axis=1)
    normed = gain * (centered * lax.rsqrt(variance + EPSILON))
    pair = 2 * group
    index = lax.broadcasted_iota(jnp.int32, (pair, cols), 0)
    for t in range(channels // pair):
        one = normed[pair * t : pair * (t + 1), :cols]
        two = normed[pair * t : pair * (t + 1), cols:]
        normed_ref[2 * t, 0] = jnp.where(index < group, one, pltpu.roll(two, group, 0)).astype(
            jnp.bfloat16
        )
        normed_ref[2 * t + 1, 0] = jnp.where(
            index < group, pltpu.roll(one, group, 0), two
        ).astype(jnp.bfloat16)


def stem(kind, image, place, weights, first, steps, devices, extra=()):
    cols, depth = image.shape[1:]
    rows = 2 * steps
    shapes = weight_shapes(weights)
    channels, third_depth = shapes[2].shape
    merged = shapes[1].shape[0]
    group = channels // devices

    def whole(array):
        return pl.BlockSpec(array.shape, lambda i, place: (0,) * len(array.shape))

    operands = list(weights) + list(extra)
    in_specs = [whole(a) for a in weights]
    out_specs = [
        pl.BlockSpec((devices, 1, 2 * group, cols), lambda i, place: (0, i, 0, 0)),
        pl.BlockSpec((2, channels, cols), lambda i, place: (i, 0, 0)),
    ]
    out_shape = [
        jax.ShapeDtypeStruct((devices, steps, 2 * group, cols), jnp.bfloat16),
        jax.ShapeDtypeStruct((rows, channels, cols), jnp.bfloat16),
    ]
    in_specs += [whole(a) for a in extra]
    macs = rows * cols * (16 * 208 * 96 + 4 * 400 * merged + third_depth * channels)
    return pl.pallas_call(
        functools.partial(stem_kernel, kind),
        grid_spec=pltpu.PrefetchScalarGridSpec(
            num_scalar_prefetch=1,
            grid=(steps,),
            in_specs=[
                pl.BlockSpec((2, cols, depth), lambda i, place: (place[0] + first + i, 0, 0)),
                pl.BlockSpec(
                    (1, cols, depth),
                    lambda i, place: (jnp.maximum(2 * (place[0] + first) - 1, 0), 0, 0),
                ),
            ]
            + in_specs,
            out_specs=out_specs,
            scratch_shapes=[pltpu.VMEM(a.shape, a.dtype) for a in shapes]
            + [pltpu.VMEM((third_depth, 2 * cols), jnp.bfloat16)],
        ),
        out_shape=out_shape,
        compiler_params=pltpu.CompilerParams(vmem_limit_bytes=VMEM_BYTES),
        cost_estimate=pl.CostEstimate(
            flops=4 * macs, bytes_accessed=rows * cols * 3000, transcendentals=0
        ),
        name="stem",
    )(place, image, image, *operands)


def symmetric_kernel(place_ref, f_ref, turn_w_ref, turn_u_ref, g_ref):
    width = g_ref.shape[3]
    for part in range(2):
        block = f_ref[0, part]
        across = jnp.dot(block, turn_w_ref[...], preferred_element_type=jnp.float32)
        turned = jnp.dot(
            turn_u_ref[...], across.astype(jnp.bfloat16), preferred_element_type=jnp.float32
        )
        own = block[:, :width].astype(jnp.float32)
        both = own + turned if part == 0 else own - turned
        g_ref[0, part] = (0.5 * both).astype(jnp.bfloat16)


def symmetric_filter(spectral_filter, place, group, width):
    full_rows, full_cols = spectral_filter.shape[2:]
    u = jnp.arange(full_rows, dtype=jnp.int32)
    w = jnp.arange(full_cols, dtype=jnp.int32)
    turn_u = ((u[:, None] + u[None, :]) % full_rows == 0).astype(jnp.bfloat16)
    turn_w = ((w[:, None] + w[None, :width]) % full_cols == 0).astype(jnp.bfloat16)
    return pl.pallas_call(
        symmetric_kernel,
        grid_spec=pltpu.PrefetchScalarGridSpec(
            num_scalar_prefetch=1,
            grid=(group,),
            in_specs=[
                pl.BlockSpec(
                    (1, 2, full_rows, full_cols), lambda i, place: (place[0] + i, 0, 0, 0)
                ),
                pl.BlockSpec(turn_w.shape, lambda i, place: (0, 0)),
                pl.BlockSpec(turn_u.shape, lambda i, place: (0, 0)),
            ],
            out_specs=pl.BlockSpec((1, 2, full_rows, width), lambda i, place: (i, 0, 0, 0)),
        ),
        out_shape=jax.ShapeDtypeStruct((group, 2, full_rows, width), jnp.bfloat16),
        compiler_params=pltpu.CompilerParams(vmem_limit_bytes=VMEM_BYTES),
        cost_estimate=pl.CostEstimate(
            flops=8 * group * full_rows * full_cols * width,
            bytes_accessed=group * full_rows * width * 14,
            transcendentals=0,
        ),
        name="symmetric_filter",
    )(place, spectral_filter, turn_w, turn_u)


def to_lane_tiles(target, rows, values):
    for j in range(target.shape[0]):
        target[j, rows, :] = values[:, 128 * j : 128 * (j + 1)]


def from_lane_tiles(source, rows):
    return jnp.concatenate([source[j, rows, :] for j in range(source.shape[0])], axis=1)


RADIX = 3
HALF_ROOT = math.sqrt(3.0) / 2.0


def repack_kernel(devices, early_ref, out_ref, held):
    group, length = out_ref.shape[:2]
    rows = length // devices
    to_lane_tiles(held, slice(None), early_ref[...].astype(jnp.float32))
    for k in range(group):
        for r in range(rows):
            values = from_lane_tiles(held, pl.ds(r * group + k, devices, stride=rows * group))
            out_ref[k, r * devices : (r + 1) * devices] = values.astype(jnp.bfloat16)


def repack(early, group, devices):
    length, cols = early.shape
    return pl.pallas_call(
        functools.partial(repack_kernel, devices),
        out_shape=jax.ShapeDtypeStruct((group, length // group, cols), jnp.bfloat16),
        scratch_shapes=[pltpu.VMEM((cols // 128, length, 128), jnp.float32)],
        compiler_params=pltpu.CompilerParams(vmem_limit_bytes=VMEM_BYTES // 4),
        cost_estimate=pl.CostEstimate(
            flops=length * cols, bytes_accessed=4 * length * cols, transcendentals=0
        ),
        name="repack",
    )(early)


def thirds(values, sign):
    (re0, im0), (re1, im1), (re2, im2) = values
    sum_re, sum_im = re1 + re2, im1 + im2
    turn_re, turn_im = HALF_ROOT * sign * (im1 - im2), HALF_ROOT * sign * (re2 - re1)
    rest_re, rest_im = re0 - 0.5 * sum_re, im0 - 0.5 * sum_im
    return (
        (re0 + sum_re, im0 + sum_im),
        (rest_re + turn_re, rest_im + turn_im),
        (rest_re - turn_re, rest_im - turn_im),
    )


def filter_kernel(
    first, devices, norm_scale, late_ref, early_ref, g_ref, row_table_ref, fwd_ref, inv_ref,
    back_ref, twiddle_ref, out_ref, held, made,
):
    step = pl.program_id(0)
    third = fwd_ref.shape[0] // 2
    full_rows = RADIX * third
    width = g_ref.shape[3]
    count = made.shape[1] // full_rows
    per_step = g_ref.shape[0]
    early = early_ref.shape[1] // devices
    late = full_rows // devices - early
    group = held.shape[1] // (late * devices)

    @pl.when(step == 0)
    def _():
        to_lane_tiles(held, slice(None), late_ref[...].astype(jnp.float32))

    def source_rows(k, row):
        if row >= late:
            begin = (row - late) * devices
            return early_ref[k, begin : begin + devices]
        begin = row * group + first + step * per_step + k
        values = from_lane_tiles(held, pl.ds(begin, devices, stride=late * group))
        return values.astype(jnp.bfloat16)

    def twiddles(r):
        cos, sin = twiddle_ref[2 * r - 2], twiddle_ref[2 * r - 1]
        times = per_step * width // 128
        return jnp.concatenate([cos] * times, axis=1), jnp.concatenate([sin] * times, axis=1)

    fields = []
    for k in range(per_step):
        rows = [
            source_rows(k, r + RADIX * q)
            for r in range(RADIX)
            for q in range((late + early) // RADIX)
        ]
        spread = jnp.dot(
            jnp.concatenate(rows, axis=0), row_table_ref[...], preferred_element_type=jnp.float32
        )
        fields.append(spread.astype(jnp.bfloat16))
    parts = []
    for r in range(RADIX):
        span = slice(r * third, (r + 1) * third)
        block = jnp.concatenate(
            [
                jnp.concatenate([f[span, :width], f[span, width:]], axis=0)
                for f in fields
            ],
            axis=1,
        )
        short = jnp.dot(fwd_ref[...], block, preferred_element_type=jnp.float32)
        real, imag = short[:third], short[third:]
        if r > 0:
            cos, sin = twiddles(r)
            real, imag = real * cos + imag * sin, imag * cos - real * sin
        parts.append((real, imag))
    weighted = []
    for r, (real, imag) in enumerate(thirds(parts, 1.0)):
        span = slice(r * third, (r + 1) * third)
        g_real, g_imag = (
            jnp.concatenate([g_ref[k, p, span] for k in range(per_step)], axis=1).astype(
                jnp.float32
            )
            for p in range(2)
        )
        weighted.append((g_real * real - g_imag * imag, g_real * imag + g_imag * real))
    for r, (real, imag) in enumerate(thirds(weighted, -1.0)):
        if r > 0:
            cos, sin = twiddles(r)
            real, imag = real * cos - imag * sin, imag * cos + real * sin
        block = jnp.concatenate([real, imag], axis=0).astype(jnp.bfloat16)
        back = jnp.dot(inv_ref[...], block, preferred_element_type=jnp.float32).astype(
            jnp.bfloat16
        )
        for k in range(per_step):
            lanes = slice(k * width, (k + 1) * width)
            both = jnp.concatenate([back[:third, lanes], back[third:, lanes]], axis=1)
            result = jnp.dot(both, back_ref[...], preferred_element_type=jnp.float32)
            rows = pl.ds(r * count + step * per_step + k, third, stride=RADIX * count)
            to_lane_tiles(made, rows, result * norm_scale)

    @pl.when(step == pl.num_programs(0) - 1)
    def _():
        out_ref[...] = from_lane_tiles(made, slice(None)).astype(jnp.bfloat16)


def filter_tables(full_rows, field_cols, width, devices):
    third = full_rows // RADIX
    per_device = third // devices
    order = (per_device * np.arange(devices)[None, :] + np.arange(per_device)[:, None]).reshape(-1)
    cos_h, sin_h = fourier_tables(third)
    cos_f, sin_f = fourier_tables(third, order.astype(np.int32))
    cos_w, sin_w = fourier_tables(field_cols)
    fwd = jnp.concatenate(
        [jnp.concatenate([cos_f, sin_f], 1), jnp.concatenate([-sin_f, cos_f], 1)], 0
    )
    inv = jnp.concatenate(
        [jnp.concatenate([cos_h, -sin_h], 1), jnp.concatenate([sin_h, cos_h], 1)], 0
    )
    w = jnp.arange(width, dtype=jnp.int32)
    half = field_cols // 2
    valid = (w <= half).astype(jnp.bfloat16)
    times = jnp.where((w == 0) | (w == half), 1.0, 2.0).astype(jnp.bfloat16) * valid
    row_table = jnp.concatenate([cos_w[:, :width] * valid, -sin_w[:, :width] * valid], 1)
    back_table = jnp.concatenate(
        [cos_w[:width] * times[:, None], -sin_w[:width] * times[:, None]], 0
    )
    turns = jnp.arange(1, RADIX)[:, None] * jnp.arange(third)[None, :]
    angles = turns.astype(jnp.float32) * (2.0 * math.pi / full_rows)
    twiddle = jnp.stack([jnp.cos(angles), jnp.sin(angles)], axis=1)
    twiddle = jnp.broadcast_to(twiddle.reshape(-1, third, 1), (2 * RADIX - 2, third, 128))
    return row_table, fwd, inv, back_table, twiddle


def filter_channels(late, early, symmetric, tables, first, count, per_step, devices):
    full_rows, width = symmetric.shape[2:]
    group, early_rows = early.shape[:2]
    cols = late.shape[1]

    def whole(array):
        return pl.BlockSpec(array.shape, lambda i: (0,) * array.ndim)

    macs = count * (4 * full_rows * full_rows * width + 4 * full_rows * cols * width)
    made = pl.pallas_call(
        functools.partial(filter_kernel, first, devices, 1.0 / (full_rows * cols)),
        grid=(count // per_step,),
        in_specs=[
            whole(late),
            pl.BlockSpec((per_step, early_rows, cols), lambda i: (first // per_step + i, 0, 0)),
            pl.BlockSpec(
                (per_step, 2, full_rows, width), lambda i: (first // per_step + i, 0, 0, 0)
            ),
        ]
        + [whole(table) for table in tables],
        out_specs=pl.BlockSpec((full_rows * count, cols), lambda i: (0, 0)),
        out_shape=jax.ShapeDtypeStruct((full_rows * count, cols), jnp.bfloat16),
        scratch_shapes=[
            pltpu.VMEM((cols // 128, late.shape[0], 128), jnp.float32),
            pltpu.VMEM((cols // 128, full_rows * count, 128), jnp.float32),
        ],
        compiler_params=pltpu.CompilerParams(vmem_limit_bytes=VMEM_BYTES),
        cost_estimate=pl.CostEstimate(
            flops=2 * macs, bytes_accessed=count * full_rows * cols * 8, transcendentals=0
        ),
        name="spectral_filter",
    )(late, early, symmetric, *tables)
    return made.reshape(devices, full_rows // devices * count, cols)


def residual_kernel(count, place_ref, kept_ref, other_ref, feat_ref, *refs):
    out_ref, held = refs[-2:]
    groups, span, cols = kept_ref.shape
    rows = held.shape[1] // count
    own = pl.multiple_of(place_ref[0] * span, 8)
    far = pl.multiple_of((1 - place_ref[0]) * span, 8)
    for g in range(groups):
        to_lane_tiles(held, pl.ds(own, span), kept_ref[g].astype(jnp.float32))
        to_lane_tiles(held, pl.ds(far, span), other_ref[g].astype(jnp.float32))
        for k in range(count):
            filtered = from_lane_tiles(held, pl.ds(k, rows, stride=count))
            out_ref[g, k] = (feat_ref[g, k].astype(jnp.float32) + filtered).astype(jnp.bfloat16)


def add_residual(place, returned, other, features, previous, first, count):
    halves, span, cols = other.shape
    group, rows = features.shape[1:3]
    groups = 4 if halves % 4 == 0 else 1
    steps = halves // groups
    operands = [returned, other, features]
    in_specs = [
        pl.BlockSpec((groups, span, cols), lambda i, place: (place[0] * steps + i, 0, 0)),
        pl.BlockSpec((groups, span, cols), lambda i, place: (i, 0, 0)),
        pl.BlockSpec(
            (groups, count, rows, cols),
            lambda i, place: (i, first // count, 0, 0),
        ),
    ]
    aliases = {}
    if previous is not None:
        operands.append(previous)
        in_specs.append(pl.BlockSpec(memory_space=pl.ANY))
        aliases = {4: 0}
    return pl.pallas_call(
        functools.partial(residual_kernel, count),
        grid_spec=pltpu.PrefetchScalarGridSpec(
            num_scalar_prefetch=1,
            grid=(steps,),
            in_specs=in_specs,
            out_specs=in_specs[2],
            scratch_shapes=[pltpu.VMEM((cols // 128, rows * count, 128), jnp.float32)],
        ),
        out_shape=jax.ShapeDtypeStruct(features.shape, jnp.bfloat16),
        input_output_aliases=aliases,
        compiler_params=pltpu.CompilerParams(vmem_limit_bytes=VMEM_BYTES),
        cost_estimate=pl.CostEstimate(
            flops=halves * count * rows * cols,
            bytes_accessed=halves * count * rows * cols * 8,
            transcendentals=0,
        ),
        name="residual",
    )(place, *operands)


def swap(block):
    return lax.ppermute(block, "section", [(0, 1), (1, 0)])


def local(
    aerial_patch_grid,
    patch_conv_weight,
    patch_bias,
    merging_conv_weight,
    merge_bias,
    down_weight,
    down_bias,
    norm_gain,
    spectral_filter,
):
    tile_rows, field_cols, depth = aerial_patch_grid.shape
    channels = down_weight.shape[3]
    tile_channels = spectral_filter.shape[0]
    full_rows = spectral_filter.shape[2]
    sections = lax.axis_size("section")
    devices = sections * lax.axis_size("tile")
    rows = tile_rows // 2
    suits = (
        sections == 2
        and tile_rows % 8 == 0
        and tile_rows >= 16
        and field_cols % 128 == 0
        and full_rows % (128 * RADIX) == 0
        and rows % RADIX == 0
        and devices % 8 == 0
        and tile_channels % 8 == 0
    )
    arguments = (
        aerial_patch_grid,
        patch_conv_weight,
        patch_bias,
        merging_conv_weight,
        merge_bias,
        down_weight,
        down_bias,
        norm_gain,
        spectral_filter,
    )
    if not suits:
        return general_local(*arguments)
    section = lax.axis_index("section")
    tile = lax.axis_index("tile")
    group = tile_channels // 2
    half_channels = channels // 2
    width = -(-(field_cols // 2 + 1) // 128) * 128

    arriving = from_behind(lower_half(aerial_patch_grid[-1]), "tile", 1)
    inside = (section > 0) | (tile > 0)
    place = jnp.stack([section * (rows // 2), inside, section == 0]).astype(jnp.int32)
    sources = weight_sources(*arguments[1:8])
    pairs = rows // 2
    early = max(pairs // 3, 1)
    late = pairs - early
    normed_early, feat_early = stem(
        "first", aerial_patch_grid, place, sources, late, early, devices
    )
    normed_early, arriving = lax.optimization_barrier((normed_early, arriving))
    normed_late, feat_late = stem(
        "last", aerial_patch_grid, place, sources, 0, late, devices, (arriving,)
    )
    spread = [
        lax.all_to_all(normed, DEVICES, split_axis=0, concat_axis=0, tiled=True).reshape(
            -1, field_cols
        )
        for normed in (normed_early, normed_late)
    ]
    early_fields = repack(spread[0], group, devices)
    late_fields = spread[1]
    features = jnp.concatenate([feat_late, feat_early], axis=0)

    channel_place = jnp.reshape(section * group, (1,)).astype(jnp.int32)
    symmetric = symmetric_filter(spectral_filter, channel_place, group, width)
    tables = filter_tables(full_rows, field_cols, width, devices)

    own = lax.dynamic_slice_in_dim(features, section * half_channels, half_channels, 1)
    sent = lax.dynamic_slice_in_dim(features, (1 - section) * half_channels, half_channels, 1)
    arrived = swap(sent)
    low = jnp.where(section == 0, own, arrived)
    high = jnp.where(section == 0, arrived, own)
    residual = jnp.transpose(jnp.concatenate([low, high], axis=0), (1, 0, 2))
    residual = residual.reshape(half_channels // group, group, tile_rows, field_cols)
    late_fields, early_fields, residual, symmetric, tables = lax.optimization_barrier(
        (late_fields, early_fields, residual, symmetric, tables)
    )

    section_place = jnp.reshape(section, (1,)).astype(jnp.int32)
    halves = devices // 2
    output = None
    for first, count in ((group - 2, 2), (0, group - 2)):
        made = filter_channels(
            late_fields, early_fields, symmetric, tables, first, count, 2, devices
        )
        returned = lax.all_to_all(made, DEVICES, split_axis=0, concat_axis=0, tiled=True)
        if output is not None:
            returned, output = lax.optimization_barrier((returned, output))
        other = swap(lax.dynamic_slice_in_dim(returned, (1 - section) * halves, halves, 0))
        output = add_residual(section_place, returned, other, residual, output, first, count)
    return output.reshape(half_channels, tile_rows, field_cols)


def solution(mesh):
    return jax.shard_map(
        local,
        mesh=mesh,
        in_specs=(
            P("tile", None, None),
            P(),
            P(),
            P(),
            P(),
            P(),
            P(),
            P(),
            P("tile", None, None, None),
        ),
        out_specs=P("section", "tile", None),
        check_vma=False,
    )
```

```python
import functools
import math

import jax
import jax.numpy as jnp
import numpy as np
from jax import lax
from jax.experimental import pallas as pl
from jax.experimental.pallas import tpu as pltpu
from jax.sharding import PartitionSpec as P

EPSILON = 1e-05


def from_behind(block, axis, distance):
    devices = range(lax.axis_size(axis))
    route = [(i - distance, i) for i in devices if i - distance in devices]
    return lax.ppermute(block, axis, route)


def fourier_tables(length, columns=None):
    indices = jnp.arange(length, dtype=jnp.int32)
    columns = indices if columns is None else jnp.asarray(columns, jnp.int32)
    product = indices[:, None] * columns[None, :] % length
    angles = product.astype(jnp.float32) * (2.0 * math.pi / length)
    return (jnp.cos(angles).astype(jnp.bfloat16), jnp.sin(angles).astype(jnp.bfloat16))


def patch_kernel_matrix(patch_conv_weight):
    identity = jnp.eye(4, dtype=jnp.float32)
    larger = jnp.einsum(
        "baqk,xy,uv->bxauqyvk", patch_conv_weight.astype(jnp.float32), identity, identity
    )
    band_count = patch_conv_weight.shape[0]
    width = patch_conv_weight.shape[3]
    return larger.reshape(band_count * 256, 16 * width).astype(jnp.bfloat16)


def merging_kernel_matrix(merging_conv_weight):
    identity = jnp.eye(2, dtype=jnp.float32)
    larger = jnp.einsum(
        "aqjk,xy,uv->xauqjyvk", merging_conv_weight.astype(jnp.float32), identity, identity
    )
    in_width = merging_conv_weight.shape[2]
    out_width = merging_conv_weight.shape[3]
    return larger.reshape(16 * in_width, 4 * out_width).astype(jnp.bfloat16)


def down_matrices(down_weight):
    nothing = jnp.zeros_like(down_weight[0, 0])
    in_width = down_weight.shape[2]
    out_width = down_weight.shape[3]

    def arrange(entries):
        return jnp.stack(
            [jnp.stack(entries[0], axis=0), jnp.stack(entries[1], axis=0)], axis=0
        ).reshape(4 * in_width, out_width)

    own_taps = arrange(
        [[down_weight[1, 1], down_weight[1, 2]], [down_weight[2, 1], down_weight[2, 2]]]
    )
    upper_taps = arrange([[nothing, nothing], [down_weight[0, 1], down_weight[0, 2]]])
    left_taps = arrange([[nothing, down_weight[1, 0]], [nothing, down_weight[2, 0]]])
    corner_taps = arrange([[nothing, nothing], [nothing, down_weight[0, 0]]])
    return (own_taps, upper_taps, left_taps, corner_taps)


def stem_layers(aerial_patch_grid, patch_conv_weight, patch_bias, merging_conv_weight, merge_bias):
    initial_layer = jnp.einsum(
        "zji,if->zjf",
        aerial_patch_grid,
        patch_kernel_matrix(patch_conv_weight),
        preferred_element_type=jnp.float32,
    )
    initial_layer = jax.nn.gelu(initial_layer + jnp.tile(patch_bias, 16), approximate=True).astype(
        jnp.bfloat16
    )
    layer_two = jnp.einsum(
        "zji,if->zjf",
        initial_layer,
        merging_kernel_matrix(merging_conv_weight),
        preferred_element_type=jnp.float32,
    )
    return jax.nn.gelu(layer_two + jnp.tile(merge_bias, 4), approximate=True).astype(jnp.bfloat16)


def rim_above(extended):
    return from_behind(extended[-1:], "tile", 1)


def down_conv(upper_rim, extended, down_weight, down_bias):
    stacked = jnp.concatenate([upper_rim, extended], axis=0)
    own_taps, upper_taps, left_taps, corner_taps = down_matrices(down_weight)
    summed = jnp.einsum(
        "rwk,kc->crw", stacked[1:, 1:], own_taps, preferred_element_type=jnp.float32
    )
    summed = summed + jnp.einsum(
        "rwk,kc->crw", stacked[:-1, 1:], upper_taps, preferred_element_type=jnp.float32
    )
    summed = summed + jnp.einsum(
        "rwk,kc->crw", stacked[1:, :-1], left_taps, preferred_element_type=jnp.float32
    )
    summed = summed + jnp.einsum(
        "rwk,kc->crw", stacked[:-1, :-1], corner_taps, preferred_element_type=jnp.float32
    )
    return (summed + down_bias[:, None, None]).astype(jnp.bfloat16)


def layer_norm(features, norm_gain):
    values = features.astype(jnp.float32)
    mean_value = jnp.mean(values, axis=0, keepdims=True)
    centered = values - mean_value
    variance = jnp.mean(centered * centered, axis=0, keepdims=True)
    return (norm_gain[:, None, None] * centered * lax.rsqrt(variance + EPSILON)).astype(
        jnp.bfloat16
    )


def filter_columns(row_spectrum, kernel, forward_h, inverse_h):
    spectrum = jnp.einsum(
        "puqh,chqw->cpuw", forward_h, row_spectrum, preferred_element_type=jnp.float32
    ).astype(jnp.bfloat16)
    spec_real = spectrum[:, 0].astype(jnp.float32)
    spec_imag = spectrum[:, 1].astype(jnp.float32)
    filter_real = kernel[:, 0].astype(jnp.float32)
    filter_imag = kernel[:, 1].astype(jnp.float32)
    weighted = jnp.stack(
        [
            filter_real * spec_real - filter_imag * spec_imag,
            filter_real * spec_imag + filter_imag * spec_real,
        ],
        axis=1,
    ).astype(jnp.bfloat16)
    return jnp.einsum(
        "qhpu,cpuw->chqw", inverse_h, weighted, preferred_element_type=jnp.float32
    ).astype(jnp.bfloat16)


def general_local(
    aerial_patch_grid,
    patch_conv_weight,
    patch_bias,
    merging_conv_weight,
    merge_bias,
    down_weight,
    down_bias,
    norm_gain,
    spectral_filter,
):
    section_index = lax.axis_index("section")
    first_section = section_index == 0
    field_cols = aerial_patch_grid.shape[1]
    channels = down_weight.shape[3]
    group_width = spectral_filter.shape[0]
    full_rows = spectral_filter.shape[2]
    half_channels = channels // 2
    cell_half = field_cols // 2
    image_part = lax.dynamic_slice_in_dim(
        aerial_patch_grid, section_index * cell_half, cell_half, 1
    )
    layer_two = stem_layers(
        image_part, patch_conv_weight, patch_bias, merging_conv_weight, merge_bias
    )
    left_column = from_behind(layer_two[:, -1:], "section", 1)
    extended = jnp.concatenate([left_column, layer_two], axis=1)
    upper_rim = rim_above(extended)
    feature_half = down_conv(upper_rim, extended, down_weight, down_bias)
    features = lax.all_gather(feature_half, "section", axis=2, tiled=True)
    normed = layer_norm(features, norm_gain)
    cos_h, sin_h = fourier_tables(full_rows)
    cos_w, sin_w = fourier_tables(field_cols)
    forward_table = jnp.stack([cos_w, -sin_w], axis=1)
    forward_h = jnp.stack(
        [jnp.stack([cos_h, sin_h], axis=1), jnp.stack([-sin_h, cos_h], axis=1)], axis=0
    )
    inverse_h = jnp.stack(
        [jnp.stack([cos_h, -sin_h], axis=1), jnp.stack([sin_h, cos_h], axis=1)], axis=0
    )
    inverse_table = jnp.stack([cos_w, -sin_w], axis=0)
    norm_scale = 1.0 / (full_rows * field_cols)
    fields = lax.all_to_all(normed, "tile", split_axis=0, concat_axis=1, tiled=True)

    def whole_filter():
        frequency_rows = jnp.einsum(
            "chx,xqw->chqw", fields, forward_table, preferred_element_type=jnp.float32
        ).astype(jnp.bfloat16)
        back_rows = filter_columns(frequency_rows, spectral_filter, forward_h, inverse_h)
        result = jnp.einsum(
            "chqw,qwv->chv", back_rows, inverse_table, preferred_element_type=jnp.float32
        )
        return (result * norm_scale).astype(jnp.bfloat16)

    def empty_fields():
        return jnp.zeros((group_width, full_rows, field_cols), jnp.bfloat16)

    filtered_fields = lax.cond(first_section, empty_fields, whole_filter)
    rows_back = lax.all_to_all(filtered_fields, "tile", split_axis=1, concat_axis=0, tiled=True)
    returned = from_behind(rows_back[:half_channels], "section", -1)
    filtered = jnp.where(first_section, returned, rows_back[half_channels:])
    own_part = lax.dynamic_slice_in_dim(features, section_index * half_channels, half_channels, 0)
    return (own_part.astype(jnp.float32) + filtered.astype(jnp.float32)).astype(jnp.bfloat16)


DEVICES = ("tile", "section")
VMEM_BYTES = 60 * 1024 * 1024
GELU_LINEAR = 2.0 * math.sqrt(2.0 / math.pi)
GELU_CUBIC = 4.0 * 0.044715 * GELU_LINEAR
ONES = (64, 128, 64)
TAPS = ((1, 1), (1, 2), (2, 1), (2, 2), (1, 0), (2, 0), (0, 1), (0, 2), (0, 0))


def bias_rows(bias, count):
    high = bias.astype(jnp.bfloat16)
    rest = bias - high.astype(jnp.float32)
    middle = rest.astype(jnp.bfloat16)
    low = (rest - middle.astype(jnp.float32)).astype(jnp.bfloat16)
    shape = (count, bias.shape[1])
    row = lax.broadcasted_iota(jnp.int32, shape, 0)
    rows = jnp.zeros(shape, jnp.float32)
    for k, part in enumerate((high, middle, low)):
        rows = jnp.where(row == k, jnp.broadcast_to(part.astype(jnp.float32), shape), rows)
    return rows.astype(jnp.bfloat16)


def build_weights(sources, targets):
    patch_ref, patch_bias_ref, merge_ref, merge_bias_ref, down_ref, down_bias_ref, gain_ref = sources
    w1_ref, w2_ref, w3_ref, column_ref = targets

    def exact(a, b):
        return jnp.dot(
            a.astype(jnp.bfloat16), b.astype(jnp.bfloat16), preferred_element_type=jnp.float32
        )

    taps, width = patch_ref.shape
    row = lax.broadcasted_iota(jnp.int32, (4 * taps, taps), 0)
    col = lax.broadcasted_iota(jnp.int32, (4 * taps, taps), 1)
    pick = jnp.where(row // 16 * 4 + row % 4 == col, 1.0, 0.0)
    row = lax.broadcasted_iota(jnp.int32, (width, 4 * width), 0)
    col = lax.broadcasted_iota(jnp.int32, (width, 4 * width), 1)
    repeat = jnp.where(col % width == row, 1.0, 0.0)
    spread = exact(pick, exact(patch_ref[...], repeat))
    row = lax.broadcasted_iota(jnp.int32, spread.shape, 0)
    col = lax.broadcasted_iota(jnp.int32, spread.shape, 1)
    spread = jnp.where(row // 4 % 4 == col // width, 0.5 * spread, 0.0).astype(jnp.bfloat16)
    bias = jnp.broadcast_to(0.5 * patch_bias_ref[...][None], (8, width))
    tiled = jnp.zeros((8, 4 * width), jnp.float32)
    for _ in range(3):
        part = bias.astype(jnp.bfloat16).astype(jnp.float32)
        tiled = tiled + exact(part, repeat)
        bias = bias - part
    first = jnp.concatenate([spread, bias_rows(tiled[:1], ONES[0])], axis=0)
    w1_ref[...] = first.T
    half = (merge_ref[...].astype(jnp.float32) * 0.5).astype(jnp.bfloat16)
    second = jnp.concatenate([half, bias_rows(0.5 * merge_bias_ref[...][None], ONES[1])], axis=0)
    w2_ref[...] = second.T
    third = [down_ref[3 * a + q] for a, q in TAPS]
    third = jnp.concatenate(third + [bias_rows(down_bias_ref[...][None], ONES[2])], axis=0)
    w3_ref[...] = third.T
    column_ref[...] = jnp.broadcast_to(gain_ref[...][None], (128, gain_ref.shape[0])).T


def weight_sources(
    patch_conv_weight, patch_bias, merging_conv_weight, merge_bias, down_weight, down_bias,
    norm_gain,
):
    width = patch_conv_weight.shape[3]
    merged = merging_conv_weight.shape[3]
    return [
        patch_conv_weight.reshape(-1, width),
        patch_bias,
        merging_conv_weight.reshape(-1, merged),
        merge_bias,
        down_weight.reshape(-1, merged, down_weight.shape[3]),
        down_bias,
        norm_gain,
    ]


def weight_shapes(sources):
    taps, width = sources[0].shape
    merged, channels = sources[4].shape[1:]
    return [
        jax.ShapeDtypeStruct((4 * width, 4 * taps + ONES[0]), jnp.bfloat16),
        jax.ShapeDtypeStruct((merged, 4 * width + ONES[1]), jnp.bfloat16),
        jax.ShapeDtypeStruct((channels, 9 * merged + ONES[2]), jnp.bfloat16),
        jax.ShapeDtypeStruct((channels, 128), jnp.float32),
    ]


def half_gelu(h):
    return h + h * jnp.tanh(h * (GELU_LINEAR + GELU_CUBIC * (h * h)))


def lower_half(row):
    depth = row.shape[1]
    return jnp.concatenate(
        [row[:, 256 * b + 128 : 256 * b + 256] for b in range(depth // 256)], axis=1
    )


def stem_kernel(kind, x_ref, above_ref, *refs):
    sources = refs[:7]
    normed_ref, feat_ref, w1_ref, w2_ref, w3_ref, gain_ref, field = refs[-7:]
    step = pl.program_id(0)
    rows, cols, depth = x_ref.shape
    bands = depth // 256
    channels = w3_ref.shape[0]
    merged = w2_ref.shape[0]
    group = normed_ref.shape[2] // rows
    cells = rows * cols

    @pl.when(step == 0)
    def _():
        build_weights(sources, (w1_ref, w2_ref, w3_ref, gain_ref))

    w1 = w1_ref[...]
    w2 = w2_ref[...]

    def ones(count, n):
        return jnp.where(lax.broadcasted_iota(jnp.int32, (count, n), 0) < 3, 1.0, 0.0).astype(
            jnp.bfloat16
        )

    def layer_one(turned, offsets):
        n = turned.shape[1]
        parts = [turned[o : o + 64] for o in offsets] + [ones(ONES[0], n)]
        h = jnp.dot(w1, jnp.concatenate(parts, axis=0), preferred_element_type=jnp.float32)
        return half_gelu(h).astype(jnp.bfloat16)

    def layer_two(upper, lower, y):
        n = upper.shape[1]
        span = slice(2 * y * (w1.shape[0] // 4), 2 * (y + 1) * (w1.shape[0] // 4))
        stacked = jnp.concatenate([upper[span], lower[span], ones(ONES[1], n)], axis=0)
        return half_gelu(jnp.dot(w2, stacked, preferred_element_type=jnp.float32))

    def shifted(values):
        lanes = lax.broadcasted_iota(jnp.int32, values.shape, 1)
        moved = pltpu.roll(values, 1, 1)
        return jnp.where(lax.rem(lanes, cols) == 0, 0.0, moved)

    def put(block, lanes, values):
        field[block * merged : (block + 1) * merged, lanes] = values.astype(jnp.bfloat16)

    first_row = slice(0, cols)
    last_row = slice(cells - cols, cells)
    later_rows = slice(cols, cells)
    earlier_rows = slice(0, cells - cols)

    @pl.when(step == 0)
    def _():
        field[9 * merged :, :] = ones(ONES[2], cells)
        above = lower_half(above_ref[0])
        keep = 1.0
        if kind == "last":
            lower_section = lax.axis_index("section") > 0
            inside = lower_section | (lax.axis_index("tile") > 0)
            keep = jnp.where(inside, 1.0, 0.0)
            above = jnp.where(lower_section, above, refs[7][...])
        turned = above.T
        upper, lower = (
            layer_one(turned, [128 * b + 64 * a for b in range(bands)]) for a in range(2)
        )
        put(6, first_row, layer_two(upper, lower, 0) * keep)
        right = layer_two(upper, lower, 1) * keep
        put(7, first_row, right)
        put(8, first_row, shifted(right))

    @pl.when(step > 0)
    def _():
        for source, target in ((2, 6), (3, 7), (5, 8)):
            field[target * merged : (target + 1) * merged, first_row] = field[
                source * merged : (source + 1) * merged, last_row
            ]

    turned = x_ref[...].reshape(cells, depth).T
    for x in range(2):
        upper, lower = (
            layer_one(turned, [256 * b + 64 * (2 * x + a) for b in range(bands)])
            for a in range(2)
        )
        left = layer_two(upper, lower, 0)
        right = layer_two(upper, lower, 1)
        put(2 * x, slice(None), left)
        put(2 * x + 1, slice(None), right)
        moved = shifted(right)
        put(4 + x, slice(None), moved)
        if x == 1:
            put(6, later_rows, left[:, earlier_rows])
            put(7, later_rows, right[:, earlier_rows])
            put(8, later_rows, moved[:, earlier_rows])

    features = jnp.dot(w3_ref[...], field[...], preferred_element_type=jnp.float32).astype(
        jnp.bfloat16
    )
    for r in range(rows):
        feat_ref[r] = features[:, r * cols : (r + 1) * cols]
    values = features.astype(jnp.float32)
    centered = values - jnp.mean(values, axis=0, keepdims=True)
    variance = jnp.mean(centered * centered, axis=0, keepdims=True)
    gain = jnp.concatenate([gain_ref[...]] * (cells // 128), axis=1)
    normed = gain * (centered * lax.rsqrt(variance + EPSILON))
    pair = 2 * group
    index = lax.broadcasted_iota(jnp.int32, (pair, cols), 0)
    for t in range(channels // pair):
        one = normed[pair * t : pair * (t + 1), :cols]
        two = normed[pair * t : pair * (t + 1), cols:]
        normed_ref[2 * t, 0] = jnp.where(index < group, one, pltpu.roll(two, group, 0)).astype(
            jnp.bfloat16
        )
        normed_ref[2 * t + 1, 0] = jnp.where(
            index < group, pltpu.roll(one, group, 0), two
        ).astype(jnp.bfloat16)


def stem(kind, image, weights, first, steps, devices, extra=()):
    cols, depth = image.shape[1:]
    rows = 2 * steps
    shapes = weight_shapes(weights)
    channels, third_depth = shapes[2].shape
    merged = shapes[1].shape[0]
    group = channels // devices

    def section_pairs():
        return lax.axis_index("section") * (image.shape[0] // 4)

    def whole(array):
        return pl.BlockSpec(array.shape, lambda i: (0,) * len(array.shape))

    operands = list(weights) + list(extra)
    in_specs = [whole(a) for a in weights]
    out_specs = [
        pl.BlockSpec((devices, 1, 2 * group, cols), lambda i: (0, i, 0, 0)),
        pl.BlockSpec((2, channels, cols), lambda i: (i, 0, 0)),
    ]
    out_shape = [
        jax.ShapeDtypeStruct((devices, steps, 2 * group, cols), jnp.bfloat16),
        jax.ShapeDtypeStruct((rows, channels, cols), jnp.bfloat16),
    ]
    in_specs += [whole(a) for a in extra]
    macs = rows * cols * (16 * 208 * 96 + 4 * 400 * merged + third_depth * channels)
    return pl.pallas_call(
        functools.partial(stem_kernel, kind),
        grid=(steps,),
        in_specs=[
            pl.BlockSpec((2, cols, depth), lambda i: (section_pairs() + first + i, 0, 0)),
            pl.BlockSpec(
                (1, cols, depth),
                lambda i: (jnp.maximum(2 * (section_pairs() + first) - 1, 0), 0, 0),
            ),
        ]
        + in_specs,
        out_specs=out_specs,
        scratch_shapes=[pltpu.VMEM(a.shape, a.dtype) for a in shapes]
        + [pltpu.VMEM((third_depth, 2 * cols), jnp.bfloat16)],
        out_shape=out_shape,
        compiler_params=pltpu.CompilerParams(vmem_limit_bytes=VMEM_BYTES),
        cost_estimate=pl.CostEstimate(
            flops=4 * macs, bytes_accessed=rows * cols * 3000, transcendentals=0
        ),
        name="stem",
    )(image, image, *operands)


def symmetric_kernel(place_ref, f_ref, turn_w_ref, turn_u_ref, g_ref):
    width = g_ref.shape[3]
    for part in range(2):
        block = f_ref[0, part]
        across = jnp.dot(block, turn_w_ref[...], preferred_element_type=jnp.float32)
        turned = jnp.dot(
            turn_u_ref[...], across.astype(jnp.bfloat16), preferred_element_type=jnp.float32
        )
        own = block[:, :width].astype(jnp.float32)
        both = own + turned if part == 0 else own - turned
        g_ref[0, part] = (0.5 * both).astype(jnp.bfloat16)


def symmetric_filter(spectral_filter, place, group, width):
    full_rows, full_cols = spectral_filter.shape[2:]
    u = jnp.arange(full_rows, dtype=jnp.int32)
    w = jnp.arange(full_cols, dtype=jnp.int32)
    turn_u = ((u[:, None] + u[None, :]) % full_rows == 0).astype(jnp.bfloat16)
    turn_w = ((w[:, None] + w[None, :width]) % full_cols == 0).astype(jnp.bfloat16)
    return pl.pallas_call(
        symmetric_kernel,
        grid_spec=pltpu.PrefetchScalarGridSpec(
            num_scalar_prefetch=1,
            grid=(group,),
            in_specs=[
                pl.BlockSpec(
                    (1, 2, full_rows, full_cols), lambda i, place: (place[0] + i, 0, 0, 0)
                ),
                pl.BlockSpec(turn_w.shape, lambda i, place: (0, 0)),
                pl.BlockSpec(turn_u.shape, lambda i, place: (0, 0)),
            ],
            out_specs=pl.BlockSpec((1, 2, full_rows, width), lambda i, place: (i, 0, 0, 0)),
        ),
        out_shape=jax.ShapeDtypeStruct((group, 2, full_rows, width), jnp.bfloat16),
        compiler_params=pltpu.CompilerParams(vmem_limit_bytes=VMEM_BYTES),
        cost_estimate=pl.CostEstimate(
            flops=8 * group * full_rows * full_cols * width,
            bytes_accessed=group * full_rows * width * 14,
            transcendentals=0,
        ),
        name="symmetric_filter",
    )(place, spectral_filter, turn_w, turn_u)


def to_lane_tiles(target, rows, values):
    for j in range(target.shape[0]):
        target[j, rows, :] = values[:, 128 * j : 128 * (j + 1)]


def from_lane_tiles(source, rows):
    return jnp.concatenate([source[j, rows, :] for j in range(source.shape[0])], axis=1)


RADIX = 3
HALF_ROOT = math.sqrt(3.0) / 2.0


def repack_kernel(devices, early_ref, out_ref, held):
    group, length = out_ref.shape[:2]
    rows = length // devices
    to_lane_tiles(held, slice(None), early_ref[...].astype(jnp.float32))
    for k in range(group):
        for r in range(rows):
            values = from_lane_tiles(held, pl.ds(r * group + k, devices, stride=rows * group))
            out_ref[k, r * devices : (r + 1) * devices] = values.astype(jnp.bfloat16)


def repack(early, group, devices):
    length, cols = early.shape
    return pl.pallas_call(
        functools.partial(repack_kernel, devices),
        out_shape=jax.ShapeDtypeStruct((group, length // group, cols), jnp.bfloat16),
        scratch_shapes=[pltpu.VMEM((cols // 128, length, 128), jnp.float32)],
        compiler_params=pltpu.CompilerParams(vmem_limit_bytes=VMEM_BYTES // 4),
        cost_estimate=pl.CostEstimate(
            flops=length * cols, bytes_accessed=4 * length * cols, transcendentals=0
        ),
        name="repack",
    )(early)


def thirds(values, sign):
    (re0, im0), (re1, im1), (re2, im2) = values
    sum_re, sum_im = re1 + re2, im1 + im2
    turn_re, turn_im = HALF_ROOT * sign * (im1 - im2), HALF_ROOT * sign * (re2 - re1)
    rest_re, rest_im = re0 - 0.5 * sum_re, im0 - 0.5 * sum_im
    return (
        (re0 + sum_re, im0 + sum_im),
        (rest_re + turn_re, rest_im + turn_im),
        (rest_re - turn_re, rest_im - turn_im),
    )


def filter_kernel(
    first, devices, norm_scale, late_ref, early_ref, g_ref, row_table_ref, fwd_ref, inv_ref,
    back_ref, twiddle_ref, out_ref, held, made,
):
    step = pl.program_id(0)
    third = fwd_ref.shape[0] // 2
    full_rows = RADIX * third
    width = g_ref.shape[3]
    count = made.shape[1] // full_rows
    per_step = g_ref.shape[0]
    early = early_ref.shape[1] // devices
    late = full_rows // devices - early
    group = held.shape[1] // (late * devices)

    @pl.when(step == 0)
    def _():
        to_lane_tiles(held, slice(None), late_ref[...].astype(jnp.float32))

    def source_rows(k, row):
        if row >= late:
            begin = (row - late) * devices
            return early_ref[k, begin : begin + devices]
        begin = row * group + first + step * per_step + k
        values = from_lane_tiles(held, pl.ds(begin, devices, stride=late * group))
        return values.astype(jnp.bfloat16)

    def twiddles(r):
        cos, sin = twiddle_ref[2 * r - 2], twiddle_ref[2 * r - 1]
        times = per_step * width // 128
        return jnp.concatenate([cos] * times, axis=1), jnp.concatenate([sin] * times, axis=1)

    fields = []
    for k in range(per_step):
        rows = [
            source_rows(k, r + RADIX * q)
            for r in range(RADIX)
            for q in range((late + early) // RADIX)
        ]
        spread = jnp.dot(
            jnp.concatenate(rows, axis=0), row_table_ref[...], preferred_element_type=jnp.float32
        )
        fields.append(spread.astype(jnp.bfloat16))
    parts = []
    for r in range(RADIX):
        span = slice(r * third, (r + 1) * third)
        block = jnp.concatenate(
            [
                jnp.concatenate([f[span, :width], f[span, width:]], axis=0)
                for f in fields
            ],
            axis=1,
        )
        short = jnp.dot(fwd_ref[...], block, preferred_element_type=jnp.float32)
        real, imag = short[:third], short[third:]
        if r > 0:
            cos, sin = twiddles(r)
            real, imag = real * cos + imag * sin, imag * cos - real * sin
        parts.append((real, imag))
    weighted = []
    for r, (real, imag) in enumerate(thirds(parts, 1.0)):
        span = slice(r * third, (r + 1) * third)
        g_real, g_imag = (
            jnp.concatenate([g_ref[k, p, span] for k in range(per_step)], axis=1).astype(
                jnp.float32
            )
            for p in range(2)
        )
        weighted.append((g_real * real - g_imag * imag, g_real * imag + g_imag * real))
    for r, (real, imag) in enumerate(thirds(weighted, -1.0)):
        if r > 0:
            cos, sin = twiddles(r)
            real, imag = real * cos - imag * sin, imag * cos + real * sin
        block = jnp.concatenate([real, imag], axis=0).astype(jnp.bfloat16)
        back = jnp.dot(inv_ref[...], block, preferred_element_type=jnp.float32).astype(
            jnp.bfloat16
        )
        for k in range(per_step):
            lanes = slice(k * width, (k + 1) * width)
            both = jnp.concatenate([back[:third, lanes], back[third:, lanes]], axis=1)
            result = jnp.dot(both, back_ref[...], preferred_element_type=jnp.float32)
            rows = pl.ds(r * count + step * per_step + k, third, stride=RADIX * count)
            to_lane_tiles(made, rows, result * norm_scale)

    @pl.when(step == pl.num_programs(0) - 1)
    def _():
        out_ref[...] = from_lane_tiles(made, slice(None)).astype(jnp.bfloat16)


def filter_tables(full_rows, field_cols, width, devices):
    third = full_rows // RADIX
    per_device = third // devices
    order = (per_device * np.arange(devices)[None, :] + np.arange(per_device)[:, None]).reshape(-1)
    cos_h, sin_h = fourier_tables(third)
    cos_f, sin_f = fourier_tables(third, order.astype(np.int32))
    cos_w, sin_w = fourier_tables(field_cols)
    fwd = jnp.concatenate(
        [jnp.concatenate([cos_f, sin_f], 1), jnp.concatenate([-sin_f, cos_f], 1)], 0
    )
    inv = jnp.concatenate(
        [jnp.concatenate([cos_h, -sin_h], 1), jnp.concatenate([sin_h, cos_h], 1)], 0
    )
    w = jnp.arange(width, dtype=jnp.int32)
    half = field_cols // 2
    valid = (w <= half).astype(jnp.bfloat16)
    times = jnp.where((w == 0) | (w == half), 1.0, 2.0).astype(jnp.bfloat16) * valid
    row_table = jnp.concatenate([cos_w[:, :width] * valid, -sin_w[:, :width] * valid], 1)
    back_table = jnp.concatenate(
        [cos_w[:width] * times[:, None], -sin_w[:width] * times[:, None]], 0
    )
    turns = np.arange(1, RADIX)[:, None] * np.arange(third)[None, :]
    angles = turns * (2.0 * math.pi / full_rows)
    twiddle = np.stack([np.cos(angles), np.sin(angles)], axis=1).reshape(-1, third, 1)
    twiddle = np.broadcast_to(twiddle.astype(np.float32), (2 * RADIX - 2, third, 128))
    twiddle = jnp.asarray(twiddle)
    return row_table, fwd, inv, back_table, twiddle


def filter_channels(late, early, symmetric, tables, first, count, per_step, devices):
    full_rows, width = symmetric.shape[2:]
    group, early_rows = early.shape[:2]
    cols = late.shape[1]

    def whole(array):
        return pl.BlockSpec(array.shape, lambda i: (0,) * array.ndim)

    macs = count * (4 * full_rows * full_rows * width + 4 * full_rows * cols * width)
    made = pl.pallas_call(
        functools.partial(filter_kernel, first, devices, 1.0 / (full_rows * cols)),
        grid=(count // per_step,),
        in_specs=[
            whole(late),
            pl.BlockSpec((per_step, early_rows, cols), lambda i: (first // per_step + i, 0, 0)),
            pl.BlockSpec(
                (per_step, 2, full_rows, width), lambda i: (first // per_step + i, 0, 0, 0)
            ),
        ]
        + [whole(table) for table in tables],
        out_specs=pl.BlockSpec((full_rows * count, cols), lambda i: (0, 0)),
        out_shape=jax.ShapeDtypeStruct((full_rows * count, cols), jnp.bfloat16),
        scratch_shapes=[
            pltpu.VMEM((cols // 128, late.shape[0], 128), jnp.float32),
            pltpu.VMEM((cols // 128, full_rows * count, 128), jnp.float32),
        ],
        compiler_params=pltpu.CompilerParams(vmem_limit_bytes=VMEM_BYTES * (2 if count == per_step else 4) // 5),
        cost_estimate=pl.CostEstimate(
            flops=2 * macs, bytes_accessed=count * full_rows * cols * 8, transcendentals=0
        ),
        name="spectral_filter",
    )(late, early, symmetric, *tables)
    return made.reshape(devices, full_rows // devices * count, cols)


def residual_kernel(count, place_ref, kept_ref, other_ref, feat_ref, *refs):
    out_ref, held = refs[-2:]
    groups, span, cols = kept_ref.shape
    rows = held.shape[1] // count
    own = pl.multiple_of(place_ref[0] * span, 8)
    far = pl.multiple_of((1 - place_ref[0]) * span, 8)
    for g in range(groups):
        to_lane_tiles(held, pl.ds(own, span), kept_ref[g].astype(jnp.float32))
        to_lane_tiles(held, pl.ds(far, span), other_ref[g].astype(jnp.float32))
        for k in range(count):
            filtered = from_lane_tiles(held, pl.ds(k, rows, stride=count))
            out_ref[g, k] = (feat_ref[g, k].astype(jnp.float32) + filtered).astype(jnp.bfloat16)


def add_residual(place, returned, other, features, previous, first, count):
    halves, span, cols = other.shape
    group, rows = features.shape[1:3]
    groups = 2 if halves % 2 == 0 else 1
    steps = halves // groups
    operands = [returned, other, features]
    in_specs = [
        pl.BlockSpec((groups, span, cols), lambda i, place: (place[0] * steps + i, 0, 0)),
        pl.BlockSpec((groups, span, cols), lambda i, place: (i, 0, 0)),
        pl.BlockSpec(
            (groups, count, rows, cols),
            lambda i, place: (i, first // count, 0, 0),
        ),
    ]
    aliases = {}
    if previous is not None:
        operands.append(previous)
        in_specs.append(pl.BlockSpec(memory_space=pl.ANY))
        aliases = {4: 0}
    return pl.pallas_call(
        functools.partial(residual_kernel, count),
        grid_spec=pltpu.PrefetchScalarGridSpec(
            num_scalar_prefetch=1,
            grid=(steps,),
            in_specs=in_specs,
            out_specs=in_specs[2],
            scratch_shapes=[pltpu.VMEM((cols // 128, rows * count, 128), jnp.float32)],
        ),
        out_shape=jax.ShapeDtypeStruct(features.shape, jnp.bfloat16),
        input_output_aliases=aliases,
        compiler_params=pltpu.CompilerParams(vmem_limit_bytes=VMEM_BYTES // 6),
        cost_estimate=pl.CostEstimate(
            flops=halves * count * rows * cols,
            bytes_accessed=halves * count * rows * cols * 8,
            transcendentals=0,
        ),
        name="residual",
    )(place, *operands)


def swap(block):
    return lax.ppermute(block, "section", [(0, 1), (1, 0)])


def local(
    aerial_patch_grid,
    patch_conv_weight,
    patch_bias,
    merging_conv_weight,
    merge_bias,
    down_weight,
    down_bias,
    norm_gain,
    spectral_filter,
):
    tile_rows, field_cols, depth = aerial_patch_grid.shape
    channels = down_weight.shape[3]
    tile_channels = spectral_filter.shape[0]
    full_rows = spectral_filter.shape[2]
    sections = lax.axis_size("section")
    devices = sections * lax.axis_size("tile")
    rows = tile_rows // 2
    suits = (
        sections == 2
        and tile_rows % 8 == 0
        and tile_rows >= 16
        and field_cols % 128 == 0
        and full_rows % (128 * RADIX) == 0
        and rows % RADIX == 0
        and devices % 8 == 0
        and tile_channels % 8 == 0
    )
    arguments = (
        aerial_patch_grid,
        patch_conv_weight,
        patch_bias,
        merging_conv_weight,
        merge_bias,
        down_weight,
        down_bias,
        norm_gain,
        spectral_filter,
    )
    if not suits:
        return general_local(*arguments)
    section = lax.axis_index("section")
    group = tile_channels // 2
    half_channels = channels // 2
    width = -(-(field_cols // 2 + 1) // 128) * 128

    arriving = from_behind(lower_half(aerial_patch_grid[-1]), "tile", 1)
    sources = weight_sources(*arguments[1:8])
    pairs = rows // 2
    early = max(pairs // 3, 1)
    late = pairs - early
    normed_early, feat_early = stem(
        "first", aerial_patch_grid, sources, late, early, devices
    )
    normed_early, arriving = lax.optimization_barrier((normed_early, arriving))
    normed_late, feat_late = stem(
        "last", aerial_patch_grid, sources, 0, late, devices, (arriving,)
    )
    spread = [
        lax.all_to_all(normed, DEVICES, split_axis=0, concat_axis=0, tiled=True).reshape(
            -1, field_cols
        )
        for normed in (normed_early, normed_late)
    ]
    early_fields = repack(spread[0], group, devices)
    late_fields = spread[1]
    features = jnp.concatenate([feat_late, feat_early], axis=0)

    channel_place = jnp.reshape(section * group, (1,)).astype(jnp.int32)
    symmetric = symmetric_filter(spectral_filter, channel_place, group, width)
    tables = filter_tables(full_rows, field_cols, width, devices)

    own = lax.dynamic_slice_in_dim(features, section * half_channels, half_channels, 1)
    sent = lax.dynamic_slice_in_dim(features, (1 - section) * half_channels, half_channels, 1)
    arrived = swap(sent)
    low = jnp.where(section == 0, own, arrived)
    high = jnp.where(section == 0, arrived, own)
    residual = jnp.transpose(jnp.concatenate([low, high], axis=0), (1, 0, 2))
    residual = residual.reshape(half_channels // group, group, tile_rows, field_cols)
    late_fields, residual = lax.optimization_barrier((late_fields, residual))

    section_place = jnp.reshape(section, (1,)).astype(jnp.int32)
    halves = devices // 2
    output = None
    rest = group - 2
    per_step = 5 if rest % 5 == 0 else 2
    for first, count, per_step in ((rest, 2, 2), (0, rest, per_step)):
        made = filter_channels(
            late_fields, early_fields, symmetric, tables, first, count, per_step, devices
        )
        returned = lax.all_to_all(made, DEVICES, split_axis=0, concat_axis=0, tiled=True)
        if output is not None:
            returned, output = lax.optimization_barrier((returned, output))
        other = swap(lax.dynamic_slice_in_dim(returned, (1 - section) * halves, halves, 0))
        output = add_residual(section_place, returned, other, residual, output, first, count)
    return output.reshape(half_channels, tile_rows, field_cols)


def solution(mesh):
    return jax.shard_map(
        local,
        mesh=mesh,
        in_specs=(
            P("tile", None, None),
            P(),
            P(),
            P(),
            P(),
            P(),
            P(),
            P(),
            P("tile", None, None, None),
        ),
        out_specs=P("section", "tile", None),
        check_vma=False,
    )
```

```python
import functools
import math

import jax
import jax.numpy as jnp
import numpy as np
from jax import lax
from jax.experimental import pallas as pl
from jax.experimental.pallas import tpu as pltpu
from jax.sharding import PartitionSpec as P

EPSILON = 1e-05


def from_behind(block, axis, distance):
    devices = range(lax.axis_size(axis))
    route = [(i - distance, i) for i in devices if i - distance in devices]
    return lax.ppermute(block, axis, route)


def fourier_tables(length, columns=None):
    indices = jnp.arange(length, dtype=jnp.int32)
    columns = indices if columns is None else jnp.asarray(columns, jnp.int32)
    product = indices[:, None] * columns[None, :] % length
    angles = product.astype(jnp.float32) * (2.0 * math.pi / length)
    return (jnp.cos(angles).astype(jnp.bfloat16), jnp.sin(angles).astype(jnp.bfloat16))


def patch_kernel_matrix(patch_conv_weight):
    identity = jnp.eye(4, dtype=jnp.float32)
    larger = jnp.einsum(
        "baqk,xy,uv->bxauqyvk", patch_conv_weight.astype(jnp.float32), identity, identity
    )
    band_count = patch_conv_weight.shape[0]
    width = patch_conv_weight.shape[3]
    return larger.reshape(band_count * 256, 16 * width).astype(jnp.bfloat16)


def merging_kernel_matrix(merging_conv_weight):
    identity = jnp.eye(2, dtype=jnp.float32)
    larger = jnp.einsum(
        "aqjk,xy,uv->xauqjyvk", merging_conv_weight.astype(jnp.float32), identity, identity
    )
    in_width = merging_conv_weight.shape[2]
    out_width = merging_conv_weight.shape[3]
    return larger.reshape(16 * in_width, 4 * out_width).astype(jnp.bfloat16)


def down_matrices(down_weight):
    nothing = jnp.zeros_like(down_weight[0, 0])
    in_width = down_weight.shape[2]
    out_width = down_weight.shape[3]

    def arrange(entries):
        return jnp.stack(
            [jnp.stack(entries[0], axis=0), jnp.stack(entries[1], axis=0)], axis=0
        ).reshape(4 * in_width, out_width)

    own_taps = arrange(
        [[down_weight[1, 1], down_weight[1, 2]], [down_weight[2, 1], down_weight[2, 2]]]
    )
    upper_taps = arrange([[nothing, nothing], [down_weight[0, 1], down_weight[0, 2]]])
    left_taps = arrange([[nothing, down_weight[1, 0]], [nothing, down_weight[2, 0]]])
    corner_taps = arrange([[nothing, nothing], [nothing, down_weight[0, 0]]])
    return (own_taps, upper_taps, left_taps, corner_taps)


def stem_layers(aerial_patch_grid, patch_conv_weight, patch_bias, merging_conv_weight, merge_bias):
    initial_layer = jnp.einsum(
        "zji,if->zjf",
        aerial_patch_grid,
        patch_kernel_matrix(patch_conv_weight),
        preferred_element_type=jnp.float32,
    )
    initial_layer = jax.nn.gelu(initial_layer + jnp.tile(patch_bias, 16), approximate=True).astype(
        jnp.bfloat16
    )
    layer_two = jnp.einsum(
        "zji,if->zjf",
        initial_layer,
        merging_kernel_matrix(merging_conv_weight),
        preferred_element_type=jnp.float32,
    )
    return jax.nn.gelu(layer_two + jnp.tile(merge_bias, 4), approximate=True).astype(jnp.bfloat16)


def rim_above(extended):
    return from_behind(extended[-1:], "tile", 1)


def down_conv(upper_rim, extended, down_weight, down_bias):
    stacked = jnp.concatenate([upper_rim, extended], axis=0)
    own_taps, upper_taps, left_taps, corner_taps = down_matrices(down_weight)
    summed = jnp.einsum(
        "rwk,kc->crw", stacked[1:, 1:], own_taps, preferred_element_type=jnp.float32
    )
    summed = summed + jnp.einsum(
        "rwk,kc->crw", stacked[:-1, 1:], upper_taps, preferred_element_type=jnp.float32
    )
    summed = summed + jnp.einsum(
        "rwk,kc->crw", stacked[1:, :-1], left_taps, preferred_element_type=jnp.float32
    )
    summed = summed + jnp.einsum(
        "rwk,kc->crw", stacked[:-1, :-1], corner_taps, preferred_element_type=jnp.float32
    )
    return (summed + down_bias[:, None, None]).astype(jnp.bfloat16)


def layer_norm(features, norm_gain):
    values = features.astype(jnp.float32)
    mean_value = jnp.mean(values, axis=0, keepdims=True)
    centered = values - mean_value
    variance = jnp.mean(centered * centered, axis=0, keepdims=True)
    return (norm_gain[:, None, None] * centered * lax.rsqrt(variance + EPSILON)).astype(
        jnp.bfloat16
    )


def filter_columns(row_spectrum, kernel, forward_h, inverse_h):
    spectrum = jnp.einsum(
        "puqh,chqw->cpuw", forward_h, row_spectrum, preferred_element_type=jnp.float32
    ).astype(jnp.bfloat16)
    spec_real = spectrum[:, 0].astype(jnp.float32)
    spec_imag = spectrum[:, 1].astype(jnp.float32)
    filter_real = kernel[:, 0].astype(jnp.float32)
    filter_imag = kernel[:, 1].astype(jnp.float32)
    weighted = jnp.stack(
        [
            filter_real * spec_real - filter_imag * spec_imag,
            filter_real * spec_imag + filter_imag * spec_real,
        ],
        axis=1,
    ).astype(jnp.bfloat16)
    return jnp.einsum(
        "qhpu,cpuw->chqw", inverse_h, weighted, preferred_element_type=jnp.float32
    ).astype(jnp.bfloat16)


def general_local(
    aerial_patch_grid,
    patch_conv_weight,
    patch_bias,
    merging_conv_weight,
    merge_bias,
    down_weight,
    down_bias,
    norm_gain,
    spectral_filter,
):
    section_index = lax.axis_index("section")
    first_section = section_index == 0
    field_cols = aerial_patch_grid.shape[1]
    channels = down_weight.shape[3]
    group_width = spectral_filter.shape[0]
    full_rows = spectral_filter.shape[2]
    half_channels = channels // 2
    cell_half = field_cols // 2
    image_part = lax.dynamic_slice_in_dim(
        aerial_patch_grid, section_index * cell_half, cell_half, 1
    )
    layer_two = stem_layers(
        image_part, patch_conv_weight, patch_bias, merging_conv_weight, merge_bias
    )
    left_column = from_behind(layer_two[:, -1:], "section", 1)
    extended = jnp.concatenate([left_column, layer_two], axis=1)
    upper_rim = rim_above(extended)
    feature_half = down_conv(upper_rim, extended, down_weight, down_bias)
    features = lax.all_gather(feature_half, "section", axis=2, tiled=True)
    normed = layer_norm(features, norm_gain)
    cos_h, sin_h = fourier_tables(full_rows)
    cos_w, sin_w = fourier_tables(field_cols)
    forward_table = jnp.stack([cos_w, -sin_w], axis=1)
    forward_h = jnp.stack(
        [jnp.stack([cos_h, sin_h], axis=1), jnp.stack([-sin_h, cos_h], axis=1)], axis=0
    )
    inverse_h = jnp.stack(
        [jnp.stack([cos_h, -sin_h], axis=1), jnp.stack([sin_h, cos_h], axis=1)], axis=0
    )
    inverse_table = jnp.stack([cos_w, -sin_w], axis=0)
    norm_scale = 1.0 / (full_rows * field_cols)
    fields = lax.all_to_all(normed, "tile", split_axis=0, concat_axis=1, tiled=True)

    def whole_filter():
        frequency_rows = jnp.einsum(
            "chx,xqw->chqw", fields, forward_table, preferred_element_type=jnp.float32
        ).astype(jnp.bfloat16)
        back_rows = filter_columns(frequency_rows, spectral_filter, forward_h, inverse_h)
        result = jnp.einsum(
            "chqw,qwv->chv", back_rows, inverse_table, preferred_element_type=jnp.float32
        )
        return (result * norm_scale).astype(jnp.bfloat16)

    def empty_fields():
        return jnp.zeros((group_width, full_rows, field_cols), jnp.bfloat16)

    filtered_fields = lax.cond(first_section, empty_fields, whole_filter)
    rows_back = lax.all_to_all(filtered_fields, "tile", split_axis=1, concat_axis=0, tiled=True)
    returned = from_behind(rows_back[:half_channels], "section", -1)
    filtered = jnp.where(first_section, returned, rows_back[half_channels:])
    own_part = lax.dynamic_slice_in_dim(features, section_index * half_channels, half_channels, 0)
    return (own_part.astype(jnp.float32) + filtered.astype(jnp.float32)).astype(jnp.bfloat16)


DEVICES = ("tile", "section")
VMEM_BYTES = 60 * 1024 * 1024
GELU_LINEAR = 2.0 * math.sqrt(2.0 / math.pi)
GELU_CUBIC = 4.0 * 0.044715 * GELU_LINEAR
ONES = (64, 128, 64)
TAPS = ((1, 1), (1, 2), (2, 1), (2, 2), (1, 0), (2, 0), (0, 1), (0, 2), (0, 0))


def bias_rows(bias, count):
    high = bias.astype(jnp.bfloat16)
    rest = bias - high.astype(jnp.float32)
    middle = rest.astype(jnp.bfloat16)
    low = (rest - middle.astype(jnp.float32)).astype(jnp.bfloat16)
    shape = (count, bias.shape[1])
    row = lax.broadcasted_iota(jnp.int32, shape, 0)
    rows = jnp.zeros(shape, jnp.float32)
    for k, part in enumerate((high, middle, low)):
        rows = jnp.where(row == k, jnp.broadcast_to(part.astype(jnp.float32), shape), rows)
    return rows.astype(jnp.bfloat16)


def build_weights(sources, targets):
    patch_ref, patch_bias_ref, merge_ref, merge_bias_ref, down_ref, down_bias_ref, gain_ref = sources
    w1_ref, w2_ref, w3_ref, column_ref = targets

    def exact(a, b):
        return jnp.dot(
            a.astype(jnp.bfloat16), b.astype(jnp.bfloat16), preferred_element_type=jnp.float32
        )

    taps, width = patch_ref.shape
    row = lax.broadcasted_iota(jnp.int32, (4 * taps, taps), 0)
    col = lax.broadcasted_iota(jnp.int32, (4 * taps, taps), 1)
    pick = jnp.where(row // 16 * 4 + row % 4 == col, 1.0, 0.0)
    row = lax.broadcasted_iota(jnp.int32, (width, 4 * width), 0)
    col = lax.broadcasted_iota(jnp.int32, (width, 4 * width), 1)
    repeat = jnp.where(col % width == row, 1.0, 0.0)
    spread = exact(pick, exact(patch_ref[...], repeat))
    row = lax.broadcasted_iota(jnp.int32, spread.shape, 0)
    col = lax.broadcasted_iota(jnp.int32, spread.shape, 1)
    spread = jnp.where(row // 4 % 4 == col // width, 0.5 * spread, 0.0).astype(jnp.bfloat16)
    bias = jnp.broadcast_to(0.5 * patch_bias_ref[...][None], (8, width))
    tiled = jnp.zeros((8, 4 * width), jnp.float32)
    for _ in range(3):
        part = bias.astype(jnp.bfloat16).astype(jnp.float32)
        tiled = tiled + exact(part, repeat)
        bias = bias - part
    first = jnp.concatenate([spread, bias_rows(tiled[:1], ONES[0])], axis=0)
    w1_ref[...] = first.T
    half = (merge_ref[...].astype(jnp.float32) * 0.5).astype(jnp.bfloat16)
    second = jnp.concatenate([half, bias_rows(0.5 * merge_bias_ref[...][None], ONES[1])], axis=0)
    w2_ref[...] = second.T
    third = [down_ref[3 * a + q] for a, q in TAPS]
    third = jnp.concatenate(third + [bias_rows(down_bias_ref[...][None], ONES[2])], axis=0)
    w3_ref[...] = third.T
    column_ref[...] = jnp.broadcast_to(gain_ref[...][None], (128, gain_ref.shape[0])).T


def weight_sources(
    patch_conv_weight, patch_bias, merging_conv_weight, merge_bias, down_weight, down_bias,
    norm_gain,
):
    width = patch_conv_weight.shape[3]
    merged = merging_conv_weight.shape[3]
    return [
        patch_conv_weight.reshape(-1, width),
        patch_bias,
        merging_conv_weight.reshape(-1, merged),
        merge_bias,
        down_weight.reshape(-1, merged, down_weight.shape[3]),
        down_bias,
        norm_gain,
    ]


def weight_shapes(sources):
    taps, width = sources[0].shape
    merged, channels = sources[4].shape[1:]
    return [
        jax.ShapeDtypeStruct((4 * width, 4 * taps + ONES[0]), jnp.bfloat16),
        jax.ShapeDtypeStruct((merged, 4 * width + ONES[1]), jnp.bfloat16),
        jax.ShapeDtypeStruct((channels, 9 * merged + ONES[2]), jnp.bfloat16),
        jax.ShapeDtypeStruct((channels, 128), jnp.float32),
    ]


def half_gelu(h):
    return h + h * jnp.tanh(h * (GELU_LINEAR + GELU_CUBIC * (h * h)))


def lower_half(row):
    depth = row.shape[1]
    return jnp.concatenate(
        [row[:, 256 * b + 128 : 256 * b + 256] for b in range(depth // 256)], axis=1
    )


def stem_kernel(kind, x_ref, above_ref, *refs):
    sources = refs[:7]
    normed_ref, feat_ref, w1_ref, w2_ref, w3_ref, gain_ref, field = refs[-7:]
    step = pl.program_id(0)
    rows, cols, depth = x_ref.shape
    bands = depth // 256
    channels = w3_ref.shape[0]
    merged = w2_ref.shape[0]
    group = normed_ref.shape[2] // rows
    cells = rows * cols

    @pl.when(step == 0)
    def _():
        build_weights(sources, (w1_ref, w2_ref, w3_ref, gain_ref))

    w1 = w1_ref[...]
    w2 = w2_ref[...]

    def ones(count, n):
        return jnp.where(lax.broadcasted_iota(jnp.int32, (count, n), 0) < 3, 1.0, 0.0).astype(
            jnp.bfloat16
        )

    def layer_one(turned, offsets):
        n = turned.shape[1]
        parts = [turned[o : o + 64] for o in offsets] + [ones(ONES[0], n)]
        h = jnp.dot(w1, jnp.concatenate(parts, axis=0), preferred_element_type=jnp.float32)
        return half_gelu(h).astype(jnp.bfloat16)

    def layer_two(upper, lower, y):
        n = upper.shape[1]
        span = slice(2 * y * (w1.shape[0] // 4), 2 * (y + 1) * (w1.shape[0] // 4))
        stacked = jnp.concatenate([upper[span], lower[span], ones(ONES[1], n)], axis=0)
        return half_gelu(jnp.dot(w2, stacked, preferred_element_type=jnp.float32))

    def shifted(values):
        lanes = lax.broadcasted_iota(jnp.int32, values.shape, 1)
        moved = pltpu.roll(values, 1, 1)
        return jnp.where(lax.rem(lanes, cols) == 0, 0.0, moved)

    def put(block, lanes, values):
        field[block * merged : (block + 1) * merged, lanes] = values.astype(jnp.bfloat16)

    first_row = slice(0, cols)
    last_row = slice(cells - cols, cells)
    later_rows = slice(cols, cells)
    earlier_rows = slice(0, cells - cols)

    @pl.when(step == 0)
    def _():
        field[9 * merged :, :] = ones(ONES[2], cells)
        above = lower_half(above_ref[0])
        keep = 1.0
        if kind == "last":
            lower_section = lax.axis_index("section") > 0
            inside = lower_section | (lax.axis_index("tile") > 0)
            keep = jnp.where(inside, 1.0, 0.0)
            above = jnp.where(lower_section, above, refs[7][...])
        turned = above.T
        upper, lower = (
            layer_one(turned, [128 * b + 64 * a for b in range(bands)]) for a in range(2)
        )
        put(6, first_row, layer_two(upper, lower, 0) * keep)
        right = layer_two(upper, lower, 1) * keep
        put(7, first_row, right)
        put(8, first_row, shifted(right))

    @pl.when(step > 0)
    def _():
        for source, target in ((2, 6), (3, 7), (5, 8)):
            field[target * merged : (target + 1) * merged, first_row] = field[
                source * merged : (source + 1) * merged, last_row
            ]

    turned = x_ref[...].reshape(cells, depth).T
    for x in range(2):
        upper, lower = (
            layer_one(turned, [256 * b + 64 * (2 * x + a) for b in range(bands)])
            for a in range(2)
        )
        left = layer_two(upper, lower, 0)
        right = layer_two(upper, lower, 1)
        put(2 * x, slice(None), left)
        put(2 * x + 1, slice(None), right)
        moved = shifted(right)
        put(4 + x, slice(None), moved)
        if x == 1:
            put(6, later_rows, left[:, earlier_rows])
            put(7, later_rows, right[:, earlier_rows])
            put(8, later_rows, moved[:, earlier_rows])

    features = jnp.dot(w3_ref[...], field[...], preferred_element_type=jnp.float32).astype(
        jnp.bfloat16
    )
    for r in range(rows):
        feat_ref[r] = features[:, r * cols : (r + 1) * cols]
    values = features.astype(jnp.float32)
    centered = values - jnp.mean(values, axis=0, keepdims=True)
    variance = jnp.mean(centered * centered, axis=0, keepdims=True)
    gain = jnp.concatenate([gain_ref[...]] * (cells // 128), axis=1)
    normed = gain * (centered * lax.rsqrt(variance + EPSILON))
    pair = 2 * group
    index = lax.broadcasted_iota(jnp.int32, (pair, cols), 0)
    for t in range(channels // pair):
        one = normed[pair * t : pair * (t + 1), :cols]
        two = normed[pair * t : pair * (t + 1), cols:]
        normed_ref[2 * t, 0] = jnp.where(index < group, one, pltpu.roll(two, group, 0)).astype(
            jnp.bfloat16
        )
        normed_ref[2 * t + 1, 0] = jnp.where(
            index < group, pltpu.roll(one, group, 0), two
        ).astype(jnp.bfloat16)


def stem(kind, image, weights, first, steps, devices, extra=()):
    cols, depth = image.shape[1:]
    rows = 2 * steps
    shapes = weight_shapes(weights)
    channels, third_depth = shapes[2].shape
    merged = shapes[1].shape[0]
    group = channels // devices

    def section_pairs():
        return lax.axis_index("section") * (image.shape[0] // 4)

    def whole(array):
        return pl.BlockSpec(array.shape, lambda i: (0,) * len(array.shape))

    operands = list(weights) + list(extra)
    in_specs = [whole(a) for a in weights]
    out_specs = [
        pl.BlockSpec((devices, 1, 2 * group, cols), lambda i: (0, i, 0, 0)),
        pl.BlockSpec((2, channels, cols), lambda i: (i, 0, 0)),
    ]
    out_shape = [
        jax.ShapeDtypeStruct((devices, steps, 2 * group, cols), jnp.bfloat16),
        jax.ShapeDtypeStruct((rows, channels, cols), jnp.bfloat16),
    ]
    in_specs += [whole(a) for a in extra]
    macs = rows * cols * (16 * 208 * 96 + 4 * 400 * merged + third_depth * channels)
    return pl.pallas_call(
        functools.partial(stem_kernel, kind),
        grid=(steps,),
        in_specs=[
            pl.BlockSpec((2, cols, depth), lambda i: (section_pairs() + first + i, 0, 0)),
            pl.BlockSpec(
                (1, cols, depth),
                lambda i: (jnp.maximum(2 * (section_pairs() + first) - 1, 0), 0, 0),
            ),
        ]
        + in_specs,
        out_specs=out_specs,
        scratch_shapes=[pltpu.VMEM(a.shape, a.dtype) for a in shapes]
        + [pltpu.VMEM((third_depth, 2 * cols), jnp.bfloat16)],
        out_shape=out_shape,
        compiler_params=pltpu.CompilerParams(vmem_limit_bytes=VMEM_BYTES + 3 * 1024 * 1024),
        cost_estimate=pl.CostEstimate(
            flops=4 * macs, bytes_accessed=rows * cols * 3000, transcendentals=0
        ),
        name="stem",
    )(image, image, *operands)


def symmetric_kernel(place_ref, f_ref, turn_w_ref, turn_u_ref, g_ref):
    width = g_ref.shape[3]
    for part in range(2):
        block = f_ref[0, part]
        across = jnp.dot(block, turn_w_ref[...], preferred_element_type=jnp.float32)
        turned = jnp.dot(
            turn_u_ref[...], across.astype(jnp.bfloat16), preferred_element_type=jnp.float32
        )
        own = block[:, :width].astype(jnp.float32)
        both = own + turned if part == 0 else own - turned
        g_ref[0, part] = (0.5 * both).astype(jnp.bfloat16)


def symmetric_filter(spectral_filter, place, group, width):
    full_rows, full_cols = spectral_filter.shape[2:]
    u = jnp.arange(full_rows, dtype=jnp.int32)
    w = jnp.arange(full_cols, dtype=jnp.int32)
    turn_u = ((u[:, None] + u[None, :]) % full_rows == 0).astype(jnp.bfloat16)
    turn_w = ((w[:, None] + w[None, :width]) % full_cols == 0).astype(jnp.bfloat16)
    return pl.pallas_call(
        symmetric_kernel,
        grid_spec=pltpu.PrefetchScalarGridSpec(
            num_scalar_prefetch=1,
            grid=(group,),
            in_specs=[
                pl.BlockSpec(
                    (1, 2, full_rows, full_cols), lambda i, place: (place[0] + i, 0, 0, 0)
                ),
                pl.BlockSpec(turn_w.shape, lambda i, place: (0, 0)),
                pl.BlockSpec(turn_u.shape, lambda i, place: (0, 0)),
            ],
            out_specs=pl.BlockSpec((1, 2, full_rows, width), lambda i, place: (i, 0, 0, 0)),
        ),
        out_shape=jax.ShapeDtypeStruct((group, 2, full_rows, width), jnp.bfloat16),
        compiler_params=pltpu.CompilerParams(vmem_limit_bytes=VMEM_BYTES),
        cost_estimate=pl.CostEstimate(
            flops=8 * group * full_rows * full_cols * width,
            bytes_accessed=group * full_rows * width * 14,
            transcendentals=0,
        ),
        name="symmetric_filter",
    )(place, spectral_filter, turn_w, turn_u)


def to_lane_tiles(target, rows, values):
    for j in range(target.shape[0]):
        target[j, rows, :] = values[:, 128 * j : 128 * (j + 1)]


def from_lane_tiles(source, rows):
    return jnp.concatenate([source[j, rows, :] for j in range(source.shape[0])], axis=1)


RADIX = 3
HALF_ROOT = math.sqrt(3.0) / 2.0


def repack_kernel(devices, early_ref, out_ref, held):
    group, length = out_ref.shape[:2]
    rows = length // devices
    to_lane_tiles(held, slice(None), early_ref[...].astype(jnp.float32))
    for k in range(group):
        for r in range(rows):
            values = from_lane_tiles(held, pl.ds(r * group + k, devices, stride=rows * group))
            out_ref[k, r * devices : (r + 1) * devices] = values.astype(jnp.bfloat16)


def repack(early, group, devices):
    length, cols = early.shape
    return pl.pallas_call(
        functools.partial(repack_kernel, devices),
        out_shape=jax.ShapeDtypeStruct((group, length // group, cols), jnp.bfloat16),
        scratch_shapes=[pltpu.VMEM((cols // 128, length, 128), jnp.float32)],
        compiler_params=pltpu.CompilerParams(vmem_limit_bytes=VMEM_BYTES // 4),
        cost_estimate=pl.CostEstimate(
            flops=length * cols, bytes_accessed=4 * length * cols, transcendentals=0
        ),
        name="repack",
    )(early)


def thirds(values, sign):
    (re0, im0), (re1, im1), (re2, im2) = values
    sum_re, sum_im = re1 + re2, im1 + im2
    turn_re, turn_im = HALF_ROOT * sign * (im1 - im2), HALF_ROOT * sign * (re2 - re1)
    rest_re, rest_im = re0 - 0.5 * sum_re, im0 - 0.5 * sum_im
    return (
        (re0 + sum_re, im0 + sum_im),
        (rest_re + turn_re, rest_im + turn_im),
        (rest_re - turn_re, rest_im - turn_im),
    )


def filter_kernel(
    first, devices, norm_scale, late_ref, early_ref, g_ref, row_table_ref, fwd_ref, inv_ref,
    back_ref, twiddle_ref, out_ref, held, made,
):
    step = pl.program_id(0)
    third = fwd_ref.shape[0] // 2
    full_rows = RADIX * third
    width = g_ref.shape[3]
    count = made.shape[1] // full_rows
    per_step = g_ref.shape[0]
    early = early_ref.shape[1] // devices
    late = full_rows // devices - early
    group = held.shape[1] // (late * devices)

    @pl.when(step == 0)
    def _():
        to_lane_tiles(held, slice(None), late_ref[...].astype(jnp.float32))

    def source_rows(k, row):
        if row >= late:
            begin = (row - late) * devices
            return early_ref[k, begin : begin + devices]
        begin = row * group + first + step * per_step + k
        values = from_lane_tiles(held, pl.ds(begin, devices, stride=late * group))
        return values.astype(jnp.bfloat16)

    def twiddles(r):
        cos, sin = twiddle_ref[2 * r - 2], twiddle_ref[2 * r - 1]
        times = per_step * width // 128
        return jnp.concatenate([cos] * times, axis=1), jnp.concatenate([sin] * times, axis=1)

    fields = []
    for k in range(per_step):
        rows = [
            source_rows(k, r + RADIX * q)
            for r in range(RADIX)
            for q in range((late + early) // RADIX)
        ]
        spread = jnp.dot(
            jnp.concatenate(rows, axis=0), row_table_ref[...], preferred_element_type=jnp.float32
        )
        fields.append(spread.astype(jnp.bfloat16))
    parts = []
    for r in range(RADIX):
        span = slice(r * third, (r + 1) * third)
        block = jnp.concatenate(
            [
                jnp.concatenate([f[span, :width], f[span, width:]], axis=0)
                for f in fields
            ],
            axis=1,
        )
        short = jnp.dot(fwd_ref[...], block, preferred_element_type=jnp.float32)
        real, imag = short[:third], short[third:]
        if r > 0:
            cos, sin = twiddles(r)
            real, imag = real * cos + imag * sin, imag * cos - real * sin
        parts.append((real, imag))
    weighted = []
    for r, (real, imag) in enumerate(thirds(parts, 1.0)):
        span = slice(r * third, (r + 1) * third)
        g_real, g_imag = (
            jnp.concatenate([g_ref[k, p, span] for k in range(per_step)], axis=1).astype(
                jnp.float32
            )
            for p in range(2)
        )
        weighted.append((g_real * real - g_imag * imag, g_real * imag + g_imag * real))
    for r, (real, imag) in enumerate(thirds(weighted, -1.0)):
        if r > 0:
            cos, sin = twiddles(r)
            real, imag = real * cos - imag * sin, imag * cos + real * sin
        block = jnp.concatenate([real, imag], axis=0).astype(jnp.bfloat16)
        back = jnp.dot(inv_ref[...], block, preferred_element_type=jnp.float32).astype(
            jnp.bfloat16
        )
        for k in range(per_step):
            lanes = slice(k * width, (k + 1) * width)
            both = jnp.concatenate([back[:third, lanes], back[third:, lanes]], axis=1)
            result = jnp.dot(both, back_ref[...], preferred_element_type=jnp.float32)
            rows = pl.ds(r * count + step * per_step + k, third, stride=RADIX * count)
            to_lane_tiles(made, rows, result * norm_scale)

    @pl.when(step == pl.num_programs(0) - 1)
    def _():
        out_ref[...] = from_lane_tiles(made, slice(None)).astype(jnp.bfloat16)


def filter_tables(full_rows, field_cols, width, devices):
    third = full_rows // RADIX
    per_device = third // devices
    order = (per_device * np.arange(devices)[None, :] + np.arange(per_device)[:, None]).reshape(-1)
    cos_h, sin_h = fourier_tables(third)
    cos_f, sin_f = fourier_tables(third, order.astype(np.int32))
    cos_w, sin_w = fourier_tables(field_cols)
    fwd = jnp.concatenate(
        [jnp.concatenate([cos_f, sin_f], 1), jnp.concatenate([-sin_f, cos_f], 1)], 0
    )
    inv = jnp.concatenate(
        [jnp.concatenate([cos_h, -sin_h], 1), jnp.concatenate([sin_h, cos_h], 1)], 0
    )
    w = jnp.arange(width, dtype=jnp.int32)
    half = field_cols // 2
    valid = (w <= half).astype(jnp.bfloat16)
    times = jnp.where((w == 0) | (w == half), 1.0, 2.0).astype(jnp.bfloat16) * valid
    row_table = jnp.concatenate([cos_w[:, :width] * valid, -sin_w[:, :width] * valid], 1)
    back_table = jnp.concatenate(
        [cos_w[:width] * times[:, None], -sin_w[:width] * times[:, None]], 0
    )
    turns = np.arange(1, RADIX)[:, None] * np.arange(third)[None, :]
    angles = turns * (2.0 * math.pi / full_rows)
    twiddle = np.stack([np.cos(angles), np.sin(angles)], axis=1).reshape(-1, third, 1)
    twiddle = np.broadcast_to(twiddle.astype(np.float32), (2 * RADIX - 2, third, 128))
    twiddle = jnp.asarray(twiddle)
    return row_table, fwd, inv, back_table, twiddle


def filter_channels(late, early, symmetric, tables, first, count, per_step, devices):
    full_rows, width = symmetric.shape[2:]
    group, early_rows = early.shape[:2]
    cols = late.shape[1]

    def whole(array):
        return pl.BlockSpec(array.shape, lambda i: (0,) * array.ndim)

    macs = count * (4 * full_rows * full_rows * width + 4 * full_rows * cols * width)
    made = pl.pallas_call(
        functools.partial(filter_kernel, first, devices, 1.0 / (full_rows * cols)),
        grid=(count // per_step,),
        in_specs=[
            whole(late),
            pl.BlockSpec((per_step, early_rows, cols), lambda i: (first // per_step + i, 0, 0)),
            pl.BlockSpec(
                (per_step, 2, full_rows, width), lambda i: (first // per_step + i, 0, 0, 0)
            ),
        ]
        + [whole(table) for table in tables],
        out_specs=pl.BlockSpec((full_rows * count, cols), lambda i: (0, 0)),
        out_shape=jax.ShapeDtypeStruct((full_rows * count, cols), jnp.bfloat16),
        scratch_shapes=[
            pltpu.VMEM((cols // 128, late.shape[0], 128), jnp.float32),
            pltpu.VMEM((cols // 128, full_rows * count, 128), jnp.float32),
        ],
        compiler_params=pltpu.CompilerParams(vmem_limit_bytes=VMEM_BYTES),
        cost_estimate=pl.CostEstimate(
            flops=2 * macs, bytes_accessed=count * full_rows * cols * 8, transcendentals=0
        ),
        name="spectral_filter",
    )(late, early, symmetric, *tables)
    return made.reshape(devices, full_rows // devices * count, cols)


def residual_kernel(count, place_ref, kept_ref, other_ref, feat_ref, *refs):
    out_ref, held = refs[-2:]
    groups, span, cols = kept_ref.shape
    rows = held.shape[1] // count
    own = pl.multiple_of(place_ref[0] * span, 8)
    far = pl.multiple_of((1 - place_ref[0]) * span, 8)
    for g in range(groups):
        to_lane_tiles(held, pl.ds(own, span), kept_ref[g].astype(jnp.float32))
        to_lane_tiles(held, pl.ds(far, span), other_ref[g].astype(jnp.float32))
        for k in range(count):
            filtered = from_lane_tiles(held, pl.ds(k, rows, stride=count))
            out_ref[g, k] = (feat_ref[g, k].astype(jnp.float32) + filtered).astype(jnp.bfloat16)


def add_residual(place, returned, other, features, previous, first, count):
    halves, span, cols = other.shape
    group, rows = features.shape[1:3]
    groups = 4 if halves % 4 == 0 else 1
    steps = halves // groups
    operands = [returned, other, features]
    in_specs = [
        pl.BlockSpec((groups, span, cols), lambda i, place: (place[0] * steps + i, 0, 0)),
        pl.BlockSpec((groups, span, cols), lambda i, place: (i, 0, 0)),
        pl.BlockSpec(
            (groups, count, rows, cols),
            lambda i, place: (i, first // count, 0, 0),
        ),
    ]
    aliases = {}
    if previous is not None:
        operands.append(previous)
        in_specs.append(pl.BlockSpec(memory_space=pl.ANY))
        aliases = {4: 0}
    return pl.pallas_call(
        functools.partial(residual_kernel, count),
        grid_spec=pltpu.PrefetchScalarGridSpec(
            num_scalar_prefetch=1,
            grid=(steps,),
            in_specs=in_specs,
            out_specs=in_specs[2],
            scratch_shapes=[pltpu.VMEM((cols // 128, rows * count, 128), jnp.float32)],
        ),
        out_shape=jax.ShapeDtypeStruct(features.shape, jnp.bfloat16),
        input_output_aliases=aliases,
        compiler_params=pltpu.CompilerParams(vmem_limit_bytes=VMEM_BYTES),
        cost_estimate=pl.CostEstimate(
            flops=halves * count * rows * cols,
            bytes_accessed=halves * count * rows * cols * 8,
            transcendentals=0,
        ),
        name="residual",
    )(place, *operands)


def swap(block):
    return lax.ppermute(block, "section", [(0, 1), (1, 0)])


def local(
    aerial_patch_grid,
    patch_conv_weight,
    patch_bias,
    merging_conv_weight,
    merge_bias,
    down_weight,
    down_bias,
    norm_gain,
    spectral_filter,
):
    tile_rows, field_cols, depth = aerial_patch_grid.shape
    channels = down_weight.shape[3]
    tile_channels = spectral_filter.shape[0]
    full_rows = spectral_filter.shape[2]
    sections = lax.axis_size("section")
    devices = sections * lax.axis_size("tile")
    rows = tile_rows // 2
    suits = (
        sections == 2
        and tile_rows % 8 == 0
        and tile_rows >= 16
        and field_cols % 128 == 0
        and full_rows % (128 * RADIX) == 0
        and rows % RADIX == 0
        and devices % 8 == 0
        and tile_channels % 8 == 0
    )
    arguments = (
        aerial_patch_grid,
        patch_conv_weight,
        patch_bias,
        merging_conv_weight,
        merge_bias,
        down_weight,
        down_bias,
        norm_gain,
        spectral_filter,
    )
    if not suits:
        return general_local(*arguments)
    section = lax.axis_index("section")
    group = tile_channels // 2
    half_channels = channels // 2
    width = -(-(field_cols // 2 + 1) // 128) * 128

    arriving = from_behind(lower_half(aerial_patch_grid[-1]), "tile", 1)
    sources = weight_sources(*arguments[1:8])
    pairs = rows // 2
    early = max(pairs // 3, 1)
    late = pairs - early
    normed_early, feat_early = stem(
        "first", aerial_patch_grid, sources, late, early, devices
    )
    normed_early, arriving = lax.optimization_barrier((normed_early, arriving))
    normed_late, feat_late = stem(
        "last", aerial_patch_grid, sources, 0, late, devices, (arriving,)
    )
    spread = [
        lax.all_to_all(normed, DEVICES, split_axis=0, concat_axis=0, tiled=True).reshape(
            -1, field_cols
        )
        for normed in (normed_early, normed_late)
    ]
    early_fields = repack(spread[0], group, devices)
    late_fields = spread[1]
    features = jnp.concatenate([feat_late, feat_early], axis=0)

    channel_place = jnp.reshape(section * group, (1,)).astype(jnp.int32)
    symmetric = symmetric_filter(spectral_filter, channel_place, group, width)
    tables = filter_tables(full_rows, field_cols, width, devices)

    own = lax.dynamic_slice_in_dim(features, section * half_channels, half_channels, 1)
    sent = lax.dynamic_slice_in_dim(features, (1 - section) * half_channels, half_channels, 1)
    arrived = swap(sent)
    low = jnp.where(section == 0, own, arrived)
    high = jnp.where(section == 0, arrived, own)
    residual = jnp.transpose(jnp.concatenate([low, high], axis=0), (1, 0, 2))
    residual = residual.reshape(half_channels // group, group, tile_rows, field_cols)
    late_fields, residual = lax.optimization_barrier((late_fields, residual))

    section_place = jnp.reshape(section, (1,)).astype(jnp.int32)
    halves = devices // 2
    output = None
    rest = group - 2
    per_step = 5 if rest % 5 == 0 else 2
    for first, count, per_step in ((rest, 2, 2), (0, rest, per_step)):
        made = filter_channels(
            late_fields, early_fields, symmetric, tables, first, count, per_step, devices
        )
        returned = lax.all_to_all(made, DEVICES, split_axis=0, concat_axis=0, tiled=True)
        if output is not None:
            returned, output = lax.optimization_barrier((returned, output))
        other = swap(lax.dynamic_slice_in_dim(returned, (1 - section) * halves, halves, 0))
        output = add_residual(section_place, returned, other, residual, output, first, count)
    return output.reshape(half_channels, tile_rows, field_cols)


def solution(mesh):
    return jax.shard_map(
        local,
        mesh=mesh,
        in_specs=(
            P("tile", None, None),
            P(),
            P(),
            P(),
            P(),
            P(),
            P(),
            P(),
            P("tile", None, None, None),
        ),
        out_specs=P("section", "tile", None),
        check_vma=False,
    )
```

```python
import functools
import math

import jax
import jax.numpy as jnp
import numpy as np
from jax import lax
from jax.experimental import pallas as pl
from jax.experimental.pallas import tpu as pltpu
from jax.sharding import PartitionSpec as P

EPSILON = 1e-05


def from_behind(block, axis, distance):
    devices = range(lax.axis_size(axis))
    route = [(i - distance, i) for i in devices if i - distance in devices]
    return lax.ppermute(block, axis, route)


def fourier_tables(length, columns=None):
    indices = jnp.arange(length, dtype=jnp.int32)
    columns = indices if columns is None else jnp.asarray(columns, jnp.int32)
    product = indices[:, None] * columns[None, :] % length
    angles = product.astype(jnp.float32) * (2.0 * math.pi / length)
    return (jnp.cos(angles).astype(jnp.bfloat16), jnp.sin(angles).astype(jnp.bfloat16))


def patch_kernel_matrix(patch_conv_weight):
    identity = jnp.eye(4, dtype=jnp.float32)
    larger = jnp.einsum(
        "baqk,xy,uv->bxauqyvk", patch_conv_weight.astype(jnp.float32), identity, identity
    )
    band_count = patch_conv_weight.shape[0]
    width = patch_conv_weight.shape[3]
    return larger.reshape(band_count * 256, 16 * width).astype(jnp.bfloat16)


def merging_kernel_matrix(merging_conv_weight):
    identity = jnp.eye(2, dtype=jnp.float32)
    larger = jnp.einsum(
        "aqjk,xy,uv->xauqjyvk", merging_conv_weight.astype(jnp.float32), identity, identity
    )
    in_width = merging_conv_weight.shape[2]
    out_width = merging_conv_weight.shape[3]
    return larger.reshape(16 * in_width, 4 * out_width).astype(jnp.bfloat16)


def down_matrices(down_weight):
    nothing = jnp.zeros_like(down_weight[0, 0])
    in_width = down_weight.shape[2]
    out_width = down_weight.shape[3]

    def arrange(entries):
        return jnp.stack(
            [jnp.stack(entries[0], axis=0), jnp.stack(entries[1], axis=0)], axis=0
        ).reshape(4 * in_width, out_width)

    own_taps = arrange(
        [[down_weight[1, 1], down_weight[1, 2]], [down_weight[2, 1], down_weight[2, 2]]]
    )
    upper_taps = arrange([[nothing, nothing], [down_weight[0, 1], down_weight[0, 2]]])
    left_taps = arrange([[nothing, down_weight[1, 0]], [nothing, down_weight[2, 0]]])
    corner_taps = arrange([[nothing, nothing], [nothing, down_weight[0, 0]]])
    return (own_taps, upper_taps, left_taps, corner_taps)


def stem_layers(aerial_patch_grid, patch_conv_weight, patch_bias, merging_conv_weight, merge_bias):
    initial_layer = jnp.einsum(
        "zji,if->zjf",
        aerial_patch_grid,
        patch_kernel_matrix(patch_conv_weight),
        preferred_element_type=jnp.float32,
    )
    initial_layer = jax.nn.gelu(initial_layer + jnp.tile(patch_bias, 16), approximate=True).astype(
        jnp.bfloat16
    )
    layer_two = jnp.einsum(
        "zji,if->zjf",
        initial_layer,
        merging_kernel_matrix(merging_conv_weight),
        preferred_element_type=jnp.float32,
    )
    return jax.nn.gelu(layer_two + jnp.tile(merge_bias, 4), approximate=True).astype(jnp.bfloat16)


def rim_above(extended):
    return from_behind(extended[-1:], "tile", 1)


def down_conv(upper_rim, extended, down_weight, down_bias):
    stacked = jnp.concatenate([upper_rim, extended], axis=0)
    own_taps, upper_taps, left_taps, corner_taps = down_matrices(down_weight)
    summed = jnp.einsum(
        "rwk,kc->crw", stacked[1:, 1:], own_taps, preferred_element_type=jnp.float32
    )
    summed = summed + jnp.einsum(
        "rwk,kc->crw", stacked[:-1, 1:], upper_taps, preferred_element_type=jnp.float32
    )
    summed = summed + jnp.einsum(
        "rwk,kc->crw", stacked[1:, :-1], left_taps, preferred_element_type=jnp.float32
    )
    summed = summed + jnp.einsum(
        "rwk,kc->crw", stacked[:-1, :-1], corner_taps, preferred_element_type=jnp.float32
    )
    return (summed + down_bias[:, None, None]).astype(jnp.bfloat16)


def layer_norm(features, norm_gain):
    values = features.astype(jnp.float32)
    mean_value = jnp.mean(values, axis=0, keepdims=True)
    centered = values - mean_value
    variance = jnp.mean(centered * centered, axis=0, keepdims=True)
    return (norm_gain[:, None, None] * centered * lax.rsqrt(variance + EPSILON)).astype(
        jnp.bfloat16
    )


def filter_columns(row_spectrum, kernel, forward_h, inverse_h):
    spectrum = jnp.einsum(
        "puqh,chqw->cpuw", forward_h, row_spectrum, preferred_element_type=jnp.float32
    ).astype(jnp.bfloat16)
    spec_real = spectrum[:, 0].astype(jnp.float32)
    spec_imag = spectrum[:, 1].astype(jnp.float32)
    filter_real = kernel[:, 0].astype(jnp.float32)
    filter_imag = kernel[:, 1].astype(jnp.float32)
    weighted = jnp.stack(
        [
            filter_real * spec_real - filter_imag * spec_imag,
            filter_real * spec_imag + filter_imag * spec_real,
        ],
        axis=1,
    ).astype(jnp.bfloat16)
    return jnp.einsum(
        "qhpu,cpuw->chqw", inverse_h, weighted, preferred_element_type=jnp.float32
    ).astype(jnp.bfloat16)


def general_local(
    aerial_patch_grid,
    patch_conv_weight,
    patch_bias,
    merging_conv_weight,
    merge_bias,
    down_weight,
    down_bias,
    norm_gain,
    spectral_filter,
):
    section_index = lax.axis_index("section")
    first_section = section_index == 0
    field_cols = aerial_patch_grid.shape[1]
    channels = down_weight.shape[3]
    group_width = spectral_filter.shape[0]
    full_rows = spectral_filter.shape[2]
    half_channels = channels // 2
    cell_half = field_cols // 2
    image_part = lax.dynamic_slice_in_dim(
        aerial_patch_grid, section_index * cell_half, cell_half, 1
    )
    layer_two = stem_layers(
        image_part, patch_conv_weight, patch_bias, merging_conv_weight, merge_bias
    )
    left_column = from_behind(layer_two[:, -1:], "section", 1)
    extended = jnp.concatenate([left_column, layer_two], axis=1)
    upper_rim = rim_above(extended)
    feature_half = down_conv(upper_rim, extended, down_weight, down_bias)
    features = lax.all_gather(feature_half, "section", axis=2, tiled=True)
    normed = layer_norm(features, norm_gain)
    cos_h, sin_h = fourier_tables(full_rows)
    cos_w, sin_w = fourier_tables(field_cols)
    forward_table = jnp.stack([cos_w, -sin_w], axis=1)
    forward_h = jnp.stack(
        [jnp.stack([cos_h, sin_h], axis=1), jnp.stack([-sin_h, cos_h], axis=1)], axis=0
    )
    inverse_h = jnp.stack(
        [jnp.stack([cos_h, -sin_h], axis=1), jnp.stack([sin_h, cos_h], axis=1)], axis=0
    )
    inverse_table = jnp.stack([cos_w, -sin_w], axis=0)
    norm_scale = 1.0 / (full_rows * field_cols)
    fields = lax.all_to_all(normed, "tile", split_axis=0, concat_axis=1, tiled=True)

    def whole_filter():
        frequency_rows = jnp.einsum(
            "chx,xqw->chqw", fields, forward_table, preferred_element_type=jnp.float32
        ).astype(jnp.bfloat16)
        back_rows = filter_columns(frequency_rows, spectral_filter, forward_h, inverse_h)
        result = jnp.einsum(
            "chqw,qwv->chv", back_rows, inverse_table, preferred_element_type=jnp.float32
        )
        return (result * norm_scale).astype(jnp.bfloat16)

    def empty_fields():
        return jnp.zeros((group_width, full_rows, field_cols), jnp.bfloat16)

    filtered_fields = lax.cond(first_section, empty_fields, whole_filter)
    rows_back = lax.all_to_all(filtered_fields, "tile", split_axis=1, concat_axis=0, tiled=True)
    returned = from_behind(rows_back[:half_channels], "section", -1)
    filtered = jnp.where(first_section, returned, rows_back[half_channels:])
    own_part = lax.dynamic_slice_in_dim(features, section_index * half_channels, half_channels, 0)
    return (own_part.astype(jnp.float32) + filtered.astype(jnp.float32)).astype(jnp.bfloat16)


DEVICES = ("tile", "section")
VMEM_BYTES = 60 * 1024 * 1024
GELU_LINEAR = 2.0 * math.sqrt(2.0 / math.pi)
GELU_CUBIC = 4.0 * 0.044715 * GELU_LINEAR
ONES = (64, 128, 64)
TAPS = ((1, 1), (1, 2), (2, 1), (2, 2), (1, 0), (2, 0), (0, 1), (0, 2), (0, 0))


def bias_rows(bias, count):
    high = bias.astype(jnp.bfloat16)
    rest = bias - high.astype(jnp.float32)
    middle = rest.astype(jnp.bfloat16)
    low = (rest - middle.astype(jnp.float32)).astype(jnp.bfloat16)
    shape = (count, bias.shape[1])
    row = lax.broadcasted_iota(jnp.int32, shape, 0)
    rows = jnp.zeros(shape, jnp.float32)
    for k, part in enumerate((high, middle, low)):
        rows = jnp.where(row == k, jnp.broadcast_to(part.astype(jnp.float32), shape), rows)
    return rows.astype(jnp.bfloat16)


def build_weights(sources, targets):
    patch_ref, patch_bias_ref, merge_ref, merge_bias_ref, down_ref, down_bias_ref, gain_ref = sources
    w1_ref, w2_ref, w3_ref, column_ref = targets

    def exact(a, b):
        return jnp.dot(
            a.astype(jnp.bfloat16), b.astype(jnp.bfloat16), preferred_element_type=jnp.float32
        )

    taps, width = patch_ref.shape
    row = lax.broadcasted_iota(jnp.int32, (4 * taps, taps), 0)
    col = lax.broadcasted_iota(jnp.int32, (4 * taps, taps), 1)
    pick = jnp.where(row // 16 * 4 + row % 4 == col, 1.0, 0.0)
    row = lax.broadcasted_iota(jnp.int32, (width, 4 * width), 0)
    col = lax.broadcasted_iota(jnp.int32, (width, 4 * width), 1)
    repeat = jnp.where(col % width == row, 1.0, 0.0)
    spread = exact(pick, exact(patch_ref[...], repeat))
    row = lax.broadcasted_iota(jnp.int32, spread.shape, 0)
    col = lax.broadcasted_iota(jnp.int32, spread.shape, 1)
    spread = jnp.where(row // 4 % 4 == col // width, 0.5 * spread, 0.0).astype(jnp.bfloat16)
    bias = jnp.broadcast_to(0.5 * patch_bias_ref[...][None], (8, width))
    tiled = jnp.zeros((8, 4 * width), jnp.float32)
    for _ in range(3):
        part = bias.astype(jnp.bfloat16).astype(jnp.float32)
        tiled = tiled + exact(part, repeat)
        bias = bias - part
    first = jnp.concatenate([spread, bias_rows(tiled[:1], ONES[0])], axis=0)
    w1_ref[...] = first.T
    half = (merge_ref[...].astype(jnp.float32) * 0.5).astype(jnp.bfloat16)
    second = jnp.concatenate([half, bias_rows(0.5 * merge_bias_ref[...][None], ONES[1])], axis=0)
    w2_ref[...] = second.T
    third = [down_ref[3 * a + q] for a, q in TAPS]
    third = jnp.concatenate(third + [bias_rows(down_bias_ref[...][None], ONES[2])], axis=0)
    w3_ref[...] = third.T
    column_ref[...] = jnp.broadcast_to(gain_ref[...][None], (128, gain_ref.shape[0])).T


def weight_sources(
    patch_conv_weight, patch_bias, merging_conv_weight, merge_bias, down_weight, down_bias,
    norm_gain,
):
    width = patch_conv_weight.shape[3]
    merged = merging_conv_weight.shape[3]
    return [
        patch_conv_weight.reshape(-1, width),
        patch_bias,
        merging_conv_weight.reshape(-1, merged),
        merge_bias,
        down_weight.reshape(-1, merged, down_weight.shape[3]),
        down_bias,
        norm_gain,
    ]


def weight_shapes(sources):
    taps, width = sources[0].shape
    merged, channels = sources[4].shape[1:]
    return [
        jax.ShapeDtypeStruct((4 * width, 4 * taps + ONES[0]), jnp.bfloat16),
        jax.ShapeDtypeStruct((merged, 4 * width + ONES[1]), jnp.bfloat16),
        jax.ShapeDtypeStruct((channels, 9 * merged + ONES[2]), jnp.bfloat16),
        jax.ShapeDtypeStruct((channels, 128), jnp.float32),
    ]


def half_gelu(h):
    return h + h * jnp.tanh(h * (GELU_LINEAR + GELU_CUBIC * (h * h)))


def lower_half(row):
    depth = row.shape[1]
    return jnp.concatenate(
        [row[:, 256 * b + 128 : 256 * b + 256] for b in range(depth // 256)], axis=1
    )


def stem_kernel(kind, x_ref, above_ref, *refs):
    sources = refs[:7]
    normed_ref, feat_ref, w1_ref, w2_ref, w3_ref, gain_ref, field = refs[-7:]
    step = pl.program_id(0)
    rows, cols, depth = x_ref.shape
    bands = depth // 256
    channels = w3_ref.shape[0]
    merged = w2_ref.shape[0]
    group = normed_ref.shape[2] // rows
    cells = rows * cols

    @pl.when(step == 0)
    def _():
        build_weights(sources, (w1_ref, w2_ref, w3_ref, gain_ref))

    w1 = w1_ref[...]
    w2 = w2_ref[...]

    def ones(count, n):
        return jnp.where(lax.broadcasted_iota(jnp.int32, (count, n), 0) < 3, 1.0, 0.0).astype(
            jnp.bfloat16
        )

    def layer_one(turned, offsets):
        n = turned.shape[1]
        parts = [turned[o : o + 64] for o in offsets] + [ones(ONES[0], n)]
        h = jnp.dot(w1, jnp.concatenate(parts, axis=0), preferred_element_type=jnp.float32)
        return half_gelu(h).astype(jnp.bfloat16)

    def layer_two(upper, lower, y):
        n = upper.shape[1]
        span = slice(2 * y * (w1.shape[0] // 4), 2 * (y + 1) * (w1.shape[0] // 4))
        stacked = jnp.concatenate([upper[span], lower[span], ones(ONES[1], n)], axis=0)
        return half_gelu(jnp.dot(w2, stacked, preferred_element_type=jnp.float32))

    def shifted(values):
        lanes = lax.broadcasted_iota(jnp.int32, values.shape, 1)
        moved = pltpu.roll(values, 1, 1)
        return jnp.where(lax.rem(lanes, cols) == 0, 0.0, moved)

    def put(block, lanes, values):
        field[block * merged : (block + 1) * merged, lanes] = values.astype(jnp.bfloat16)

    first_row = slice(0, cols)
    last_row = slice(cells - cols, cells)
    later_rows = slice(cols, cells)
    earlier_rows = slice(0, cells - cols)

    @pl.when(step == 0)
    def _():
        field[9 * merged :, :] = ones(ONES[2], cells)
        above = lower_half(above_ref[0])
        keep = 1.0
        if kind == "last":
            lower_section = lax.axis_index("section") > 0
            inside = lower_section | (lax.axis_index("tile") > 0)
            keep = jnp.where(inside, 1.0, 0.0)
            above = jnp.where(lower_section, above, refs[7][...])
        turned = above.T
        upper, lower = (
            layer_one(turned, [128 * b + 64 * a for b in range(bands)]) for a in range(2)
        )
        put(6, first_row, layer_two(upper, lower, 0) * keep)
        right = layer_two(upper, lower, 1) * keep
        put(7, first_row, right)
        put(8, first_row, shifted(right))

    @pl.when(step > 0)
    def _():
        for source, target in ((2, 6), (3, 7), (5, 8)):
            field[target * merged : (target + 1) * merged, first_row] = field[
                source * merged : (source + 1) * merged, last_row
            ]

    turned = x_ref[...].reshape(cells, depth).T
    for x in range(2):
        upper, lower = (
            layer_one(turned, [256 * b + 64 * (2 * x + a) for b in range(bands)])
            for a in range(2)
        )
        left = layer_two(upper, lower, 0)
        right = layer_two(upper, lower, 1)
        put(2 * x, slice(None), left)
        put(2 * x + 1, slice(None), right)
        moved = shifted(right)
        put(4 + x, slice(None), moved)
        if x == 1:
            put(6, later_rows, left[:, earlier_rows])
            put(7, later_rows, right[:, earlier_rows])
            put(8, later_rows, moved[:, earlier_rows])

    features = jnp.dot(w3_ref[...], field[...], preferred_element_type=jnp.float32).astype(
        jnp.bfloat16
    )
    for r in range(rows):
        feat_ref[r] = features[:, r * cols : (r + 1) * cols]
    values = features.astype(jnp.float32)
    centered = values - jnp.mean(values, axis=0, keepdims=True)
    variance = jnp.mean(centered * centered, axis=0, keepdims=True)
    gain = jnp.concatenate([gain_ref[...]] * (cells // 128), axis=1)
    normed = gain * (centered * lax.rsqrt(variance + EPSILON))
    pair = 2 * group
    index = lax.broadcasted_iota(jnp.int32, (pair, cols), 0)
    for t in range(channels // pair):
        one = normed[pair * t : pair * (t + 1), :cols]
        two = normed[pair * t : pair * (t + 1), cols:]
        normed_ref[2 * t, 0] = jnp.where(index < group, one, pltpu.roll(two, group, 0)).astype(
            jnp.bfloat16
        )
        normed_ref[2 * t + 1, 0] = jnp.where(
            index < group, pltpu.roll(one, group, 0), two
        ).astype(jnp.bfloat16)


def stem(kind, image, weights, first, steps, devices, extra=()):
    cols, depth = image.shape[1:]
    rows = 2 * steps
    shapes = weight_shapes(weights)
    channels, third_depth = shapes[2].shape
    merged = shapes[1].shape[0]
    group = channels // devices

    def section_pairs():
        return lax.axis_index("section") * (image.shape[0] // 4)

    def whole(array):
        return pl.BlockSpec(array.shape, lambda i: (0,) * len(array.shape))

    operands = list(weights) + list(extra)
    in_specs = [whole(a) for a in weights]
    out_specs = [
        pl.BlockSpec((devices, 1, 2 * group, cols), lambda i: (0, i, 0, 0)),
        pl.BlockSpec((2, channels, cols), lambda i: (i, 0, 0)),
    ]
    out_shape = [
        jax.ShapeDtypeStruct((devices, steps, 2 * group, cols), jnp.bfloat16),
        jax.ShapeDtypeStruct((rows, channels, cols), jnp.bfloat16),
    ]
    in_specs += [whole(a) for a in extra]
    macs = rows * cols * (16 * 208 * 96 + 4 * 400 * merged + third_depth * channels)
    return pl.pallas_call(
        functools.partial(stem_kernel, kind),
        grid=(steps,),
        in_specs=[
            pl.BlockSpec((2, cols, depth), lambda i: (section_pairs() + first + i, 0, 0)),
            pl.BlockSpec(
                (1, cols, depth),
                lambda i: (jnp.maximum(2 * (section_pairs() + first) - 1, 0), 0, 0),
            ),
        ]
        + in_specs,
        out_specs=out_specs,
        scratch_shapes=[pltpu.VMEM(a.shape, a.dtype) for a in shapes]
        + [pltpu.VMEM((third_depth, 2 * cols), jnp.bfloat16)],
        out_shape=out_shape,
        compiler_params=pltpu.CompilerParams(vmem_limit_bytes=VMEM_BYTES + 3 * 1024 * 1024),
        cost_estimate=pl.CostEstimate(
            flops=4 * macs, bytes_accessed=rows * cols * 3000, transcendentals=0
        ),
        name="stem",
    )(image, image, *operands)


def symmetric_kernel(place_ref, f_ref, turn_w_ref, turn_u_ref, g_ref):
    width = g_ref.shape[3]
    for part in range(2):
        block = f_ref[0, part]
        across = jnp.dot(block, turn_w_ref[...], preferred_element_type=jnp.float32)
        turned = jnp.dot(
            turn_u_ref[...], across.astype(jnp.bfloat16), preferred_element_type=jnp.float32
        )
        own = block[:, :width].astype(jnp.float32)
        both = own + turned if part == 0 else own - turned
        g_ref[0, part] = (0.5 * both).astype(jnp.bfloat16)


def symmetric_filter(spectral_filter, place, group, width):
    full_rows, full_cols = spectral_filter.shape[2:]
    u = jnp.arange(full_rows, dtype=jnp.int32)
    w = jnp.arange(full_cols, dtype=jnp.int32)
    turn_u = ((u[:, None] + u[None, :]) % full_rows == 0).astype(jnp.bfloat16)
    turn_w = ((w[:, None] + w[None, :width]) % full_cols == 0).astype(jnp.bfloat16)
    return pl.pallas_call(
        symmetric_kernel,
        grid_spec=pltpu.PrefetchScalarGridSpec(
            num_scalar_prefetch=1,
            grid=(group,),
            in_specs=[
                pl.BlockSpec(
                    (1, 2, full_rows, full_cols), lambda i, place: (place[0] + i, 0, 0, 0)
                ),
                pl.BlockSpec(turn_w.shape, lambda i, place: (0, 0)),
                pl.BlockSpec(turn_u.shape, lambda i, place: (0, 0)),
            ],
            out_specs=pl.BlockSpec((1, 2, full_rows, width), lambda i, place: (i, 0, 0, 0)),
        ),
        out_shape=jax.ShapeDtypeStruct((group, 2, full_rows, width), jnp.bfloat16),
        compiler_params=pltpu.CompilerParams(vmem_limit_bytes=VMEM_BYTES),
        cost_estimate=pl.CostEstimate(
            flops=8 * group * full_rows * full_cols * width,
            bytes_accessed=group * full_rows * width * 14,
            transcendentals=0,
        ),
        name="symmetric_filter",
    )(place, spectral_filter, turn_w, turn_u)


def to_lane_tiles(target, rows, values):
    for j in range(target.shape[0]):
        target[j, rows, :] = values[:, 128 * j : 128 * (j + 1)]


def from_lane_tiles(source, rows):
    return jnp.concatenate([source[j, rows, :] for j in range(source.shape[0])], axis=1)


RADIX = 3
HALF_ROOT = math.sqrt(3.0) / 2.0


def repack_kernel(devices, early_ref, twiddle_ref, out_ref, turn_ref, held):
    group, length = out_ref.shape[:2]
    turn_ref[...] = twiddle_ref[...]
    rows = length // devices
    to_lane_tiles(held, slice(None), early_ref[...].astype(jnp.float32))
    for k in range(group):
        for r in range(rows):
            values = from_lane_tiles(held, pl.ds(r * group + k, devices, stride=rows * group))
            out_ref[k, r * devices : (r + 1) * devices] = values.astype(jnp.bfloat16)


def repack(early, twiddle, group, devices):
    length, cols = early.shape
    return pl.pallas_call(
        functools.partial(repack_kernel, devices),
        out_shape=[
            jax.ShapeDtypeStruct((group, length // group, cols), jnp.bfloat16),
            jax.ShapeDtypeStruct(twiddle.shape, twiddle.dtype),
        ],
        scratch_shapes=[pltpu.VMEM((cols // 128, length, 128), jnp.float32)],
        compiler_params=pltpu.CompilerParams(vmem_limit_bytes=VMEM_BYTES),
        cost_estimate=pl.CostEstimate(
            flops=length * cols, bytes_accessed=4 * length * cols, transcendentals=0
        ),
        name="repack",
    )(early, twiddle)


def thirds(values, sign):
    (re0, im0), (re1, im1), (re2, im2) = values
    sum_re, sum_im = re1 + re2, im1 + im2
    turn_re, turn_im = HALF_ROOT * sign * (im1 - im2), HALF_ROOT * sign * (re2 - re1)
    rest_re, rest_im = re0 - 0.5 * sum_re, im0 - 0.5 * sum_im
    return (
        (re0 + sum_re, im0 + sum_im),
        (rest_re + turn_re, rest_im + turn_im),
        (rest_re - turn_re, rest_im - turn_im),
    )


def filter_kernel(
    first, devices, norm_scale, late_ref, early_ref, g_ref, row_table_ref, fwd_ref, inv_ref,
    back_ref, twiddle_ref, out_ref, held, made,
):
    step = pl.program_id(0)
    third = fwd_ref.shape[0] // 2
    full_rows = RADIX * third
    width = g_ref.shape[3]
    count = made.shape[1] // full_rows
    per_step = g_ref.shape[0]
    early = early_ref.shape[1] // devices
    late = full_rows // devices - early
    group = held.shape[1] // (late * devices)

    @pl.when(step == 0)
    def _():
        to_lane_tiles(held, slice(None), late_ref[...].astype(jnp.float32))

    def source_rows(k, row):
        if row >= late:
            begin = (row - late) * devices
            return early_ref[k, begin : begin + devices]
        begin = row * group + first + step * per_step + k
        values = from_lane_tiles(held, pl.ds(begin, devices, stride=late * group))
        return values.astype(jnp.bfloat16)

    def twiddles(r):
        cos, sin = twiddle_ref[2 * r - 2], twiddle_ref[2 * r - 1]
        times = per_step * width // 128
        return jnp.concatenate([cos] * times, axis=1), jnp.concatenate([sin] * times, axis=1)

    fields = []
    for k in range(per_step):
        rows = [
            source_rows(k, r + RADIX * q)
            for r in range(RADIX)
            for q in range((late + early) // RADIX)
        ]
        spread = jnp.dot(
            jnp.concatenate(rows, axis=0), row_table_ref[...], preferred_element_type=jnp.float32
        )
        fields.append(spread.astype(jnp.bfloat16))
    parts = []
    for r in range(RADIX):
        span = slice(r * third, (r + 1) * third)
        block = jnp.concatenate(
            [
                jnp.concatenate([f[span, :width], f[span, width:]], axis=0)
                for f in fields
            ],
            axis=1,
        )
        short = jnp.dot(fwd_ref[...], block, preferred_element_type=jnp.float32)
        real, imag = short[:third], short[third:]
        if r > 0:
            cos, sin = twiddles(r)
            real, imag = real * cos + imag * sin, imag * cos - real * sin
        parts.append((real, imag))
    weighted = []
    for r, (real, imag) in enumerate(thirds(parts, 1.0)):
        span = slice(r * third, (r + 1) * third)
        g_real, g_imag = (
            jnp.concatenate([g_ref[k, p, span] for k in range(per_step)], axis=1).astype(
                jnp.float32
            )
            for p in range(2)
        )
        weighted.append((g_real * real - g_imag * imag, g_real * imag + g_imag * real))
    for r, (real, imag) in enumerate(thirds(weighted, -1.0)):
        if r > 0:
            cos, sin = twiddles(r)
            real, imag = real * cos - imag * sin, imag * cos + real * sin
        block = jnp.concatenate([real, imag], axis=0).astype(jnp.bfloat16)
        back = jnp.dot(inv_ref[...], block, preferred_element_type=jnp.float32).astype(
            jnp.bfloat16
        )
        for k in range(per_step):
            lanes = slice(k * width, (k + 1) * width)
            both = jnp.concatenate([back[:third, lanes], back[third:, lanes]], axis=1)
            result = jnp.dot(both, back_ref[...], preferred_element_type=jnp.float32)
            rows = pl.ds(r * count + step * per_step + k, third, stride=RADIX * count)
            to_lane_tiles(made, rows, result * norm_scale)

    @pl.when(step == pl.num_programs(0) - 1)
    def _():
        out_ref[...] = from_lane_tiles(made, slice(None)).astype(jnp.bfloat16)


def filter_tables(full_rows, field_cols, width, devices):
    third = full_rows // RADIX
    per_device = third // devices
    order = (per_device * np.arange(devices)[None, :] + np.arange(per_device)[:, None]).reshape(-1)
    cos_h, sin_h = fourier_tables(third)
    cos_f, sin_f = fourier_tables(third, order.astype(np.int32))
    cos_w, sin_w = fourier_tables(field_cols)
    fwd = jnp.concatenate(
        [jnp.concatenate([cos_f, sin_f], 1), jnp.concatenate([-sin_f, cos_f], 1)], 0
    )
    inv = jnp.concatenate(
        [jnp.concatenate([cos_h, -sin_h], 1), jnp.concatenate([sin_h, cos_h], 1)], 0
    )
    w = jnp.arange(width, dtype=jnp.int32)
    half = field_cols // 2
    valid = (w <= half).astype(jnp.bfloat16)
    times = jnp.where((w == 0) | (w == half), 1.0, 2.0).astype(jnp.bfloat16) * valid
    row_table = jnp.concatenate([cos_w[:, :width] * valid, -sin_w[:, :width] * valid], 1)
    back_table = jnp.concatenate(
        [cos_w[:width] * times[:, None], -sin_w[:width] * times[:, None]], 0
    )
    turns = np.arange(1, RADIX)[:, None] * np.arange(third)[None, :]
    angles = turns * (2.0 * math.pi / full_rows)
    twiddle = np.stack([np.cos(angles), np.sin(angles)], axis=1).reshape(-1, third, 1)
    twiddle = np.broadcast_to(twiddle.astype(np.float32), (2 * RADIX - 2, third, 128))
    twiddle = jnp.asarray(twiddle)
    return row_table, fwd, inv, back_table, twiddle


def filter_channels(late, early, symmetric, tables, first, count, per_step, devices):
    full_rows, width = symmetric.shape[2:]
    group, early_rows = early.shape[:2]
    cols = late.shape[1]

    def whole(array):
        return pl.BlockSpec(array.shape, lambda i: (0,) * array.ndim)

    macs = count * (4 * full_rows * full_rows * width + 4 * full_rows * cols * width)
    made = pl.pallas_call(
        functools.partial(filter_kernel, first, devices, 1.0 / (full_rows * cols)),
        grid=(count // per_step,),
        in_specs=[
            whole(late),
            pl.BlockSpec((per_step, early_rows, cols), lambda i: (first // per_step + i, 0, 0)),
            pl.BlockSpec(
                (per_step, 2, full_rows, width), lambda i: (first // per_step + i, 0, 0, 0)
            ),
        ]
        + [whole(table) for table in tables],
        out_specs=pl.BlockSpec((full_rows * count, cols), lambda i: (0, 0)),
        out_shape=jax.ShapeDtypeStruct((full_rows * count, cols), jnp.bfloat16),
        scratch_shapes=[
            pltpu.VMEM((cols // 128, late.shape[0], 128), jnp.float32),
            pltpu.VMEM((cols // 128, full_rows * count, 128), jnp.float32),
        ],
        compiler_params=pltpu.CompilerParams(vmem_limit_bytes=VMEM_BYTES),
        cost_estimate=pl.CostEstimate(
            flops=2 * macs, bytes_accessed=count * full_rows * cols * 8, transcendentals=0
        ),
        name="spectral_filter",
    )(late, early, symmetric, *tables)
    return made.reshape(devices, full_rows // devices * count, cols)


def residual_kernel(count, place_ref, kept_ref, other_ref, feat_ref, *refs):
    out_ref, held = refs[-2:]
    groups, span, cols = kept_ref.shape
    rows = held.shape[1] // count
    own = pl.multiple_of(place_ref[0] * span, 8)
    far = pl.multiple_of((1 - place_ref[0]) * span, 8)
    for g in range(groups):
        to_lane_tiles(held, pl.ds(own, span), kept_ref[g].astype(jnp.float32))
        to_lane_tiles(held, pl.ds(far, span), other_ref[g].astype(jnp.float32))
        for k in range(count):
            filtered = from_lane_tiles(held, pl.ds(k, rows, stride=count))
            out_ref[g, k] = (feat_ref[g, k].astype(jnp.float32) + filtered).astype(jnp.bfloat16)


def add_residual(place, returned, other, features, previous, first, count):
    halves, span, cols = other.shape
    group, rows = features.shape[1:3]
    groups = 8 if halves % 8 == 0 else 1
    steps = halves // groups
    operands = [returned, other, features]
    in_specs = [
        pl.BlockSpec((groups, span, cols), lambda i, place: (place[0] * steps + i, 0, 0)),
        pl.BlockSpec((groups, span, cols), lambda i, place: (i, 0, 0)),
        pl.BlockSpec(
            (groups, count, rows, cols),
            lambda i, place: (i, first // count, 0, 0),
        ),
    ]
    aliases = {}
    if previous is not None:
        operands.append(previous)
        in_specs.append(pl.BlockSpec(memory_space=pl.ANY))
        aliases = {4: 0}
    return pl.pallas_call(
        functools.partial(residual_kernel, count),
        grid_spec=pltpu.PrefetchScalarGridSpec(
            num_scalar_prefetch=1,
            grid=(steps,),
            in_specs=in_specs,
            out_specs=in_specs[2],
            scratch_shapes=[pltpu.VMEM((cols // 128, rows * count, 128), jnp.float32)],
        ),
        out_shape=jax.ShapeDtypeStruct(features.shape, jnp.bfloat16),
        input_output_aliases=aliases,
        compiler_params=pltpu.CompilerParams(vmem_limit_bytes=VMEM_BYTES),
        cost_estimate=pl.CostEstimate(
            flops=halves * count * rows * cols,
            bytes_accessed=halves * count * rows * cols * 8,
            transcendentals=0,
        ),
        name="residual",
    )(place, *operands)


def swap(block):
    return lax.ppermute(block, "section", [(0, 1), (1, 0)])


def local(
    aerial_patch_grid,
    patch_conv_weight,
    patch_bias,
    merging_conv_weight,
    merge_bias,
    down_weight,
    down_bias,
    norm_gain,
    spectral_filter,
):
    tile_rows, field_cols, depth = aerial_patch_grid.shape
    channels = down_weight.shape[3]
    tile_channels = spectral_filter.shape[0]
    full_rows = spectral_filter.shape[2]
    sections = lax.axis_size("section")
    devices = sections * lax.axis_size("tile")
    rows = tile_rows // 2
    suits = (
        sections == 2
        and tile_rows % 8 == 0
        and tile_rows >= 16
        and field_cols % 128 == 0
        and full_rows % (128 * RADIX) == 0
        and rows % RADIX == 0
        and devices % 8 == 0
        and tile_channels % 8 == 0
    )
    arguments = (
        aerial_patch_grid,
        patch_conv_weight,
        patch_bias,
        merging_conv_weight,
        merge_bias,
        down_weight,
        down_bias,
        norm_gain,
        spectral_filter,
    )
    if not suits:
        return general_local(*arguments)
    section = lax.axis_index("section")
    group = tile_channels // 2
    half_channels = channels // 2
    width = -(-(field_cols // 2 + 1) // 128) * 128

    arriving = lax.ppermute(
        lower_half(aerial_patch_grid[-1]),
        ("section", "tile"),
        [(i, i + 1) for i in range(lax.axis_size("tile") - 1)],
    )
    sources = weight_sources(*arguments[1:8])
    pairs = rows // 2
    early = max(pairs // 3, 1)
    late = pairs - early
    normed_early, feat_early = stem(
        "first", aerial_patch_grid, sources, late, early, devices
    )
    normed_early, arriving = lax.optimization_barrier((normed_early, arriving))
    normed_late, feat_late = stem(
        "last", aerial_patch_grid, sources, 0, late, devices, (arriving,)
    )
    spread = [
        lax.all_to_all(normed, DEVICES, split_axis=0, concat_axis=0, tiled=True).reshape(
            -1, field_cols
        )
        for normed in (normed_early, normed_late)
    ]
    late_fields = spread[1]
    features = jnp.concatenate([feat_late, feat_early], axis=0)

    channel_place = jnp.reshape(section * group, (1,)).astype(jnp.int32)
    symmetric = symmetric_filter(spectral_filter, channel_place, group, width)
    *tables, twiddle = filter_tables(full_rows, field_cols, width, devices)
    early_fields, twiddle = repack(spread[0], twiddle, group, devices)
    tables.append(twiddle)

    own = lax.dynamic_slice_in_dim(features, section * half_channels, half_channels, 1)
    sent = lax.dynamic_slice_in_dim(features, (1 - section) * half_channels, half_channels, 1)
    arrived = swap(sent)
    low = jnp.where(section == 0, own, arrived)
    high = jnp.where(section == 0, arrived, own)
    residual = jnp.transpose(jnp.concatenate([low, high], axis=0), (1, 0, 2))
    residual = residual.reshape(half_channels // group, group, tile_rows, field_cols)
    late_fields, residual = lax.optimization_barrier((late_fields, residual))

    section_place = jnp.reshape(section, (1,)).astype(jnp.int32)
    halves = devices // 2
    output = None
    rest = group - 2
    per_step = 5 if rest % 5 == 0 else 2
    for first, count, per_step in ((rest, 2, 2), (0, rest, per_step)):
        made = filter_channels(
            late_fields, early_fields, symmetric, tables, first, count, per_step, devices
        )
        returned = lax.all_to_all(made, DEVICES, split_axis=0, concat_axis=0, tiled=True)
        if output is not None:
            returned, output = lax.optimization_barrier((returned, output))
        other = swap(lax.dynamic_slice_in_dim(returned, (1 - section) * halves, halves, 0))
        output = add_residual(section_place, returned, other, residual, output, first, count)
    return output.reshape(half_channels, tile_rows, field_cols)


def solution(mesh):
    return jax.shard_map(
        local,
        mesh=mesh,
        in_specs=(
            P("tile", None, None),
            P(),
            P(),
            P(),
            P(),
            P(),
            P(),
            P(),
            P("tile", None, None, None),
        ),
        out_specs=P("section", "tile", None),
        check_vma=False,
    )
```

```python
import functools
import math

import jax
import jax.numpy as jnp
import numpy as np
from jax import lax
from jax.experimental import pallas as pl
from jax.experimental.pallas import tpu as pltpu
from jax.sharding import PartitionSpec as P

EPSILON = 1e-05


def from_behind(block, axis, distance):
    devices = range(lax.axis_size(axis))
    route = [(i - distance, i) for i in devices if i - distance in devices]
    return lax.ppermute(block, axis, route)


def fourier_tables(length, columns=None):
    indices = jnp.arange(length, dtype=jnp.int32)
    columns = indices if columns is None else jnp.asarray(columns, jnp.int32)
    product = indices[:, None] * columns[None, :] % length
    angles = product.astype(jnp.float32) * (2.0 * math.pi / length)
    return (jnp.cos(angles).astype(jnp.bfloat16), jnp.sin(angles).astype(jnp.bfloat16))


def patch_kernel_matrix(patch_conv_weight):
    identity = jnp.eye(4, dtype=jnp.float32)
    larger = jnp.einsum(
        "baqk,xy,uv->bxauqyvk", patch_conv_weight.astype(jnp.float32), identity, identity
    )
    band_count = patch_conv_weight.shape[0]
    width = patch_conv_weight.shape[3]
    return larger.reshape(band_count * 256, 16 * width).astype(jnp.bfloat16)


def merging_kernel_matrix(merging_conv_weight):
    identity = jnp.eye(2, dtype=jnp.float32)
    larger = jnp.einsum(
        "aqjk,xy,uv->xauqjyvk", merging_conv_weight.astype(jnp.float32), identity, identity
    )
    in_width = merging_conv_weight.shape[2]
    out_width = merging_conv_weight.shape[3]
    return larger.reshape(16 * in_width, 4 * out_width).astype(jnp.bfloat16)


def down_matrices(down_weight):
    nothing = jnp.zeros_like(down_weight[0, 0])
    in_width = down_weight.shape[2]
    out_width = down_weight.shape[3]

    def arrange(entries):
        return jnp.stack(
            [jnp.stack(entries[0], axis=0), jnp.stack(entries[1], axis=0)], axis=0
        ).reshape(4 * in_width, out_width)

    own_taps = arrange(
        [[down_weight[1, 1], down_weight[1, 2]], [down_weight[2, 1], down_weight[2, 2]]]
    )
    upper_taps = arrange([[nothing, nothing], [down_weight[0, 1], down_weight[0, 2]]])
    left_taps = arrange([[nothing, down_weight[1, 0]], [nothing, down_weight[2, 0]]])
    corner_taps = arrange([[nothing, nothing], [nothing, down_weight[0, 0]]])
    return (own_taps, upper_taps, left_taps, corner_taps)


def stem_layers(aerial_patch_grid, patch_conv_weight, patch_bias, merging_conv_weight, merge_bias):
    initial_layer = jnp.einsum(
        "zji,if->zjf",
        aerial_patch_grid,
        patch_kernel_matrix(patch_conv_weight),
        preferred_element_type=jnp.float32,
    )
    initial_layer = jax.nn.gelu(initial_layer + jnp.tile(patch_bias, 16), approximate=True).astype(
        jnp.bfloat16
    )
    layer_two = jnp.einsum(
        "zji,if->zjf",
        initial_layer,
        merging_kernel_matrix(merging_conv_weight),
        preferred_element_type=jnp.float32,
    )
    return jax.nn.gelu(layer_two + jnp.tile(merge_bias, 4), approximate=True).astype(jnp.bfloat16)


def rim_above(extended):
    return from_behind(extended[-1:], "tile", 1)


def down_conv(upper_rim, extended, down_weight, down_bias):
    stacked = jnp.concatenate([upper_rim, extended], axis=0)
    own_taps, upper_taps, left_taps, corner_taps = down_matrices(down_weight)
    summed = jnp.einsum(
        "rwk,kc->crw", stacked[1:, 1:], own_taps, preferred_element_type=jnp.float32
    )
    summed = summed + jnp.einsum(
        "rwk,kc->crw", stacked[:-1, 1:], upper_taps, preferred_element_type=jnp.float32
    )
    summed = summed + jnp.einsum(
        "rwk,kc->crw", stacked[1:, :-1], left_taps, preferred_element_type=jnp.float32
    )
    summed = summed + jnp.einsum(
        "rwk,kc->crw", stacked[:-1, :-1], corner_taps, preferred_element_type=jnp.float32
    )
    return (summed + down_bias[:, None, None]).astype(jnp.bfloat16)


def layer_norm(features, norm_gain):
    values = features.astype(jnp.float32)
    mean_value = jnp.mean(values, axis=0, keepdims=True)
    centered = values - mean_value
    variance = jnp.mean(centered * centered, axis=0, keepdims=True)
    return (norm_gain[:, None, None] * centered * lax.rsqrt(variance + EPSILON)).astype(
        jnp.bfloat16
    )


def filter_columns(row_spectrum, kernel, forward_h, inverse_h):
    spectrum = jnp.einsum(
        "puqh,chqw->cpuw", forward_h, row_spectrum, preferred_element_type=jnp.float32
    ).astype(jnp.bfloat16)
    spec_real = spectrum[:, 0].astype(jnp.float32)
    spec_imag = spectrum[:, 1].astype(jnp.float32)
    filter_real = kernel[:, 0].astype(jnp.float32)
    filter_imag = kernel[:, 1].astype(jnp.float32)
    weighted = jnp.stack(
        [
            filter_real * spec_real - filter_imag * spec_imag,
            filter_real * spec_imag + filter_imag * spec_real,
        ],
        axis=1,
    ).astype(jnp.bfloat16)
    return jnp.einsum(
        "qhpu,cpuw->chqw", inverse_h, weighted, preferred_element_type=jnp.float32
    ).astype(jnp.bfloat16)


def general_local(
    aerial_patch_grid,
    patch_conv_weight,
    patch_bias,
    merging_conv_weight,
    merge_bias,
    down_weight,
    down_bias,
    norm_gain,
    spectral_filter,
):
    section_index = lax.axis_index("section")
    first_section = section_index == 0
    field_cols = aerial_patch_grid.shape[1]
    channels = down_weight.shape[3]
    group_width = spectral_filter.shape[0]
    full_rows = spectral_filter.shape[2]
    half_channels = channels // 2
    cell_half = field_cols // 2
    image_part = lax.dynamic_slice_in_dim(
        aerial_patch_grid, section_index * cell_half, cell_half, 1
    )
    layer_two = stem_layers(
        image_part, patch_conv_weight, patch_bias, merging_conv_weight, merge_bias
    )
    left_column = from_behind(layer_two[:, -1:], "section", 1)
    extended = jnp.concatenate([left_column, layer_two], axis=1)
    upper_rim = rim_above(extended)
    feature_half = down_conv(upper_rim, extended, down_weight, down_bias)
    features = lax.all_gather(feature_half, "section", axis=2, tiled=True)
    normed = layer_norm(features, norm_gain)
    cos_h, sin_h = fourier_tables(full_rows)
    cos_w, sin_w = fourier_tables(field_cols)
    forward_table = jnp.stack([cos_w, -sin_w], axis=1)
    forward_h = jnp.stack(
        [jnp.stack([cos_h, sin_h], axis=1), jnp.stack([-sin_h, cos_h], axis=1)], axis=0
    )
    inverse_h = jnp.stack(
        [jnp.stack([cos_h, -sin_h], axis=1), jnp.stack([sin_h, cos_h], axis=1)], axis=0
    )
    inverse_table = jnp.stack([cos_w, -sin_w], axis=0)
    norm_scale = 1.0 / (full_rows * field_cols)
    fields = lax.all_to_all(normed, "tile", split_axis=0, concat_axis=1, tiled=True)

    def whole_filter():
        frequency_rows = jnp.einsum(
            "chx,xqw->chqw", fields, forward_table, preferred_element_type=jnp.float32
        ).astype(jnp.bfloat16)
        back_rows = filter_columns(frequency_rows, spectral_filter, forward_h, inverse_h)
        result = jnp.einsum(
            "chqw,qwv->chv", back_rows, inverse_table, preferred_element_type=jnp.float32
        )
        return (result * norm_scale).astype(jnp.bfloat16)

    def empty_fields():
        return jnp.zeros((group_width, full_rows, field_cols), jnp.bfloat16)

    filtered_fields = lax.cond(first_section, empty_fields, whole_filter)
    rows_back = lax.all_to_all(filtered_fields, "tile", split_axis=1, concat_axis=0, tiled=True)
    returned = from_behind(rows_back[:half_channels], "section", -1)
    filtered = jnp.where(first_section, returned, rows_back[half_channels:])
    own_part = lax.dynamic_slice_in_dim(features, section_index * half_channels, half_channels, 0)
    return (own_part.astype(jnp.float32) + filtered.astype(jnp.float32)).astype(jnp.bfloat16)


DEVICES = ("tile", "section")
VMEM_BYTES = 60 * 1024 * 1024
GELU_LINEAR = 2.0 * math.sqrt(2.0 / math.pi)
GELU_CUBIC = 4.0 * 0.044715 * GELU_LINEAR
ONES = (64, 128, 64)
TAPS = ((1, 1), (1, 2), (2, 1), (2, 2), (1, 0), (2, 0), (0, 1), (0, 2), (0, 0))


def bias_rows(bias, count):
    high = bias.astype(jnp.bfloat16)
    rest = bias - high.astype(jnp.float32)
    middle = rest.astype(jnp.bfloat16)
    low = (rest - middle.astype(jnp.float32)).astype(jnp.bfloat16)
    shape = (count, bias.shape[1])
    row = lax.broadcasted_iota(jnp.int32, shape, 0)
    rows = jnp.zeros(shape, jnp.float32)
    for k, part in enumerate((high, middle, low)):
        rows = jnp.where(row == k, jnp.broadcast_to(part.astype(jnp.float32), shape), rows)
    return rows.astype(jnp.bfloat16)


def build_weights(sources, targets):
    patch_ref, patch_bias_ref, merge_ref, merge_bias_ref, down_ref, down_bias_ref, gain_ref = sources
    w1_ref, w2_ref, w3_ref, column_ref = targets

    def exact(a, b):
        return jnp.dot(
            a.astype(jnp.bfloat16), b.astype(jnp.bfloat16), preferred_element_type=jnp.float32
        )

    taps, width = patch_ref.shape
    row = lax.broadcasted_iota(jnp.int32, (4 * taps, taps), 0)
    col = lax.broadcasted_iota(jnp.int32, (4 * taps, taps), 1)
    pick = jnp.where(row // 16 * 4 + row % 4 == col, 1.0, 0.0)
    row = lax.broadcasted_iota(jnp.int32, (width, 4 * width), 0)
    col = lax.broadcasted_iota(jnp.int32, (width, 4 * width), 1)
    repeat = jnp.where(col % width == row, 1.0, 0.0)
    spread = exact(pick, exact(patch_ref[...], repeat))
    row = lax.broadcasted_iota(jnp.int32, spread.shape, 0)
    col = lax.broadcasted_iota(jnp.int32, spread.shape, 1)
    spread = jnp.where(row // 4 % 4 == col // width, 0.5 * spread, 0.0).astype(jnp.bfloat16)
    bias = jnp.broadcast_to(0.5 * patch_bias_ref[...][None], (8, width))
    tiled = jnp.zeros((8, 4 * width), jnp.float32)
    for _ in range(3):
        part = bias.astype(jnp.bfloat16).astype(jnp.float32)
        tiled = tiled + exact(part, repeat)
        bias = bias - part
    first = jnp.concatenate([spread, bias_rows(tiled[:1], ONES[0])], axis=0)
    w1_ref[...] = first.T
    half = (merge_ref[...].astype(jnp.float32) * 0.5).astype(jnp.bfloat16)
    second = jnp.concatenate([half, bias_rows(0.5 * merge_bias_ref[...][None], ONES[1])], axis=0)
    w2_ref[...] = second.T
    third = [down_ref[3 * a + q] for a, q in TAPS]
    third = jnp.concatenate(third + [bias_rows(down_bias_ref[...][None], ONES[2])], axis=0)
    w3_ref[...] = third.T
    column_ref[...] = jnp.broadcast_to(gain_ref[...][None], (128, gain_ref.shape[0])).T


def weight_sources(
    patch_conv_weight, patch_bias, merging_conv_weight, merge_bias, down_weight, down_bias,
    norm_gain,
):
    width = patch_conv_weight.shape[3]
    merged = merging_conv_weight.shape[3]
    return [
        patch_conv_weight.reshape(-1, width),
        patch_bias,
        merging_conv_weight.reshape(-1, merged),
        merge_bias,
        down_weight.reshape(-1, merged, down_weight.shape[3]),
        down_bias,
        norm_gain,
    ]


def weight_shapes(sources):
    taps, width = sources[0].shape
    merged, channels = sources[4].shape[1:]
    return [
        jax.ShapeDtypeStruct((4 * width, 4 * taps + ONES[0]), jnp.bfloat16),
        jax.ShapeDtypeStruct((merged, 4 * width + ONES[1]), jnp.bfloat16),
        jax.ShapeDtypeStruct((channels, 9 * merged + ONES[2]), jnp.bfloat16),
        jax.ShapeDtypeStruct((channels, 128), jnp.float32),
    ]


def half_gelu(h):
    return h + h * jnp.tanh(h * (GELU_LINEAR + GELU_CUBIC * (h * h)))


def lower_half(row):
    depth = row.shape[1]
    return jnp.concatenate(
        [row[:, 256 * b + 128 : 256 * b + 256] for b in range(depth // 256)], axis=1
    )


def stem_kernel(kind, x_ref, above_ref, *refs):
    sources = refs[:7]
    normed_ref, feat_ref, w1_ref, w2_ref, w3_ref, gain_ref, field = refs[-7:]
    step = pl.program_id(0)
    rows, cols, depth = x_ref.shape
    bands = depth // 256
    channels = w3_ref.shape[0]
    merged = w2_ref.shape[0]
    group = normed_ref.shape[2] // 2
    cells = rows * cols

    @pl.when(step == 0)
    def _():
        build_weights(sources, (w1_ref, w2_ref, w3_ref, gain_ref))

    w1 = w1_ref[...]
    w2 = w2_ref[...]

    def ones(count, n):
        return jnp.where(lax.broadcasted_iota(jnp.int32, (count, n), 0) < 3, 1.0, 0.0).astype(
            jnp.bfloat16
        )

    def layer_one(turned, offsets):
        n = turned.shape[1]
        parts = [turned[o : o + 64] for o in offsets] + [ones(ONES[0], n)]
        h = jnp.dot(w1, jnp.concatenate(parts, axis=0), preferred_element_type=jnp.float32)
        return half_gelu(h).astype(jnp.bfloat16)

    def layer_two(upper, lower, y):
        n = upper.shape[1]
        span = slice(2 * y * (w1.shape[0] // 4), 2 * (y + 1) * (w1.shape[0] // 4))
        stacked = jnp.concatenate([upper[span], lower[span], ones(ONES[1], n)], axis=0)
        return half_gelu(jnp.dot(w2, stacked, preferred_element_type=jnp.float32))

    def shifted(values):
        lanes = lax.broadcasted_iota(jnp.int32, values.shape, 1)
        moved = pltpu.roll(values, 1, 1)
        return jnp.where(lax.rem(lanes, cols) == 0, 0.0, moved)

    def put(block, lanes, values):
        field[block * merged : (block + 1) * merged, lanes] = values.astype(jnp.bfloat16)

    first_row = slice(0, cols)
    last_row = slice(cells - cols, cells)
    later_rows = slice(cols, cells)
    earlier_rows = slice(0, cells - cols)

    @pl.when(step == 0)
    def _():
        field[9 * merged :, :] = ones(ONES[2], cells)
        above = lower_half(above_ref[0])
        keep = 1.0
        if kind == "last":
            lower_section = lax.axis_index("section") > 0
            inside = lower_section | (lax.axis_index("tile") > 0)
            keep = jnp.where(inside, 1.0, 0.0)
            above = jnp.where(lower_section, above, refs[7][...])
        turned = above.T
        upper, lower = (
            layer_one(turned, [128 * b + 64 * a for b in range(bands)]) for a in range(2)
        )
        put(6, first_row, layer_two(upper, lower, 0) * keep)
        right = layer_two(upper, lower, 1) * keep
        put(7, first_row, right)
        put(8, first_row, shifted(right))

    @pl.when(step > 0)
    def _():
        for source, target in ((2, 6), (3, 7), (5, 8)):
            field[target * merged : (target + 1) * merged, first_row] = field[
                source * merged : (source + 1) * merged, last_row
            ]

    turned = x_ref[...].reshape(cells, depth).T
    for x in range(2):
        upper, lower = (
            layer_one(turned, [256 * b + 64 * (2 * x + a) for b in range(bands)])
            for a in range(2)
        )
        left = layer_two(upper, lower, 0)
        right = layer_two(upper, lower, 1)
        put(2 * x, slice(None), left)
        put(2 * x + 1, slice(None), right)
        moved = shifted(right)
        put(4 + x, slice(None), moved)
        if x == 1:
            put(6, later_rows, left[:, earlier_rows])
            put(7, later_rows, right[:, earlier_rows])
            put(8, later_rows, moved[:, earlier_rows])

    features = jnp.dot(w3_ref[...], field[...], preferred_element_type=jnp.float32).astype(
        jnp.bfloat16
    )
    for r in range(rows):
        feat_ref[r] = features[:, r * cols : (r + 1) * cols]
    values = features.astype(jnp.float32)
    centered = values - jnp.mean(values, axis=0, keepdims=True)
    variance = jnp.mean(centered * centered, axis=0, keepdims=True)
    gain = jnp.concatenate([gain_ref[...]] * (cells // 128), axis=1)
    normed = gain * (centered * lax.rsqrt(variance + EPSILON))
    pair = 2 * group
    index = lax.broadcasted_iota(jnp.int32, (pair, cols), 0)
    for t in range(channels // pair):
        for p in range(rows // 2):
            span = slice(pair * t, pair * (t + 1))
            one = normed[span, 2 * p * cols : (2 * p + 1) * cols]
            two = normed[span, (2 * p + 1) * cols : (2 * p + 2) * cols]
            normed_ref[2 * t, p] = jnp.where(
                index < group, one, pltpu.roll(two, group, 0)
            ).astype(jnp.bfloat16)
            normed_ref[2 * t + 1, p] = jnp.where(
                index < group, pltpu.roll(one, group, 0), two
            ).astype(jnp.bfloat16)


def stem(kind, image, weights, first, pairs, devices, extra=()):
    cols, depth = image.shape[1:]
    rows = 2 * pairs
    per_step = 1
    if kind == "first" and all(n % 2 == 0 for n in (pairs, first, image.shape[0] // 4)):
        per_step = 2
    steps = pairs // per_step
    span = 2 * per_step
    shapes = weight_shapes(weights)
    channels, third_depth = shapes[2].shape
    merged = shapes[1].shape[0]
    group = channels // devices

    def section_pairs():
        return lax.axis_index("section") * (image.shape[0] // 4)

    def whole(array):
        return pl.BlockSpec(array.shape, lambda i: (0,) * len(array.shape))

    operands = list(weights) + list(extra)
    in_specs = [whole(a) for a in weights]
    out_specs = [
        pl.BlockSpec((devices, per_step, 2 * group, cols), lambda i: (0, i, 0, 0)),
        pl.BlockSpec((span, channels, cols), lambda i: (i, 0, 0)),
    ]
    out_shape = [
        jax.ShapeDtypeStruct((devices, pairs, 2 * group, cols), jnp.bfloat16),
        jax.ShapeDtypeStruct((rows, channels, cols), jnp.bfloat16),
    ]
    in_specs += [whole(a) for a in extra]
    macs = rows * cols * (16 * 208 * 96 + 4 * 400 * merged + third_depth * channels)
    return pl.pallas_call(
        functools.partial(stem_kernel, kind),
        grid=(steps,),
        in_specs=[
            pl.BlockSpec(
                (span, cols, depth),
                lambda i: ((section_pairs() + first) // per_step + i, 0, 0),
            ),
            pl.BlockSpec(
                (1, cols, depth),
                lambda i: (jnp.maximum(2 * (section_pairs() + first) - 1, 0), 0, 0),
            ),
        ]
        + in_specs,
        out_specs=out_specs,
        scratch_shapes=[pltpu.VMEM(a.shape, a.dtype) for a in shapes]
        + [pltpu.VMEM((third_depth, span * cols), jnp.bfloat16)],
        out_shape=out_shape,
        compiler_params=pltpu.CompilerParams(vmem_limit_bytes=VMEM_BYTES + 3 * 1024 * 1024),
        cost_estimate=pl.CostEstimate(
            flops=4 * macs, bytes_accessed=rows * cols * 3000, transcendentals=0
        ),
        name="stem",
    )(image, image, *operands)


def symmetric_kernel(place_ref, f_ref, turn_w_ref, turn_u_ref, g_ref):
    width = g_ref.shape[3]
    for part in range(2):
        block = f_ref[0, part]
        across = jnp.dot(block, turn_w_ref[...], preferred_element_type=jnp.float32)
        turned = jnp.dot(
            turn_u_ref[...], across.astype(jnp.bfloat16), preferred_element_type=jnp.float32
        )
        own = block[:, :width].astype(jnp.float32)
        both = own + turned if part == 0 else own - turned
        g_ref[0, part] = (0.5 * both).astype(jnp.bfloat16)


def symmetric_filter(spectral_filter, place, group, width):
    full_rows, full_cols = spectral_filter.shape[2:]
    u = jnp.arange(full_rows, dtype=jnp.int32)
    w = jnp.arange(full_cols, dtype=jnp.int32)
    turn_u = ((u[:, None] + u[None, :]) % full_rows == 0).astype(jnp.bfloat16)
    turn_w = ((w[:, None] + w[None, :width]) % full_cols == 0).astype(jnp.bfloat16)
    return pl.pallas_call(
        symmetric_kernel,
        grid_spec=pltpu.PrefetchScalarGridSpec(
            num_scalar_prefetch=1,
            grid=(group,),
            in_specs=[
                pl.BlockSpec(
                    (1, 2, full_rows, full_cols), lambda i, place: (place[0] + i, 0, 0, 0)
                ),
                pl.BlockSpec(turn_w.shape, lambda i, place: (0, 0)),
                pl.BlockSpec(turn_u.shape, lambda i, place: (0, 0)),
            ],
            out_specs=pl.BlockSpec((1, 2, full_rows, width), lambda i, place: (i, 0, 0, 0)),
        ),
        out_shape=jax.ShapeDtypeStruct((group, 2, full_rows, width), jnp.bfloat16),
        compiler_params=pltpu.CompilerParams(vmem_limit_bytes=VMEM_BYTES),
        cost_estimate=pl.CostEstimate(
            flops=8 * group * full_rows * full_cols * width,
            bytes_accessed=group * full_rows * width * 14,
            transcendentals=0,
        ),
        name="symmetric_filter",
    )(place, spectral_filter, turn_w, turn_u)


def to_lane_tiles(target, rows, values):
    for j in range(target.shape[0]):
        target[j, rows, :] = values[:, 128 * j : 128 * (j + 1)]


def from_lane_tiles(source, rows):
    return jnp.concatenate([source[j, rows, :] for j in range(source.shape[0])], axis=1)


RADIX = 3
HALF_ROOT = math.sqrt(3.0) / 2.0


def repack_kernel(devices, early_ref, twiddle_ref, out_ref, turn_ref, held):
    group, length = out_ref.shape[:2]
    turn_ref[...] = twiddle_ref[...]
    rows = length // devices
    to_lane_tiles(held, slice(0, early_ref.shape[0]), early_ref[...].astype(jnp.float32))
    for k in range(group):
        for r in range(rows):
            values = from_lane_tiles(held, pl.ds(r * group + k, devices, stride=rows * group))
            out_ref[k, r * devices : (r + 1) * devices] = values.astype(jnp.bfloat16)


def repack(early, twiddle, group, devices):
    length, cols = early.shape
    return pl.pallas_call(
        functools.partial(repack_kernel, devices),
        out_shape=[
            jax.ShapeDtypeStruct((group, length // group, cols), jnp.bfloat16),
            jax.ShapeDtypeStruct(twiddle.shape, twiddle.dtype),
        ],
        scratch_shapes=[pltpu.VMEM((cols // 128, length + length // devices, 128), jnp.float32)],
        compiler_params=pltpu.CompilerParams(vmem_limit_bytes=VMEM_BYTES),
        cost_estimate=pl.CostEstimate(
            flops=length * cols, bytes_accessed=4 * length * cols, transcendentals=0
        ),
        name="repack",
    )(early, twiddle)


def thirds(values, sign):
    (re0, im0), (re1, im1), (re2, im2) = values
    sum_re, sum_im = re1 + re2, im1 + im2
    turn_re, turn_im = HALF_ROOT * sign * (im1 - im2), HALF_ROOT * sign * (re2 - re1)
    rest_re, rest_im = re0 - 0.5 * sum_re, im0 - 0.5 * sum_im
    return (
        (re0 + sum_re, im0 + sum_im),
        (rest_re + turn_re, rest_im + turn_im),
        (rest_re - turn_re, rest_im - turn_im),
    )


def filter_kernel(
    first, devices, norm_scale, late_ref, early_ref, g_ref, row_table_ref, fwd_ref, inv_ref,
    back_ref, twiddle_ref, out_ref, held, made,
):
    step = pl.program_id(0)
    third = fwd_ref.shape[0] // 2
    full_rows = RADIX * third
    width = g_ref.shape[3]
    count = out_ref.shape[0] // full_rows
    per_step = g_ref.shape[0]
    early = early_ref.shape[1] // devices
    late = full_rows // devices - early
    group = late_ref.shape[0] // (late * devices)

    @pl.when(step == 0)
    def _():
        to_lane_tiles(held, slice(0, late_ref.shape[0]), late_ref[...].astype(jnp.float32))

    def source_rows(k, row):
        if row >= late:
            begin = (row - late) * devices
            return early_ref[k, begin : begin + devices]
        begin = row * group + first + step * per_step + k
        values = from_lane_tiles(held, pl.ds(begin, devices, stride=late * group))
        return values.astype(jnp.bfloat16)

    def twiddles(r):
        cos, sin = twiddle_ref[2 * r - 2], twiddle_ref[2 * r - 1]
        times = per_step * width // 128
        return jnp.concatenate([cos] * times, axis=1), jnp.concatenate([sin] * times, axis=1)

    fields = []
    for k in range(per_step):
        rows = [
            source_rows(k, r + RADIX * q)
            for r in range(RADIX)
            for q in range((late + early) // RADIX)
        ]
        spread = jnp.dot(
            jnp.concatenate(rows, axis=0), row_table_ref[...], preferred_element_type=jnp.float32
        )
        fields.append(spread.astype(jnp.bfloat16))
    parts = []
    for r in range(RADIX):
        span = slice(r * third, (r + 1) * third)
        block = jnp.concatenate(
            [
                jnp.concatenate([f[span, :width], f[span, width:]], axis=0)
                for f in fields
            ],
            axis=1,
        )
        short = jnp.dot(fwd_ref[...], block, preferred_element_type=jnp.float32)
        real, imag = short[:third], short[third:]
        if r > 0:
            cos, sin = twiddles(r)
            real, imag = real * cos + imag * sin, imag * cos - real * sin
        parts.append((real, imag))
    weighted = []
    for r, (real, imag) in enumerate(thirds(parts, 1.0)):
        span = slice(r * third, (r + 1) * third)
        g_real, g_imag = (
            jnp.concatenate([g_ref[k, p, span] for k in range(per_step)], axis=1).astype(
                jnp.float32
            )
            for p in range(2)
        )
        weighted.append((g_real * real - g_imag * imag, g_real * imag + g_imag * real))
    for r, (real, imag) in enumerate(thirds(weighted, -1.0)):
        if r > 0:
            cos, sin = twiddles(r)
            real, imag = real * cos - imag * sin, imag * cos + real * sin
        block = jnp.concatenate([real, imag], axis=0).astype(jnp.bfloat16)
        back = jnp.dot(inv_ref[...], block, preferred_element_type=jnp.float32).astype(
            jnp.bfloat16
        )
        for k in range(per_step):
            lanes = slice(k * width, (k + 1) * width)
            both = jnp.concatenate([back[:third, lanes], back[third:, lanes]], axis=1)
            result = jnp.dot(both, back_ref[...], preferred_element_type=jnp.float32)
            rows = pl.ds(r * count + step * per_step + k, third, stride=RADIX * count)
            to_lane_tiles(made, rows, result * norm_scale)

    @pl.when(step == pl.num_programs(0) - 1)
    def _():
        out_ref[...] = from_lane_tiles(made, slice(0, out_ref.shape[0])).astype(jnp.bfloat16)


def filter_tables(full_rows, field_cols, width, devices):
    third = full_rows // RADIX
    per_device = third // devices
    order = (per_device * np.arange(devices)[None, :] + np.arange(per_device)[:, None]).reshape(-1)
    cos_h, sin_h = fourier_tables(third)
    cos_f, sin_f = fourier_tables(third, order.astype(np.int32))
    cos_w, sin_w = fourier_tables(field_cols)
    fwd = jnp.concatenate(
        [jnp.concatenate([cos_f, sin_f], 1), jnp.concatenate([-sin_f, cos_f], 1)], 0
    )
    inv = jnp.concatenate(
        [jnp.concatenate([cos_h, -sin_h], 1), jnp.concatenate([sin_h, cos_h], 1)], 0
    )
    w = jnp.arange(width, dtype=jnp.int32)
    half = field_cols // 2
    valid = (w <= half).astype(jnp.bfloat16)
    times = jnp.where((w == 0) | (w == half), 1.0, 2.0).astype(jnp.bfloat16) * valid
    row_table = jnp.concatenate([cos_w[:, :width] * valid, -sin_w[:, :width] * valid], 1)
    back_table = jnp.concatenate(
        [cos_w[:width] * times[:, None], -sin_w[:width] * times[:, None]], 0
    )
    turns = np.arange(1, RADIX)[:, None] * np.arange(third)[None, :]
    angles = turns * (2.0 * math.pi / full_rows)
    twiddle = np.stack([np.cos(angles), np.sin(angles)], axis=1).reshape(-1, third, 1)
    twiddle = np.broadcast_to(twiddle.astype(np.float32), (2 * RADIX - 2, third, 128))
    twiddle = jnp.asarray(twiddle)
    return row_table, fwd, inv, back_table, twiddle


def filter_channels(late, early, symmetric, tables, first, count, per_step, devices):
    full_rows, width = symmetric.shape[2:]
    group, early_rows = early.shape[:2]
    cols = late.shape[1]

    def whole(array):
        return pl.BlockSpec(array.shape, lambda i: (0,) * array.ndim)

    macs = count * (4 * full_rows * full_rows * width + 4 * full_rows * cols * width)
    made = pl.pallas_call(
        functools.partial(filter_kernel, first, devices, 1.0 / (full_rows * cols)),
        grid=(count // per_step,),
        in_specs=[
            whole(late),
            pl.BlockSpec((per_step, early_rows, cols), lambda i: (first // per_step + i, 0, 0)),
            pl.BlockSpec(
                (per_step, 2, full_rows, width), lambda i: (first // per_step + i, 0, 0, 0)
            ),
        ]
        + [whole(table) for table in tables],
        out_specs=pl.BlockSpec((full_rows * count, cols), lambda i: (0, 0)),
        out_shape=jax.ShapeDtypeStruct((full_rows * count, cols), jnp.bfloat16),
        scratch_shapes=[
            pltpu.VMEM((cols // 128, late.shape[0] + late.shape[0] // devices, 128), jnp.float32),
            pltpu.VMEM((cols // 128, (full_rows + 8) * count, 128), jnp.float32),
        ],
        compiler_params=pltpu.CompilerParams(vmem_limit_bytes=VMEM_BYTES),
        cost_estimate=pl.CostEstimate(
            flops=2 * macs, bytes_accessed=count * full_rows * cols * 8, transcendentals=0
        ),
        name="spectral_filter",
    )(late, early, symmetric, *tables)
    return made.reshape(devices, full_rows // devices * count, cols)


def residual_kernel(count, place_ref, kept_ref, other_ref, feat_ref, *refs):
    out_ref, held = refs[-2:]
    groups, span, cols = kept_ref.shape
    rows = 2 * span // count
    own = pl.multiple_of(place_ref[0] * span, 8)
    far = pl.multiple_of((1 - place_ref[0]) * span, 8)
    for g in range(groups):
        to_lane_tiles(held, pl.ds(own, span), kept_ref[g].astype(jnp.float32))
        to_lane_tiles(held, pl.ds(far, span), other_ref[g].astype(jnp.float32))
        for k in range(count):
            filtered = from_lane_tiles(held, pl.ds(k, rows, stride=count))
            out_ref[g, k] = (feat_ref[g, k].astype(jnp.float32) + filtered).astype(jnp.bfloat16)


def add_residual(place, returned, other, features, previous, first, count):
    halves, span, cols = other.shape
    group, rows = features.shape[1:3]
    groups = 8 if halves % 8 == 0 else 1
    steps = halves // groups
    operands = [returned, other, features]
    in_specs = [
        pl.BlockSpec((groups, span, cols), lambda i, place: (place[0] * steps + i, 0, 0)),
        pl.BlockSpec((groups, span, cols), lambda i, place: (i, 0, 0)),
        pl.BlockSpec(
            (groups, count, rows, cols),
            lambda i, place: (i, first // count, 0, 0),
        ),
    ]
    aliases = {}
    if previous is not None:
        operands.append(previous)
        in_specs.append(pl.BlockSpec(memory_space=pl.ANY))
        aliases = {4: 0}
    return pl.pallas_call(
        functools.partial(residual_kernel, count),
        grid_spec=pltpu.PrefetchScalarGridSpec(
            num_scalar_prefetch=1,
            grid=(steps,),
            in_specs=in_specs,
            out_specs=in_specs[2],
            scratch_shapes=[pltpu.VMEM((cols // 128, (rows + 8) * count, 128), jnp.float32)],
        ),
        out_shape=jax.ShapeDtypeStruct(features.shape, jnp.bfloat16),
        input_output_aliases=aliases,
        compiler_params=pltpu.CompilerParams(vmem_limit_bytes=VMEM_BYTES),
        cost_estimate=pl.CostEstimate(
            flops=halves * count * rows * cols,
            bytes_accessed=halves * count * rows * cols * 8,
            transcendentals=0,
        ),
        name="residual",
    )(place, *operands)


def swap(block):
    return lax.ppermute(block, "section", [(0, 1), (1, 0)])


def local(
    aerial_patch_grid,
    patch_conv_weight,
    patch_bias,
    merging_conv_weight,
    merge_bias,
    down_weight,
    down_bias,
    norm_gain,
    spectral_filter,
):
    tile_rows, field_cols, depth = aerial_patch_grid.shape
    channels = down_weight.shape[3]
    tile_channels = spectral_filter.shape[0]
    full_rows = spectral_filter.shape[2]
    sections = lax.axis_size("section")
    devices = sections * lax.axis_size("tile")
    rows = tile_rows // 2
    suits = (
        sections == 2
        and tile_rows % 8 == 0
        and tile_rows >= 16
        and field_cols % 128 == 0
        and full_rows % (128 * RADIX) == 0
        and rows % RADIX == 0
        and devices % 8 == 0
        and tile_channels % 8 == 0
    )
    arguments = (
        aerial_patch_grid,
        patch_conv_weight,
        patch_bias,
        merging_conv_weight,
        merge_bias,
        down_weight,
        down_bias,
        norm_gain,
        spectral_filter,
    )
    if not suits:
        return general_local(*arguments)
    section = lax.axis_index("section")
    group = tile_channels // 2
    half_channels = channels // 2
    width = -(-(field_cols // 2 + 1) // 128) * 128

    arriving = lax.ppermute(
        lower_half(aerial_patch_grid[-1]),
        ("section", "tile"),
        [(i, i + 1) for i in range(lax.axis_size("tile") - 1)],
    )
    sources = weight_sources(*arguments[1:8])
    pairs = rows // 2
    early = max(pairs // 3, 1)
    late = pairs - early
    normed_early, feat_early = stem(
        "first", aerial_patch_grid, sources, late, early, devices
    )
    normed_early, arriving = lax.optimization_barrier((normed_early, arriving))
    normed_late, feat_late = stem(
        "last", aerial_patch_grid, sources, 0, late, devices, (arriving,)
    )
    spread = [
        lax.all_to_all(normed, DEVICES, split_axis=0, concat_axis=0, tiled=True).reshape(
            -1, field_cols
        )
        for normed in (normed_early, normed_late)
    ]
    late_fields = spread[1]
    features = jnp.concatenate([feat_late, feat_early], axis=0)

    channel_place = jnp.reshape(section * group, (1,)).astype(jnp.int32)
    symmetric = symmetric_filter(spectral_filter, channel_place, group, width)
    *tables, twiddle = filter_tables(full_rows, field_cols, width, devices)
    early_fields, twiddle = repack(spread[0], twiddle, group, devices)
    tables.append(twiddle)

    own = lax.dynamic_slice_in_dim(features, section * half_channels, half_channels, 1)
    sent = lax.dynamic_slice_in_dim(features, (1 - section) * half_channels, half_channels, 1)
    arrived = swap(sent)
    low = jnp.where(section == 0, own, arrived)
    high = jnp.where(section == 0, arrived, own)
    residual = jnp.transpose(jnp.concatenate([low, high], axis=0), (1, 0, 2))
    residual = residual.reshape(half_channels // group, group, tile_rows, field_cols)
    late_fields, residual = lax.optimization_barrier((late_fields, residual))

    section_place = jnp.reshape(section, (1,)).astype(jnp.int32)
    halves = devices // 2
    output = None
    rest = group - 2
    per_step = 5 if rest % 5 == 0 else 2
    for first, count, per_step in ((rest, 2, 2), (0, rest, per_step)):
        made = filter_channels(
            late_fields, early_fields, symmetric, tables, first, count, per_step, devices
        )
        returned = lax.all_to_all(made, DEVICES, split_axis=0, concat_axis=0, tiled=True)
        if output is not None:
            returned, output = lax.optimization_barrier((returned, output))
        other = swap(lax.dynamic_slice_in_dim(returned, (1 - section) * halves, halves, 0))
        output = add_residual(section_place, returned, other, residual, output, first, count)
    return output.reshape(half_channels, tile_rows, field_cols)


def solution(mesh):
    return jax.shard_map(
        local,
        mesh=mesh,
        in_specs=(
            P("tile", None, None),
            P(),
            P(),
            P(),
            P(),
            P(),
            P(),
            P(),
            P("tile", None, None, None),
        ),
        out_specs=P("section", "tile", None),
        check_vma=False,
    )
```

```python
import functools
import math

import jax
import jax.numpy as jnp
import numpy as np
from jax import lax
from jax.experimental import pallas as pl
from jax.experimental.pallas import tpu as pltpu
from jax.sharding import PartitionSpec as P

EPSILON = 1e-05


def from_behind(block, axis, distance):
    devices = range(lax.axis_size(axis))
    route = [(i - distance, i) for i in devices if i - distance in devices]
    return lax.ppermute(block, axis, route)


def fourier_tables(length, columns=None):
    indices = jnp.arange(length, dtype=jnp.int32)
    columns = indices if columns is None else jnp.asarray(columns, jnp.int32)
    product = indices[:, None] * columns[None, :] % length
    angles = product.astype(jnp.float32) * (2.0 * math.pi / length)
    return (jnp.cos(angles).astype(jnp.bfloat16), jnp.sin(angles).astype(jnp.bfloat16))


def patch_kernel_matrix(patch_conv_weight):
    identity = jnp.eye(4, dtype=jnp.float32)
    larger = jnp.einsum(
        "baqk,xy,uv->bxauqyvk", patch_conv_weight.astype(jnp.float32), identity, identity
    )
    band_count = patch_conv_weight.shape[0]
    width = patch_conv_weight.shape[3]
    return larger.reshape(band_count * 256, 16 * width).astype(jnp.bfloat16)


def merging_kernel_matrix(merging_conv_weight):
    identity = jnp.eye(2, dtype=jnp.float32)
    larger = jnp.einsum(
        "aqjk,xy,uv->xauqjyvk", merging_conv_weight.astype(jnp.float32), identity, identity
    )
    in_width = merging_conv_weight.shape[2]
    out_width = merging_conv_weight.shape[3]
    return larger.reshape(16 * in_width, 4 * out_width).astype(jnp.bfloat16)


def down_matrices(down_weight):
    nothing = jnp.zeros_like(down_weight[0, 0])
    in_width = down_weight.shape[2]
    out_width = down_weight.shape[3]

    def arrange(entries):
        return jnp.stack(
            [jnp.stack(entries[0], axis=0), jnp.stack(entries[1], axis=0)], axis=0
        ).reshape(4 * in_width, out_width)

    own_taps = arrange(
        [[down_weight[1, 1], down_weight[1, 2]], [down_weight[2, 1], down_weight[2, 2]]]
    )
    upper_taps = arrange([[nothing, nothing], [down_weight[0, 1], down_weight[0, 2]]])
    left_taps = arrange([[nothing, down_weight[1, 0]], [nothing, down_weight[2, 0]]])
    corner_taps = arrange([[nothing, nothing], [nothing, down_weight[0, 0]]])
    return (own_taps, upper_taps, left_taps, corner_taps)


def stem_layers(aerial_patch_grid, patch_conv_weight, patch_bias, merging_conv_weight, merge_bias):
    initial_layer = jnp.einsum(
        "zji,if->zjf",
        aerial_patch_grid,
        patch_kernel_matrix(patch_conv_weight),
        preferred_element_type=jnp.float32,
    )
    initial_layer = jax.nn.gelu(initial_layer + jnp.tile(patch_bias, 16), approximate=True).astype(
        jnp.bfloat16
    )
    layer_two = jnp.einsum(
        "zji,if->zjf",
        initial_layer,
        merging_kernel_matrix(merging_conv_weight),
        preferred_element_type=jnp.float32,
    )
    return jax.nn.gelu(layer_two + jnp.tile(merge_bias, 4), approximate=True).astype(jnp.bfloat16)


def rim_above(extended):
    return from_behind(extended[-1:], "tile", 1)


def down_conv(upper_rim, extended, down_weight, down_bias):
    stacked = jnp.concatenate([upper_rim, extended], axis=0)
    own_taps, upper_taps, left_taps, corner_taps = down_matrices(down_weight)
    summed = jnp.einsum(
        "rwk,kc->crw", stacked[1:, 1:], own_taps, preferred_element_type=jnp.float32
    )
    summed = summed + jnp.einsum(
        "rwk,kc->crw", stacked[:-1, 1:], upper_taps, preferred_element_type=jnp.float32
    )
    summed = summed + jnp.einsum(
        "rwk,kc->crw", stacked[1:, :-1], left_taps, preferred_element_type=jnp.float32
    )
    summed = summed + jnp.einsum(
        "rwk,kc->crw", stacked[:-1, :-1], corner_taps, preferred_element_type=jnp.float32
    )
    return (summed + down_bias[:, None, None]).astype(jnp.bfloat16)


def layer_norm(features, norm_gain):
    values = features.astype(jnp.float32)
    mean_value = jnp.mean(values, axis=0, keepdims=True)
    centered = values - mean_value
    variance = jnp.mean(centered * centered, axis=0, keepdims=True)
    return (norm_gain[:, None, None] * centered * lax.rsqrt(variance + EPSILON)).astype(
        jnp.bfloat16
    )


def filter_columns(row_spectrum, kernel, forward_h, inverse_h):
    spectrum = jnp.einsum(
        "puqh,chqw->cpuw", forward_h, row_spectrum, preferred_element_type=jnp.float32
    ).astype(jnp.bfloat16)
    spec_real = spectrum[:, 0].astype(jnp.float32)
    spec_imag = spectrum[:, 1].astype(jnp.float32)
    filter_real = kernel[:, 0].astype(jnp.float32)
    filter_imag = kernel[:, 1].astype(jnp.float32)
    weighted = jnp.stack(
        [
            filter_real * spec_real - filter_imag * spec_imag,
            filter_real * spec_imag + filter_imag * spec_real,
        ],
        axis=1,
    ).astype(jnp.bfloat16)
    return jnp.einsum(
        "qhpu,cpuw->chqw", inverse_h, weighted, preferred_element_type=jnp.float32
    ).astype(jnp.bfloat16)


def general_local(
    aerial_patch_grid,
    patch_conv_weight,
    patch_bias,
    merging_conv_weight,
    merge_bias,
    down_weight,
    down_bias,
    norm_gain,
    spectral_filter,
):
    section_index = lax.axis_index("section")
    first_section = section_index == 0
    field_cols = aerial_patch_grid.shape[1]
    channels = down_weight.shape[3]
    group_width = spectral_filter.shape[0]
    full_rows = spectral_filter.shape[2]
    half_channels = channels // 2
    cell_half = field_cols // 2
    image_part = lax.dynamic_slice_in_dim(
        aerial_patch_grid, section_index * cell_half, cell_half, 1
    )
    layer_two = stem_layers(
        image_part, patch_conv_weight, patch_bias, merging_conv_weight, merge_bias
    )
    left_column = from_behind(layer_two[:, -1:], "section", 1)
    extended = jnp.concatenate([left_column, layer_two], axis=1)
    upper_rim = rim_above(extended)
    feature_half = down_conv(upper_rim, extended, down_weight, down_bias)
    features = lax.all_gather(feature_half, "section", axis=2, tiled=True)
    normed = layer_norm(features, norm_gain)
    cos_h, sin_h = fourier_tables(full_rows)
    cos_w, sin_w = fourier_tables(field_cols)
    forward_table = jnp.stack([cos_w, -sin_w], axis=1)
    forward_h = jnp.stack(
        [jnp.stack([cos_h, sin_h], axis=1), jnp.stack([-sin_h, cos_h], axis=1)], axis=0
    )
    inverse_h = jnp.stack(
        [jnp.stack([cos_h, -sin_h], axis=1), jnp.stack([sin_h, cos_h], axis=1)], axis=0
    )
    inverse_table = jnp.stack([cos_w, -sin_w], axis=0)
    norm_scale = 1.0 / (full_rows * field_cols)
    fields = lax.all_to_all(normed, "tile", split_axis=0, concat_axis=1, tiled=True)

    def whole_filter():
        frequency_rows = jnp.einsum(
            "chx,xqw->chqw", fields, forward_table, preferred_element_type=jnp.float32
        ).astype(jnp.bfloat16)
        back_rows = filter_columns(frequency_rows, spectral_filter, forward_h, inverse_h)
        result = jnp.einsum(
            "chqw,qwv->chv", back_rows, inverse_table, preferred_element_type=jnp.float32
        )
        return (result * norm_scale).astype(jnp.bfloat16)

    def empty_fields():
        return jnp.zeros((group_width, full_rows, field_cols), jnp.bfloat16)

    filtered_fields = lax.cond(first_section, empty_fields, whole_filter)
    rows_back = lax.all_to_all(filtered_fields, "tile", split_axis=1, concat_axis=0, tiled=True)
    returned = from_behind(rows_back[:half_channels], "section", -1)
    filtered = jnp.where(first_section, returned, rows_back[half_channels:])
    own_part = lax.dynamic_slice_in_dim(features, section_index * half_channels, half_channels, 0)
    return (own_part.astype(jnp.float32) + filtered.astype(jnp.float32)).astype(jnp.bfloat16)


DEVICES = ("tile", "section")
VMEM_BYTES = 60 * 1024 * 1024
GELU_LINEAR = 2.0 * math.sqrt(2.0 / math.pi)
GELU_CUBIC = 4.0 * 0.044715 * GELU_LINEAR
ONES = (64, 128, 64)
TAPS = ((1, 1), (1, 2), (2, 1), (2, 2), (1, 0), (2, 0), (0, 1), (0, 2), (0, 0))


def bias_rows(bias, count):
    high = bias.astype(jnp.bfloat16)
    rest = bias - high.astype(jnp.float32)
    middle = rest.astype(jnp.bfloat16)
    low = (rest - middle.astype(jnp.float32)).astype(jnp.bfloat16)
    shape = (count, bias.shape[1])
    row = lax.broadcasted_iota(jnp.int32, shape, 0)
    rows = jnp.zeros(shape, jnp.float32)
    for k, part in enumerate((high, middle, low)):
        rows = jnp.where(row == k, jnp.broadcast_to(part.astype(jnp.float32), shape), rows)
    return rows.astype(jnp.bfloat16)


def build_weights(sources, targets):
    patch_ref, patch_bias_ref, merge_ref, merge_bias_ref, down_ref, down_bias_ref, gain_ref = sources
    w1_ref, w2_ref, w3_ref, column_ref = targets

    def exact(a, b):
        return jnp.dot(
            a.astype(jnp.bfloat16), b.astype(jnp.bfloat16), preferred_element_type=jnp.float32
        )

    taps, width = patch_ref.shape
    row = lax.broadcasted_iota(jnp.int32, (4 * taps, taps), 0)
    col = lax.broadcasted_iota(jnp.int32, (4 * taps, taps), 1)
    pick = jnp.where(row // 16 * 4 + row % 4 == col, 1.0, 0.0)
    row = lax.broadcasted_iota(jnp.int32, (width, 4 * width), 0)
    col = lax.broadcasted_iota(jnp.int32, (width, 4 * width), 1)
    repeat = jnp.where(col % width == row, 1.0, 0.0)
    spread = exact(pick, exact(patch_ref[...], repeat))
    row = lax.broadcasted_iota(jnp.int32, spread.shape, 0)
    col = lax.broadcasted_iota(jnp.int32, spread.shape, 1)
    spread = jnp.where(row // 4 % 4 == col // width, 0.5 * spread, 0.0).astype(jnp.bfloat16)
    bias = jnp.broadcast_to(0.5 * patch_bias_ref[...][None], (8, width))
    tiled = jnp.zeros((8, 4 * width), jnp.float32)
    for _ in range(3):
        part = bias.astype(jnp.bfloat16).astype(jnp.float32)
        tiled = tiled + exact(part, repeat)
        bias = bias - part
    first = jnp.concatenate([spread, bias_rows(tiled[:1], ONES[0])], axis=0)
    w1_ref[...] = first.T
    half = (merge_ref[...].astype(jnp.float32) * 0.5).astype(jnp.bfloat16)
    second = jnp.concatenate([half, bias_rows(0.5 * merge_bias_ref[...][None], ONES[1])], axis=0)
    w2_ref[...] = second.T
    third = [down_ref[3 * a + q] for a, q in TAPS]
    third = jnp.concatenate(third + [bias_rows(down_bias_ref[...][None], ONES[2])], axis=0)
    w3_ref[...] = third.T
    column_ref[...] = jnp.broadcast_to(gain_ref[...][None], (128, gain_ref.shape[0])).T


def weight_sources(
    patch_conv_weight, patch_bias, merging_conv_weight, merge_bias, down_weight, down_bias,
    norm_gain,
):
    width = patch_conv_weight.shape[3]
    merged = merging_conv_weight.shape[3]
    return [
        patch_conv_weight.reshape(-1, width),
        patch_bias,
        merging_conv_weight.reshape(-1, merged),
        merge_bias,
        down_weight.reshape(-1, merged, down_weight.shape[3]),
        down_bias,
        norm_gain,
    ]


def weight_shapes(sources):
    taps, width = sources[0].shape
    merged, channels = sources[4].shape[1:]
    return [
        jax.ShapeDtypeStruct((4 * width, 4 * taps + ONES[0]), jnp.bfloat16),
        jax.ShapeDtypeStruct((merged, 4 * width + ONES[1]), jnp.bfloat16),
        jax.ShapeDtypeStruct((channels, 9 * merged + ONES[2]), jnp.bfloat16),
        jax.ShapeDtypeStruct((channels, 128), jnp.float32),
    ]


def half_gelu(h):
    return h + h * jnp.tanh(h * (GELU_LINEAR + GELU_CUBIC * (h * h)))


def lower_half(row):
    depth = row.shape[1]
    return jnp.concatenate(
        [row[:, 256 * b + 128 : 256 * b + 256] for b in range(depth // 256)], axis=1
    )


def stem_kernel(kind, x_ref, above_ref, *refs):
    sources = refs[:7]
    normed_ref, feat_ref, w1_ref, w2_ref, w3_ref, gain_ref, field = refs[-7:]
    step = pl.program_id(0)
    rows, cols, depth = x_ref.shape
    bands = depth // 256
    channels = w3_ref.shape[0]
    merged = w2_ref.shape[0]
    group = normed_ref.shape[2] // 2
    cells = rows * cols

    @pl.when(step == 0)
    def _():
        build_weights(sources, (w1_ref, w2_ref, w3_ref, gain_ref))

    w1 = w1_ref[...]
    w2 = w2_ref[...]

    def ones(count, n):
        return jnp.where(lax.broadcasted_iota(jnp.int32, (count, n), 0) < 3, 1.0, 0.0).astype(
            jnp.bfloat16
        )

    def layer_one(turned, offsets):
        n = turned.shape[1]
        parts = [turned[o : o + 64] for o in offsets] + [ones(ONES[0], n)]
        h = jnp.dot(w1, jnp.concatenate(parts, axis=0), preferred_element_type=jnp.float32)
        return half_gelu(h).astype(jnp.bfloat16)

    def layer_two(upper, lower, y):
        n = upper.shape[1]
        span = slice(2 * y * (w1.shape[0] // 4), 2 * (y + 1) * (w1.shape[0] // 4))
        stacked = jnp.concatenate([upper[span], lower[span], ones(ONES[1], n)], axis=0)
        return half_gelu(jnp.dot(w2, stacked, preferred_element_type=jnp.float32))

    def shifted(values):
        lanes = lax.broadcasted_iota(jnp.int32, values.shape, 1)
        moved = pltpu.roll(values, 1, 1)
        return jnp.where(lax.rem(lanes, cols) == 0, 0.0, moved)

    def put(block, lanes, values):
        field[block * merged : (block + 1) * merged, lanes] = values.astype(jnp.bfloat16)

    first_row = slice(0, cols)
    last_row = slice(cells - cols, cells)
    later_rows = slice(cols, cells)
    earlier_rows = slice(0, cells - cols)

    @pl.when(step == 0)
    def _():
        field[9 * merged :, :] = ones(ONES[2], cells)
        above = lower_half(above_ref[0])
        keep = 1.0
        if kind == "last":
            lower_section = lax.axis_index("section") > 0
            inside = lower_section | (lax.axis_index("tile") > 0)
            keep = jnp.where(inside, 1.0, 0.0)
            above = jnp.where(lower_section, above, refs[7][...])
        turned = above.T
        upper, lower = (
            layer_one(turned, [128 * b + 64 * a for b in range(bands)]) for a in range(2)
        )
        put(6, first_row, layer_two(upper, lower, 0) * keep)
        right = layer_two(upper, lower, 1) * keep
        put(7, first_row, right)
        put(8, first_row, shifted(right))

    @pl.when(step > 0)
    def _():
        for source, target in ((2, 6), (3, 7), (5, 8)):
            field[target * merged : (target + 1) * merged, first_row] = field[
                source * merged : (source + 1) * merged, last_row
            ]

    turned = x_ref[...].reshape(cells, depth).T
    for x in range(2):
        upper, lower = (
            layer_one(turned, [256 * b + 64 * (2 * x + a) for b in range(bands)])
            for a in range(2)
        )
        left = layer_two(upper, lower, 0)
        right = layer_two(upper, lower, 1)
        put(2 * x, slice(None), left)
        put(2 * x + 1, slice(None), right)
        moved = shifted(right)
        put(4 + x, slice(None), moved)
        if x == 1:
            put(6, later_rows, left[:, earlier_rows])
            put(7, later_rows, right[:, earlier_rows])
            put(8, later_rows, moved[:, earlier_rows])

    features = jnp.dot(w3_ref[...], field[...], preferred_element_type=jnp.float32).astype(
        jnp.bfloat16
    )
    for r in range(rows):
        feat_ref[r] = features[:, r * cols : (r + 1) * cols]
    values = features.astype(jnp.float32)
    centered = values - jnp.mean(values, axis=0, keepdims=True)
    variance = jnp.mean(centered * centered, axis=0, keepdims=True)
    gain = jnp.concatenate([gain_ref[...]] * (cells // 128), axis=1)
    normed = gain * (centered * lax.rsqrt(variance + EPSILON))
    pair = 2 * group
    index = lax.broadcasted_iota(jnp.int32, (pair, cols), 0)
    for t in range(channels // pair):
        for p in range(rows // 2):
            span = slice(pair * t, pair * (t + 1))
            one = normed[span, 2 * p * cols : (2 * p + 1) * cols]
            two = normed[span, (2 * p + 1) * cols : (2 * p + 2) * cols]
            normed_ref[2 * t, p] = jnp.where(
                index < group, one, pltpu.roll(two, group, 0)
            ).astype(jnp.bfloat16)
            normed_ref[2 * t + 1, p] = jnp.where(
                index < group, pltpu.roll(one, group, 0), two
            ).astype(jnp.bfloat16)


def stem(kind, image, weights, first, pairs, devices, extra=()):
    cols, depth = image.shape[1:]
    rows = 2 * pairs
    per_step = 1
    if kind == "first" and all(n % 2 == 0 for n in (pairs, first, image.shape[0] // 4)):
        per_step = 2
    steps = pairs // per_step
    span = 2 * per_step
    shapes = weight_shapes(weights)
    channels, third_depth = shapes[2].shape
    merged = shapes[1].shape[0]
    group = channels // devices

    def section_pairs():
        return lax.axis_index("section") * (image.shape[0] // 4)

    def whole(array):
        return pl.BlockSpec(array.shape, lambda i: (0,) * len(array.shape))

    operands = list(weights) + list(extra)
    in_specs = [whole(a) for a in weights]
    out_specs = [
        pl.BlockSpec((devices, per_step, 2 * group, cols), lambda i: (0, i, 0, 0)),
        pl.BlockSpec((span, channels, cols), lambda i: (i, 0, 0)),
    ]
    out_shape = [
        jax.ShapeDtypeStruct((devices, pairs, 2 * group, cols), jnp.bfloat16),
        jax.ShapeDtypeStruct((rows, channels, cols), jnp.bfloat16),
    ]
    in_specs += [whole(a) for a in extra]
    macs = rows * cols * (16 * 208 * 96 + 4 * 400 * merged + third_depth * channels)
    return pl.pallas_call(
        functools.partial(stem_kernel, kind),
        grid=(steps,),
        in_specs=[
            pl.BlockSpec(
                (span, cols, depth),
                lambda i: ((section_pairs() + first) // per_step + i, 0, 0),
            ),
            pl.BlockSpec(
                (1, cols, depth),
                lambda i: (jnp.maximum(2 * (section_pairs() + first) - 1, 0), 0, 0),
            ),
        ]
        + in_specs,
        out_specs=out_specs,
        scratch_shapes=[pltpu.VMEM(a.shape, a.dtype) for a in shapes]
        + [pltpu.VMEM((third_depth, span * cols), jnp.bfloat16)],
        out_shape=out_shape,
        compiler_params=pltpu.CompilerParams(vmem_limit_bytes=VMEM_BYTES + 3 * 1024 * 1024),
        cost_estimate=pl.CostEstimate(
            flops=4 * macs, bytes_accessed=rows * cols * 3000, transcendentals=0
        ),
        name="stem",
    )(image, image, *operands)


def symmetric_kernel(place_ref, f_ref, turn_w_ref, turn_u_ref, g_ref):
    width = g_ref.shape[3]
    for part in range(2):
        block = f_ref[0, part]
        across = jnp.dot(block, turn_w_ref[...], preferred_element_type=jnp.float32)
        turned = jnp.dot(
            turn_u_ref[...], across.astype(jnp.bfloat16), preferred_element_type=jnp.float32
        )
        own = block[:, :width].astype(jnp.float32)
        both = own + turned if part == 0 else own - turned
        g_ref[0, part] = (0.5 * both).astype(jnp.bfloat16)


def symmetric_filter(spectral_filter, place, group, width):
    full_rows, full_cols = spectral_filter.shape[2:]
    u = jnp.arange(full_rows, dtype=jnp.int32)
    w = jnp.arange(full_cols, dtype=jnp.int32)
    turn_u = ((u[:, None] + u[None, :]) % full_rows == 0).astype(jnp.bfloat16)
    turn_w = ((w[:, None] + w[None, :width]) % full_cols == 0).astype(jnp.bfloat16)
    return pl.pallas_call(
        symmetric_kernel,
        grid_spec=pltpu.PrefetchScalarGridSpec(
            num_scalar_prefetch=1,
            grid=(group,),
            in_specs=[
                pl.BlockSpec(
                    (1, 2, full_rows, full_cols), lambda i, place: (place[0] + i, 0, 0, 0)
                ),
                pl.BlockSpec(turn_w.shape, lambda i, place: (0, 0)),
                pl.BlockSpec(turn_u.shape, lambda i, place: (0, 0)),
            ],
            out_specs=pl.BlockSpec((1, 2, full_rows, width), lambda i, place: (i, 0, 0, 0)),
        ),
        out_shape=jax.ShapeDtypeStruct((group, 2, full_rows, width), jnp.bfloat16),
        compiler_params=pltpu.CompilerParams(vmem_limit_bytes=VMEM_BYTES),
        cost_estimate=pl.CostEstimate(
            flops=8 * group * full_rows * full_cols * width,
            bytes_accessed=group * full_rows * width * 14,
            transcendentals=0,
        ),
        name="symmetric_filter",
    )(place, spectral_filter, turn_w, turn_u)


def to_lane_tiles(target, rows, values):
    for j in range(target.shape[0]):
        target[j, rows, :] = values[:, 128 * j : 128 * (j + 1)]


def from_lane_tiles(source, rows):
    return jnp.concatenate([source[j, rows, :] for j in range(source.shape[0])], axis=1)


RADIX = 3
HALF_ROOT = math.sqrt(3.0) / 2.0


def repack_kernel(devices, early_ref, twiddle_ref, out_ref, turn_ref, held):
    group, length = out_ref.shape[:2]
    turn_ref[...] = twiddle_ref[...]
    rows = length // devices
    to_lane_tiles(held, slice(0, early_ref.shape[0]), early_ref[...].astype(jnp.float32))
    for k in range(group):
        for r in range(rows):
            values = from_lane_tiles(held, pl.ds(r * group + k, devices, stride=rows * group))
            out_ref[k, r * devices : (r + 1) * devices] = values.astype(jnp.bfloat16)


def repack(early, twiddle, group, devices):
    length, cols = early.shape
    return pl.pallas_call(
        functools.partial(repack_kernel, devices),
        out_shape=[
            jax.ShapeDtypeStruct((group, length // group, cols), jnp.bfloat16),
            jax.ShapeDtypeStruct(twiddle.shape, twiddle.dtype),
        ],
        scratch_shapes=[pltpu.VMEM((cols // 128, length + length // devices, 128), jnp.float32)],
        compiler_params=pltpu.CompilerParams(vmem_limit_bytes=VMEM_BYTES),
        cost_estimate=pl.CostEstimate(
            flops=length * cols, bytes_accessed=4 * length * cols, transcendentals=0
        ),
        name="repack",
    )(early, twiddle)


def thirds(values, sign):
    (re0, im0), (re1, im1), (re2, im2) = values
    sum_re, sum_im = re1 + re2, im1 + im2
    turn_re, turn_im = HALF_ROOT * sign * (im1 - im2), HALF_ROOT * sign * (re2 - re1)
    rest_re, rest_im = re0 - 0.5 * sum_re, im0 - 0.5 * sum_im
    return (
        (re0 + sum_re, im0 + sum_im),
        (rest_re + turn_re, rest_im + turn_im),
        (rest_re - turn_re, rest_im - turn_im),
    )


def filter_kernel(
    first, devices, norm_scale, late_ref, early_ref, g_ref, row_table_ref, fwd_ref, inv_ref,
    back_ref, twiddle_ref, out_ref, held, made,
):
    step = pl.program_id(0)
    third = fwd_ref.shape[0] // 2
    full_rows = RADIX * third
    width = g_ref.shape[3]
    count = out_ref.shape[0] // full_rows
    per_step = g_ref.shape[0]
    early = early_ref.shape[1] // devices
    late = full_rows // devices - early
    group = late_ref.shape[0] // (late * devices)

    @pl.when(step == 0)
    def _():
        to_lane_tiles(held, slice(0, late_ref.shape[0]), late_ref[...].astype(jnp.float32))

    def source_rows(k, row):
        if row >= late:
            begin = (row - late) * devices
            return early_ref[k, begin : begin + devices]
        begin = row * group + first + step * per_step + k
        values = from_lane_tiles(held, pl.ds(begin, devices, stride=late * group))
        return values.astype(jnp.bfloat16)

    def twiddles(r):
        cos, sin = twiddle_ref[2 * r - 2], twiddle_ref[2 * r - 1]
        times = per_step * width // 128
        return jnp.concatenate([cos] * times, axis=1), jnp.concatenate([sin] * times, axis=1)

    fields = []
    for k in range(per_step):
        rows = [
            source_rows(k, r + RADIX * q)
            for r in range(RADIX)
            for q in range((late + early) // RADIX)
        ]
        spread = jnp.dot(
            jnp.concatenate(rows, axis=0), row_table_ref[...], preferred_element_type=jnp.float32
        )
        fields.append(spread.astype(jnp.bfloat16))
    parts = []
    for r in range(RADIX):
        span = slice(r * third, (r + 1) * third)
        block = jnp.concatenate(
            [
                jnp.concatenate([f[span, :width], f[span, width:]], axis=0)
                for f in fields
            ],
            axis=1,
        )
        short = jnp.dot(fwd_ref[...], block, preferred_element_type=jnp.float32)
        real, imag = short[:third], short[third:]
        if r > 0:
            cos, sin = twiddles(r)
            real, imag = real * cos + imag * sin, imag * cos - real * sin
        parts.append((real, imag))
    weighted = []
    for r, (real, imag) in enumerate(thirds(parts, 1.0)):
        span = slice(r * third, (r + 1) * third)
        g_real, g_imag = (
            jnp.concatenate([g_ref[k, p, span] for k in range(per_step)], axis=1).astype(
                jnp.float32
            )
            for p in range(2)
        )
        weighted.append((g_real * real - g_imag * imag, g_real * imag + g_imag * real))
    for r, (real, imag) in enumerate(thirds(weighted, -1.0)):
        if r > 0:
            cos, sin = twiddles(r)
            real, imag = real * cos - imag * sin, imag * cos + real * sin
        block = jnp.concatenate([real, imag], axis=0).astype(jnp.bfloat16)
        back = jnp.dot(inv_ref[...], block, preferred_element_type=jnp.float32).astype(
            jnp.bfloat16
        )
        for k in range(per_step):
            lanes = slice(k * width, (k + 1) * width)
            both = jnp.concatenate([back[:third, lanes], back[third:, lanes]], axis=1)
            result = jnp.dot(both, back_ref[...], preferred_element_type=jnp.float32)
            rows = pl.ds(r * count + step * per_step + k, third, stride=RADIX * count)
            to_lane_tiles(made, rows, result * norm_scale)

    @pl.when(step == pl.num_programs(0) - 1)
    def _():
        out_ref[...] = from_lane_tiles(made, slice(0, out_ref.shape[0])).astype(jnp.bfloat16)


def filter_tables(full_rows, field_cols, width, devices):
    third = full_rows // RADIX
    per_device = third // devices
    order = (per_device * np.arange(devices)[None, :] + np.arange(per_device)[:, None]).reshape(-1)
    cos_h, sin_h = fourier_tables(third)
    cos_f, sin_f = fourier_tables(third, order.astype(np.int32))
    cos_w, sin_w = fourier_tables(field_cols)
    fwd = jnp.concatenate(
        [jnp.concatenate([cos_f, sin_f], 1), jnp.concatenate([-sin_f, cos_f], 1)], 0
    )
    inv = jnp.concatenate(
        [jnp.concatenate([cos_h, -sin_h], 1), jnp.concatenate([sin_h, cos_h], 1)], 0
    )
    w = jnp.arange(width, dtype=jnp.int32)
    half = field_cols // 2
    valid = (w <= half).astype(jnp.bfloat16)
    times = jnp.where((w == 0) | (w == half), 1.0, 2.0).astype(jnp.bfloat16) * valid
    row_table = jnp.concatenate([cos_w[:, :width] * valid, -sin_w[:, :width] * valid], 1)
    back_table = jnp.concatenate(
        [cos_w[:width] * times[:, None], -sin_w[:width] * times[:, None]], 0
    )
    turns = np.arange(1, RADIX)[:, None] * np.arange(third)[None, :]
    angles = turns * (2.0 * math.pi / full_rows)
    twiddle = np.stack([np.cos(angles), np.sin(angles)], axis=1).reshape(-1, third, 1)
    twiddle = np.broadcast_to(twiddle.astype(np.float32), (2 * RADIX - 2, third, 128))
    twiddle = jnp.asarray(twiddle)
    return row_table, fwd, inv, back_table, twiddle


def filter_channels(late, early, symmetric, tables, first, count, per_step, devices):
    full_rows, width = symmetric.shape[2:]
    group, early_rows = early.shape[:2]
    cols = late.shape[1]

    def whole(array):
        return pl.BlockSpec(array.shape, lambda i: (0,) * array.ndim)

    macs = count * (4 * full_rows * full_rows * width + 4 * full_rows * cols * width)
    made = pl.pallas_call(
        functools.partial(filter_kernel, first, devices, 1.0 / (full_rows * cols)),
        grid=(count // per_step,),
        in_specs=[
            whole(late),
            pl.BlockSpec((per_step, early_rows, cols), lambda i: (first // per_step + i, 0, 0)),
            pl.BlockSpec(
                (per_step, 2, full_rows, width), lambda i: (first // per_step + i, 0, 0, 0)
            ),
        ]
        + [whole(table) for table in tables],
        out_specs=pl.BlockSpec((full_rows * count, cols), lambda i: (0, 0)),
        out_shape=jax.ShapeDtypeStruct((full_rows * count, cols), jnp.bfloat16),
        scratch_shapes=[
            pltpu.VMEM((cols // 128, late.shape[0] + late.shape[0] // devices, 128), jnp.float32),
            pltpu.VMEM((cols // 128, (full_rows + 8) * count, 128), jnp.float32),
        ],
        compiler_params=pltpu.CompilerParams(vmem_limit_bytes=VMEM_BYTES),
        cost_estimate=pl.CostEstimate(
            flops=2 * macs, bytes_accessed=count * full_rows * cols * 8, transcendentals=0
        ),
        name="spectral_filter",
    )(late, early, symmetric, *tables)
    return made.reshape(devices, full_rows // devices * count, cols)


def residual_kernel(first, count, chunks, kept_hbm, other_hbm, feat_hbm, *refs):
    out_hbm, kept, other, feat, out, held, done = refs[-7:]
    halves, span = other.shape[:2]
    rows = 2 * span // count
    groups = halves // chunks
    section = lax.axis_index("section")

    def block(c):
        return pl.ds(c * groups, groups)

    def copies(c):
        source = pl.ds(section * halves + c * groups, groups)
        channels = pl.ds(first, count)
        return [
            pltpu.make_async_copy(kept_hbm.at[source], kept.at[block(c)], done.at[0, c]),
            pltpu.make_async_copy(other_hbm.at[block(c)], other.at[block(c)], done.at[1, c]),
            pltpu.make_async_copy(
                feat_hbm.at[block(c), channels], feat.at[block(c)], done.at[2, c]
            ),
        ]

    def result(c):
        channels = pl.ds(first, count)
        return pltpu.make_async_copy(
            out.at[block(c)], out_hbm.at[block(c), channels], done.at[3, c]
        )

    for c in range(chunks):
        for copy in copies(c):
            copy.start()
    own = pl.multiple_of(section * span, 8)
    far = pl.multiple_of((1 - section) * span, 8)
    for c in range(chunks):
        for copy in copies(c):
            copy.wait()
        for g in range(c * groups, (c + 1) * groups):
            to_lane_tiles(held, pl.ds(own, span), kept[g].astype(jnp.float32))
            to_lane_tiles(held, pl.ds(far, span), other[g].astype(jnp.float32))
            for k in range(count):
                filtered = from_lane_tiles(held, pl.ds(k, rows, stride=count))
                out[g, k] = (feat[g, k].astype(jnp.float32) + filtered).astype(jnp.bfloat16)
        result(c).start()
    for c in range(chunks):
        result(c).wait()


def add_residual(returned, other, features, previous, first, count):
    halves, span, cols = other.shape
    group, rows = features.shape[1:3]
    chunks = 4 if halves % 4 == 0 else 1
    operands = [returned, other, features]
    aliases = {}
    if previous is not None:
        operands.append(previous)
        aliases = {3: 0}
    return pl.pallas_call(
        functools.partial(residual_kernel, first, count, chunks),
        in_specs=[pl.BlockSpec(memory_space=pl.ANY)] * len(operands),
        out_specs=pl.BlockSpec(memory_space=pl.ANY),
        scratch_shapes=[
            pltpu.VMEM((halves, span, cols), jnp.bfloat16),
            pltpu.VMEM((halves, span, cols), jnp.bfloat16),
            pltpu.VMEM((halves, count, rows, cols), jnp.bfloat16),
            pltpu.VMEM((halves, count, rows, cols), jnp.bfloat16),
            pltpu.VMEM((cols // 128, (rows + 8) * count, 128), jnp.float32),
            pltpu.SemaphoreType.DMA((4, chunks)),
        ],
        out_shape=jax.ShapeDtypeStruct(features.shape, jnp.bfloat16),
        input_output_aliases=aliases,
        compiler_params=pltpu.CompilerParams(vmem_limit_bytes=VMEM_BYTES // 4),
        cost_estimate=pl.CostEstimate(
            flops=halves * count * rows * cols,
            bytes_accessed=halves * count * rows * cols * 8,
            transcendentals=0,
        ),
        name="residual",
    )(*operands)


def swap(block):
    return lax.ppermute(block, "section", [(0, 1), (1, 0)])


def local(
    aerial_patch_grid,
    patch_conv_weight,
    patch_bias,
    merging_conv_weight,
    merge_bias,
    down_weight,
    down_bias,
    norm_gain,
    spectral_filter,
):
    tile_rows, field_cols, depth = aerial_patch_grid.shape
    channels = down_weight.shape[3]
    tile_channels = spectral_filter.shape[0]
    full_rows = spectral_filter.shape[2]
    sections = lax.axis_size("section")
    devices = sections * lax.axis_size("tile")
    rows = tile_rows // 2
    suits = (
        sections == 2
        and tile_rows % 8 == 0
        and tile_rows >= 16
        and field_cols % 128 == 0
        and full_rows % (128 * RADIX) == 0
        and rows % RADIX == 0
        and devices % 8 == 0
        and tile_channels % 8 == 0
    )
    arguments = (
        aerial_patch_grid,
        patch_conv_weight,
        patch_bias,
        merging_conv_weight,
        merge_bias,
        down_weight,
        down_bias,
        norm_gain,
        spectral_filter,
    )
    if not suits:
        return general_local(*arguments)
    section = lax.axis_index("section")
    group = tile_channels // 2
    half_channels = channels // 2
    width = -(-(field_cols // 2 + 1) // 128) * 128

    arriving = lax.ppermute(
        lower_half(aerial_patch_grid[-1]),
        ("section", "tile"),
        [(i, i + 1) for i in range(lax.axis_size("tile") - 1)],
    )
    sources = weight_sources(*arguments[1:8])
    pairs = rows // 2
    early = max(pairs // 3, 1)
    late = pairs - early
    normed_early, feat_early = stem(
        "first", aerial_patch_grid, sources, late, early, devices
    )
    normed_early, arriving = lax.optimization_barrier((normed_early, arriving))
    normed_late, feat_late = stem(
        "last", aerial_patch_grid, sources, 0, late, devices, (arriving,)
    )
    spread = [
        lax.all_to_all(normed, DEVICES, split_axis=0, concat_axis=0, tiled=True).reshape(
            -1, field_cols
        )
        for normed in (normed_early, normed_late)
    ]
    late_fields = spread[1]
    features = jnp.concatenate([feat_late, feat_early], axis=0)

    channel_place = jnp.reshape(section * group, (1,)).astype(jnp.int32)
    symmetric = symmetric_filter(spectral_filter, channel_place, group, width)
    *tables, twiddle = filter_tables(full_rows, field_cols, width, devices)
    early_fields, twiddle = repack(spread[0], twiddle, group, devices)
    tables.append(twiddle)

    own = lax.dynamic_slice_in_dim(features, section * half_channels, half_channels, 1)
    sent = lax.dynamic_slice_in_dim(features, (1 - section) * half_channels, half_channels, 1)
    arrived = swap(sent)
    low = jnp.where(section == 0, own, arrived)
    high = jnp.where(section == 0, arrived, own)
    residual = jnp.transpose(jnp.concatenate([low, high], axis=0), (1, 0, 2))
    residual = residual.reshape(half_channels // group, group, tile_rows, field_cols)
    late_fields, residual = lax.optimization_barrier((late_fields, residual))

    halves = devices // 2
    output = None
    rest = group - 2
    per_step = 5 if rest % 5 == 0 else 2
    for first, count, per_step in ((rest, 2, 2), (0, rest, per_step)):
        made = filter_channels(
            late_fields, early_fields, symmetric, tables, first, count, per_step, devices
        )
        returned = lax.all_to_all(made, DEVICES, split_axis=0, concat_axis=0, tiled=True)
        if output is not None:
            returned, output = lax.optimization_barrier((returned, output))
        other = swap(lax.dynamic_slice_in_dim(returned, (1 - section) * halves, halves, 0))
        output = add_residual(returned, other, residual, output, first, count)
    return output.reshape(half_channels, tile_rows, field_cols)


def solution(mesh):
    return jax.shard_map(
        local,
        mesh=mesh,
        in_specs=(
            P("tile", None, None),
            P(),
            P(),
            P(),
            P(),
            P(),
            P(),
            P(),
            P("tile", None, None, None),
        ),
        out_specs=P("section", "tile", None),
        check_vma=False,
    )
```

```python
import functools
import math

import jax
import jax.numpy as jnp
import numpy as np
from jax import lax
from jax.experimental import pallas as pl
from jax.experimental.pallas import tpu as pltpu
from jax.sharding import PartitionSpec as P

EPSILON = 1e-05


def from_behind(block, axis, distance):
    devices = range(lax.axis_size(axis))
    route = [(i - distance, i) for i in devices if i - distance in devices]
    return lax.ppermute(block, axis, route)


def fourier_tables(length, columns=None):
    indices = jnp.arange(length, dtype=jnp.int32)
    columns = indices if columns is None else jnp.asarray(columns, jnp.int32)
    product = indices[:, None] * columns[None, :] % length
    angles = product.astype(jnp.float32) * (2.0 * math.pi / length)
    return (jnp.cos(angles).astype(jnp.bfloat16), jnp.sin(angles).astype(jnp.bfloat16))


def patch_kernel_matrix(patch_conv_weight):
    identity = jnp.eye(4, dtype=jnp.float32)
    larger = jnp.einsum(
        "baqk,xy,uv->bxauqyvk", patch_conv_weight.astype(jnp.float32), identity, identity
    )
    band_count = patch_conv_weight.shape[0]
    width = patch_conv_weight.shape[3]
    return larger.reshape(band_count * 256, 16 * width).astype(jnp.bfloat16)


def merging_kernel_matrix(merging_conv_weight):
    identity = jnp.eye(2, dtype=jnp.float32)
    larger = jnp.einsum(
        "aqjk,xy,uv->xauqjyvk", merging_conv_weight.astype(jnp.float32), identity, identity
    )
    in_width = merging_conv_weight.shape[2]
    out_width = merging_conv_weight.shape[3]
    return larger.reshape(16 * in_width, 4 * out_width).astype(jnp.bfloat16)


def down_matrices(down_weight):
    nothing = jnp.zeros_like(down_weight[0, 0])
    in_width = down_weight.shape[2]
    out_width = down_weight.shape[3]

    def arrange(entries):
        return jnp.stack(
            [jnp.stack(entries[0], axis=0), jnp.stack(entries[1], axis=0)], axis=0
        ).reshape(4 * in_width, out_width)

    own_taps = arrange(
        [[down_weight[1, 1], down_weight[1, 2]], [down_weight[2, 1], down_weight[2, 2]]]
    )
    upper_taps = arrange([[nothing, nothing], [down_weight[0, 1], down_weight[0, 2]]])
    left_taps = arrange([[nothing, down_weight[1, 0]], [nothing, down_weight[2, 0]]])
    corner_taps = arrange([[nothing, nothing], [nothing, down_weight[0, 0]]])
    return (own_taps, upper_taps, left_taps, corner_taps)


def stem_layers(aerial_patch_grid, patch_conv_weight, patch_bias, merging_conv_weight, merge_bias):
    initial_layer = jnp.einsum(
        "zji,if->zjf",
        aerial_patch_grid,
        patch_kernel_matrix(patch_conv_weight),
        preferred_element_type=jnp.float32,
    )
    initial_layer = jax.nn.gelu(initial_layer + jnp.tile(patch_bias, 16), approximate=True).astype(
        jnp.bfloat16
    )
    layer_two = jnp.einsum(
        "zji,if->zjf",
        initial_layer,
        merging_kernel_matrix(merging_conv_weight),
        preferred_element_type=jnp.float32,
    )
    return jax.nn.gelu(layer_two + jnp.tile(merge_bias, 4), approximate=True).astype(jnp.bfloat16)


def rim_above(extended):
    return from_behind(extended[-1:], "tile", 1)


def down_conv(upper_rim, extended, down_weight, down_bias):
    stacked = jnp.concatenate([upper_rim, extended], axis=0)
    own_taps, upper_taps, left_taps, corner_taps = down_matrices(down_weight)
    summed = jnp.einsum(
        "rwk,kc->crw", stacked[1:, 1:], own_taps, preferred_element_type=jnp.float32
    )
    summed = summed + jnp.einsum(
        "rwk,kc->crw", stacked[:-1, 1:], upper_taps, preferred_element_type=jnp.float32
    )
    summed = summed + jnp.einsum(
        "rwk,kc->crw", stacked[1:, :-1], left_taps, preferred_element_type=jnp.float32
    )
    summed = summed + jnp.einsum(
        "rwk,kc->crw", stacked[:-1, :-1], corner_taps, preferred_element_type=jnp.float32
    )
    return (summed + down_bias[:, None, None]).astype(jnp.bfloat16)


def layer_norm(features, norm_gain):
    values = features.astype(jnp.float32)
    mean_value = jnp.mean(values, axis=0, keepdims=True)
    centered = values - mean_value
    variance = jnp.mean(centered * centered, axis=0, keepdims=True)
    return (norm_gain[:, None, None] * centered * lax.rsqrt(variance + EPSILON)).astype(
        jnp.bfloat16
    )


def filter_columns(row_spectrum, kernel, forward_h, inverse_h):
    spectrum = jnp.einsum(
        "puqh,chqw->cpuw", forward_h, row_spectrum, preferred_element_type=jnp.float32
    ).astype(jnp.bfloat16)
    spec_real = spectrum[:, 0].astype(jnp.float32)
    spec_imag = spectrum[:, 1].astype(jnp.float32)
    filter_real = kernel[:, 0].astype(jnp.float32)
    filter_imag = kernel[:, 1].astype(jnp.float32)
    weighted = jnp.stack(
        [
            filter_real * spec_real - filter_imag * spec_imag,
            filter_real * spec_imag + filter_imag * spec_real,
        ],
        axis=1,
    ).astype(jnp.bfloat16)
    return jnp.einsum(
        "qhpu,cpuw->chqw", inverse_h, weighted, preferred_element_type=jnp.float32
    ).astype(jnp.bfloat16)


def general_local(
    aerial_patch_grid,
    patch_conv_weight,
    patch_bias,
    merging_conv_weight,
    merge_bias,
    down_weight,
    down_bias,
    norm_gain,
    spectral_filter,
):
    section_index = lax.axis_index("section")
    first_section = section_index == 0
    field_cols = aerial_patch_grid.shape[1]
    channels = down_weight.shape[3]
    group_width = spectral_filter.shape[0]
    full_rows = spectral_filter.shape[2]
    half_channels = channels // 2
    cell_half = field_cols // 2
    image_part = lax.dynamic_slice_in_dim(
        aerial_patch_grid, section_index * cell_half, cell_half, 1
    )
    layer_two = stem_layers(
        image_part, patch_conv_weight, patch_bias, merging_conv_weight, merge_bias
    )
    left_column = from_behind(layer_two[:, -1:], "section", 1)
    extended = jnp.concatenate([left_column, layer_two], axis=1)
    upper_rim = rim_above(extended)
    feature_half = down_conv(upper_rim, extended, down_weight, down_bias)
    features = lax.all_gather(feature_half, "section", axis=2, tiled=True)
    normed = layer_norm(features, norm_gain)
    cos_h, sin_h = fourier_tables(full_rows)
    cos_w, sin_w = fourier_tables(field_cols)
    forward_table = jnp.stack([cos_w, -sin_w], axis=1)
    forward_h = jnp.stack(
        [jnp.stack([cos_h, sin_h], axis=1), jnp.stack([-sin_h, cos_h], axis=1)], axis=0
    )
    inverse_h = jnp.stack(
        [jnp.stack([cos_h, -sin_h], axis=1), jnp.stack([sin_h, cos_h], axis=1)], axis=0
    )
    inverse_table = jnp.stack([cos_w, -sin_w], axis=0)
    norm_scale = 1.0 / (full_rows * field_cols)
    fields = lax.all_to_all(normed, "tile", split_axis=0, concat_axis=1, tiled=True)

    def whole_filter():
        frequency_rows = jnp.einsum(
            "chx,xqw->chqw", fields, forward_table, preferred_element_type=jnp.float32
        ).astype(jnp.bfloat16)
        back_rows = filter_columns(frequency_rows, spectral_filter, forward_h, inverse_h)
        result = jnp.einsum(
            "chqw,qwv->chv", back_rows, inverse_table, preferred_element_type=jnp.float32
        )
        return (result * norm_scale).astype(jnp.bfloat16)

    def empty_fields():
        return jnp.zeros((group_width, full_rows, field_cols), jnp.bfloat16)

    filtered_fields = lax.cond(first_section, empty_fields, whole_filter)
    rows_back = lax.all_to_all(filtered_fields, "tile", split_axis=1, concat_axis=0, tiled=True)
    returned = from_behind(rows_back[:half_channels], "section", -1)
    filtered = jnp.where(first_section, returned, rows_back[half_channels:])
    own_part = lax.dynamic_slice_in_dim(features, section_index * half_channels, half_channels, 0)
    return (own_part.astype(jnp.float32) + filtered.astype(jnp.float32)).astype(jnp.bfloat16)


DEVICES = ("tile", "section")
VMEM_BYTES = 60 * 1024 * 1024
GELU_LINEAR = 2.0 * math.sqrt(2.0 / math.pi)
GELU_CUBIC = 4.0 * 0.044715 * GELU_LINEAR
ONES = (64, 128, 64)
TAPS = ((1, 1), (1, 2), (2, 1), (2, 2), (1, 0), (2, 0), (0, 1), (0, 2), (0, 0))


def bias_rows(bias, count):
    high = bias.astype(jnp.bfloat16)
    rest = bias - high.astype(jnp.float32)
    middle = rest.astype(jnp.bfloat16)
    low = (rest - middle.astype(jnp.float32)).astype(jnp.bfloat16)
    shape = (count, bias.shape[1])
    row = lax.broadcasted_iota(jnp.int32, shape, 0)
    rows = jnp.zeros(shape, jnp.float32)
    for k, part in enumerate((high, middle, low)):
        rows = jnp.where(row == k, jnp.broadcast_to(part.astype(jnp.float32), shape), rows)
    return rows.astype(jnp.bfloat16)


def build_weights(sources, targets):
    patch_ref, patch_bias_ref, merge_ref, merge_bias_ref, down_ref, down_bias_ref, gain_ref = sources
    w1_ref, w2_ref, w3_ref, column_ref = targets

    def exact(a, b):
        return jnp.dot(
            a.astype(jnp.bfloat16), b.astype(jnp.bfloat16), preferred_element_type=jnp.float32
        )

    taps, width = patch_ref.shape
    row = lax.broadcasted_iota(jnp.int32, (4 * taps, taps), 0)
    col = lax.broadcasted_iota(jnp.int32, (4 * taps, taps), 1)
    pick = jnp.where(row // 16 * 4 + row % 4 == col, 1.0, 0.0)
    row = lax.broadcasted_iota(jnp.int32, (width, 4 * width), 0)
    col = lax.broadcasted_iota(jnp.int32, (width, 4 * width), 1)
    repeat = jnp.where(col % width == row, 1.0, 0.0)
    spread = exact(pick, exact(patch_ref[...], repeat))
    row = lax.broadcasted_iota(jnp.int32, spread.shape, 0)
    col = lax.broadcasted_iota(jnp.int32, spread.shape, 1)
    spread = jnp.where(row // 4 % 4 == col // width, 0.5 * spread, 0.0).astype(jnp.bfloat16)
    bias = jnp.broadcast_to(0.5 * patch_bias_ref[...][None], (8, width))
    tiled = jnp.zeros((8, 4 * width), jnp.float32)
    for _ in range(3):
        part = bias.astype(jnp.bfloat16).astype(jnp.float32)
        tiled = tiled + exact(part, repeat)
        bias = bias - part
    first = jnp.concatenate([spread, bias_rows(tiled[:1], ONES[0])], axis=0)
    w1_ref[...] = first.T
    half = (merge_ref[...].astype(jnp.float32) * 0.5).astype(jnp.bfloat16)
    second = jnp.concatenate([half, bias_rows(0.5 * merge_bias_ref[...][None], ONES[1])], axis=0)
    w2_ref[...] = second.T
    third = [down_ref[3 * a + q] for a, q in TAPS]
    third = jnp.concatenate(third + [bias_rows(down_bias_ref[...][None], ONES[2])], axis=0)
    w3_ref[...] = third.T
    column_ref[...] = jnp.broadcast_to(gain_ref[...][None], (128, gain_ref.shape[0])).T


def weight_sources(
    patch_conv_weight, patch_bias, merging_conv_weight, merge_bias, down_weight, down_bias,
    norm_gain,
):
    width = patch_conv_weight.shape[3]
    merged = merging_conv_weight.shape[3]
    return [
        patch_conv_weight.reshape(-1, width),
        patch_bias,
        merging_conv_weight.reshape(-1, merged),
        merge_bias,
        down_weight.reshape(-1, merged, down_weight.shape[3]),
        down_bias,
        norm_gain,
    ]


def weight_shapes(sources):
    taps, width = sources[0].shape
    merged, channels = sources[4].shape[1:]
    return [
        jax.ShapeDtypeStruct((4 * width, 4 * taps + ONES[0]), jnp.bfloat16),
        jax.ShapeDtypeStruct((merged, 4 * width + ONES[1]), jnp.bfloat16),
        jax.ShapeDtypeStruct((channels, 9 * merged + ONES[2]), jnp.bfloat16),
        jax.ShapeDtypeStruct((channels, 128), jnp.float32),
    ]


def half_gelu(h):
    return h + h * jnp.tanh(h * (GELU_LINEAR + GELU_CUBIC * (h * h)))


def lower_half(row):
    depth = row.shape[1]
    return jnp.concatenate(
        [row[:, 256 * b + 128 : 256 * b + 256] for b in range(depth // 256)], axis=1
    )


def stem_kernel(kind, x_ref, above_ref, *refs):
    sources = refs[:7]
    normed_ref, feat_ref, w1_ref, w2_ref, w3_ref, gain_ref, field = refs[-7:]
    step = pl.program_id(0)
    rows, cols, depth = x_ref.shape
    bands = depth // 256
    channels = w3_ref.shape[0]
    merged = w2_ref.shape[0]
    group = normed_ref.shape[2] // 2
    cells = rows * cols

    @pl.when(step == 0)
    def _():
        build_weights(sources, (w1_ref, w2_ref, w3_ref, gain_ref))

    w1 = w1_ref[...]
    w2 = w2_ref[...]

    def ones(count, n):
        return jnp.where(lax.broadcasted_iota(jnp.int32, (count, n), 0) < 3, 1.0, 0.0).astype(
            jnp.bfloat16
        )

    def layer_one(turned, offsets):
        n = turned.shape[1]
        parts = [turned[o : o + 64] for o in offsets] + [ones(ONES[0], n)]
        h = jnp.dot(w1, jnp.concatenate(parts, axis=0), preferred_element_type=jnp.float32)
        return half_gelu(h).astype(jnp.bfloat16)

    def layer_two(upper, lower, y):
        n = upper.shape[1]
        span = slice(2 * y * (w1.shape[0] // 4), 2 * (y + 1) * (w1.shape[0] // 4))
        stacked = jnp.concatenate([upper[span], lower[span], ones(ONES[1], n)], axis=0)
        return half_gelu(jnp.dot(w2, stacked, preferred_element_type=jnp.float32))

    def shifted(values):
        lanes = lax.broadcasted_iota(jnp.int32, values.shape, 1)
        moved = pltpu.roll(values, 1, 1)
        return jnp.where(lax.rem(lanes, cols) == 0, 0.0, moved)

    def put(block, lanes, values):
        field[block * merged : (block + 1) * merged, lanes] = values.astype(jnp.bfloat16)

    first_row = slice(0, cols)
    last_row = slice(cells - cols, cells)
    later_rows = slice(cols, cells)
    earlier_rows = slice(0, cells - cols)

    @pl.when(step == 0)
    def _():
        field[9 * merged :, :] = ones(ONES[2], cells)
        above = lower_half(above_ref[0])
        keep = 1.0
        if kind == "last":
            lower_section = lax.axis_index("section") > 0
            inside = lower_section | (lax.axis_index("tile") > 0)
            keep = jnp.where(inside, 1.0, 0.0)
            above = jnp.where(lower_section, above, refs[7][...])
        turned = above.T
        upper, lower = (
            layer_one(turned, [128 * b + 64 * a for b in range(bands)]) for a in range(2)
        )
        put(6, first_row, layer_two(upper, lower, 0) * keep)
        right = layer_two(upper, lower, 1) * keep
        put(7, first_row, right)
        put(8, first_row, shifted(right))

    @pl.when(step > 0)
    def _():
        for source, target in ((2, 6), (3, 7), (5, 8)):
            field[target * merged : (target + 1) * merged, first_row] = field[
                source * merged : (source + 1) * merged, last_row
            ]

    turned = x_ref[...].reshape(cells, depth).T
    for x in range(2):
        upper, lower = (
            layer_one(turned, [256 * b + 64 * (2 * x + a) for b in range(bands)])
            for a in range(2)
        )
        left = layer_two(upper, lower, 0)
        right = layer_two(upper, lower, 1)
        put(2 * x, slice(None), left)
        put(2 * x + 1, slice(None), right)
        moved = shifted(right)
        put(4 + x, slice(None), moved)
        if x == 1:
            put(6, later_rows, left[:, earlier_rows])
            put(7, later_rows, right[:, earlier_rows])
            put(8, later_rows, moved[:, earlier_rows])

    features = jnp.dot(w3_ref[...], field[...], preferred_element_type=jnp.float32).astype(
        jnp.bfloat16
    )
    for r in range(rows):
        feat_ref[r] = features[:, r * cols : (r + 1) * cols]
    values = features.astype(jnp.float32)
    centered = values - jnp.mean(values, axis=0, keepdims=True)
    variance = jnp.mean(centered * centered, axis=0, keepdims=True)
    gain = jnp.concatenate([gain_ref[...]] * (cells // 128), axis=1)
    normed = gain * (centered * lax.rsqrt(variance + EPSILON))
    pair = 2 * group
    index = lax.broadcasted_iota(jnp.int32, (pair, cols), 0)
    for t in range(channels // pair):
        for p in range(rows // 2):
            span = slice(pair * t, pair * (t + 1))
            one = normed[span, 2 * p * cols : (2 * p + 1) * cols]
            two = normed[span, (2 * p + 1) * cols : (2 * p + 2) * cols]
            normed_ref[2 * t, p] = jnp.where(
                index < group, one, pltpu.roll(two, group, 0)
            ).astype(jnp.bfloat16)
            normed_ref[2 * t + 1, p] = jnp.where(
                index < group, pltpu.roll(one, group, 0), two
            ).astype(jnp.bfloat16)


def stem(kind, image, weights, first, pairs, devices, extra=()):
    cols, depth = image.shape[1:]
    rows = 2 * pairs
    per_step = 1
    if kind == "first" and all(n % 2 == 0 for n in (pairs, first, image.shape[0] // 4)):
        per_step = 2
    steps = pairs // per_step
    span = 2 * per_step
    shapes = weight_shapes(weights)
    channels, third_depth = shapes[2].shape
    merged = shapes[1].shape[0]
    group = channels // devices

    def section_pairs():
        return lax.axis_index("section") * (image.shape[0] // 4)

    def whole(array):
        return pl.BlockSpec(array.shape, lambda i: (0,) * len(array.shape))

    operands = list(weights) + list(extra)
    in_specs = [whole(a) for a in weights]
    out_specs = [
        pl.BlockSpec((devices, per_step, 2 * group, cols), lambda i: (0, i, 0, 0)),
        pl.BlockSpec((span, channels, cols), lambda i: (i, 0, 0)),
    ]
    out_shape = [
        jax.ShapeDtypeStruct((devices, pairs, 2 * group, cols), jnp.bfloat16),
        jax.ShapeDtypeStruct((rows, channels, cols), jnp.bfloat16),
    ]
    in_specs += [whole(a) for a in extra]
    macs = rows * cols * (16 * 208 * 96 + 4 * 400 * merged + third_depth * channels)
    return pl.pallas_call(
        functools.partial(stem_kernel, kind),
        grid=(steps,),
        in_specs=[
            pl.BlockSpec(
                (span, cols, depth),
                lambda i: ((section_pairs() + first) // per_step + i, 0, 0),
            ),
            pl.BlockSpec(
                (1, cols, depth),
                lambda i: (jnp.maximum(2 * (section_pairs() + first) - 1, 0), 0, 0),
            ),
        ]
        + in_specs,
        out_specs=out_specs,
        scratch_shapes=[pltpu.VMEM(a.shape, a.dtype) for a in shapes]
        + [pltpu.VMEM((third_depth, span * cols), jnp.bfloat16)],
        out_shape=out_shape,
        compiler_params=pltpu.CompilerParams(vmem_limit_bytes=VMEM_BYTES + 3 * 1024 * 1024),
        cost_estimate=pl.CostEstimate(
            flops=4 * macs, bytes_accessed=rows * cols * 3000, transcendentals=0
        ),
        name="stem",
    )(image, image, *operands)


def symmetric_kernel(place_ref, f_ref, turn_w_ref, turn_u_ref, g_ref):
    width = g_ref.shape[3]
    for part in range(2):
        block = f_ref[0, part]
        across = jnp.dot(block, turn_w_ref[...], preferred_element_type=jnp.float32)
        turned = jnp.dot(
            turn_u_ref[...], across.astype(jnp.bfloat16), preferred_element_type=jnp.float32
        )
        own = block[:, :width].astype(jnp.float32)
        both = own + turned if part == 0 else own - turned
        g_ref[0, part] = (0.5 * both).astype(jnp.bfloat16)


def symmetric_filter(spectral_filter, place, group, width):
    full_rows, full_cols = spectral_filter.shape[2:]
    u = jnp.arange(full_rows, dtype=jnp.int32)
    w = jnp.arange(full_cols, dtype=jnp.int32)
    turn_u = ((u[:, None] + u[None, :]) % full_rows == 0).astype(jnp.bfloat16)
    turn_w = ((w[:, None] + w[None, :width]) % full_cols == 0).astype(jnp.bfloat16)
    return pl.pallas_call(
        symmetric_kernel,
        grid_spec=pltpu.PrefetchScalarGridSpec(
            num_scalar_prefetch=1,
            grid=(group,),
            in_specs=[
                pl.BlockSpec(
                    (1, 2, full_rows, full_cols), lambda i, place: (place[0] + i, 0, 0, 0)
                ),
                pl.BlockSpec(turn_w.shape, lambda i, place: (0, 0)),
                pl.BlockSpec(turn_u.shape, lambda i, place: (0, 0)),
            ],
            out_specs=pl.BlockSpec((1, 2, full_rows, width), lambda i, place: (i, 0, 0, 0)),
        ),
        out_shape=jax.ShapeDtypeStruct((group, 2, full_rows, width), jnp.bfloat16),
        compiler_params=pltpu.CompilerParams(vmem_limit_bytes=VMEM_BYTES),
        cost_estimate=pl.CostEstimate(
            flops=8 * group * full_rows * full_cols * width,
            bytes_accessed=group * full_rows * width * 14,
            transcendentals=0,
        ),
        name="symmetric_filter",
    )(place, spectral_filter, turn_w, turn_u)


def to_lane_tiles(target, rows, values):
    for j in range(target.shape[0]):
        target[j, rows, :] = values[:, 128 * j : 128 * (j + 1)]


def from_lane_tiles(source, rows):
    return jnp.concatenate([source[j, rows, :] for j in range(source.shape[0])], axis=1)


RADIX = 3
HALF_ROOT = math.sqrt(3.0) / 2.0


def repack_kernel(devices, early_ref, twiddle_ref, out_ref, turn_ref, held):
    group, length = out_ref.shape[:2]
    turn_ref[...] = twiddle_ref[...]
    rows = length // devices
    to_lane_tiles(held, slice(0, early_ref.shape[0]), early_ref[...].astype(jnp.float32))
    for k in range(group):
        for r in range(rows):
            values = from_lane_tiles(held, pl.ds(r * group + k, devices, stride=rows * group))
            out_ref[k, r * devices : (r + 1) * devices] = values.astype(jnp.bfloat16)


def repack(early, twiddle, group, devices):
    length, cols = early.shape
    return pl.pallas_call(
        functools.partial(repack_kernel, devices),
        out_shape=[
            jax.ShapeDtypeStruct((group, length // group, cols), jnp.bfloat16),
            jax.ShapeDtypeStruct(twiddle.shape, twiddle.dtype),
        ],
        scratch_shapes=[pltpu.VMEM((cols // 128, length + length // devices, 128), jnp.float32)],
        compiler_params=pltpu.CompilerParams(vmem_limit_bytes=VMEM_BYTES),
        cost_estimate=pl.CostEstimate(
            flops=length * cols, bytes_accessed=4 * length * cols, transcendentals=0
        ),
        name="repack",
    )(early, twiddle)


def thirds(values, sign):
    (re0, im0), (re1, im1), (re2, im2) = values
    sum_re, sum_im = re1 + re2, im1 + im2
    turn_re, turn_im = HALF_ROOT * sign * (im1 - im2), HALF_ROOT * sign * (re2 - re1)
    rest_re, rest_im = re0 - 0.5 * sum_re, im0 - 0.5 * sum_im
    return (
        (re0 + sum_re, im0 + sum_im),
        (rest_re + turn_re, rest_im + turn_im),
        (rest_re - turn_re, rest_im - turn_im),
    )


def filter_kernel(
    first, devices, norm_scale, late_ref, early_ref, g_ref, row_table_ref, fwd_ref, inv_ref,
    back_ref, twiddle_ref, out_ref, held, made,
):
    step = pl.program_id(0)
    third = fwd_ref.shape[0] // 2
    full_rows = RADIX * third
    width = g_ref.shape[3]
    count = out_ref.shape[0] // full_rows
    per_step = g_ref.shape[0]
    early = early_ref.shape[1] // devices
    late = full_rows // devices - early
    group = late_ref.shape[0] // (late * devices)

    @pl.when(step == 0)
    def _():
        to_lane_tiles(held, slice(0, late_ref.shape[0]), late_ref[...].astype(jnp.float32))

    def source_rows(k, row):
        if row >= late:
            begin = (row - late) * devices
            return early_ref[k, begin : begin + devices]
        begin = row * group + first + step * per_step + k
        values = from_lane_tiles(held, pl.ds(begin, devices, stride=late * group))
        return values.astype(jnp.bfloat16)

    def twiddles(r):
        cos, sin = twiddle_ref[2 * r - 2], twiddle_ref[2 * r - 1]
        times = per_step * width // 128
        return jnp.concatenate([cos] * times, axis=1), jnp.concatenate([sin] * times, axis=1)

    fields = []
    for k in range(per_step):
        rows = [
            source_rows(k, r + RADIX * q)
            for r in range(RADIX)
            for q in range((late + early) // RADIX)
        ]
        spread = jnp.dot(
            jnp.concatenate(rows, axis=0), row_table_ref[...], preferred_element_type=jnp.float32
        )
        fields.append(spread.astype(jnp.bfloat16))
    parts = []
    for r in range(RADIX):
        span = slice(r * third, (r + 1) * third)
        block = jnp.concatenate(
            [
                jnp.concatenate([f[span, :width], f[span, width:]], axis=0)
                for f in fields
            ],
            axis=1,
        )
        short = jnp.dot(fwd_ref[...], block, preferred_element_type=jnp.float32)
        real, imag = short[:third], short[third:]
        if r > 0:
            cos, sin = twiddles(r)
            real, imag = real * cos + imag * sin, imag * cos - real * sin
        parts.append((real, imag))
    weighted = []
    for r, (real, imag) in enumerate(thirds(parts, 1.0)):
        span = slice(r * third, (r + 1) * third)
        g_real, g_imag = (
            jnp.concatenate([g_ref[k, p, span] for k in range(per_step)], axis=1).astype(
                jnp.float32
            )
            for p in range(2)
        )
        weighted.append((g_real * real - g_imag * imag, g_real * imag + g_imag * real))
    for r, (real, imag) in enumerate(thirds(weighted, -1.0)):
        if r > 0:
            cos, sin = twiddles(r)
            real, imag = real * cos - imag * sin, imag * cos + real * sin
        block = jnp.concatenate([real, imag], axis=0).astype(jnp.bfloat16)
        back = jnp.dot(inv_ref[...], block, preferred_element_type=jnp.float32).astype(
            jnp.bfloat16
        )
        for k in range(per_step):
            lanes = slice(k * width, (k + 1) * width)
            both = jnp.concatenate([back[:third, lanes], back[third:, lanes]], axis=1)
            result = jnp.dot(both, back_ref[...], preferred_element_type=jnp.float32)
            rows = pl.ds(r * count + step * per_step + k, third, stride=RADIX * count)
            to_lane_tiles(made, rows, result * norm_scale)

    @pl.when(step == pl.num_programs(0) - 1)
    def _():
        out_ref[...] = from_lane_tiles(made, slice(0, out_ref.shape[0])).astype(jnp.bfloat16)


def filter_tables(full_rows, field_cols, width, devices):
    third = full_rows // RADIX
    per_device = third // devices
    order = (per_device * np.arange(devices)[None, :] + np.arange(per_device)[:, None]).reshape(-1)
    cos_h, sin_h = fourier_tables(third)
    cos_f, sin_f = fourier_tables(third, order.astype(np.int32))
    cos_w, sin_w = fourier_tables(field_cols)
    fwd = jnp.concatenate(
        [jnp.concatenate([cos_f, sin_f], 1), jnp.concatenate([-sin_f, cos_f], 1)], 0
    )
    inv = jnp.concatenate(
        [jnp.concatenate([cos_h, -sin_h], 1), jnp.concatenate([sin_h, cos_h], 1)], 0
    )
    w = jnp.arange(width, dtype=jnp.int32)
    half = field_cols // 2
    valid = (w <= half).astype(jnp.bfloat16)
    times = jnp.where((w == 0) | (w == half), 1.0, 2.0).astype(jnp.bfloat16) * valid
    row_table = jnp.concatenate([cos_w[:, :width] * valid, -sin_w[:, :width] * valid], 1)
    back_table = jnp.concatenate(
        [cos_w[:width] * times[:, None], -sin_w[:width] * times[:, None]], 0
    )
    turns = np.arange(1, RADIX)[:, None] * np.arange(third)[None, :]
    angles = turns * (2.0 * math.pi / full_rows)
    twiddle = np.stack([np.cos(angles), np.sin(angles)], axis=1).reshape(-1, third, 1)
    twiddle = np.broadcast_to(twiddle.astype(np.float32), (2 * RADIX - 2, third, 128))
    twiddle = jnp.asarray(twiddle)
    return row_table, fwd, inv, back_table, twiddle


def filter_channels(late, early, symmetric, tables, first, count, per_step, devices):
    full_rows, width = symmetric.shape[2:]
    group, early_rows = early.shape[:2]
    cols = late.shape[1]

    def whole(array):
        return pl.BlockSpec(array.shape, lambda i: (0,) * array.ndim)

    macs = count * (4 * full_rows * full_rows * width + 4 * full_rows * cols * width)
    made = pl.pallas_call(
        functools.partial(filter_kernel, first, devices, 1.0 / (full_rows * cols)),
        grid=(count // per_step,),
        in_specs=[
            whole(late),
            pl.BlockSpec((per_step, early_rows, cols), lambda i: (first // per_step + i, 0, 0)),
            pl.BlockSpec(
                (per_step, 2, full_rows, width), lambda i: (first // per_step + i, 0, 0, 0)
            ),
        ]
        + [whole(table) for table in tables],
        out_specs=pl.BlockSpec((full_rows * count, cols), lambda i: (0, 0)),
        out_shape=jax.ShapeDtypeStruct((full_rows * count, cols), jnp.bfloat16),
        scratch_shapes=[
            pltpu.VMEM((cols // 128, late.shape[0] + late.shape[0] // devices, 128), jnp.float32),
            pltpu.VMEM((cols // 128, (full_rows + 8) * count, 128), jnp.float32),
        ],
        compiler_params=pltpu.CompilerParams(vmem_limit_bytes=VMEM_BYTES),
        cost_estimate=pl.CostEstimate(
            flops=2 * macs, bytes_accessed=count * full_rows * cols * 8, transcendentals=0
        ),
        name="spectral_filter",
    )(late, early, symmetric, *tables)
    return made.reshape(devices, full_rows // devices * count, cols)


def residual_kernel(first, count, chunks, kept_hbm, other_hbm, feat_hbm, *refs):
    out_hbm, kept, other, feat, out, held, done = refs[-7:]
    halves, span = other.shape[:2]
    rows = 2 * span // count
    groups = halves // chunks
    section = lax.axis_index("section")

    def block(c):
        return pl.ds(c * groups, groups)

    def copies(c):
        source = pl.ds(section * halves + c * groups, groups)
        channels = pl.ds(first, count)
        return [
            pltpu.make_async_copy(kept_hbm.at[source], kept.at[block(c)], done.at[0, c]),
            pltpu.make_async_copy(other_hbm.at[block(c)], other.at[block(c)], done.at[1, c]),
            pltpu.make_async_copy(
                feat_hbm.at[block(c), channels], feat.at[block(c)], done.at[2, c]
            ),
        ]

    def result(c):
        channels = pl.ds(first, count)
        return pltpu.make_async_copy(
            out.at[block(c)], out_hbm.at[block(c), channels], done.at[3, c]
        )

    for c in range(chunks):
        for copy in copies(c):
            copy.start()
    own = pl.multiple_of(section * span, 8)
    far = pl.multiple_of((1 - section) * span, 8)
    for c in range(chunks):
        for copy in copies(c):
            copy.wait()
        for g in range(c * groups, (c + 1) * groups):
            to_lane_tiles(held, pl.ds(own, span), kept[g].astype(jnp.float32))
            to_lane_tiles(held, pl.ds(far, span), other[g].astype(jnp.float32))
            for k in range(count):
                filtered = from_lane_tiles(held, pl.ds(k, rows, stride=count))
                out[g, k] = (feat[g, k].astype(jnp.float32) + filtered).astype(jnp.bfloat16)
        result(c).start()
    for c in range(chunks):
        result(c).wait()


def add_residual(returned, other, features, previous, first, count):
    halves, span, cols = other.shape
    group, rows = features.shape[1:3]
    chunks = 4 if halves % 4 == 0 else 1
    operands = [returned, other, features]
    aliases = {}
    if previous is not None:
        operands.append(previous)
        aliases = {3: 0}
    return pl.pallas_call(
        functools.partial(residual_kernel, first, count, chunks),
        in_specs=[pl.BlockSpec(memory_space=pl.ANY)] * len(operands),
        out_specs=pl.BlockSpec(memory_space=pl.ANY),
        scratch_shapes=[
            pltpu.VMEM((halves, span, cols), jnp.bfloat16),
            pltpu.VMEM((halves, span, cols), jnp.bfloat16),
            pltpu.VMEM((halves, count, rows, cols), jnp.bfloat16),
            pltpu.VMEM((halves, count, rows, cols), jnp.bfloat16),
            pltpu.VMEM((cols // 128, (rows + 8) * count, 128), jnp.float32),
            pltpu.SemaphoreType.DMA((4, chunks)),
        ],
        out_shape=jax.ShapeDtypeStruct(features.shape, jnp.bfloat16),
        input_output_aliases=aliases,
        compiler_params=pltpu.CompilerParams(vmem_limit_bytes=VMEM_BYTES if previous is None else VMEM_BYTES // 4),
        cost_estimate=pl.CostEstimate(
            flops=halves * count * rows * cols,
            bytes_accessed=halves * count * rows * cols * 8,
            transcendentals=0,
        ),
        name="residual",
    )(*operands)


def swap(block):
    return lax.ppermute(block, "section", [(0, 1), (1, 0)])


def local(
    aerial_patch_grid,
    patch_conv_weight,
    patch_bias,
    merging_conv_weight,
    merge_bias,
    down_weight,
    down_bias,
    norm_gain,
    spectral_filter,
):
    tile_rows, field_cols, depth = aerial_patch_grid.shape
    channels = down_weight.shape[3]
    tile_channels = spectral_filter.shape[0]
    full_rows = spectral_filter.shape[2]
    sections = lax.axis_size("section")
    devices = sections * lax.axis_size("tile")
    rows = tile_rows // 2
    suits = (
        sections == 2
        and tile_rows % 8 == 0
        and tile_rows >= 16
        and field_cols % 128 == 0
        and full_rows % (128 * RADIX) == 0
        and rows % RADIX == 0
        and devices % 8 == 0
        and tile_channels % 8 == 0
    )
    arguments = (
        aerial_patch_grid,
        patch_conv_weight,
        patch_bias,
        merging_conv_weight,
        merge_bias,
        down_weight,
        down_bias,
        norm_gain,
        spectral_filter,
    )
    if not suits:
        return general_local(*arguments)
    section = lax.axis_index("section")
    group = tile_channels // 2
    half_channels = channels // 2
    width = -(-(field_cols // 2 + 1) // 128) * 128

    arriving = lax.ppermute(
        lower_half(aerial_patch_grid[-1]),
        ("section", "tile"),
        [(i, i + 1) for i in range(lax.axis_size("tile") - 1)],
    )
    sources = weight_sources(*arguments[1:8])
    pairs = rows // 2
    early = max(pairs // 3, 1)
    late = pairs - early
    normed_early, feat_early = stem(
        "first", aerial_patch_grid, sources, late, early, devices
    )
    normed_early, arriving = lax.optimization_barrier((normed_early, arriving))
    normed_late, feat_late = stem(
        "last", aerial_patch_grid, sources, 0, late, devices, (arriving,)
    )
    spread = [
        lax.all_to_all(normed, DEVICES, split_axis=0, concat_axis=0, tiled=True).reshape(
            -1, field_cols
        )
        for normed in (normed_early, normed_late)
    ]
    late_fields = spread[1]
    features = jnp.concatenate([feat_late, feat_early], axis=0)

    channel_place = jnp.reshape(section * group, (1,)).astype(jnp.int32)
    symmetric = symmetric_filter(spectral_filter, channel_place, group, width)
    *tables, twiddle = filter_tables(full_rows, field_cols, width, devices)
    early_fields, twiddle = repack(spread[0], twiddle, group, devices)
    tables.append(twiddle)

    own = lax.dynamic_slice_in_dim(features, section * half_channels, half_channels, 1)
    sent = lax.dynamic_slice_in_dim(features, (1 - section) * half_channels, half_channels, 1)
    arrived = swap(sent)
    low = jnp.where(section == 0, own, arrived)
    high = jnp.where(section == 0, arrived, own)
    residual = jnp.transpose(jnp.concatenate([low, high], axis=0), (1, 0, 2))
    residual = residual.reshape(half_channels // group, group, tile_rows, field_cols)
    late_fields, residual = lax.optimization_barrier((late_fields, residual))

    halves = devices // 2
    output = None
    rest = group - 2
    per_step = 5 if rest % 5 == 0 else 2
    for first, count, per_step in ((rest, 2, 2), (0, rest, per_step)):
        made = filter_channels(
            late_fields, early_fields, symmetric, tables, first, count, per_step, devices
        )
        returned = lax.all_to_all(made, DEVICES, split_axis=0, concat_axis=0, tiled=True)
        if output is not None:
            returned, output = lax.optimization_barrier((returned, output))
        other = swap(lax.dynamic_slice_in_dim(returned, (1 - section) * halves, halves, 0))
        output = add_residual(returned, other, residual, output, first, count)
    return output.reshape(half_channels, tile_rows, field_cols)


def solution(mesh):
    return jax.shard_map(
        local,
        mesh=mesh,
        in_specs=(
            P("tile", None, None),
            P(),
            P(),
            P(),
            P(),
            P(),
            P(),
            P(),
            P("tile", None, None, None),
        ),
        out_specs=P("section", "tile", None),
        check_vma=False,
    )
```

```python
import functools
import math

import jax
import jax.numpy as jnp
import numpy as np
from jax import lax
from jax.experimental import pallas as pl
from jax.experimental.pallas import tpu as pltpu
from jax.sharding import PartitionSpec as P

EPSILON = 1e-05


def from_behind(block, axis, distance):
    devices = range(lax.axis_size(axis))
    route = [(i - distance, i) for i in devices if i - distance in devices]
    return lax.ppermute(block, axis, route)


def fourier_tables(length, columns=None):
    indices = jnp.arange(length, dtype=jnp.int32)
    columns = indices if columns is None else jnp.asarray(columns, jnp.int32)
    product = indices[:, None] * columns[None, :] % length
    angles = product.astype(jnp.float32) * (2.0 * math.pi / length)
    return (jnp.cos(angles).astype(jnp.bfloat16), jnp.sin(angles).astype(jnp.bfloat16))


def patch_kernel_matrix(patch_conv_weight):
    identity = jnp.eye(4, dtype=jnp.float32)
    larger = jnp.einsum(
        "baqk,xy,uv->bxauqyvk", patch_conv_weight.astype(jnp.float32), identity, identity
    )
    band_count = patch_conv_weight.shape[0]
    width = patch_conv_weight.shape[3]
    return larger.reshape(band_count * 256, 16 * width).astype(jnp.bfloat16)


def merging_kernel_matrix(merging_conv_weight):
    identity = jnp.eye(2, dtype=jnp.float32)
    larger = jnp.einsum(
        "aqjk,xy,uv->xauqjyvk", merging_conv_weight.astype(jnp.float32), identity, identity
    )
    in_width = merging_conv_weight.shape[2]
    out_width = merging_conv_weight.shape[3]
    return larger.reshape(16 * in_width, 4 * out_width).astype(jnp.bfloat16)


def down_matrices(down_weight):
    nothing = jnp.zeros_like(down_weight[0, 0])
    in_width = down_weight.shape[2]
    out_width = down_weight.shape[3]

    def arrange(entries):
        return jnp.stack(
            [jnp.stack(entries[0], axis=0), jnp.stack(entries[1], axis=0)], axis=0
        ).reshape(4 * in_width, out_width)

    own_taps = arrange(
        [[down_weight[1, 1], down_weight[1, 2]], [down_weight[2, 1], down_weight[2, 2]]]
    )
    upper_taps = arrange([[nothing, nothing], [down_weight[0, 1], down_weight[0, 2]]])
    left_taps = arrange([[nothing, down_weight[1, 0]], [nothing, down_weight[2, 0]]])
    corner_taps = arrange([[nothing, nothing], [nothing, down_weight[0, 0]]])
    return (own_taps, upper_taps, left_taps, corner_taps)


def stem_layers(aerial_patch_grid, patch_conv_weight, patch_bias, merging_conv_weight, merge_bias):
    initial_layer = jnp.einsum(
        "zji,if->zjf",
        aerial_patch_grid,
        patch_kernel_matrix(patch_conv_weight),
        preferred_element_type=jnp.float32,
    )
    initial_layer = jax.nn.gelu(initial_layer + jnp.tile(patch_bias, 16), approximate=True).astype(
        jnp.bfloat16
    )
    layer_two = jnp.einsum(
        "zji,if->zjf",
        initial_layer,
        merging_kernel_matrix(merging_conv_weight),
        preferred_element_type=jnp.float32,
    )
    return jax.nn.gelu(layer_two + jnp.tile(merge_bias, 4), approximate=True).astype(jnp.bfloat16)


def rim_above(extended):
    return from_behind(extended[-1:], "tile", 1)


def down_conv(upper_rim, extended, down_weight, down_bias):
    stacked = jnp.concatenate([upper_rim, extended], axis=0)
    own_taps, upper_taps, left_taps, corner_taps = down_matrices(down_weight)
    summed = jnp.einsum(
        "rwk,kc->crw", stacked[1:, 1:], own_taps, preferred_element_type=jnp.float32
    )
    summed = summed + jnp.einsum(
        "rwk,kc->crw", stacked[:-1, 1:], upper_taps, preferred_element_type=jnp.float32
    )
    summed = summed + jnp.einsum(
        "rwk,kc->crw", stacked[1:, :-1], left_taps, preferred_element_type=jnp.float32
    )
    summed = summed + jnp.einsum(
        "rwk,kc->crw", stacked[:-1, :-1], corner_taps, preferred_element_type=jnp.float32
    )
    return (summed + down_bias[:, None, None]).astype(jnp.bfloat16)


def layer_norm(features, norm_gain):
    values = features.astype(jnp.float32)
    mean_value = jnp.mean(values, axis=0, keepdims=True)
    centered = values - mean_value
    variance = jnp.mean(centered * centered, axis=0, keepdims=True)
    return (norm_gain[:, None, None] * centered * lax.rsqrt(variance + EPSILON)).astype(
        jnp.bfloat16
    )


def filter_columns(row_spectrum, kernel, forward_h, inverse_h):
    spectrum = jnp.einsum(
        "puqh,chqw->cpuw", forward_h, row_spectrum, preferred_element_type=jnp.float32
    ).astype(jnp.bfloat16)
    spec_real = spectrum[:, 0].astype(jnp.float32)
    spec_imag = spectrum[:, 1].astype(jnp.float32)
    filter_real = kernel[:, 0].astype(jnp.float32)
    filter_imag = kernel[:, 1].astype(jnp.float32)
    weighted = jnp.stack(
        [
            filter_real * spec_real - filter_imag * spec_imag,
            filter_real * spec_imag + filter_imag * spec_real,
        ],
        axis=1,
    ).astype(jnp.bfloat16)
    return jnp.einsum(
        "qhpu,cpuw->chqw", inverse_h, weighted, preferred_element_type=jnp.float32
    ).astype(jnp.bfloat16)


def general_local(
    aerial_patch_grid,
    patch_conv_weight,
    patch_bias,
    merging_conv_weight,
    merge_bias,
    down_weight,
    down_bias,
    norm_gain,
    spectral_filter,
):
    section_index = lax.axis_index("section")
    first_section = section_index == 0
    field_cols = aerial_patch_grid.shape[1]
    channels = down_weight.shape[3]
    group_width = spectral_filter.shape[0]
    full_rows = spectral_filter.shape[2]
    half_channels = channels // 2
    cell_half = field_cols // 2
    image_part = lax.dynamic_slice_in_dim(
        aerial_patch_grid, section_index * cell_half, cell_half, 1
    )
    layer_two = stem_layers(
        image_part, patch_conv_weight, patch_bias, merging_conv_weight, merge_bias
    )
    left_column = from_behind(layer_two[:, -1:], "section", 1)
    extended = jnp.concatenate([left_column, layer_two], axis=1)
    upper_rim = rim_above(extended)
    feature_half = down_conv(upper_rim, extended, down_weight, down_bias)
    features = lax.all_gather(feature_half, "section", axis=2, tiled=True)
    normed = layer_norm(features, norm_gain)
    cos_h, sin_h = fourier_tables(full_rows)
    cos_w, sin_w = fourier_tables(field_cols)
    forward_table = jnp.stack([cos_w, -sin_w], axis=1)
    forward_h = jnp.stack(
        [jnp.stack([cos_h, sin_h], axis=1), jnp.stack([-sin_h, cos_h], axis=1)], axis=0
    )
    inverse_h = jnp.stack(
        [jnp.stack([cos_h, -sin_h], axis=1), jnp.stack([sin_h, cos_h], axis=1)], axis=0
    )
    inverse_table = jnp.stack([cos_w, -sin_w], axis=0)
    norm_scale = 1.0 / (full_rows * field_cols)
    fields = lax.all_to_all(normed, "tile", split_axis=0, concat_axis=1, tiled=True)

    def whole_filter():
        frequency_rows = jnp.einsum(
            "chx,xqw->chqw", fields, forward_table, preferred_element_type=jnp.float32
        ).astype(jnp.bfloat16)
        back_rows = filter_columns(frequency_rows, spectral_filter, forward_h, inverse_h)
        result = jnp.einsum(
            "chqw,qwv->chv", back_rows, inverse_table, preferred_element_type=jnp.float32
        )
        return (result * norm_scale).astype(jnp.bfloat16)

    def empty_fields():
        return jnp.zeros((group_width, full_rows, field_cols), jnp.bfloat16)

    filtered_fields = lax.cond(first_section, empty_fields, whole_filter)
    rows_back = lax.all_to_all(filtered_fields, "tile", split_axis=1, concat_axis=0, tiled=True)
    returned = from_behind(rows_back[:half_channels], "section", -1)
    filtered = jnp.where(first_section, returned, rows_back[half_channels:])
    own_part = lax.dynamic_slice_in_dim(features, section_index * half_channels, half_channels, 0)
    return (own_part.astype(jnp.float32) + filtered.astype(jnp.float32)).astype(jnp.bfloat16)


DEVICES = ("tile", "section")
VMEM_BYTES = 60 * 1024 * 1024
GELU_LINEAR = 2.0 * math.sqrt(2.0 / math.pi)
GELU_CUBIC = 4.0 * 0.044715 * GELU_LINEAR
ONES = (64, 128, 64)
TAPS = ((1, 1), (1, 2), (2, 1), (2, 2), (1, 0), (2, 0), (0, 1), (0, 2), (0, 0))


def bias_rows(bias, count):
    high = bias.astype(jnp.bfloat16)
    rest = bias - high.astype(jnp.float32)
    middle = rest.astype(jnp.bfloat16)
    low = (rest - middle.astype(jnp.float32)).astype(jnp.bfloat16)
    shape = (count, bias.shape[1])
    row = lax.broadcasted_iota(jnp.int32, shape, 0)
    rows = jnp.zeros(shape, jnp.float32)
    for k, part in enumerate((high, middle, low)):
        rows = jnp.where(row == k, jnp.broadcast_to(part.astype(jnp.float32), shape), rows)
    return rows.astype(jnp.bfloat16)


def build_weights(sources, targets):
    patch_ref, patch_bias_ref, merge_ref, merge_bias_ref, down_ref, down_bias_ref, gain_ref = sources
    w1_ref, w2_ref, w3_ref, column_ref = targets

    def exact(a, b):
        return jnp.dot(
            a.astype(jnp.bfloat16), b.astype(jnp.bfloat16), preferred_element_type=jnp.float32
        )

    taps, width = patch_ref.shape
    row = lax.broadcasted_iota(jnp.int32, (4 * taps, taps), 0)
    col = lax.broadcasted_iota(jnp.int32, (4 * taps, taps), 1)
    pick = jnp.where(row // 16 * 4 + row % 4 == col, 1.0, 0.0)
    row = lax.broadcasted_iota(jnp.int32, (width, 4 * width), 0)
    col = lax.broadcasted_iota(jnp.int32, (width, 4 * width), 1)
    repeat = jnp.where(col % width == row, 1.0, 0.0)
    spread = exact(pick, exact(patch_ref[...], repeat))
    row = lax.broadcasted_iota(jnp.int32, spread.shape, 0)
    col = lax.broadcasted_iota(jnp.int32, spread.shape, 1)
    spread = jnp.where(row // 4 % 4 == col // width, 0.5 * spread, 0.0).astype(jnp.bfloat16)
    bias = jnp.broadcast_to(0.5 * patch_bias_ref[...][None], (8, width))
    tiled = jnp.zeros((8, 4 * width), jnp.float32)
    for _ in range(3):
        part = bias.astype(jnp.bfloat16).astype(jnp.float32)
        tiled = tiled + exact(part, repeat)
        bias = bias - part
    first = jnp.concatenate([spread, bias_rows(tiled[:1], ONES[0])], axis=0)
    w1_ref[...] = first.T
    half = (merge_ref[...].astype(jnp.float32) * 0.5).astype(jnp.bfloat16)
    second = jnp.concatenate([half, bias_rows(0.5 * merge_bias_ref[...][None], ONES[1])], axis=0)
    w2_ref[...] = second.T
    third = [down_ref[3 * a + q] for a, q in TAPS]
    third = jnp.concatenate(third + [bias_rows(down_bias_ref[...][None], ONES[2])], axis=0)
    w3_ref[...] = third.T
    column_ref[...] = jnp.broadcast_to(gain_ref[...][None], (128, gain_ref.shape[0])).T


def weight_sources(
    patch_conv_weight, patch_bias, merging_conv_weight, merge_bias, down_weight, down_bias,
    norm_gain,
):
    width = patch_conv_weight.shape[3]
    merged = merging_conv_weight.shape[3]
    return [
        patch_conv_weight.reshape(-1, width),
        patch_bias,
        merging_conv_weight.reshape(-1, merged),
        merge_bias,
        down_weight.reshape(-1, merged, down_weight.shape[3]),
        down_bias,
        norm_gain,
    ]


def weight_shapes(sources):
    taps, width = sources[0].shape
    merged, channels = sources[4].shape[1:]
    return [
        jax.ShapeDtypeStruct((4 * width, 4 * taps + ONES[0]), jnp.bfloat16),
        jax.ShapeDtypeStruct((merged, 4 * width + ONES[1]), jnp.bfloat16),
        jax.ShapeDtypeStruct((channels, 9 * merged + ONES[2]), jnp.bfloat16),
        jax.ShapeDtypeStruct((channels, 128), jnp.float32),
    ]


def half_gelu(h):
    return h + h * jnp.tanh(h * (GELU_LINEAR + GELU_CUBIC * (h * h)))


def lower_half(row):
    depth = row.shape[1]
    return jnp.concatenate(
        [row[:, 256 * b + 128 : 256 * b + 256] for b in range(depth // 256)], axis=1
    )


def stem_kernel(kind, x_ref, above_ref, *refs):
    sources = refs[:7]
    normed_ref, feat_ref, w1_ref, w2_ref, w3_ref, gain_ref, field = refs[-7:]
    step = pl.program_id(0)
    rows, cols, depth = x_ref.shape
    bands = depth // 256
    channels = w3_ref.shape[0]
    merged = w2_ref.shape[0]
    group = normed_ref.shape[2] // 2
    cells = rows * cols

    @pl.when(step == 0)
    def _():
        build_weights(sources, (w1_ref, w2_ref, w3_ref, gain_ref))

    w1 = w1_ref[...]
    w2 = w2_ref[...]

    def ones(count, n):
        return jnp.where(lax.broadcasted_iota(jnp.int32, (count, n), 0) < 3, 1.0, 0.0).astype(
            jnp.bfloat16
        )

    def layer_one(turned, offsets):
        n = turned.shape[1]
        parts = [turned[o : o + 64] for o in offsets] + [ones(ONES[0], n)]
        h = jnp.dot(w1, jnp.concatenate(parts, axis=0), preferred_element_type=jnp.float32)
        return half_gelu(h).astype(jnp.bfloat16)

    def layer_two(upper, lower, y):
        n = upper.shape[1]
        span = slice(2 * y * (w1.shape[0] // 4), 2 * (y + 1) * (w1.shape[0] // 4))
        stacked = jnp.concatenate([upper[span], lower[span], ones(ONES[1], n)], axis=0)
        return half_gelu(jnp.dot(w2, stacked, preferred_element_type=jnp.float32))

    def shifted(values):
        lanes = lax.broadcasted_iota(jnp.int32, values.shape, 1)
        moved = pltpu.roll(values, 1, 1)
        return jnp.where(lax.rem(lanes, cols) == 0, 0.0, moved)

    def put(block, lanes, values):
        field[block * merged : (block + 1) * merged, lanes] = values.astype(jnp.bfloat16)

    first_row = slice(0, cols)
    last_row = slice(cells - cols, cells)
    later_rows = slice(cols, cells)
    earlier_rows = slice(0, cells - cols)

    @pl.when(step == 0)
    def _():
        field[9 * merged :, :] = ones(ONES[2], cells)
        above = lower_half(above_ref[0])
        keep = 1.0
        if kind == "last":
            lower_section = lax.axis_index("section") > 0
            inside = lower_section | (lax.axis_index("tile") > 0)
            keep = jnp.where(inside, 1.0, 0.0)
            above = jnp.where(lower_section, above, lower_half(refs[7][...]))
        turned = above.T
        upper, lower = (
            layer_one(turned, [128 * b + 64 * a for b in range(bands)]) for a in range(2)
        )
        put(6, first_row, layer_two(upper, lower, 0) * keep)
        right = layer_two(upper, lower, 1) * keep
        put(7, first_row, right)
        put(8, first_row, shifted(right))

    @pl.when(step > 0)
    def _():
        for source, target in ((2, 6), (3, 7), (5, 8)):
            field[target * merged : (target + 1) * merged, first_row] = field[
                source * merged : (source + 1) * merged, last_row
            ]

    turned = x_ref[...].reshape(cells, depth).T
    for x in range(2):
        upper, lower = (
            layer_one(turned, [256 * b + 64 * (2 * x + a) for b in range(bands)])
            for a in range(2)
        )
        left = layer_two(upper, lower, 0)
        right = layer_two(upper, lower, 1)
        put(2 * x, slice(None), left)
        put(2 * x + 1, slice(None), right)
        moved = shifted(right)
        put(4 + x, slice(None), moved)
        if x == 1:
            put(6, later_rows, left[:, earlier_rows])
            put(7, later_rows, right[:, earlier_rows])
            put(8, later_rows, moved[:, earlier_rows])

    features = jnp.dot(w3_ref[...], field[...], preferred_element_type=jnp.float32).astype(
        jnp.bfloat16
    )
    for r in range(rows):
        feat_ref[r] = features[:, r * cols : (r + 1) * cols]
    values = features.astype(jnp.float32)
    centered = values - jnp.mean(values, axis=0, keepdims=True)
    variance = jnp.mean(centered * centered, axis=0, keepdims=True)
    gain = jnp.concatenate([gain_ref[...]] * (cells // 128), axis=1)
    normed = gain * (centered * lax.rsqrt(variance + EPSILON))
    pair = 2 * group
    index = lax.broadcasted_iota(jnp.int32, (pair, cols), 0)
    for t in range(channels // pair):
        for p in range(rows // 2):
            span = slice(pair * t, pair * (t + 1))
            one = normed[span, 2 * p * cols : (2 * p + 1) * cols]
            two = normed[span, (2 * p + 1) * cols : (2 * p + 2) * cols]
            normed_ref[2 * t, p] = jnp.where(
                index < group, one, pltpu.roll(two, group, 0)
            ).astype(jnp.bfloat16)
            normed_ref[2 * t + 1, p] = jnp.where(
                index < group, pltpu.roll(one, group, 0), two
            ).astype(jnp.bfloat16)


def stem(kind, image, weights, first, pairs, devices, extra=()):
    cols, depth = image.shape[1:]
    rows = 2 * pairs
    per_step = 1
    if kind == "first" and all(n % 2 == 0 for n in (pairs, first, image.shape[0] // 4)):
        per_step = 2
    steps = pairs // per_step
    span = 2 * per_step
    shapes = weight_shapes(weights)
    channels, third_depth = shapes[2].shape
    merged = shapes[1].shape[0]
    group = channels // devices

    def section_pairs():
        return lax.axis_index("section") * (image.shape[0] // 4)

    def whole(array):
        return pl.BlockSpec(array.shape, lambda i: (0,) * len(array.shape))

    operands = list(weights) + list(extra)
    in_specs = [whole(a) for a in weights]
    out_specs = [
        pl.BlockSpec((devices, per_step, 2 * group, cols), lambda i: (0, i, 0, 0)),
        pl.BlockSpec((span, channels, cols), lambda i: (i, 0, 0)),
    ]
    out_shape = [
        jax.ShapeDtypeStruct((devices, pairs, 2 * group, cols), jnp.bfloat16),
        jax.ShapeDtypeStruct((rows, channels, cols), jnp.bfloat16),
    ]
    in_specs += [whole(a) for a in extra]
    macs = rows * cols * (16 * 208 * 96 + 4 * 400 * merged + third_depth * channels)
    return pl.pallas_call(
        functools.partial(stem_kernel, kind),
        grid=(steps,),
        in_specs=[
            pl.BlockSpec(
                (span, cols, depth),
                lambda i: ((section_pairs() + first) // per_step + i, 0, 0),
            ),
            pl.BlockSpec(
                (1, cols, depth),
                lambda i: (jnp.maximum(2 * (section_pairs() + first) - 1, 0), 0, 0),
            ),
        ]
        + in_specs,
        out_specs=out_specs,
        scratch_shapes=[pltpu.VMEM(a.shape, a.dtype) for a in shapes]
        + [pltpu.VMEM((third_depth, span * cols), jnp.bfloat16)],
        out_shape=out_shape,
        compiler_params=pltpu.CompilerParams(vmem_limit_bytes=VMEM_BYTES + 3 * 1024 * 1024),
        cost_estimate=pl.CostEstimate(
            flops=4 * macs, bytes_accessed=rows * cols * 3000, transcendentals=0
        ),
        name="stem",
    )(image, image, *operands)


def symmetric_kernel(place_ref, f_ref, turn_w_ref, turn_u_ref, g_ref):
    width = g_ref.shape[3]
    for part in range(2):
        block = f_ref[0, part]
        across = jnp.dot(block, turn_w_ref[...], preferred_element_type=jnp.float32)
        turned = jnp.dot(
            turn_u_ref[...], across.astype(jnp.bfloat16), preferred_element_type=jnp.float32
        )
        own = block[:, :width].astype(jnp.float32)
        both = own + turned if part == 0 else own - turned
        g_ref[0, part] = (0.5 * both).astype(jnp.bfloat16)


def symmetric_filter(spectral_filter, place, group, width):
    full_rows, full_cols = spectral_filter.shape[2:]
    u = jnp.arange(full_rows, dtype=jnp.int32)
    w = jnp.arange(full_cols, dtype=jnp.int32)
    turn_u = ((u[:, None] + u[None, :]) % full_rows == 0).astype(jnp.bfloat16)
    turn_w = ((w[:, None] + w[None, :width]) % full_cols == 0).astype(jnp.bfloat16)
    return pl.pallas_call(
        symmetric_kernel,
        grid_spec=pltpu.PrefetchScalarGridSpec(
            num_scalar_prefetch=1,
            grid=(group,),
            in_specs=[
                pl.BlockSpec(
                    (1, 2, full_rows, full_cols), lambda i, place: (place[0] + i, 0, 0, 0)
                ),
                pl.BlockSpec(turn_w.shape, lambda i, place: (0, 0)),
                pl.BlockSpec(turn_u.shape, lambda i, place: (0, 0)),
            ],
            out_specs=pl.BlockSpec((1, 2, full_rows, width), lambda i, place: (i, 0, 0, 0)),
        ),
        out_shape=jax.ShapeDtypeStruct((group, 2, full_rows, width), jnp.bfloat16),
        compiler_params=pltpu.CompilerParams(vmem_limit_bytes=VMEM_BYTES),
        cost_estimate=pl.CostEstimate(
            flops=8 * group * full_rows * full_cols * width,
            bytes_accessed=group * full_rows * width * 14,
            transcendentals=0,
        ),
        name="symmetric_filter",
    )(place, spectral_filter, turn_w, turn_u)


def to_lane_tiles(target, rows, values):
    for j in range(target.shape[0]):
        target[j, rows, :] = values[:, 128 * j : 128 * (j + 1)]


def from_lane_tiles(source, rows):
    return jnp.concatenate([source[j, rows, :] for j in range(source.shape[0])], axis=1)


RADIX = 3
HALF_ROOT = math.sqrt(3.0) / 2.0


def repack_kernel(devices, early_ref, twiddle_ref, out_ref, turn_ref, held):
    group, length = out_ref.shape[:2]
    turn_ref[...] = twiddle_ref[...]
    rows = length // devices
    to_lane_tiles(held, slice(0, early_ref.shape[0]), early_ref[...].astype(jnp.float32))
    for k in range(group):
        for r in range(rows):
            values = from_lane_tiles(held, pl.ds(r * group + k, devices, stride=rows * group))
            out_ref[k, r * devices : (r + 1) * devices] = values.astype(jnp.bfloat16)


def repack(early, twiddle, group, devices):
    length, cols = early.shape
    return pl.pallas_call(
        functools.partial(repack_kernel, devices),
        out_shape=[
            jax.ShapeDtypeStruct((group, length // group, cols), jnp.bfloat16),
            jax.ShapeDtypeStruct(twiddle.shape, twiddle.dtype),
        ],
        scratch_shapes=[pltpu.VMEM((cols // 128, length + length // devices, 128), jnp.float32)],
        compiler_params=pltpu.CompilerParams(vmem_limit_bytes=VMEM_BYTES),
        cost_estimate=pl.CostEstimate(
            flops=length * cols, bytes_accessed=4 * length * cols, transcendentals=0
        ),
        name="repack",
    )(early, twiddle)


def thirds(values, sign):
    (re0, im0), (re1, im1), (re2, im2) = values
    sum_re, sum_im = re1 + re2, im1 + im2
    turn_re, turn_im = HALF_ROOT * sign * (im1 - im2), HALF_ROOT * sign * (re2 - re1)
    rest_re, rest_im = re0 - 0.5 * sum_re, im0 - 0.5 * sum_im
    return (
        (re0 + sum_re, im0 + sum_im),
        (rest_re + turn_re, rest_im + turn_im),
        (rest_re - turn_re, rest_im - turn_im),
    )


def filter_kernel(
    first, devices, norm_scale, late_ref, early_ref, g_ref, row_table_ref, fwd_ref, inv_ref,
    back_ref, twiddle_ref, out_ref, held, made,
):
    step = pl.program_id(0)
    third = fwd_ref.shape[0] // 2
    full_rows = RADIX * third
    width = g_ref.shape[3]
    count = out_ref.shape[0] // full_rows
    per_step = g_ref.shape[0]
    early = early_ref.shape[1] // devices
    late = full_rows // devices - early
    group = late_ref.shape[0] // (late * devices)

    @pl.when(step == 0)
    def _():
        to_lane_tiles(held, slice(0, late_ref.shape[0]), late_ref[...].astype(jnp.float32))

    def source_rows(k, row):
        if row >= late:
            begin = (row - late) * devices
            return early_ref[k, begin : begin + devices]
        begin = row * group + first + step * per_step + k
        values = from_lane_tiles(held, pl.ds(begin, devices, stride=late * group))
        return values.astype(jnp.bfloat16)

    def twiddles(r):
        cos, sin = twiddle_ref[2 * r - 2], twiddle_ref[2 * r - 1]
        times = per_step * width // 128
        return jnp.concatenate([cos] * times, axis=1), jnp.concatenate([sin] * times, axis=1)

    fields = []
    for k in range(per_step):
        rows = [
            source_rows(k, r + RADIX * q)
            for r in range(RADIX)
            for q in range((late + early) // RADIX)
        ]
        spread = jnp.dot(
            jnp.concatenate(rows, axis=0), row_table_ref[...], preferred_element_type=jnp.float32
        )
        fields.append(spread.astype(jnp.bfloat16))
    parts = []
    for r in range(RADIX):
        span = slice(r * third, (r + 1) * third)
        block = jnp.concatenate(
            [
                jnp.concatenate([f[span, :width], f[span, width:]], axis=0)
                for f in fields
            ],
            axis=1,
        )
        short = jnp.dot(fwd_ref[...], block, preferred_element_type=jnp.float32)
        real, imag = short[:third], short[third:]
        if r > 0:
            cos, sin = twiddles(r)
            real, imag = real * cos + imag * sin, imag * cos - real * sin
        parts.append((real, imag))
    weighted = []
    for r, (real, imag) in enumerate(thirds(parts, 1.0)):
        span = slice(r * third, (r + 1) * third)
        g_real, g_imag = (
            jnp.concatenate([g_ref[k, p, span] for k in range(per_step)], axis=1).astype(
                jnp.float32
            )
            for p in range(2)
        )
        weighted.append((g_real * real - g_imag * imag, g_real * imag + g_imag * real))
    for r, (real, imag) in enumerate(thirds(weighted, -1.0)):
        if r > 0:
            cos, sin = twiddles(r)
            real, imag = real * cos - imag * sin, imag * cos + real * sin
        block = jnp.concatenate([real, imag], axis=0).astype(jnp.bfloat16)
        back = jnp.dot(inv_ref[...], block, preferred_element_type=jnp.float32).astype(
            jnp.bfloat16
        )
        for k in range(per_step):
            lanes = slice(k * width, (k + 1) * width)
            both = jnp.concatenate([back[:third, lanes], back[third:, lanes]], axis=1)
            result = jnp.dot(both, back_ref[...], preferred_element_type=jnp.float32)
            rows = pl.ds(r * count + step * per_step + k, third, stride=RADIX * count)
            to_lane_tiles(made, rows, result * norm_scale)

    @pl.when(step == pl.num_programs(0) - 1)
    def _():
        out_ref[...] = from_lane_tiles(made, slice(0, out_ref.shape[0])).astype(jnp.bfloat16)


def filter_tables(full_rows, field_cols, width, devices):
    third = full_rows // RADIX
    per_device = third // devices
    order = (per_device * np.arange(devices)[None, :] + np.arange(per_device)[:, None]).reshape(-1)
    cos_h, sin_h = fourier_tables(third)
    cos_f, sin_f = fourier_tables(third, order.astype(np.int32))
    cos_w, sin_w = fourier_tables(field_cols)
    fwd = jnp.concatenate(
        [jnp.concatenate([cos_f, sin_f], 1), jnp.concatenate([-sin_f, cos_f], 1)], 0
    )
    inv = jnp.concatenate(
        [jnp.concatenate([cos_h, -sin_h], 1), jnp.concatenate([sin_h, cos_h], 1)], 0
    )
    w = jnp.arange(width, dtype=jnp.int32)
    half = field_cols // 2
    valid = (w <= half).astype(jnp.bfloat16)
    times = jnp.where((w == 0) | (w == half), 1.0, 2.0).astype(jnp.bfloat16) * valid
    row_table = jnp.concatenate([cos_w[:, :width] * valid, -sin_w[:, :width] * valid], 1)
    back_table = jnp.concatenate(
        [cos_w[:width] * times[:, None], -sin_w[:width] * times[:, None]], 0
    )
    turns = np.arange(1, RADIX)[:, None] * np.arange(third)[None, :]
    angles = turns * (2.0 * math.pi / full_rows)
    twiddle = np.stack([np.cos(angles), np.sin(angles)], axis=1).reshape(-1, third, 1)
    twiddle = np.broadcast_to(twiddle.astype(np.float32), (2 * RADIX - 2, third, 128))
    twiddle = jnp.asarray(twiddle)
    return row_table, fwd, inv, back_table, twiddle


def filter_channels(late, early, symmetric, tables, first, count, per_step, devices):
    full_rows, width = symmetric.shape[2:]
    group, early_rows = early.shape[:2]
    cols = late.shape[1]

    def whole(array):
        return pl.BlockSpec(array.shape, lambda i: (0,) * array.ndim)

    macs = count * (4 * full_rows * full_rows * width + 4 * full_rows * cols * width)
    made = pl.pallas_call(
        functools.partial(filter_kernel, first, devices, 1.0 / (full_rows * cols)),
        grid=(count // per_step,),
        in_specs=[
            whole(late),
            pl.BlockSpec((per_step, early_rows, cols), lambda i: (first // per_step + i, 0, 0)),
            pl.BlockSpec(
                (per_step, 2, full_rows, width), lambda i: (first // per_step + i, 0, 0, 0)
            ),
        ]
        + [whole(table) for table in tables],
        out_specs=pl.BlockSpec((full_rows * count, cols), lambda i: (0, 0)),
        out_shape=jax.ShapeDtypeStruct((full_rows * count, cols), jnp.bfloat16),
        scratch_shapes=[
            pltpu.VMEM((cols // 128, late.shape[0] + late.shape[0] // devices, 128), jnp.float32),
            pltpu.VMEM((cols // 128, (full_rows + 8) * count, 128), jnp.float32),
        ],
        compiler_params=pltpu.CompilerParams(vmem_limit_bytes=VMEM_BYTES),
        cost_estimate=pl.CostEstimate(
            flops=2 * macs, bytes_accessed=count * full_rows * cols * 8, transcendentals=0
        ),
        name="spectral_filter",
    )(late, early, symmetric, *tables)
    return made.reshape(devices, full_rows // devices * count, cols)


def residual_kernel(first, count, chunks, kept_hbm, other_hbm, feat_hbm, *refs):
    out_hbm, kept, other, feat, out, held, done = refs[-7:]
    halves, span = other.shape[:2]
    rows = 2 * span // count
    groups = halves // chunks
    section = lax.axis_index("section")

    def block(c):
        return pl.ds(c * groups, groups)

    def copies(c):
        source = pl.ds(section * halves + c * groups, groups)
        channels = pl.ds(first, count)
        return [
            pltpu.make_async_copy(kept_hbm.at[source], kept.at[block(c)], done.at[0, c]),
            pltpu.make_async_copy(other_hbm.at[block(c)], other.at[block(c)], done.at[1, c]),
            pltpu.make_async_copy(
                feat_hbm.at[block(c), channels], feat.at[block(c)], done.at[2, c]
            ),
        ]

    def result(c):
        channels = pl.ds(first, count)
        return pltpu.make_async_copy(
            out.at[block(c)], out_hbm.at[block(c), channels], done.at[3, c]
        )

    for c in range(chunks):
        for copy in copies(c):
            copy.start()
    own = pl.multiple_of(section * span, 8)
    far = pl.multiple_of((1 - section) * span, 8)
    for c in range(chunks):
        for copy in copies(c):
            copy.wait()
        for g in range(c * groups, (c + 1) * groups):
            to_lane_tiles(held, pl.ds(own, span), kept[g].astype(jnp.float32))
            to_lane_tiles(held, pl.ds(far, span), other[g].astype(jnp.float32))
            for k in range(count):
                filtered = from_lane_tiles(held, pl.ds(k, rows, stride=count))
                out[g, k] = (feat[g, k].astype(jnp.float32) + filtered).astype(jnp.bfloat16)
        result(c).start()
    for c in range(chunks):
        result(c).wait()


def add_residual(returned, other, features, previous, first, count):
    halves, span, cols = other.shape
    group, rows = features.shape[1:3]
    chunks = 4 if halves % 4 == 0 else 1
    operands = [returned, other, features]
    aliases = {}
    if previous is not None:
        operands.append(previous)
        aliases = {3: 0}
    return pl.pallas_call(
        functools.partial(residual_kernel, first, count, chunks),
        in_specs=[pl.BlockSpec(memory_space=pl.ANY)] * len(operands),
        out_specs=pl.BlockSpec(memory_space=pl.ANY),
        scratch_shapes=[
            pltpu.VMEM((halves, span, cols), jnp.bfloat16),
            pltpu.VMEM((halves, span, cols), jnp.bfloat16),
            pltpu.VMEM((halves, count, rows, cols), jnp.bfloat16),
            pltpu.VMEM((halves, count, rows, cols), jnp.bfloat16),
            pltpu.VMEM((cols // 128, (rows + 8) * count, 128), jnp.float32),
            pltpu.SemaphoreType.DMA((4, chunks)),
        ],
        out_shape=jax.ShapeDtypeStruct(features.shape, jnp.bfloat16),
        input_output_aliases=aliases,
        compiler_params=pltpu.CompilerParams(vmem_limit_bytes=VMEM_BYTES),
        cost_estimate=pl.CostEstimate(
            flops=halves * count * rows * cols,
            bytes_accessed=halves * count * rows * cols * 8,
            transcendentals=0,
        ),
        name="residual",
    )(*operands)


def swap(block):
    return lax.ppermute(block, "section", [(0, 1), (1, 0)])


def local(
    aerial_patch_grid,
    patch_conv_weight,
    patch_bias,
    merging_conv_weight,
    merge_bias,
    down_weight,
    down_bias,
    norm_gain,
    spectral_filter,
):
    tile_rows, field_cols, depth = aerial_patch_grid.shape
    channels = down_weight.shape[3]
    tile_channels = spectral_filter.shape[0]
    full_rows = spectral_filter.shape[2]
    sections = lax.axis_size("section")
    devices = sections * lax.axis_size("tile")
    rows = tile_rows // 2
    suits = (
        sections == 2
        and tile_rows % 8 == 0
        and tile_rows >= 16
        and field_cols % 128 == 0
        and full_rows % (128 * RADIX) == 0
        and rows % RADIX == 0
        and devices % 8 == 0
        and tile_channels % 8 == 0
    )
    arguments = (
        aerial_patch_grid,
        patch_conv_weight,
        patch_bias,
        merging_conv_weight,
        merge_bias,
        down_weight,
        down_bias,
        norm_gain,
        spectral_filter,
    )
    if not suits:
        return general_local(*arguments)
    section = lax.axis_index("section")
    group = tile_channels // 2
    half_channels = channels // 2
    width = -(-(field_cols // 2 + 1) // 128) * 128

    arriving = lax.ppermute(
        aerial_patch_grid[-1],
        ("section", "tile"),
        [(i, i + 1) for i in range(lax.axis_size("tile") - 1)],
    )
    sources = weight_sources(*arguments[1:8])
    pairs = rows // 2
    early = max(pairs // 3, 1)
    late = pairs - early
    normed_early, feat_early = stem(
        "first", aerial_patch_grid, sources, late, early, devices
    )
    normed_early, arriving = lax.optimization_barrier((normed_early, arriving))
    normed_late, feat_late = stem(
        "last", aerial_patch_grid, sources, 0, late, devices, (arriving,)
    )
    spread = [
        lax.all_to_all(normed, DEVICES, split_axis=0, concat_axis=0, tiled=True).reshape(
            -1, field_cols
        )
        for normed in (normed_early, normed_late)
    ]
    late_fields = spread[1]
    features = jnp.concatenate([feat_late, feat_early], axis=0)

    channel_place = jnp.reshape(section * group, (1,)).astype(jnp.int32)
    symmetric = symmetric_filter(spectral_filter, channel_place, group, width)
    *tables, twiddle = filter_tables(full_rows, field_cols, width, devices)
    early_fields, twiddle = repack(spread[0], twiddle, group, devices)
    tables.append(twiddle)

    own = lax.dynamic_slice_in_dim(features, section * half_channels, half_channels, 1)
    sent = lax.dynamic_slice_in_dim(features, (1 - section) * half_channels, half_channels, 1)
    arrived = swap(sent)
    low = jnp.where(section == 0, own, arrived)
    high = jnp.where(section == 0, arrived, own)
    residual = jnp.transpose(jnp.concatenate([low, high], axis=0), (1, 0, 2))
    residual = residual.reshape(half_channels // group, group, tile_rows, field_cols)
    late_fields, residual = lax.optimization_barrier((late_fields, residual))

    halves = devices // 2
    output = None
    rest = group - 2
    per_step = 5 if rest % 5 == 0 else 2
    for first, count, per_step in ((rest, 2, 2), (0, rest, per_step)):
        made = filter_channels(
            late_fields, early_fields, symmetric, tables, first, count, per_step, devices
        )
        returned = lax.all_to_all(made, DEVICES, split_axis=0, concat_axis=0, tiled=True)
        if output is not None:
            returned, output = lax.optimization_barrier((returned, output))
        other = swap(lax.dynamic_slice_in_dim(returned, (1 - section) * halves, halves, 0))
        output = add_residual(returned, other, residual, output, first, count)
    return output.reshape(half_channels, tile_rows, field_cols)


def solution(mesh):
    return jax.shard_map(
        local,
        mesh=mesh,
        in_specs=(
            P("tile", None, None),
            P(),
            P(),
            P(),
            P(),
            P(),
            P(),
            P(),
            P("tile", None, None, None),
        ),
        out_specs=P("section", "tile", None),
        check_vma=False,
    )
```
